32 devices in a mesh: sweep: 4 (over z), plane: 8 (over y, x, core).
Axes of the slice: x: 2, y: 2, z: 4, core: 2. Of those that a mesh axis runs over, the one named last changes fastest.
Arguments:
- rhs_field: float32 [8, 2, 8, 8192], P('sweep', None, None, 'plane'), may hold values from -6 to 6
- front_inverse: bfloat16 [8, 2, 4096, 4096], P('sweep', None, 'plane'), may hold values from -1.5 to 1.5
- interior_scale: float32 [8, 8192], P('sweep', 'plane'), may hold values from 0.7 to 1.2
- forward_coupling: float32 [8, 8192], P('sweep', 'plane'), may hold values from 0.85 to 1
- backward_coupling: float32 [8, 8192], P('sweep', 'plane'), may hold values from 0.85 to 1
- front_cells: int32 [8, 4096], P('sweep', 'plane'), may hold values from 0 to 1023, as said below
- section_layers: int32 [4], replicated, may hold values from 1 to 2, 6 in all
Outputs:
- sweep_out: float32 [8, 2, 8, 8192], P('sweep', None, None, 'plane')
The draws below stay inside these ranges and needn't reach their ends.
Inputs may be any that keep to these rules, and one draw needn't show every extreme that they name: `front_cells`: entry f of a layer indexes a cell within the brick of device f // 512 of plane; the 512 entries of one layer and device are distinct, and the two layers of one section name disjoint cells on every device. `section_layers`: A section with 1 has no second layer.
All inputs are finite; a program needn't handle non-finite values.
Results may differ from the reference program's by a relative error of at most 0.0044.
Values may be sent and summed in bfloat16 or wider, within the bound.
No kernel may reach another device: no remote copies, remote signals or barrier semaphores. Data moves between devices by JAX's collectives and lax.ppermute only.
A program may use at most 64 MiB of HBM per device.

```python
import math
import jax
import jax.numpy as jnp
import numpy as np

FRONT = 4096
BRICK = 1024
RHS = 8
FR_DEV = 512
SECTIONS = 4
LAYERS = 8
CELLS = 8192


def draw_front_inverse(key, part):
    full_shape = (LAYERS, 2, FRONT, FRONT)
    spread = 0.5 * FRONT ** (-0.5)
    offdiag = jax.random.truncated_normal(key, -4.0, 4.0, full_shape, jnp.float32) * spread
    row_index = jnp.arange(FRONT)[:, None]
    col_index = jnp.arange(FRONT)[None, :]
    diagonal = (row_index == col_index).astype(jnp.float32)
    component = (jnp.arange(2) == 0).astype(jnp.float32)[:, None, None]
    return (offdiag + component * diagonal).astype(jnp.bfloat16)


def draw_front_cells(key, part):
    sections = LAYERS // 2
    owners = FRONT // FR_DEV
    subkeys = jax.random.split(key, sections * owners)
    orders = jax.vmap(lambda single: jax.random.permutation(single, BRICK))(subkeys)
    chosen = orders[:, :2 * FR_DEV].reshape(sections, owners, 2, FR_DEV)
    return chosen.transpose(0, 2, 1, 3).reshape(LAYERS, FRONT).astype(jnp.int32)


def shard_levels(rng, shape, cuts, least, top_value):
    factor_of = 1.0
    for axis_at, blocks in cuts:
        draws = jax.random.uniform(jax.random.fold_in(jax.random.fold_in(rng, 6), axis_at), (blocks,), jnp.float32, least / len(cuts), top_value / len(cuts))
        factor_of = factor_of * jnp.repeat(jnp.exp(draws), shape[axis_at] // blocks).reshape((-1,) + (1,) * (len(shape) - 1 - axis_at))
    return factor_of


def length_profile(number_of, total, limit, skew):
    portions = [(1 << 20) // math.isqrt(standing ** skew) + 1 for standing in range(2, number_of + 1)]
    rest, counts = total - limit - (number_of - 1), [1] * (number_of - 1)
    while rest > 0:
        free = [i for i in range(number_of - 1) if counts[i] < limit]
        mass, budget = sum([portions[i] for i in free]), rest
        for i in free:
            more = min(limit - counts[i], max(1, budget * portions[i] // mass), rest)
            counts[i] = counts[i] + more
            rest = rest - more
    return np.array([limit] + counts)


def uneven(stream_key, number_of, total, bound, skew):
    if number_of == 2:
        one = jax.random.randint(stream_key, (), max(1, total - bound), min(bound, total - 1) + 1)
        return jnp.stack([one, total - one])
    lengths = jnp.asarray(length_profile(number_of, total, bound, skew), jnp.int32)
    pairs = (number_of - 1) // 2
    giver, sink = lengths[1:1 + 2 * pairs:2], lengths[2:2 + 2 * pairs:2]
    room = jnp.minimum(giver - 1, bound - sink)
    shifted = jax.random.randint(jax.random.fold_in(stream_key, 1), (pairs,), 0, 1 << 20) % (room + 1)
    lengths = lengths.at[1:1 + 2 * pairs:2].set(giver - shifted).at[2:2 + 2 * pairs:2].set(sink + shifted)
    return lengths[jax.random.permutation(jax.random.fold_in(stream_key, 2), number_of)]


def centred(rng, extent, deviation, bound, shards=(), kind=jnp.bfloat16):
    drawn = deviation * jax.random.normal(rng, extent, jnp.float32)
    if shards:
        drawn = drawn * shard_levels(rng, extent, shards, -0.22, 0.18)
    return jnp.clip(drawn, -bound, bound).astype(kind)


def setup_inputs(seed: int = 0) -> dict:
    key_list = jax.random.split(jax.random.key(seed), 8)
    return {
        "rhs_field": centred(key_list[0], (LAYERS, 2, RHS, CELLS), 1.0, 6.0, ((0, 4), (3, 8)), jnp.float32),
        "front_inverse": draw_front_inverse(jax.random.fold_in(key_list[7], 71), 0),
        "interior_scale": jnp.clip(0.7 + 0.50000006 * jax.random.uniform(key_list[2], (LAYERS, CELLS), jnp.float32) ** shard_levels(key_list[2], (LAYERS, CELLS), ((0, 4), (1, 8)), -0.2, 0.2), 0.7, 1.2),
        "forward_coupling": jnp.clip(0.85 + 0.14999998 * jax.random.uniform(key_list[3], (LAYERS, CELLS), jnp.float32) ** shard_levels(key_list[3], (LAYERS, CELLS), ((0, 4), (1, 8)), -0.2, 0.2), 0.85, 1.0),
        "backward_coupling": jnp.clip(0.85 + 0.14999998 * jax.random.uniform(key_list[4], (LAYERS, CELLS), jnp.float32) ** shard_levels(key_list[4], (LAYERS, CELLS), ((0, 4), (1, 8)), -0.2, 0.2), 0.85, 1.0),
        "front_cells": draw_front_cells(jax.random.fold_in(key_list[7], 71), 0),
        "section_layers": uneven(key_list[6], SECTIONS, SECTIONS * 3 // 2, 2, 0).astype(jnp.int32),
    }


def front_positions(front_cells, layer_index):
    owners = jnp.arange(FRONT, dtype=jnp.int32) // FR_DEV
    return (owners * BRICK + front_cells[layer_index]).astype(jnp.int32)


def front_solve(front_inverse, layer_index, layer_field, positions):
    values = jnp.take(layer_field, positions, axis=2).astype(jnp.bfloat16)
    stacked = jnp.concatenate([values[0], values[1]], axis=0)
    direct = jnp.dot(front_inverse[layer_index, 0], stacked.T, preferred_element_type=jnp.float32)
    crossed = jnp.dot(front_inverse[layer_index, 1], stacked.T, preferred_element_type=jnp.float32)
    real_part = (direct[:, :RHS] - crossed[:, RHS:]).T
    imag_part = (direct[:, RHS:] + crossed[:, :RHS]).T
    return jnp.stack([real_part, imag_part])


def replace_cells(layer_field, positions, values):
    return layer_field.at[:, :, positions].set(values)


def reference(rhs_field, front_inverse, interior_scale, forward_coupling, backward_coupling, front_cells, section_layers):
    incoming = jnp.zeros((2, RHS, CELLS), jnp.float32)
    forward_layers = []
    for section in range(SECTIONS):
        first = 2 * section
        second = first + 1
        active = section_layers[section] == 2
        first_cells = front_positions(front_cells, first)
        second_cells = front_positions(front_cells, second)
        first_res = rhs_field[first] - forward_coupling[first] * incoming
        first_sol = replace_cells(interior_scale[first] * first_res, first_cells,
                                  front_solve(front_inverse, first, first_res, first_cells))
        second_res = rhs_field[second] - forward_coupling[second] * first_sol
        second_sol = replace_cells(interior_scale[second] * second_res, second_cells,
                                   front_solve(front_inverse, second, second_res, second_cells))
        forward_layers.append(first_sol)
        forward_layers.append(second_sol)
        incoming = jnp.where(active, second_sol, first_sol)
    outgoing = jnp.zeros((2, RHS, CELLS), jnp.float32)
    results = [None] * LAYERS
    for section in reversed(range(SECTIONS)):
        first = 2 * section
        second = first + 1
        active = section_layers[section] == 2
        first_cells = front_positions(front_cells, first)
        second_cells = front_positions(front_cells, second)
        first_fwd = forward_layers[first]
        second_fwd = forward_layers[second]
        second_z = backward_coupling[second] * outgoing
        second_sol = replace_cells(second_fwd - interior_scale[second] * second_z, second_cells,
                                   jnp.take(second_fwd, second_cells, axis=2)
                                   - front_solve(front_inverse, second, second_z, second_cells))
        following = jnp.where(active, second_sol, outgoing)
        first_z = backward_coupling[first] * following
        first_sol = replace_cells(first_fwd - interior_scale[first] * first_z, first_cells,
                                  jnp.take(first_fwd, first_cells, axis=2)
                                  - front_solve(front_inverse, first, first_z, first_cells))
        results[first] = first_sol
        results[second] = jnp.where(active, second_sol, 0.0)
        outgoing = first_sol
    return jnp.stack(results)
```

```python
import functools

import jax
import jax.numpy as jnp
from jax import lax
from jax.experimental import pallas as pl
from jax.experimental.pallas import tpu as pltpu
from jax.sharding import PartitionSpec as P

LANES = 128
ISC, FWD, BWD, PICK = 0, 2, 4, 6
F32, BF16 = jnp.float32, jnp.bfloat16


def split(field):
    return [field[:, at:at + LANES] for at in range(0, field.shape[1], LANES)]


def gather_lanes(chunks, index, beyond=None):
    result = []
    for place, part in enumerate(split(index)):
        part = jnp.broadcast_to(part, chunks[0].shape)
        lane, chunk = part & (LANES - 1), part >> (LANES.bit_length() - 1)
        total = jnp.zeros(chunks[0].shape, F32) if beyond is None else beyond[place]
        for number, source in enumerate(chunks):
            found = jnp.take_along_axis(source, lane, axis=1, mode="promise_in_bounds")
            total = jnp.where(chunk == number, found, total)
        result.append(total)
    return result


def scaled(row, chunks):
    return [part * chunk for part, chunk in zip(split(row), chunks)]


def minus(left, right):
    return [a - b for a, b in zip(left, right)]


def choose(flag, left, right):
    return [jnp.where(flag, a, b) for a, b in zip(left, right)]


def rounded(chunks):
    return [c.astype(BF16).astype(F32) for c in chunks]


def row_of(ref, at):
    return ref[at:at + 1, :]


def picks(ref, at, width):
    return ref[at:at + 1, :width].astype(jnp.int32)


def forward_front(rhs_a, rhs_b, small, incoming, width):
    first = rhs_a if incoming is None else minus(rhs_a, scaled(row_of(small, FWD), incoming))
    second = minus(rhs_b, scaled(row_of(small, FWD + 1), scaled(row_of(small, ISC), first)))
    return (
        gather_lanes(rounded(first), picks(small, PICK, width))
        + gather_lanes(rounded(second), picks(small, PICK + 1, width))
    )


def backward_front(small, incoming, second_fwd, both, width):
    z = scaled(row_of(small, BWD + 1), incoming)
    local = minus(second_fwd, scaled(row_of(small, ISC + 1), z))
    first = scaled(row_of(small, BWD), choose(both, local, incoming))
    return (
        gather_lanes(rounded(first), picks(small, PICK, width))
        + gather_lanes(rounded(z), picks(small, PICK + 1, width))
    )


def write_packet(ref, fronts, field):
    at = 0
    for chunk in fronts:
        ref[at] = chunk.astype(BF16)
        at += 1
    high = [c.astype(BF16) for c in field]
    low = [(c - h.astype(F32)).astype(BF16) for c, h in zip(field, high)]
    for chunk in high + low:
        ref[at] = chunk
        at += 1


def read_field(ref, start, count):
    return [
        ref[start + i].astype(F32) + ref[start + count + i].astype(F32) for i in range(count)
    ]


def solve(gathered, inverse, stacked, solved, layer):
    owners, slots = gathered.shape[:2]
    per_layer = slots // 2
    half = gathered.shape[2] // 2
    for owner in range(owners):
        for i in range(per_layer):
            at = (owner * per_layer + i) * LANES
            piece = gathered[owner, layer * per_layer + i]
            wide = piece.astype(F32)
            turned = jnp.concatenate([-wide[half:], wide[:half]], axis=0)
            stacked[0, :, at:at + LANES] = piece
            stacked[1, :, at:at + LANES] = turned.astype(BF16)
    dims = (((1,), (1,)), ((), ()))
    out = lax.dot_general(inverse[layer, 0], stacked[0], dims, preferred_element_type=F32)
    out = out + lax.dot_general(inverse[layer, 1], stacked[1], dims, preferred_element_type=F32)
    rows = out.shape[0]
    if rows % LANES:
        out = jnp.concatenate([out, jnp.zeros((-rows % LANES, out.shape[1]), F32)], axis=0)
    solved[layer] = out.T


def places(picked_column, cells):
    rows = picked_column.shape[0]
    cell = lax.broadcasted_iota(jnp.int32, (rows, cells), 1)
    row = lax.broadcasted_iota(jnp.int32, (rows, cells), 0)
    return jnp.max(jnp.where(picked_column == cell, row, -1), axis=0, keepdims=True)


def first_kernel(width, rhs, isc, fwd, bwd, picked, column, packet, small, place, front):
    cells = rhs.shape[-1]
    count = rhs.shape[1]
    small[ISC:ISC + 2, :] = isc[...]
    small[FWD:FWD + 2, :] = fwd[...]
    small[BWD:BWD + 2, :] = bwd[...]
    small[PICK:PICK + 2, :] = jnp.full((2, cells), -1, F32)
    small[PICK:PICK + 2, :width] = picked[...].astype(F32)
    packet[0:count, :] = rhs[0]
    packet[count:2 * count, :] = rhs[1]
    packet[2 * count:, :] = small[...]
    for layer in range(2):
        place[layer:layer + 1, :] = places(column[layer], cells)
    chunks = forward_front(split(rhs[0]), split(rhs[1]), small, None, width)
    for owner in range(front.shape[0]):
        for at, chunk in enumerate(chunks):
            front[owner, at] = chunk.astype(BF16)


def forward_kernel(
    step, sections, width, layers, gathered, inverse, rhs, small, place, after, incoming,
    before, kept, packet, stacked, solved,
):
    own = lax.axis_index("sweep")
    cells = rhs.shape[-1]
    count = cells // LANES
    fronts = 2 * width // LANES
    rows = rhs.shape[1]

    @pl.when(own != step)
    def _():
        kept[...] = before[...]

    @pl.when(own == step)
    def _():
        both = layers[own] == 2
        solve(gathered, inverse, stacked, solved, 0)

        @pl.when(both)
        def _():
            solve(gathered, inverse, stacked, solved, 1)

        arriving = None if step == 0 else read_field(incoming, fronts, count)
        rhs_a, rhs_b = split(rhs[0]), split(rhs[1])
        first_res = rhs_a
        if arriving is not None:
            first_res = minus(rhs_a, scaled(row_of(small, FWD), arriving))
        first = gather_lanes(
            split(solved[0]), place[0:1, :], scaled(row_of(small, ISC), first_res)
        )
        second_res = minus(rhs_b, scaled(row_of(small, FWD + 1), first))
        second = gather_lanes(
            split(solved[1]), place[1:2, :], scaled(row_of(small, ISC + 1), second_res)
        )
        for i in range(count):
            kept[0, :, i * LANES:(i + 1) * LANES] = first[i]
            kept[1, :, i * LANES:(i + 1) * LANES] = second[i]
        if step < sections - 1:
            outgoing = choose(both, second, first)
            ahead = after.at[2 * rows:]
            chunks = forward_front(
                split(after[0:rows, :]), split(after[rows:2 * rows, :]), ahead, outgoing, width
            )
            write_packet(packet, chunks, outgoing)
        else:
            z = scaled(row_of(small, BWD), choose(both, second, [jnp.zeros_like(c) for c in first]))
            chunks = gather_lanes(rounded(z), picks(small, PICK, width))
            for owner in range(packet.shape[0]):
                for at, chunk in enumerate(chunks):
                    packet[owner, at] = chunk.astype(BF16)
                for at in range(len(chunks), fronts):
                    packet[owner, at] = jnp.zeros_like(chunks[0]).astype(BF16)


def backward_kernel(
    step, sections, width, layers, gathered, inverse, small, place, behind, held, kept,
    incoming, before, result, packet, stacked, solved,
):
    own = lax.axis_index("sweep")
    cells = kept.shape[-1]
    count = cells // LANES
    fronts = 2 * width // LANES
    last = step == sections - 1

    @pl.when(own != step)
    def _():
        result[...] = before[...]

    @pl.when(own == step)
    def _():
        both = layers[own] == 2

        def first_solve():
            solve(gathered, inverse, stacked, solved, 0)

        if last:
            pl.when(both)(first_solve)
        else:
            first_solve()

            @pl.when(both)
            def _():
                solve(gathered, inverse, stacked, solved, 1)

        first_fwd, second_fwd = split(kept[0]), split(kept[1])
        zero = [jnp.zeros_like(c) for c in first_fwd]
        if last:
            second, arriving = second_fwd, zero
        else:
            arriving = read_field(incoming, fronts, count)
            z = scaled(row_of(small, BWD + 1), arriving)
            local = scaled(row_of(small, ISC + 1), z)
            second = minus(second_fwd, gather_lanes(split(solved[1]), place[1:2, :], local))
        following = choose(both, second, arriving)
        z = scaled(row_of(small, BWD), following)
        local = scaled(row_of(small, ISC), z)
        change = gather_lanes(split(solved[0]), place[0:1, :], local)
        if last:
            change = choose(both, change, zero)
        first = minus(first_fwd, change)
        second = choose(both, second, zero)
        for i in range(count):
            result[0, :, i * LANES:(i + 1) * LANES] = first[i]
            result[1, :, i * LANES:(i + 1) * LANES] = second[i]
        if step > 0:
            chunks = backward_front(
                behind, first, read_field(held, fronts, count), layers[own - 1] == 2, width
            )
            write_packet(packet, chunks, first)


def whole(space=pltpu.VMEM):
    return pl.BlockSpec(memory_space=space)


def call(kernel, operands, outs, scratch, name):
    specs = [whole(pltpu.SMEM) if o.ndim == 1 else whole() for o in operands]
    return pl.pallas_call(
        kernel,
        in_specs=specs,
        out_specs=[whole()] * len(outs),
        out_shape=[jax.ShapeDtypeStruct(s, t) for s, t in outs],
        scratch_shapes=scratch,
        compiler_params=pltpu.CompilerParams(vmem_limit_bytes=8 * 2**20),
        name=name,
    )(*operands)


def shards(
    rhs_field,
    front_inverse,
    interior_scale,
    forward_coupling,
    backward_coupling,
    front_cells,
    section_layers,
):
    sections, planes = lax.axis_size("sweep"), lax.axis_size("plane")
    layer_slots, parts, columns, cells = rhs_field.shape
    rows = parts * columns
    owned, order = front_inverse.shape[2:]
    width = -(-owned // LANES) * LANES
    count, per_layer = cells // LANES, width // LANES
    fronts = 2 * per_layer

    rhs = rhs_field.reshape(layer_slots, rows, cells)
    picked = jnp.pad(front_cells, ((0, 0), (0, width - owned)), constant_values=-1)
    inverse = pltpu.with_memory_space_constraint(front_inverse, pltpu.VMEM)

    front_shape = ((planes, fronts, rows, LANES), BF16)
    packet_shape = ((fronts + 2 * count, rows, LANES), BF16)
    field_shape = ((layer_slots, rows, cells), F32)
    scratch = [
        pltpu.VMEM((2, rows, order), BF16),
        pltpu.VMEM((2, rows, width), F32),
    ]

    def exchange(spread):
        gathered = lax.all_to_all(spread, "plane", 0, 0)
        if owned != width:
            gathered = gathered.reshape(planes, 2, per_layer, rows, LANES)
            gathered = gathered.transpose(1, 3, 0, 2, 4).reshape(2, rows, planes, width)
            gathered = gathered[..., :owned].reshape(2, rows, order // LANES, LANES)
            gathered = gathered.transpose(0, 2, 1, 3).reshape(1, 2 * order // LANES, rows, LANES)
        return gathered

    def everywhere(packet):
        return jnp.broadcast_to(packet[None, :fronts], front_shape[0])

    packet, small, place, front = call(
        functools.partial(first_kernel, width),
        [rhs, interior_scale, forward_coupling, backward_coupling, picked,
         front_cells[:, :, None]],
        [((2 * rows + 8, cells), F32), ((8, cells), F32), ((2, cells), jnp.int32), front_shape],
        [],
        "first_fronts",
    )
    upward = [(i, i + 1) for i in range(sections - 1)]
    downward = [(i + 1, i) for i in range(sections - 1)]
    after = lax.ppermute(packet, "sweep", downward)
    behind = lax.ppermute(small, "sweep", upward)

    kept = jnp.zeros(field_shape[0], F32)
    held = jnp.zeros(packet_shape[0], BF16)
    incoming = held
    for step in range(sections):
        final = step == sections - 1
        gathered = exchange(front)
        kept, packet = call(
            functools.partial(forward_kernel, step, sections, width),
            [section_layers, gathered, inverse, rhs, small, place, after, incoming, kept],
            [field_shape, front_shape if final else packet_shape],
            scratch,
            f"forward_section_{step}",
        )
        if final:
            front = packet
        else:
            incoming = lax.ppermute(packet, "sweep", [(step, step + 1)])
            held = jnp.where(lax.axis_index("sweep") == step + 1, incoming, held)
            front = everywhere(incoming)

    result = kept
    for step in reversed(range(sections)):
        gathered = exchange(front)
        result, packet = call(
            functools.partial(backward_kernel, step, sections, width),
            [section_layers, gathered, inverse, small, place, behind, held, kept, incoming, result],
            [field_shape, packet_shape],
            scratch,
            f"backward_section_{step}",
        )
        if step:
            incoming = lax.ppermute(packet, "sweep", [(step, step - 1)])
            front = everywhere(incoming)
    return result.reshape(rhs_field.shape)


def solution(mesh):
    in_specs = (
        P("sweep", None, None, "plane"),
        P("sweep", None, "plane", None),
        P("sweep", "plane"),
        P("sweep", "plane"),
        P("sweep", "plane"),
        P("sweep", "plane"),
        P(),
    )
    out_specs = P("sweep", None, None, "plane")
    return jax.shard_map(shards, mesh=mesh, in_specs=in_specs, out_specs=out_specs, check_vma=False)
```

```python
import functools

import jax
import jax.numpy as jnp
from jax import lax
from jax.experimental import pallas as pl
from jax.experimental.pallas import tpu as pltpu
from jax.sharding import PartitionSpec as P

LANES = 128
CORES = 2
ISC, FWD, BWD, PICK = 0, 2, 4, 6
F32, BF16 = jnp.float32, jnp.bfloat16


def split(field):
    return [field[:, at:at + LANES] for at in range(0, field.shape[1], LANES)]


def gather_lanes(chunks, index, beyond=None):
    result = []
    for place, part in enumerate(split(index)):
        part = jnp.broadcast_to(part, chunks[0].shape)
        lane, chunk = part & (LANES - 1), part >> (LANES.bit_length() - 1)
        total = jnp.zeros(chunks[0].shape, F32) if beyond is None else beyond[place]
        for number, source in enumerate(chunks):
            found = jnp.take_along_axis(source, lane, axis=1, mode="promise_in_bounds")
            total = jnp.where(chunk == number, found, total)
        result.append(total)
    return result


def scaled(row, chunks):
    return [part * chunk for part, chunk in zip(split(row), chunks)]


def minus(left, right):
    return [a - b for a, b in zip(left, right)]


def choose(flag, left, right):
    return [jnp.where(flag, a, b) for a, b in zip(left, right)]


def rounded(chunks):
    return [c.astype(BF16).astype(F32) for c in chunks]


def row_of(ref, at):
    return ref[at:at + 1, :]


def picks(ref, at, width):
    return ref[at:at + 1, :width].astype(jnp.int32)


def forward_front(rhs_a, rhs_b, small, incoming, width):
    first = rhs_a if incoming is None else minus(rhs_a, scaled(row_of(small, FWD), incoming))
    second = minus(rhs_b, scaled(row_of(small, FWD + 1), scaled(row_of(small, ISC), first)))
    return (
        gather_lanes(rounded(first), picks(small, PICK, width))
        + gather_lanes(rounded(second), picks(small, PICK + 1, width))
    )


def backward_front(small, incoming, second_fwd, both, width):
    z = scaled(row_of(small, BWD + 1), incoming)
    local = minus(second_fwd, scaled(row_of(small, ISC + 1), z))
    first = scaled(row_of(small, BWD), choose(both, local, incoming))
    return (
        gather_lanes(rounded(first), picks(small, PICK, width))
        + gather_lanes(rounded(z), picks(small, PICK + 1, width))
    )


def write_front(ref, chunks):
    for at, chunk in enumerate(chunks):
        ref[at] = chunk.astype(BF16)
    for at in range(len(chunks), ref.shape[0]):
        ref[at] = jnp.zeros(ref.shape[1:], BF16)


def write_field(ref, chunks):
    for at, chunk in enumerate(chunks):
        ref[:, at * LANES:(at + 1) * LANES] = chunk


def sources(blocks, planes):
    if len(blocks) == 1:
        return [range(blocks[0].shape[0])]
    chips = planes // CORES
    own = lax.axis_index("plane")
    chip, core = own // CORES, lax.rem(own, CORES)
    behind = [lax.rem(chip - step + chips, chips) * CORES for step in range(chips)]
    return [[b + core for b in behind], [b + (CORES - 1 - core) for b in behind]]


def solve(blocks, planes, inverse, stacked, solved, layer):
    for gathered, owners in zip(blocks, sources(blocks, planes)):
        per_layer = gathered.shape[1] // 2
        half = gathered.shape[2] // 2
        for block, owner in enumerate(owners):
            for i in range(per_layer):
                at = pl.multiple_of((owner * per_layer + i) * LANES, LANES)
                piece = gathered[block, layer * per_layer + i]
                wide = piece.astype(F32)
                turned = jnp.concatenate([-wide[half:], wide[:half]], axis=0)
                stacked[0, :, pl.ds(at, LANES)] = piece
                stacked[1, :, pl.ds(at, LANES)] = turned.astype(BF16)
    dims = (((1,), (1,)), ((), ()))
    out = lax.dot_general(inverse[layer, 0], stacked[0], dims, preferred_element_type=F32)
    out = out + lax.dot_general(inverse[layer, 1], stacked[1], dims, preferred_element_type=F32)
    rows = out.shape[0]
    if rows % LANES:
        out = jnp.concatenate([out, jnp.zeros((-rows % LANES, out.shape[1]), F32)], axis=0)
    solved[layer] = out.T


def places(picked, cells):
    rows = picked.shape[1]
    column = jnp.broadcast_to(picked.astype(F32), (8, rows)).T[:, 0:1].astype(jnp.int32)
    cell = lax.broadcasted_iota(jnp.int32, (rows, cells), 1)
    row = lax.broadcasted_iota(jnp.int32, (rows, cells), 0)
    return jnp.max(jnp.where(column == cell, row, -1), axis=0, keepdims=True)


def first_kernel(
    width, rhs_in, isc_in, fwd_in, bwd_in, picked_in, packet, small, place, front,
    rhs, isc, fwd, bwd, picked, sems,
):
    pairs = ((rhs_in, rhs), (isc_in, isc), (fwd_in, fwd), (bwd_in, bwd), (picked_in, picked))
    copies = [pltpu.make_async_copy(a, b, sems.at[i]) for i, (a, b) in enumerate(pairs)]
    for copy in copies:
        copy.start()
    for copy in copies:
        copy.wait()
    cells = rhs.shape[-1]
    count = rhs.shape[1]
    small[ISC:ISC + 2, :] = isc[...]
    small[FWD:FWD + 2, :] = fwd[...]
    small[BWD:BWD + 2, :] = bwd[...]
    small[PICK:PICK + 2, :] = jnp.full((2, cells), -1, F32)
    small[PICK:PICK + 2, :width] = picked[...].astype(F32)
    packet[0:count, :] = rhs[0]
    packet[count:2 * count, :] = rhs[1]
    packet[2 * count:, :] = small[...]
    for layer in range(2):
        place[layer:layer + 1, :] = places(picked[layer:layer + 1, :], cells)
    write_front(front, forward_front(split(rhs[0]), split(rhs[1]), small, None, width))


def forward_kernel(step, sections, planes, width, blocks, layers, inverse, packet, place, *rest):
    gathered, rest = rest[:blocks], rest[blocks:]
    if step:
        incoming, *rest = rest
    if step < sections - 1:
        after, *rest = rest
    kept, front, *rest = rest
    if step < sections - 1:
        field, *rest = rest
    stacked, solved = rest
    own = lax.axis_index("sweep")
    cells = packet.shape[-1]
    rows = kept.shape[1]
    small = packet.at[2 * rows:]

    @pl.when(own == step)
    def _():
        both = layers[own] == 2
        solve(gathered, planes, inverse, stacked, solved, 0)

        @pl.when(both)
        def _():
            solve(gathered, planes, inverse, stacked, solved, 1)

        rhs_a, rhs_b = split(packet[0:rows, :]), split(packet[rows:2 * rows, :])
        first_res = rhs_a
        if step:
            first_res = minus(rhs_a, scaled(row_of(small, FWD), split(incoming[...])))
        first = gather_lanes(
            split(solved[0]), place[0:1, :], scaled(row_of(small, ISC), first_res)
        )
        second_res = minus(rhs_b, scaled(row_of(small, FWD + 1), first))
        second = gather_lanes(
            split(solved[1]), place[1:2, :], scaled(row_of(small, ISC + 1), second_res)
        )
        write_field(kept.at[0], first)
        write_field(kept.at[1], second)
        if step < sections - 1:
            outgoing = choose(both, second, first)
            write_field(field, outgoing)
            ahead = after.at[2 * rows:]
            write_front(front, forward_front(
                split(after[0:rows, :]), split(after[rows:2 * rows, :]), ahead, outgoing, width
            ))
        else:
            z = scaled(row_of(small, BWD), choose(both, second, [jnp.zeros_like(c) for c in first]))
            write_front(front, gather_lanes(rounded(z), picks(small, PICK, width)))


def backward_kernel(step, sections, planes, width, blocks, layers, inverse, small, place, *rest):
    gathered, rest = rest[:blocks], rest[blocks:]
    kept, *rest = rest
    last = step == sections - 1
    if not last:
        incoming, before, *rest = rest
    if step:
        behind, held, *rest = rest
    result, *rest = rest
    if step:
        front, field, *rest = rest
    stacked, solved = rest
    own = lax.axis_index("sweep")

    if not last:
        @pl.when(own != step)
        def _():
            result[...] = before[...]

    @pl.when(own == step)
    def _():
        both = layers[own] == 2

        def first_solve():
            solve(gathered, planes, inverse, stacked, solved, 0)

        if last:
            pl.when(both)(first_solve)
        else:
            first_solve()

            @pl.when(both)
            def _():
                solve(gathered, planes, inverse, stacked, solved, 1)

        first_fwd, second_fwd = split(kept[0]), split(kept[1])
        zero = [jnp.zeros_like(c) for c in first_fwd]
        if last:
            second, arriving = second_fwd, zero
        else:
            arriving = split(incoming[...])
            z = scaled(row_of(small, BWD + 1), arriving)
            local = scaled(row_of(small, ISC + 1), z)
            second = minus(second_fwd, gather_lanes(split(solved[1]), place[1:2, :], local))
        following = choose(both, second, arriving)
        z = scaled(row_of(small, BWD), following)
        local = scaled(row_of(small, ISC), z)
        change = gather_lanes(split(solved[0]), place[0:1, :], local)
        if last:
            change = choose(both, change, zero)
        first = minus(first_fwd, change)
        write_field(result.at[0], first)
        write_field(result.at[1], choose(both, second, zero))
        if step:
            write_field(field, first)
            write_front(front, backward_front(
                behind, first, split(held[...]), layers[own - 1] == 2, width
            ))


def whole(space=pltpu.VMEM):
    return pl.BlockSpec(memory_space=space)


def call(kernel, operands, outs, scratch, name, space=pltpu.VMEM):
    specs = [whole(pltpu.SMEM if o.ndim == 1 else space) for o in operands]
    return pl.pallas_call(
        kernel,
        in_specs=specs,
        out_specs=[whole()] * len(outs),
        out_shape=[jax.ShapeDtypeStruct(s, t) for s, t in outs],
        scratch_shapes=scratch,
        compiler_params=pltpu.CompilerParams(vmem_limit_bytes=8 * 2**20),
        name=name,
    )(*operands)


def shards(
    rhs_field,
    front_inverse,
    interior_scale,
    forward_coupling,
    backward_coupling,
    front_cells,
    section_layers,
):
    sections, planes = lax.axis_size("sweep"), lax.axis_size("plane")
    layer_slots, parts, columns, cells = rhs_field.shape
    rows = parts * columns
    owned, order = front_inverse.shape[2:]
    width = -(-owned // LANES) * LANES
    per_layer = width // LANES
    chips = planes // CORES
    direct = planes == chips * CORES and chips <= 4 and owned == width

    rhs = rhs_field.reshape(layer_slots, rows, cells)
    picked = jnp.pad(front_cells, ((0, 0), (0, width - owned)), constant_values=-1)
    inverse = pltpu.with_memory_space_constraint(front_inverse, pltpu.VMEM)

    front_shape = ((2 * per_layer, rows, LANES), BF16)
    field_shape = ((rows, cells), F32)
    layers_shape = ((layer_slots, rows, cells), F32)
    scratch = [
        pltpu.VMEM((2, rows, order), BF16),
        pltpu.VMEM((2, rows, width), F32),
    ]

    def send(block, start, stop, chip_step=0, other_core=False):
        route = []
        for own in range(planes):
            chip, core = own // CORES, own % CORES
            chip = (chip + chip_step) % chips
            core = CORES - 1 - core if other_core else core
            route.append((start * planes + own, stop * planes + chip * CORES + core))
        return lax.ppermute(block, ("sweep", "plane"), route)

    def pass_on(block, start, stop):
        return lax.ppermute(block, "sweep", [(start, stop)])

    def exchange(front, start, stop):
        if not direct:
            if start != stop:
                front = pass_on(front, start, stop)
            gathered = lax.all_gather(front, "plane")
            if owned != width:
                gathered = gathered.reshape(planes, 2, per_layer, rows, LANES)
                gathered = gathered.transpose(1, 3, 0, 2, 4).reshape(2, rows, planes, width)
                gathered = gathered[..., :owned].reshape(2, rows, order // LANES, LANES)
                gathered = gathered.transpose(0, 2, 1, 3)
                gathered = gathered.reshape(1, 2 * order // LANES, rows, LANES)
            return [gathered]
        mine = [
            front if start == stop and not step else send(front, start, stop, step)
            for step in range(chips)
        ]
        mine = jnp.stack(mine)
        return [mine, send(mine, stop, stop, other_core=True)]

    packet, small, place, front = call(
        functools.partial(first_kernel, width),
        [rhs, interior_scale, forward_coupling, backward_coupling, picked],
        [((2 * rows + 8, cells), F32), ((8, cells), F32), ((2, cells), jnp.int32), front_shape],
        [
            pltpu.VMEM(rhs.shape, F32),
            pltpu.VMEM(interior_scale.shape, F32),
            pltpu.VMEM(forward_coupling.shape, F32),
            pltpu.VMEM(backward_coupling.shape, F32),
            pltpu.VMEM(picked.shape, jnp.int32),
            pltpu.SemaphoreType.DMA((5,)),
        ],
        "first_fronts",
        pltpu.HBM,
    )
    gathered = exchange(front, 0, 0)
    after = lax.ppermute(packet, "sweep", [(i + 1, i) for i in range(sections - 1)])
    behind = lax.ppermute(small, "sweep", [(i, i + 1) for i in range(sections - 1)])

    kept, held = [], [None]
    for step in range(sections):
        final = step == sections - 1
        extra = ([held[step]] if step else []) + ([] if final else [after])
        outs = call(
            functools.partial(forward_kernel, step, sections, planes, width, len(gathered)),
            [section_layers, inverse, packet, place, *gathered, *extra],
            [layers_shape, front_shape] + ([] if final else [field_shape]),
            scratch,
            f"forward_section_{step}",
        )
        kept.append(outs[0])
        gathered = exchange(outs[1], step, step if final else step + 1)
        if not final:
            held.append(pass_on(outs[2], step, step + 1))

    result = incoming = None
    for step in reversed(range(sections)):
        extra = ([] if result is None else [incoming, result]) + ([behind, held[step]] if step else [])
        outs = call(
            functools.partial(backward_kernel, step, sections, planes, width, len(gathered)),
            [section_layers, inverse, small, place, *gathered, kept[step], *extra],
            [layers_shape] + ([front_shape, field_shape] if step else []),
            scratch,
            f"backward_section_{step}",
        )
        result = outs[0]
        if step:
            gathered = exchange(outs[1], step, step - 1)
            incoming = pass_on(outs[2], step, step - 1)
    return result.reshape(rhs_field.shape)


def solution(mesh):
    in_specs = (
        P("sweep", None, None, "plane"),
        P("sweep", None, "plane", None),
        P("sweep", "plane"),
        P("sweep", "plane"),
        P("sweep", "plane"),
        P("sweep", "plane"),
        P(),
    )
    out_specs = P("sweep", None, None, "plane")
    return jax.shard_map(shards, mesh=mesh, in_specs=in_specs, out_specs=out_specs, check_vma=False)
```

```python
import functools

import jax
import jax.numpy as jnp
from jax import lax
from jax.experimental import pallas as pl
from jax.experimental.pallas import tpu as pltpu
from jax.sharding import PartitionSpec as P

LANES = 128
CORES = 2
ISC, FWD, BWD, PICK = 0, 2, 4, 6
F32, BF16 = jnp.float32, jnp.bfloat16


def split(field):
    return [field[:, at:at + LANES] for at in range(0, field.shape[1], LANES)]


def gather_lanes(chunks, index, beyond=None):
    result = []
    for place, part in enumerate(split(index)):
        part = jnp.broadcast_to(part, chunks[0].shape)
        lane, chunk = part & (LANES - 1), part >> (LANES.bit_length() - 1)
        total = jnp.zeros(chunks[0].shape, F32) if beyond is None else beyond[place]
        for number, source in enumerate(chunks):
            found = jnp.take_along_axis(source, lane, axis=1, mode="promise_in_bounds")
            total = jnp.where(chunk == number, found, total)
        result.append(total)
    return result


def scaled(row, chunks):
    return [part * chunk for part, chunk in zip(split(row), chunks)]


def minus(left, right):
    return [a - b for a, b in zip(left, right)]


def choose(flag, left, right):
    return [jnp.where(flag, a, b) for a, b in zip(left, right)]


def rounded(chunks):
    return [c.astype(BF16).astype(F32) for c in chunks]


def row_of(ref, at):
    return ref[at:at + 1, :]


def picks(ref, at, width):
    return ref[at:at + 1, :width].astype(jnp.int32)


def forward_front(rhs_a, rhs_b, small, incoming, width):
    first = rhs_a if incoming is None else minus(rhs_a, scaled(row_of(small, FWD), incoming))
    second = minus(rhs_b, scaled(row_of(small, FWD + 1), scaled(row_of(small, ISC), first)))
    return (
        gather_lanes(rounded(first), picks(small, PICK, width))
        + gather_lanes(rounded(second), picks(small, PICK + 1, width))
    )


def backward_front(small, incoming, second_fwd, both, width):
    z = scaled(row_of(small, BWD + 1), incoming)
    local = minus(second_fwd, scaled(row_of(small, ISC + 1), z))
    first = scaled(row_of(small, BWD), choose(both, local, incoming))
    return (
        gather_lanes(rounded(first), picks(small, PICK, width))
        + gather_lanes(rounded(z), picks(small, PICK + 1, width))
    )


def write_front(ref, chunks, field=()):
    high = [c.astype(BF16) for c in field]
    low = [(c - h.astype(F32)).astype(BF16) for c, h in zip(field, high)]
    for at, chunk in enumerate(chunks + high + low):
        ref[at] = chunk.astype(BF16)


def read_field(packet, count):
    start = packet.shape[0] - 2 * count
    return [
        packet[start + i].astype(F32) + packet[start + count + i].astype(F32)
        for i in range(count)
    ]


def write_field(ref, chunks):
    for at, chunk in enumerate(chunks):
        ref[:, at * LANES:(at + 1) * LANES] = chunk


def owner_of(place, planes):
    if isinstance(place, int):
        return place
    step, other = place
    chips = planes // CORES
    own = lax.axis_index("plane")
    chip, core = own // CORES, lax.rem(own, CORES)
    chip = lax.rem(chip - step + chips, chips) if step else chip
    return chip * CORES + (CORES - 1 - core if other else core)


def stack_fronts(blocks, owners, planes, per_layer, stacked, layer):
    for ref, places in zip(blocks, owners):
        for number, place in enumerate(places):
            owner = owner_of(place, planes)
            for i in range(per_layer):
                at = pl.multiple_of((owner * per_layer + i) * LANES, LANES)
                slot = layer * per_layer + i
                piece = ref[slot] if len(ref.shape) == 3 else ref[number, slot]
                half = piece.shape[0] // 2
                wide = piece.astype(F32)
                turned = jnp.concatenate([-wide[half:], wide[:half]], axis=0)
                stacked[0, :, pl.ds(at, LANES)] = piece
                stacked[1, :, pl.ds(at, LANES)] = turned.astype(BF16)


def product(matrix, columns):
    return lax.dot_general(
        matrix, columns, (((1,), (1,)), ((), ())), preferred_element_type=F32
    )


def store_solved(solved, layer, out):
    rows = out.shape[0]
    if rows % LANES:
        out = jnp.concatenate([out, jnp.zeros((-rows % LANES, out.shape[1]), F32)], axis=0)
    solved[layer] = out.T


def solve(inverse, stacked, solved, layer):
    out = product(inverse[layer, 0], stacked[0]) + product(inverse[layer, 1], stacked[1])
    store_solved(solved, layer, out)


def places(picked, cells):
    rows = picked.shape[1]
    column = jnp.broadcast_to(picked.astype(F32), (8, rows)).T[:, 0:1].astype(jnp.int32)
    cell = lax.broadcasted_iota(jnp.int32, (rows, cells), 1)
    row = lax.broadcasted_iota(jnp.int32, (rows, cells), 0)
    return jnp.max(jnp.where(column == cell, row, -1), axis=0, keepdims=True)


def first_kernel(
    width, rhs_in, isc_in, fwd_in, bwd_in, picked_in, packet, small, place, front,
    rhs, isc, fwd, bwd, picked, sems,
):
    pairs = ((rhs_in, rhs), (isc_in, isc), (fwd_in, fwd), (bwd_in, bwd), (picked_in, picked))
    copies = [pltpu.make_async_copy(a, b, sems.at[i]) for i, (a, b) in enumerate(pairs)]
    for copy in copies:
        copy.start()
    for copy in copies:
        copy.wait()
    cells = rhs.shape[-1]
    count = rhs.shape[1]
    small[ISC:ISC + 2, :] = isc[...]
    small[FWD:FWD + 2, :] = fwd[...]
    small[BWD:BWD + 2, :] = bwd[...]
    small[PICK:PICK + 2, :] = jnp.full((2, cells), -1, F32)
    small[PICK:PICK + 2, :width] = picked[...].astype(F32)
    packet[0:count, :] = rhs[0]
    packet[count:2 * count, :] = rhs[1]
    packet[2 * count:, :] = small[...]
    for layer in range(2):
        place[layer:layer + 1, :] = places(picked[layer:layer + 1, :], cells)
    write_front(front, forward_front(split(rhs[0]), split(rhs[1]), small, None, width))


def forward_kernel(
    step, sections, planes, width, per_layer, owners, layers, inverse, packet, place, *rest
):
    blocks, rest = rest[:len(owners)], rest[len(owners):]
    final = step == sections - 1
    if step:
        incoming, *rest = rest
    if not final:
        after, *rest = rest
    kept, front, *rest = rest
    if not final:
        outgoing_packet, *rest = rest
    if step:
        resident, (stacked, solved) = inverse, rest
    else:
        resident, stacked, solved, kept_sum, sems = rest
    own = lax.axis_index("sweep")
    cells = packet.shape[-1]
    count = cells // LANES
    rows = kept.shape[1]
    order = inverse.shape[-1]
    small = packet.at[2 * rows:]
    mine = own == step
    both = layers[step] == 2

    def fill(layer):
        stack_fronts(blocks, owners, planes, per_layer, stacked, layer)

    if step:
        @pl.when(mine)
        def _():
            fill(0)
            solve(resident, stacked, solved, 0)

        @pl.when(mine & both)
        def _():
            fill(1)
            solve(resident, stacked, solved, 1)
    else:
        cuts = 2 if order % (2 * LANES) == 0 else 1
        depth = order // cuts
        copies = {}
        for layer in range(2):
            for cut in range(cuts):
                for part in range(2):
                    piece = (layer, part, slice(None), pl.ds(cut * depth, depth))
                    copies[layer, cut, part] = pltpu.make_async_copy(
                        inverse.at[piece], resident.at[piece], sems.at[len(copies)]
                    )
        for copy in copies.values():
            copy.start()
        for layer in range(2):
            needed = mine if layer == 0 else mine & both

            @pl.when(needed)
            def _():
                fill(layer)

            for cut in range(cuts):
                for part in range(2):
                    copies[layer, cut, part].wait()

                @pl.when(needed)
                def _():
                    columns = pl.ds(cut * depth, depth)
                    out = product(resident[layer, 0, :, columns], stacked[0, :, columns])
                    out = out + product(resident[layer, 1, :, columns], stacked[1, :, columns])
                    if cut == cuts - 1:
                        if cut:
                            out = out + kept_sum[...]
                        store_solved(solved, layer, out)
                    else:
                        kept_sum[...] = out

    @pl.when(mine)
    def _():
        rhs_a, rhs_b = split(packet[0:rows, :]), split(packet[rows:2 * rows, :])
        first_res = rhs_a
        if step:
            first_res = minus(rhs_a, scaled(row_of(small, FWD), read_field(incoming, count)))
        first = gather_lanes(
            split(solved[0]), place[0:1, :], scaled(row_of(small, ISC), first_res)
        )
        second_res = minus(rhs_b, scaled(row_of(small, FWD + 1), first))
        second = gather_lanes(
            split(solved[1]), place[1:2, :], scaled(row_of(small, ISC + 1), second_res)
        )
        if final:
            z = scaled(row_of(small, BWD), choose(both, second, [jnp.zeros_like(c) for c in first]))
            write_front(front, gather_lanes(rounded(z), picks(small, PICK, width)))
        else:
            outgoing = choose(both, second, first)
            ahead = after.at[2 * rows:]
            chunks = forward_front(
                split(after[0:rows, :]), split(after[rows:2 * rows, :]), ahead, outgoing, width
            )
            write_front(front, chunks)
            write_front(outgoing_packet, chunks, outgoing)
        write_field(kept.at[0], first)
        write_field(kept.at[1], second)


def backward_kernel(
    step, sections, planes, width, per_layer, owners, layers, inverse, small, place, *rest
):
    blocks, rest = rest[:len(owners)], rest[len(owners):]
    kept, *rest = rest
    last = step == sections - 1
    if not last:
        incoming, before, *rest = rest
    if step:
        behind, *rest = rest
        held, *rest = rest
    result, *rest = rest
    if step:
        front, outgoing_packet, *rest = rest
    stacked, solved = rest
    own = lax.axis_index("sweep")
    count = kept.shape[-1] // LANES
    mine = own == step
    both = layers[step] == 2

    def whole_solve(layer):
        stack_fronts(blocks, owners, planes, per_layer, stacked, layer)
        solve(inverse, stacked, solved, layer)

    if not last:
        @pl.when(own != step)
        def _():
            result[...] = before[...]

        @pl.when(mine & both)
        def _():
            whole_solve(1)

    @pl.when(mine & both if last else mine)
    def _():
        whole_solve(0)

    @pl.when(mine)
    def _():
        first_fwd, second_fwd = split(kept[0]), split(kept[1])
        zero = [jnp.zeros_like(c) for c in first_fwd]
        if last:
            second, arriving = second_fwd, zero
        else:
            arriving = read_field(incoming, count)
            z = scaled(row_of(small, BWD + 1), arriving)
            local = scaled(row_of(small, ISC + 1), z)
            second = minus(second_fwd, gather_lanes(split(solved[1]), place[1:2, :], local))
        following = choose(both, second, arriving)
        z = scaled(row_of(small, BWD), following)
        local = scaled(row_of(small, ISC), z)
        change = gather_lanes(split(solved[0]), place[0:1, :], local)
        if last:
            change = choose(both, change, zero)
        first = minus(first_fwd, change)
        if step:
            chunks = backward_front(
                behind, first, read_field(held, count), layers[step - 1] == 2, width
            )
            write_front(front, chunks)
            write_front(outgoing_packet, chunks, first)
        write_field(result.at[0], first)
        write_field(result.at[1], choose(both, second, zero))


def whole(space=pltpu.VMEM):
    return pl.BlockSpec(memory_space=space)


def call(kernel, operands, outs, scratch, name, spaces=()):
    specs = [whole(pltpu.SMEM if o.ndim == 1 else pltpu.VMEM) for o in operands]
    for at, space in spaces:
        specs[at] = whole(space)
    return pl.pallas_call(
        kernel,
        in_specs=specs,
        out_specs=[whole()] * len(outs),
        out_shape=[jax.ShapeDtypeStruct(*o) if isinstance(o, tuple) else o for o in outs],
        scratch_shapes=scratch,
        compiler_params=pltpu.CompilerParams(vmem_limit_bytes=8 * 2**20),
        name=name,
    )(*operands)


def in_hbm(array):
    return pltpu.with_memory_space_constraint(array, pltpu.HBM)


def shards(
    rhs_field,
    front_inverse,
    interior_scale,
    forward_coupling,
    backward_coupling,
    front_cells,
    section_layers,
):
    sections, planes = lax.axis_size("sweep"), lax.axis_size("plane")
    layer_slots, parts, columns, cells = rhs_field.shape
    rows = parts * columns
    owned, order = front_inverse.shape[2:]
    width = -(-owned // LANES) * LANES
    per_layer = width // LANES
    chips = planes // CORES
    direct = planes == chips * CORES and chips <= 4 and owned == width

    rhs = rhs_field.reshape(layer_slots, rows, cells)
    picked = jnp.pad(front_cells, ((0, 0), (0, width - owned)), constant_values=-1)
    layers = section_layers

    half_shape = ((per_layer, rows, LANES), BF16)
    front_shape = ((2 * per_layer, rows, LANES), BF16)
    packet_shape = ((2 * per_layer + 2 * (cells // LANES), rows, LANES), BF16)
    layers_shape = ((layer_slots, rows, cells), F32)
    scratch = [
        pltpu.VMEM((2, rows, order), BF16),
        pltpu.VMEM((2, rows, width), F32),
    ]

    def send(block, start, stop, chip_step=0, other_core=False):
        route = []
        for own in range(planes):
            chip, core = own // CORES, own % CORES
            chip = (chip + chip_step) % chips
            core = CORES - 1 - core if other_core else core
            route.append((start * planes + own, stop * planes + chip * CORES + core))
        return lax.ppermute(block, ("sweep", "plane"), route)

    def everywhere(front):
        slots = front.shape[0] // per_layer
        gathered = lax.all_gather(front, "plane")
        if owned != width:
            gathered = gathered.reshape(planes, slots, per_layer, rows, LANES)
            gathered = gathered.transpose(1, 3, 0, 2, 4).reshape(slots, rows, planes, width)
            gathered = gathered[..., :owned].reshape(slots, rows, order // LANES, LANES)
            gathered = gathered.transpose(0, 2, 1, 3)
            gathered = gathered.reshape(slots * order // LANES, rows, LANES)
            return [gathered], [[0]], order // LANES
        return [gathered], [list(range(planes))], per_layer

    def within(front, section):
        if not direct:
            return everywhere(front)
        mine = [front] + [send(front, section, section, s) for s in range(1, chips)]
        swapped = send(jnp.stack(mine), section, section, other_core=True)
        owners = [[(s, False)] for s in range(chips)] + [[(s, True) for s in range(chips)]]
        return mine + [swapped], owners, per_layer

    def between(front, packet, start, stop):
        if not direct:
            packet = lax.ppermute(packet, "sweep", [(start, stop)])
            return *everywhere(packet[:2 * per_layer]), packet
        other = send(front, start, stop, other_core=True)
        across = [send(front, start, stop, s) for s in range(1, chips)]
        packet = send(packet, start, stop)
        relayed = [send(other, stop, stop, s) for s in range(1, chips)]
        owners = [[(0, True)], [(0, False)]]
        owners += [[(s, False)] for s in range(1, chips)] + [[(s, True)] for s in range(1, chips)]
        return [other, packet] + across + relayed, owners, per_layer, packet

    packet, small, place, front = call(
        functools.partial(first_kernel, width),
        [in_hbm(a) for a in (rhs, interior_scale, forward_coupling, backward_coupling, picked)],
        [((2 * rows + 8, cells), F32), ((8, cells), F32), ((2, cells), jnp.int32), front_shape],
        [
            pltpu.VMEM(rhs.shape, F32),
            pltpu.VMEM(interior_scale.shape, F32),
            pltpu.VMEM(forward_coupling.shape, F32),
            pltpu.VMEM(backward_coupling.shape, F32),
            pltpu.VMEM(picked.shape, jnp.int32),
            pltpu.SemaphoreType.DMA((5,)),
        ],
        "first_fronts",
        [(i, pltpu.HBM) for i in range(5)],
    )
    gathered, owners, slots = within(front, 0)
    after = lax.ppermute(packet, "sweep", [(i + 1, i) for i in range(sections - 1)])
    behind = lax.ppermute(small, "sweep", [(i, i + 1) for i in range(sections - 1)])

    inverse = in_hbm(front_inverse)
    kept, held = [], [None]
    for step in range(sections):
        final = step == sections - 1
        extra = ([held[step]] if step else []) + ([] if final else [after])
        outs = [layers_shape, half_shape if final else front_shape]
        outs += [] if final else [packet_shape]
        outs += [] if step else [pltpu.VMEM(front_inverse.shape, BF16)]
        room = [] if step else [
            pltpu.VMEM((owned, rows), F32), pltpu.SemaphoreType.DMA((8,))
        ]
        outs = call(
            functools.partial(
                forward_kernel, step, sections, planes, width, slots, owners
            ),
            [layers, inverse, packet, place, *gathered, *extra],
            outs,
            scratch + room,
            f"forward_section_{step}",
            [] if step else [(1, pltpu.HBM)],
        )
        if not step:
            inverse = outs[-1]
        kept.append(outs[0])
        if final:
            gathered, owners, slots = within(outs[1], step)
        else:
            gathered, owners, slots, incoming = between(outs[1], outs[2], step, step + 1)
            held.append(incoming)

    result = incoming = None
    for step in reversed(range(sections)):
        extra = ([] if result is None else [incoming, result]) + ([behind, held[step]] if step else [])
        outs = call(
            functools.partial(
                backward_kernel, step, sections, planes, width, slots, owners
            ),
            [layers, inverse, small, place, *gathered, kept[step], *extra],
            [layers_shape] + ([front_shape, packet_shape] if step else []),
            scratch,
            f"backward_section_{step}",
        )
        result = outs[0]
        if step:
            gathered, owners, slots, incoming = between(outs[1], outs[2], step, step - 1)
    return result.reshape(rhs_field.shape)


def solution(mesh):
    in_specs = (
        P("sweep", None, None, "plane"),
        P("sweep", None, "plane", None),
        P("sweep", "plane"),
        P("sweep", "plane"),
        P("sweep", "plane"),
        P("sweep", "plane"),
        P(),
    )
    out_specs = P("sweep", None, None, "plane")
    return jax.shard_map(shards, mesh=mesh, in_specs=in_specs, out_specs=out_specs, check_vma=False)
```

```python
import functools

import jax
import jax.numpy as jnp
from jax import lax
from jax.experimental import pallas as pl
from jax.experimental.pallas import tpu as pltpu
from jax.sharding import PartitionSpec as P

LANES = 128
CORES = 2
ISC, FWD, BWD, PICK = 0, 2, 4, 6
F32, BF16 = jnp.float32, jnp.bfloat16


def split(field):
    return [field[:, at:at + LANES] for at in range(0, field.shape[1], LANES)]


def gather_lanes(chunks, index, beyond=None):
    result = []
    for place, part in enumerate(split(index)):
        part = jnp.broadcast_to(part, chunks[0].shape)
        lane, chunk = part & (LANES - 1), part >> (LANES.bit_length() - 1)
        total = jnp.zeros(chunks[0].shape, F32) if beyond is None else beyond[place]
        for number, source in enumerate(chunks):
            found = jnp.take_along_axis(source, lane, axis=1, mode="promise_in_bounds")
            total = jnp.where(chunk == number, found, total)
        result.append(total)
    return result


def scaled(row, chunks):
    return [part * chunk for part, chunk in zip(split(row), chunks)]


def minus(left, right):
    return [a - b for a, b in zip(left, right)]


def choose(flag, left, right):
    return [jnp.where(flag, a, b) for a, b in zip(left, right)]


def rounded(chunks):
    return [c.astype(BF16).astype(F32) for c in chunks]


def row_of(ref, at):
    return ref[at:at + 1, :]


def picks(ref, at, width):
    return ref[at:at + 1, :width].astype(jnp.int32)


def forward_front(rhs_a, rhs_b, small, incoming, width):
    first = rhs_a if incoming is None else minus(rhs_a, scaled(row_of(small, FWD), incoming))
    second = minus(rhs_b, scaled(row_of(small, FWD + 1), scaled(row_of(small, ISC), first)))
    return (
        gather_lanes(rounded(first), picks(small, PICK, width))
        + gather_lanes(rounded(second), picks(small, PICK + 1, width))
    )


def backward_front(small, incoming, second_fwd, both, width):
    z = scaled(row_of(small, BWD + 1), incoming)
    local = minus(second_fwd, scaled(row_of(small, ISC + 1), z))
    first = scaled(row_of(small, BWD), choose(both, local, incoming))
    return (
        gather_lanes(rounded(first), picks(small, PICK, width))
        + gather_lanes(rounded(z), picks(small, PICK + 1, width))
    )


def write_front(ref, chunks, field=()):
    high = [c.astype(BF16) for c in field]
    low = [(c - h.astype(F32)).astype(BF16) for c, h in zip(field, high)]
    for at, chunk in enumerate(chunks + high + low):
        ref[at] = chunk.astype(BF16)


def read_field(packet, count):
    start = packet.shape[0] - 2 * count
    return [
        packet[start + i].astype(F32) + packet[start + count + i].astype(F32)
        for i in range(count)
    ]


def write_field(ref, chunks):
    for at, chunk in enumerate(chunks):
        ref[:, at * LANES:(at + 1) * LANES] = chunk


def owner_of(place, planes):
    if isinstance(place, int):
        return place
    step, other = place
    return lax.bitwise_xor(lax.axis_index("plane"), step * CORES + int(other))


def stack_fronts(blocks, owners, planes, per_layer, stacked, layer):
    for ref, places in zip(blocks, owners):
        for number, place in enumerate(places):
            owner = owner_of(place, planes)
            for i in range(per_layer):
                at = pl.multiple_of((owner * per_layer + i) * LANES, LANES)
                slot = layer * per_layer + i
                piece = ref[slot] if len(ref.shape) == 3 else ref[number, slot]
                half = piece.shape[0] // 2
                wide = piece.astype(F32)
                turned = jnp.concatenate([-wide[half:], wide[:half]], axis=0)
                stacked[0, :, pl.ds(at, LANES)] = piece
                stacked[1, :, pl.ds(at, LANES)] = turned.astype(BF16)


def product(matrix, columns):
    return lax.dot_general(
        matrix, columns, (((1,), (1,)), ((), ())), preferred_element_type=F32
    )


def store_solved(solved, layer, out):
    rows = out.shape[0]
    if rows % LANES:
        out = jnp.concatenate([out, jnp.zeros((-rows % LANES, out.shape[1]), F32)], axis=0)
    solved[layer] = out.T


def solve(inverse, stacked, solved, layer):
    out = product(inverse[layer, 0], stacked[0]) + product(inverse[layer, 1], stacked[1])
    store_solved(solved, layer, out)


def places(picked, cells):
    rows = picked.shape[1]
    column = jnp.broadcast_to(picked.astype(F32), (8, rows)).T[:, 0:1].astype(jnp.int32)
    cell = lax.broadcasted_iota(jnp.int32, (rows, cells), 1)
    row = lax.broadcasted_iota(jnp.int32, (rows, cells), 0)
    return jnp.max(jnp.where(column == cell, row, -1), axis=0, keepdims=True)


def first_kernel(
    width, rhs_in, isc_in, fwd_in, bwd_in, picked_in, packet, small, place, front,
    rhs, isc, fwd, bwd, picked, sems,
):
    pairs = ((rhs_in, rhs), (isc_in, isc), (fwd_in, fwd), (bwd_in, bwd), (picked_in, picked))
    copies = [pltpu.make_async_copy(a, b, sems.at[i]) for i, (a, b) in enumerate(pairs)]
    for copy in copies:
        copy.start()
    for copy in copies:
        copy.wait()
    cells = rhs.shape[-1]
    count = rhs.shape[1]
    small[ISC:ISC + 2, :] = isc[...]
    small[FWD:FWD + 2, :] = fwd[...]
    small[BWD:BWD + 2, :] = bwd[...]
    small[PICK:PICK + 2, :] = jnp.full((2, cells), -1, F32)
    small[PICK:PICK + 2, :width] = picked[...].astype(F32)
    packet[0:count, :] = rhs[0]
    packet[count:2 * count, :] = rhs[1]
    packet[2 * count:, :] = small[...]
    for layer in range(2):
        place[layer:layer + 1, :] = places(picked[layer:layer + 1, :], cells)
    write_front(front, forward_front(split(rhs[0]), split(rhs[1]), small, None, width))


def forward_kernel(
    step, sections, planes, width, per_layer, owners, layers, inverse, packet, place, *rest
):
    blocks, rest = rest[:len(owners)], rest[len(owners):]
    final = step == sections - 1
    if step:
        incoming, *rest = rest
    if not final:
        after, *rest = rest
    kept, front, *rest = rest
    if not final:
        outgoing_packet, *rest = rest
    if step:
        resident, (stacked, solved) = inverse, rest
    else:
        resident, stacked, solved, kept_sum, sems = rest
    own = lax.axis_index("sweep")
    cells = packet.shape[-1]
    count = cells // LANES
    rows = kept.shape[1]
    order = inverse.shape[-1]
    small = packet.at[2 * rows:]
    mine = own == step
    both = layers[step] == 2

    def fill(layer):
        stack_fronts(blocks, owners, planes, per_layer, stacked, layer)

    if step:
        @pl.when(mine)
        def _():
            fill(0)
            solve(resident, stacked, solved, 0)

        @pl.when(mine & both)
        def _():
            fill(1)
            solve(resident, stacked, solved, 1)
    else:
        cuts = 2 if order % (2 * LANES) == 0 else 1
        depth = order // cuts
        copies = {}
        for layer in range(2):
            for cut in range(cuts):
                for part in range(2):
                    piece = (layer, part, slice(None), pl.ds(cut * depth, depth))
                    copies[layer, cut, part] = pltpu.make_async_copy(
                        inverse.at[piece], resident.at[piece], sems.at[len(copies)]
                    )
        for copy in copies.values():
            copy.start()
        for layer in range(2):
            needed = mine if layer == 0 else mine & both

            @pl.when(needed)
            def _():
                fill(layer)

            for cut in range(cuts):
                for part in range(2):
                    copies[layer, cut, part].wait()

                @pl.when(needed)
                def _():
                    columns = pl.ds(cut * depth, depth)
                    out = product(resident[layer, 0, :, columns], stacked[0, :, columns])
                    out = out + product(resident[layer, 1, :, columns], stacked[1, :, columns])
                    if cut == cuts - 1:
                        if cut:
                            out = out + kept_sum[...]
                        store_solved(solved, layer, out)
                    else:
                        kept_sum[...] = out

    @pl.when(mine)
    def _():
        rhs_a, rhs_b = split(packet[0:rows, :]), split(packet[rows:2 * rows, :])
        first_res = rhs_a
        if step:
            first_res = minus(rhs_a, scaled(row_of(small, FWD), read_field(incoming, count)))
        first = gather_lanes(
            split(solved[0]), place[0:1, :], scaled(row_of(small, ISC), first_res)
        )
        second_res = minus(rhs_b, scaled(row_of(small, FWD + 1), first))
        second = gather_lanes(
            split(solved[1]), place[1:2, :], scaled(row_of(small, ISC + 1), second_res)
        )
        if final:
            z = scaled(row_of(small, BWD), choose(both, second, [jnp.zeros_like(c) for c in first]))
            write_front(front, gather_lanes(rounded(z), picks(small, PICK, width)))
        else:
            outgoing = choose(both, second, first)
            ahead = after.at[2 * rows:]
            chunks = forward_front(
                split(after[0:rows, :]), split(after[rows:2 * rows, :]), ahead, outgoing, width
            )
            write_front(front, chunks)
            write_front(outgoing_packet, chunks, outgoing)
        write_field(kept.at[0], first)
        write_field(kept.at[1], second)


def backward_kernel(
    step, sections, planes, width, per_layer, owners, layers, inverse, small, place, *rest
):
    blocks, rest = rest[:len(owners)], rest[len(owners):]
    kept, *rest = rest
    last = step == sections - 1
    if not last:
        incoming, before, *rest = rest
    if step:
        behind, *rest = rest
        held, *rest = rest
    result, *rest = rest
    if step:
        front, outgoing_packet, *rest = rest
    stacked, solved = rest
    own = lax.axis_index("sweep")
    count = kept.shape[-1] // LANES
    mine = own == step
    both = layers[step] == 2

    def whole_solve(layer):
        stack_fronts(blocks, owners, planes, per_layer, stacked, layer)
        solve(inverse, stacked, solved, layer)

    if not last:
        @pl.when(own != step)
        def _():
            result[...] = before[...]

        @pl.when(mine & both)
        def _():
            whole_solve(1)

    @pl.when(mine & both if last else mine)
    def _():
        whole_solve(0)

    @pl.when(mine)
    def _():
        first_fwd, second_fwd = split(kept[0]), split(kept[1])
        zero = [jnp.zeros_like(c) for c in first_fwd]
        if last:
            second, arriving = second_fwd, zero
        else:
            arriving = read_field(incoming, count)
            z = scaled(row_of(small, BWD + 1), arriving)
            local = scaled(row_of(small, ISC + 1), z)
            second = minus(second_fwd, gather_lanes(split(solved[1]), place[1:2, :], local))
        following = choose(both, second, arriving)
        z = scaled(row_of(small, BWD), following)
        local = scaled(row_of(small, ISC), z)
        change = gather_lanes(split(solved[0]), place[0:1, :], local)
        if last:
            change = choose(both, change, zero)
        first = minus(first_fwd, change)
        if step:
            chunks = backward_front(
                behind, first, read_field(held, count), layers[step - 1] == 2, width
            )
            write_front(front, chunks)
            write_front(outgoing_packet, chunks, first)
        write_field(result.at[0], first)
        write_field(result.at[1], choose(both, second, zero))


def whole(space=pltpu.VMEM):
    return pl.BlockSpec(memory_space=space)


def call(kernel, operands, outs, scratch, name, spaces=()):
    specs = [whole(pltpu.SMEM if o.ndim == 1 else pltpu.VMEM) for o in operands]
    for at, space in spaces:
        specs[at] = whole(space)
    return pl.pallas_call(
        kernel,
        in_specs=specs,
        out_specs=[whole()] * len(outs),
        out_shape=[jax.ShapeDtypeStruct(*o) if isinstance(o, tuple) else o for o in outs],
        scratch_shapes=scratch,
        compiler_params=pltpu.CompilerParams(vmem_limit_bytes=8 * 2**20),
        name=name,
    )(*operands)


def in_hbm(array):
    return pltpu.with_memory_space_constraint(array, pltpu.HBM)


def shards(
    rhs_field,
    front_inverse,
    interior_scale,
    forward_coupling,
    backward_coupling,
    front_cells,
    section_layers,
):
    sections, planes = lax.axis_size("sweep"), lax.axis_size("plane")
    layer_slots, parts, columns, cells = rhs_field.shape
    rows = parts * columns
    owned, order = front_inverse.shape[2:]
    width = -(-owned // LANES) * LANES
    per_layer = width // LANES
    chips = planes // CORES
    direct = planes in (2, 4, 8) and owned == width

    rhs = rhs_field.reshape(layer_slots, rows, cells)
    picked = jnp.pad(front_cells, ((0, 0), (0, width - owned)), constant_values=-1)
    layers = section_layers

    half_shape = ((per_layer, rows, LANES), BF16)
    front_shape = ((2 * per_layer, rows, LANES), BF16)
    packet_shape = ((2 * per_layer + 2 * (cells // LANES), rows, LANES), BF16)
    layers_shape = ((layer_slots, rows, cells), F32)
    scratch = [
        pltpu.VMEM((2, rows, order), BF16),
        pltpu.VMEM((2, rows, width), F32),
    ]

    def send(block, start, stop, step=0, other_core=False):
        flip = step * CORES + int(other_core)
        pairs = [(start, stop)] if start is not None else [(i, i) for i in range(sections)]
        route = [
            (i * planes + own, j * planes + (own ^ flip)) for i, j in pairs for own in range(planes)
        ]
        return lax.ppermute(block, ("sweep", "plane"), route)

    def everywhere(front):
        slots = front.shape[0] // per_layer
        gathered = lax.all_gather(front, "plane")
        if owned != width:
            gathered = gathered.reshape(planes, slots, per_layer, rows, LANES)
            gathered = gathered.transpose(1, 3, 0, 2, 4).reshape(slots, rows, planes, width)
            gathered = gathered[..., :owned].reshape(slots, rows, order // LANES, LANES)
            gathered = gathered.transpose(0, 2, 1, 3)
            gathered = gathered.reshape(slots * order // LANES, rows, LANES)
            return [gathered], [[0]], order // LANES
        return [gathered], [list(range(planes))], per_layer

    def within(front):
        if not direct:
            return everywhere(front)
        mine = [front] + [send(front, None, None, s) for s in range(1, chips)]
        swapped = send(jnp.stack(mine), None, None, other_core=True)
        owners = [[(s, False)] for s in range(chips)] + [[(s, True) for s in range(chips)]]
        return mine + [swapped], owners, per_layer

    def between(front, packet, start, stop):
        if not direct:
            packet = lax.ppermute(packet, "sweep", [(start, stop)])
            return *everywhere(packet[:2 * per_layer]), packet
        packet = send(packet, start, stop)
        mine = [packet] + [send(front, start, stop, s) for s in range(1, chips)]
        swapped = jnp.stack([packet[:2 * per_layer]] + mine[1:])
        swapped = send(swapped, None, None, other_core=True)
        owners = [[(s, False)] for s in range(chips)] + [[(s, True) for s in range(chips)]]
        return mine + [swapped], owners, per_layer, packet

    packet, small, place, front = call(
        functools.partial(first_kernel, width),
        [in_hbm(a) for a in (rhs, interior_scale, forward_coupling, backward_coupling, picked)],
        [((2 * rows + 8, cells), F32), ((8, cells), F32), ((2, cells), jnp.int32), front_shape],
        [
            pltpu.VMEM(rhs.shape, F32),
            pltpu.VMEM(interior_scale.shape, F32),
            pltpu.VMEM(forward_coupling.shape, F32),
            pltpu.VMEM(backward_coupling.shape, F32),
            pltpu.VMEM(picked.shape, jnp.int32),
            pltpu.SemaphoreType.DMA((5,)),
        ],
        "first_fronts",
        [(i, pltpu.HBM) for i in range(5)],
    )
    gathered, owners, slots = within(front)
    after = lax.ppermute(packet, "sweep", [(i + 1, i) for i in range(sections - 1)])
    behind = lax.ppermute(small, "sweep", [(i, i + 1) for i in range(sections - 1)])

    inverse = in_hbm(front_inverse)
    kept, held = [], [None]
    for step in range(sections):
        final = step == sections - 1
        extra = ([held[step]] if step else []) + ([] if final else [after])
        outs = [layers_shape, half_shape if final else front_shape]
        outs += [] if final else [packet_shape]
        outs += [] if step else [pltpu.VMEM(front_inverse.shape, BF16)]
        room = [] if step else [
            pltpu.VMEM((owned, rows), F32), pltpu.SemaphoreType.DMA((8,))
        ]
        outs = call(
            functools.partial(
                forward_kernel, step, sections, planes, width, slots, owners
            ),
            [layers, inverse, packet, place, *gathered, *extra],
            outs,
            scratch + room,
            f"forward_section_{step}",
            [] if step else [(1, pltpu.HBM)],
        )
        if not step:
            inverse = outs[-1]
        kept.append(outs[0])
        if final:
            gathered, owners, slots = within(outs[1])
        else:
            gathered, owners, slots, incoming = between(*outs[1:3], step, step + 1)
            held.append(incoming)

    result = incoming = None
    for step in reversed(range(sections)):
        extra = ([] if result is None else [incoming, result]) + ([behind, held[step]] if step else [])
        outs = call(
            functools.partial(
                backward_kernel, step, sections, planes, width, slots, owners
            ),
            [layers, inverse, small, place, *gathered, kept[step], *extra],
            [layers_shape] + ([front_shape, packet_shape] if step else []),
            scratch,
            f"backward_section_{step}",
        )
        result = outs[0]
        if step:
            gathered, owners, slots, incoming = between(*outs[1:3], step, step - 1)
    return result.reshape(rhs_field.shape)


def solution(mesh):
    in_specs = (
        P("sweep", None, None, "plane"),
        P("sweep", None, "plane", None),
        P("sweep", "plane"),
        P("sweep", "plane"),
        P("sweep", "plane"),
        P("sweep", "plane"),
        P(),
    )
    out_specs = P("sweep", None, None, "plane")
    return jax.shard_map(shards, mesh=mesh, in_specs=in_specs, out_specs=out_specs, check_vma=False)
```

```python
import functools

import jax
import jax.numpy as jnp
from jax import lax
from jax.experimental import pallas as pl
from jax.experimental.pallas import tpu as pltpu
from jax.sharding import PartitionSpec as P

LANES = 128
CORES = 2
ISC, FWD, BWD, PICK = 0, 2, 4, 6
F32, BF16 = jnp.float32, jnp.bfloat16


def split(field):
    return [field[:, at:at + LANES] for at in range(0, field.shape[1], LANES)]


def gather_lanes(chunks, index, beyond=None):
    result = []
    for place, part in enumerate(split(index)):
        part = jnp.broadcast_to(part, chunks[0].shape)
        lane, chunk = part & (LANES - 1), part >> (LANES.bit_length() - 1)
        total = jnp.zeros(chunks[0].shape, F32) if beyond is None else beyond[place]
        for number, source in enumerate(chunks):
            found = jnp.take_along_axis(source, lane, axis=1, mode="promise_in_bounds")
            total = jnp.where(chunk == number, found, total)
        result.append(total)
    return result


def scaled(row, chunks):
    return [part * chunk for part, chunk in zip(split(row), chunks)]


def minus(left, right):
    return [a - b for a, b in zip(left, right)]


def choose(flag, left, right):
    return [jnp.where(flag, a, b) for a, b in zip(left, right)]


def rounded(chunks):
    return [c.astype(BF16).astype(F32) for c in chunks]


def row_of(ref, at):
    return ref[at:at + 1, :]


def picks(ref, at, width):
    return ref[at:at + 1, :width].astype(jnp.int32)


def forward_front(rhs_a, rhs_b, small, incoming, width):
    first = rhs_a if incoming is None else minus(rhs_a, scaled(row_of(small, FWD), incoming))
    second = minus(rhs_b, scaled(row_of(small, FWD + 1), scaled(row_of(small, ISC), first)))
    return (
        gather_lanes(rounded(first), picks(small, PICK, width))
        + gather_lanes(rounded(second), picks(small, PICK + 1, width))
    )


def backward_front(small, incoming, second_fwd, both, width):
    z = scaled(row_of(small, BWD + 1), incoming)
    local = minus(second_fwd, scaled(row_of(small, ISC + 1), z))
    first = scaled(row_of(small, BWD), choose(both, local, incoming))
    return (
        gather_lanes(rounded(first), picks(small, PICK, width))
        + gather_lanes(rounded(z), picks(small, PICK + 1, width))
    )


def write_front(ref, chunks, field=()):
    high = [c.astype(BF16) for c in field]
    low = [(c - h.astype(F32)).astype(BF16) for c, h in zip(field, high)]
    for at, chunk in enumerate(chunks + high + low):
        ref[at] = chunk.astype(BF16)


def read_field(packet, count):
    start = packet.shape[0] - 2 * count
    return [
        packet[start + i].astype(F32) + packet[start + count + i].astype(F32)
        for i in range(count)
    ]


def write_field(ref, chunks):
    for at, chunk in enumerate(chunks):
        ref[:, at * LANES:(at + 1) * LANES] = chunk


def owner_of(place, planes):
    if isinstance(place, int):
        return place
    step, other = place
    return lax.bitwise_xor(lax.axis_index("plane"), step * CORES + int(other))


def stack_fronts(blocks, owners, planes, per_layer, stacked, layer):
    for ref, places in zip(blocks, owners):
        for number, place in enumerate(places):
            owner = owner_of(place, planes)
            for i in range(per_layer):
                at = pl.multiple_of((owner * per_layer + i) * LANES, LANES)
                slot = layer * per_layer + i
                piece = ref[slot] if len(ref.shape) == 3 else ref[number, slot]
                half = piece.shape[0] // 2
                wide = piece.astype(F32)
                turned = jnp.concatenate([-wide[half:], wide[:half]], axis=0)
                stacked[0, :, pl.ds(at, LANES)] = piece
                stacked[1, :, pl.ds(at, LANES)] = turned.astype(BF16)


def product(matrix, columns):
    return lax.dot_general(
        matrix, columns, (((1,), (1,)), ((), ())), preferred_element_type=F32
    )


def store_solved(solved, layer, out):
    rows = out.shape[0]
    if rows % LANES:
        out = jnp.concatenate([out, jnp.zeros((-rows % LANES, out.shape[1]), F32)], axis=0)
    solved[layer] = out.T


def solve(inverse, stacked, solved, layer):
    out = product(inverse[layer, 0], stacked[0]) + product(inverse[layer, 1], stacked[1])
    store_solved(solved, layer, out)


def places(picked, cells):
    rows = picked.shape[1]
    column = jnp.broadcast_to(picked.astype(F32), (8, rows)).T[:, 0:1].astype(jnp.int32)
    cell = lax.broadcasted_iota(jnp.int32, (rows, cells), 1)
    row = lax.broadcasted_iota(jnp.int32, (rows, cells), 0)
    return jnp.max(jnp.where(column == cell, row, -1), axis=0, keepdims=True)


def first_kernel(
    width, layers, rhs_in, isc_in, fwd_in, bwd_in, picked_in, packet, small, place, front,
    layers_out, rhs, isc, fwd, bwd, picked, sems,
):
    pairs = ((rhs_in, rhs), (isc_in, isc), (fwd_in, fwd), (bwd_in, bwd), (picked_in, picked))
    copies = [pltpu.make_async_copy(a, b, sems.at[i]) for i, (a, b) in enumerate(pairs)]
    for copy in copies:
        copy.start()
    for at in range(layers.shape[0]):
        layers_out[at] = layers[at]
    for copy in copies:
        copy.wait()
    cells = rhs.shape[-1]
    count = rhs.shape[1]
    small[ISC:ISC + 2, :] = isc[...]
    small[FWD:FWD + 2, :] = fwd[...]
    small[BWD:BWD + 2, :] = bwd[...]
    small[PICK:PICK + 2, :] = jnp.full((2, cells), -1, F32)
    small[PICK:PICK + 2, :width] = picked[...].astype(F32)
    packet[0:count, :] = rhs[0]
    packet[count:2 * count, :] = rhs[1]
    packet[2 * count:, :] = small[...]
    for layer in range(2):
        place[layer:layer + 1, :] = places(picked[layer:layer + 1, :], cells)
    write_front(front, forward_front(split(rhs[0]), split(rhs[1]), small, None, width))


def forward_kernel(
    step, sections, planes, width, per_layer, owners, layers, inverse, packet, place, *rest
):
    blocks, rest = rest[:len(owners)], rest[len(owners):]
    final = step == sections - 1
    if step:
        incoming, *rest = rest
    if not final:
        after, *rest = rest
    if not step:
        _, *rest = rest
    kept, front, *rest = rest
    if not final:
        outgoing_packet, *rest = rest
    if step:
        resident, (stacked, solved) = inverse, rest
    else:
        resident, stacked, solved, kept_sum, sems = rest
    own = lax.axis_index("sweep")
    cells = packet.shape[-1]
    count = cells // LANES
    rows = kept.shape[1]
    order = inverse.shape[-1]
    small = packet.at[2 * rows:]
    mine = own == step
    both = layers[step] == 2

    def fill(layer):
        stack_fronts(blocks, owners, planes, per_layer, stacked, layer)

    if step:
        @pl.when(mine)
        def _():
            fill(0)
            solve(resident, stacked, solved, 0)

        @pl.when(mine & both)
        def _():
            fill(1)
            solve(resident, stacked, solved, 1)
    else:
        cuts = 2 if order % (2 * LANES) == 0 else 1
        depth = order // cuts
        copies = {}
        for layer in range(2):
            for cut in range(cuts):
                for part in range(2):
                    piece = (layer, part, slice(None), pl.ds(cut * depth, depth))
                    copies[layer, cut, part] = pltpu.make_async_copy(
                        inverse.at[piece], resident.at[piece], sems.at[len(copies)]
                    )
        for copy in copies.values():
            copy.start()
        for layer in range(2):
            needed = mine if layer == 0 else mine & both

            @pl.when(needed)
            def _():
                fill(layer)

            for cut in range(cuts):
                for part in range(2):
                    copies[layer, cut, part].wait()

                @pl.when(needed)
                def _():
                    columns = pl.ds(cut * depth, depth)
                    out = product(resident[layer, 0, :, columns], stacked[0, :, columns])
                    out = out + product(resident[layer, 1, :, columns], stacked[1, :, columns])
                    if cut == cuts - 1:
                        if cut:
                            out = out + kept_sum[...]
                        store_solved(solved, layer, out)
                    else:
                        kept_sum[...] = out

    @pl.when(mine)
    def _():
        rhs_a, rhs_b = split(packet[0:rows, :]), split(packet[rows:2 * rows, :])
        first_res = rhs_a
        if step:
            first_res = minus(rhs_a, scaled(row_of(small, FWD), read_field(incoming, count)))
        first = gather_lanes(
            split(solved[0]), place[0:1, :], scaled(row_of(small, ISC), first_res)
        )
        second_res = minus(rhs_b, scaled(row_of(small, FWD + 1), first))
        second = gather_lanes(
            split(solved[1]), place[1:2, :], scaled(row_of(small, ISC + 1), second_res)
        )
        if final:
            z = scaled(row_of(small, BWD), choose(both, second, [jnp.zeros_like(c) for c in first]))
            write_front(front, gather_lanes(rounded(z), picks(small, PICK, width)))
        else:
            outgoing = choose(both, second, first)
            ahead = after.at[2 * rows:]
            chunks = forward_front(
                split(after[0:rows, :]), split(after[rows:2 * rows, :]), ahead, outgoing, width
            )
            write_front(front, chunks)
            write_front(outgoing_packet, chunks, outgoing)
        write_field(kept.at[0], first)
        write_field(kept.at[1], second)


def backward_kernel(
    step, sections, planes, width, per_layer, owners, layers, inverse, small, place, *rest
):
    blocks, rest = rest[:len(owners)], rest[len(owners):]
    kept, *rest = rest
    last = step == sections - 1
    if not last:
        incoming, before, *rest = rest
    if step:
        behind, *rest = rest
        held, *rest = rest
    result, *rest = rest
    if step:
        front, outgoing_packet, *rest = rest
    stacked, solved = rest
    own = lax.axis_index("sweep")
    count = kept.shape[-1] // LANES
    mine = own == step
    both = layers[step] == 2

    def whole_solve(layer):
        stack_fronts(blocks, owners, planes, per_layer, stacked, layer)
        solve(inverse, stacked, solved, layer)

    if not last:
        @pl.when(own != step)
        def _():
            result[...] = before[...]

        @pl.when(mine & both)
        def _():
            whole_solve(1)

    @pl.when(mine & both if last else mine)
    def _():
        whole_solve(0)

    @pl.when(mine)
    def _():
        first_fwd, second_fwd = split(kept[0]), split(kept[1])
        zero = [jnp.zeros_like(c) for c in first_fwd]
        if last:
            second, arriving = second_fwd, zero
        else:
            arriving = read_field(incoming, count)
            z = scaled(row_of(small, BWD + 1), arriving)
            local = scaled(row_of(small, ISC + 1), z)
            second = minus(second_fwd, gather_lanes(split(solved[1]), place[1:2, :], local))
        following = choose(both, second, arriving)
        z = scaled(row_of(small, BWD), following)
        local = scaled(row_of(small, ISC), z)
        change = gather_lanes(split(solved[0]), place[0:1, :], local)
        if last:
            change = choose(both, change, zero)
        first = minus(first_fwd, change)
        if step:
            chunks = backward_front(
                behind, first, read_field(held, count), layers[step - 1] == 2, width
            )
            write_front(front, chunks)
            write_front(outgoing_packet, chunks, first)
        write_field(result.at[0], first)
        write_field(result.at[1], choose(both, second, zero))


def whole(space=pltpu.VMEM):
    return pl.BlockSpec(memory_space=space)


def call(kernel, operands, outs, scratch, name, spaces=()):
    outs = [jax.ShapeDtypeStruct(*o) if isinstance(o, tuple) else o for o in outs]
    specs = [whole(pltpu.SMEM if o.ndim == 1 else pltpu.VMEM) for o in operands]
    for at, space in spaces:
        specs[at] = whole(space)
    return pl.pallas_call(
        kernel,
        in_specs=specs,
        out_specs=[whole(pltpu.SMEM if len(o.shape) == 1 else pltpu.VMEM) for o in outs],
        out_shape=outs,
        scratch_shapes=scratch,
        compiler_params=pltpu.CompilerParams(vmem_limit_bytes=8 * 2**20),
        name=name,
    )(*operands)


def in_hbm(array):
    return pltpu.with_memory_space_constraint(array, pltpu.HBM)


def shards(
    rhs_field,
    front_inverse,
    interior_scale,
    forward_coupling,
    backward_coupling,
    front_cells,
    section_layers,
):
    sections, planes = lax.axis_size("sweep"), lax.axis_size("plane")
    layer_slots, parts, columns, cells = rhs_field.shape
    rows = parts * columns
    owned, order = front_inverse.shape[2:]
    width = -(-owned // LANES) * LANES
    per_layer = width // LANES
    chips = planes // CORES
    direct = planes in (2, 4, 8) and owned == width

    rhs = rhs_field.reshape(layer_slots, rows, cells)
    picked = jnp.pad(front_cells, ((0, 0), (0, width - owned)), constant_values=-1)

    half_shape = ((per_layer, rows, LANES), BF16)
    front_shape = ((2 * per_layer, rows, LANES), BF16)
    packet_shape = ((2 * per_layer + 2 * (cells // LANES), rows, LANES), BF16)
    layers_shape = ((layer_slots, rows, cells), F32)
    scratch = [
        pltpu.VMEM((2, rows, order), BF16),
        pltpu.VMEM((2, rows, width), F32),
    ]

    def send(block, shift, step=0, other_core=False):
        flip = step * CORES + int(other_core)
        route = [
            (i * planes + own, (i + shift) % sections * planes + (own ^ flip))
            for i in range(sections) for own in range(planes)
        ]
        return lax.ppermute(block, ("sweep", "plane"), route)

    def everywhere(front):
        slots = front.shape[0] // per_layer
        gathered = lax.all_gather(front, "plane")
        if owned != width:
            gathered = gathered.reshape(planes, slots, per_layer, rows, LANES)
            gathered = gathered.transpose(1, 3, 0, 2, 4).reshape(slots, rows, planes, width)
            gathered = gathered[..., :owned].reshape(slots, rows, order // LANES, LANES)
            gathered = gathered.transpose(0, 2, 1, 3)
            gathered = gathered.reshape(slots * order // LANES, rows, LANES)
            return [gathered], [[0]], order // LANES
        return [gathered], [list(range(planes))], per_layer

    def swap(mine):
        mine = [m[:2 * per_layer] for m in mine]
        owners = [[(s, False)] for s in range(chips)] + [[(s, True) for s in range(chips)]]
        return send(jnp.stack(mine), 0, other_core=True), owners

    def within(front):
        if not direct:
            return everywhere(front)
        mine = [front] + [send(front, 0, s) for s in range(1, chips)]
        swapped, owners = swap(mine)
        return mine + [swapped], owners, per_layer

    def between(front, packet, shift):
        packet = send(packet, shift)
        if not direct:
            return *everywhere(packet[:2 * per_layer]), packet
        mine = [packet] + [send(front, shift, s) for s in range(1, chips)]
        swapped, owners = swap(mine)
        return mine + [swapped], owners, per_layer, packet

    packet, small, place, front, layers = call(
        functools.partial(first_kernel, width),
        [section_layers]
        + [in_hbm(a) for a in (rhs, interior_scale, forward_coupling, backward_coupling, picked)],
        [
            ((2 * rows + 8, cells), F32),
            ((8, cells), F32),
            ((2, cells), jnp.int32),
            front_shape,
            (section_layers.shape, jnp.int32),
        ],
        [
            pltpu.VMEM(rhs.shape, F32),
            pltpu.VMEM(interior_scale.shape, F32),
            pltpu.VMEM(forward_coupling.shape, F32),
            pltpu.VMEM(backward_coupling.shape, F32),
            pltpu.VMEM(picked.shape, jnp.int32),
            pltpu.SemaphoreType.DMA((5,)),
        ],
        "first_fronts",
        [(i, pltpu.HBM) for i in range(1, 6)],
    )
    gathered, owners, slots = within(front)
    after, behind = send(packet, -1), send(small, 1)

    inverse = in_hbm(front_inverse)
    kept, held = [], [None]
    for step in range(sections):
        final = step == sections - 1
        extra = ([held[step]] if step else []) + ([] if final else [after])
        extra += [] if step else [behind]
        outs = [layers_shape, half_shape if final else front_shape]
        outs += [] if final else [packet_shape]
        outs += [] if step else [pltpu.VMEM(front_inverse.shape, BF16)]
        room = [] if step else [
            pltpu.VMEM((owned, rows), F32), pltpu.SemaphoreType.DMA((8,))
        ]
        outs = call(
            functools.partial(
                forward_kernel, step, sections, planes, width, slots, owners
            ),
            [layers, inverse, packet, place, *gathered, *extra],
            outs,
            scratch + room,
            f"forward_section_{step}",
            [] if step else [(1, pltpu.HBM)],
        )
        if not step:
            inverse = outs[-1]
        kept.append(outs[0])
        if final:
            gathered, owners, slots = within(outs[1])
        else:
            gathered, owners, slots, incoming = between(*outs[1:3], 1)
            held.append(incoming)

    result = incoming = None
    for step in reversed(range(sections)):
        extra = ([] if result is None else [incoming, result]) + ([behind, held[step]] if step else [])
        outs = call(
            functools.partial(
                backward_kernel, step, sections, planes, width, slots, owners
            ),
            [layers, inverse, small, place, *gathered, kept[step], *extra],
            [layers_shape] + ([front_shape, packet_shape] if step else []),
            scratch,
            f"backward_section_{step}",
        )
        result = outs[0]
        if step:
            gathered, owners, slots, incoming = between(*outs[1:3], -1)
    return result.reshape(rhs_field.shape)


def solution(mesh):
    in_specs = (
        P("sweep", None, None, "plane"),
        P("sweep", None, "plane", None),
        P("sweep", "plane"),
        P("sweep", "plane"),
        P("sweep", "plane"),
        P("sweep", "plane"),
        P(),
    )
    out_specs = P("sweep", None, None, "plane")
    return jax.shard_map(shards, mesh=mesh, in_specs=in_specs, out_specs=out_specs, check_vma=False)
```

```python
import functools

import jax
import jax.numpy as jnp
from jax import lax
from jax.experimental import pallas as pl
from jax.experimental.pallas import tpu as pltpu
from jax.sharding import PartitionSpec as P

LANES = 128
CORES = 2
ISC, FWD, BWD, PICK = 0, 2, 4, 6
F32, BF16 = jnp.float32, jnp.bfloat16


def split(field):
    return [field[:, at:at + LANES] for at in range(0, field.shape[1], LANES)]


def gather_lanes(chunks, index, beyond=None):
    result = []
    for place, part in enumerate(split(index)):
        part = jnp.broadcast_to(part, chunks[0].shape)
        lane, chunk = part & (LANES - 1), part >> (LANES.bit_length() - 1)
        total = jnp.zeros(chunks[0].shape, F32) if beyond is None else beyond[place]
        for number, source in enumerate(chunks):
            found = jnp.take_along_axis(source, lane, axis=1, mode="promise_in_bounds")
            total = jnp.where(chunk == number, found, total)
        result.append(total)
    return result


def scaled(row, chunks):
    return [part * chunk for part, chunk in zip(split(row), chunks)]


def minus(left, right):
    return [a - b for a, b in zip(left, right)]


def choose(flag, left, right):
    return [jnp.where(flag, a, b) for a, b in zip(left, right)]


def rounded(chunks):
    return [c.astype(BF16).astype(F32) for c in chunks]


def row_of(ref, at):
    return ref[at:at + 1, :]


def picks(ref, at, width):
    return ref[at:at + 1, :width].astype(jnp.int32)


def forward_front(rhs_a, rhs_b, small, incoming, width):
    first = rhs_a if incoming is None else minus(rhs_a, scaled(row_of(small, FWD), incoming))
    second = minus(rhs_b, scaled(row_of(small, FWD + 1), scaled(row_of(small, ISC), first)))
    return (
        gather_lanes(rounded(first), picks(small, PICK, width))
        + gather_lanes(rounded(second), picks(small, PICK + 1, width))
    )


def backward_front(small, incoming, second_fwd, both, width):
    z = scaled(row_of(small, BWD + 1), incoming)
    local = minus(second_fwd, scaled(row_of(small, ISC + 1), z))
    first = scaled(row_of(small, BWD), choose(both, local, incoming))
    return (
        gather_lanes(rounded(first), picks(small, PICK, width))
        + gather_lanes(rounded(z), picks(small, PICK + 1, width))
    )


def write_front(ref, chunks, field=()):
    high = [c.astype(BF16) for c in field]
    low = [(c - h.astype(F32)).astype(BF16) for c, h in zip(field, high)]
    for at, chunk in enumerate(chunks + high + low):
        ref[at] = chunk.astype(BF16)


def read_field(packet, count):
    start = packet.shape[0] - 2 * count
    return [
        packet[start + i].astype(F32) + packet[start + count + i].astype(F32)
        for i in range(count)
    ]


def write_field(ref, chunks):
    for at, chunk in enumerate(chunks):
        ref[:, at * LANES:(at + 1) * LANES] = chunk


def owner_of(place, planes):
    if isinstance(place, int):
        return place
    own = lax.axis_index("plane")
    return lax.bitwise_xor(own, jnp.where(lax.rem(own, CORES) == 0, place[0], place[1]))


def stack_fronts(blocks, owners, planes, per_layer, stacked, layer):
    for ref, places in zip(blocks, owners):
        for number, place in enumerate(places):
            owner = owner_of(place, planes)
            for i in range(per_layer):
                at = pl.multiple_of((owner * per_layer + i) * LANES, LANES)
                slot = layer * per_layer + i
                piece = ref[slot] if len(ref.shape) == 3 else ref[number, slot]
                half = piece.shape[0] // 2
                wide = piece.astype(F32)
                turned = jnp.concatenate([-wide[half:], wide[:half]], axis=0)
                stacked[0, :, pl.ds(at, LANES)] = piece
                stacked[1, :, pl.ds(at, LANES)] = turned.astype(BF16)


def product(matrix, columns):
    return lax.dot_general(
        matrix, columns, (((1,), (1,)), ((), ())), preferred_element_type=F32
    )


def store_solved(solved, layer, out):
    rows = out.shape[0]
    if rows % LANES:
        out = jnp.concatenate([out, jnp.zeros((-rows % LANES, out.shape[1]), F32)], axis=0)
    solved[layer] = out.T


def solve(inverse, stacked, solved, layer):
    out = product(inverse[0], stacked[0]) + product(inverse[1], stacked[1])
    store_solved(solved, layer, out)


def places(picked, cells):
    rows = picked.shape[1]
    column = jnp.broadcast_to(picked.astype(F32), (8, rows)).T[:, 0:1].astype(jnp.int32)
    cell = lax.broadcasted_iota(jnp.int32, (rows, cells), 1)
    row = lax.broadcasted_iota(jnp.int32, (rows, cells), 0)
    return jnp.max(jnp.where(column == cell, row, -1), axis=0, keepdims=True)


def first_kernel(
    width, layers_in, rhs_in, isc_in, fwd_in, bwd_in, picked_in, inverse, packet, place, front,
    layers, first_inverse, rhs, isc, fwd, bwd, picked, sems, load_sem,
):
    pairs = (
        (rhs_in, rhs), (isc_in, isc), (fwd_in, fwd), (bwd_in, bwd), (picked_in, picked),
        (layers_in, layers),
    )
    copies = [pltpu.make_async_copy(a, b, sems.at[i]) for i, (a, b) in enumerate(pairs)]
    load = pltpu.make_async_copy(inverse.at[0], first_inverse, load_sem.at[0])
    for copy in copies:
        copy.start()
    load.start()
    for copy in copies:
        copy.wait()
    cells = rhs.shape[-1]
    count = rhs.shape[1]
    small = packet.at[2 * count:]
    small[ISC:ISC + 2, :] = isc[...]
    small[FWD:FWD + 2, :] = fwd[...]
    small[BWD:BWD + 2, :] = bwd[...]
    small[PICK:PICK + 2, :] = jnp.full((2, cells), -1, F32)
    small[PICK:PICK + 2, :width] = picked[...].astype(F32)
    packet[0:count, :] = rhs[0]
    packet[count:2 * count, :] = rhs[1]
    for layer in range(2):
        place[layer:layer + 1, :] = places(picked[layer:layer + 1, :], cells)
    write_front(front, forward_front(split(rhs[0]), split(rhs[1]), small, None, width))
    load.wait()


def forward_kernel(
    step, sections, planes, width, per_layer, owners, layers, first_inverse, inverse, packet,
    place, *rest
):
    blocks, rest = rest[:len(owners)], rest[len(owners):]
    final = step == sections - 1
    if step:
        incoming, *rest = rest
    if not final:
        after, *rest = rest
    if not step:
        _, *rest = rest
    kept, front, *rest = rest
    if not final:
        outgoing_packet, *rest = rest
    if not step:
        second_inverse, stacked, solved, sems = rest
    else:
        second_inverse, (stacked, solved) = inverse, rest
    own = lax.axis_index("sweep")
    cells = packet.shape[-1]
    count = cells // LANES
    rows = kept.shape[1]
    small = packet.at[2 * rows:]
    mine = own == step
    both = layers[step] == 2
    load = None
    if not step:
        load = pltpu.make_async_copy(inverse.at[1], second_inverse, sems.at[0])
        load.start()

    def whole_solve(layer, matrices):
        stack_fronts(blocks, owners, planes, per_layer, stacked, layer)
        solve(matrices, stacked, solved, layer)

    @pl.when(mine)
    def _():
        whole_solve(0, first_inverse)

    if load is not None:
        load.wait()

    @pl.when(mine & both)
    def _():
        whole_solve(1, second_inverse)

    @pl.when(mine)
    def _():
        rhs_a, rhs_b = split(packet[0:rows, :]), split(packet[rows:2 * rows, :])
        first_res = rhs_a
        if step:
            first_res = minus(rhs_a, scaled(row_of(small, FWD), read_field(incoming, count)))
        first = gather_lanes(
            split(solved[0]), place[0:1, :], scaled(row_of(small, ISC), first_res)
        )
        second_res = minus(rhs_b, scaled(row_of(small, FWD + 1), first))
        second = gather_lanes(
            split(solved[1]), place[1:2, :], scaled(row_of(small, ISC + 1), second_res)
        )
        if final:
            z = scaled(row_of(small, BWD), choose(both, second, [jnp.zeros_like(c) for c in first]))
            write_front(front, gather_lanes(rounded(z), picks(small, PICK, width)))
        else:
            outgoing = choose(both, second, first)
            ahead = after.at[2 * rows:]
            chunks = forward_front(
                split(after[0:rows, :]), split(after[rows:2 * rows, :]), ahead, outgoing, width
            )
            write_front(front, chunks)
            write_front(outgoing_packet, chunks, outgoing)
        write_field(kept.at[0], first)
        write_field(kept.at[1], second)


def backward_kernel(
    step, sections, planes, width, per_layer, owners, layers, first_inverse, second_inverse,
    packet, place, *rest
):
    blocks, rest = rest[:len(owners)], rest[len(owners):]
    kept, *rest = rest
    last = step == sections - 1
    if not last:
        incoming, before, *rest = rest
    if step:
        behind, *rest = rest
        held, *rest = rest
    result, *rest = rest
    if step:
        front, outgoing_packet, *rest = rest
    stacked, solved = rest
    own = lax.axis_index("sweep")
    count = kept.shape[-1] // LANES
    small = packet.at[2 * kept.shape[1]:]
    mine = own == step
    both = layers[step] == 2

    def whole_solve(layer):
        stack_fronts(blocks, owners, planes, per_layer, stacked, layer)
        solve((first_inverse, second_inverse)[layer], stacked, solved, layer)

    if not last:
        @pl.when(own != step)
        def _():
            result[...] = before[...]

        @pl.when(mine & both)
        def _():
            whole_solve(1)

    @pl.when(mine & both if last else mine)
    def _():
        whole_solve(0)

    @pl.when(mine)
    def _():
        first_fwd, second_fwd = split(kept[0]), split(kept[1])
        zero = [jnp.zeros_like(c) for c in first_fwd]
        if last:
            second, arriving = second_fwd, zero
        else:
            arriving = read_field(incoming, count)
            z = scaled(row_of(small, BWD + 1), arriving)
            local = scaled(row_of(small, ISC + 1), z)
            second = minus(second_fwd, gather_lanes(split(solved[1]), place[1:2, :], local))
        following = choose(both, second, arriving)
        z = scaled(row_of(small, BWD), following)
        local = scaled(row_of(small, ISC), z)
        change = gather_lanes(split(solved[0]), place[0:1, :], local)
        if last:
            change = choose(both, change, zero)
        first = minus(first_fwd, change)
        if step:
            chunks = backward_front(
                behind.at[2 * kept.shape[1]:], first, read_field(held, count),
                layers[step - 1] == 2, width
            )
            write_front(front, chunks)
            write_front(outgoing_packet, chunks, first)
        write_field(result.at[0], first)
        write_field(result.at[1], choose(both, second, zero))


def whole(space=pltpu.VMEM):
    return pl.BlockSpec(memory_space=space)


def call(kernel, operands, outs, scratch, name, in_place=()):
    outs = [jax.ShapeDtypeStruct(*o) if isinstance(o, tuple) else o for o in outs]
    specs = [whole(pltpu.SMEM if o.ndim == 1 else pltpu.VMEM) for o in operands]
    for at in in_place:
        specs[at] = whole(pltpu.HBM)
    return pl.pallas_call(
        kernel,
        in_specs=specs,
        out_specs=[whole(pltpu.SMEM if len(o.shape) == 1 else pltpu.VMEM) for o in outs],
        out_shape=outs,
        scratch_shapes=scratch,
        compiler_params=pltpu.CompilerParams(vmem_limit_bytes=8 * 2**20),
        name=name,
    )(*operands)


def in_hbm(array):
    return pltpu.with_memory_space_constraint(array, pltpu.HBM)


def shards(
    rhs_field,
    front_inverse,
    interior_scale,
    forward_coupling,
    backward_coupling,
    front_cells,
    section_layers,
):
    sections, planes = lax.axis_size("sweep"), lax.axis_size("plane")
    layer_slots, parts, columns, cells = rhs_field.shape
    rows = parts * columns
    owned, order = front_inverse.shape[2:]
    width = -(-owned // LANES) * LANES
    per_layer = width // LANES
    chips = planes // CORES
    direct = planes in (2, 4, 8) and owned == width

    rhs = rhs_field.reshape(layer_slots, rows, cells)
    picked = jnp.pad(front_cells, ((0, 0), (0, width - owned)), constant_values=-1)
    layers = section_layers

    half_shape = ((per_layer, rows, LANES), BF16)
    front_shape = ((2 * per_layer, rows, LANES), BF16)
    packet_shape = ((2 * per_layer + 2 * (cells // LANES), rows, LANES), BF16)
    layers_shape = ((layer_slots, rows, cells), F32)
    scratch = [
        pltpu.VMEM((2, rows, order), BF16),
        pltpu.VMEM((2, rows, width), F32),
    ]

    def send(block, pair, *flips):
        pairs = [pair] if pair else [(i, i) for i in range(sections)]
        route = [
            (i * planes + own, j * planes + (own ^ flips[own % CORES % len(flips)]))
            for i, j in pairs for own in range(planes)
        ]
        return lax.ppermute(block, ("sweep", "plane"), route)

    def everywhere(front):
        slots = front.shape[0] // per_layer
        gathered = lax.all_gather(front, "plane")
        if owned != width:
            gathered = gathered.reshape(planes, slots, per_layer, rows, LANES)
            gathered = gathered.transpose(1, 3, 0, 2, 4).reshape(slots, rows, planes, width)
            gathered = gathered[..., :owned].reshape(slots, rows, order // LANES, LANES)
            gathered = gathered.transpose(0, 2, 1, 3)
            gathered = gathered.reshape(slots * order // LANES, rows, LANES)
            return [gathered], [[0]], order // LANES
        return [gathered], [list(range(planes))], per_layer

    def spread(front, straight, pair):
        blocks, owners = [straight], [[(0, 0)]]
        for step in [1] if chips == 2 else range(3, chips):
            blocks.append(send(front, pair, CORES * step))
            owners.append([(CORES * step, CORES * step)])
        if chips == 4:
            both = jnp.stack([front, send(front, None, 1)])
            blocks.append(send(both, pair, CORES, 2 * CORES))
            owners += [[(CORES + core, 2 * CORES + core) for core in range(CORES)]]
        short = [b[:2 * per_layer] if b.ndim == 3 else b for b in blocks]
        mine = jnp.concatenate([b[None] if b.ndim == 3 else b for b in short])
        blocks.append(send(mine, None, 1))
        owners.append([(one ^ 1, zero ^ 1) for places in owners for zero, one in places])
        return blocks, owners, per_layer

    def within(front):
        return spread(front, front, None) if direct else everywhere(front)

    def between(front, packet, start, stop):
        if not direct:
            packet = lax.ppermute(packet, "sweep", [(start, stop)])
            return *everywhere(packet[:2 * per_layer]), packet
        packet = send(packet, (start, stop), 0)
        return *spread(front, packet, (start, stop)), packet

    inverse = in_hbm(front_inverse)
    half_inverse = pltpu.VMEM(front_inverse.shape[1:], BF16)
    coefficients = (interior_scale, forward_coupling, backward_coupling)
    operands = [section_layers, rhs, *coefficients, picked]
    packet, place, front, layers, first_inverse = call(
        functools.partial(first_kernel, width),
        [in_hbm(a) for a in operands] + [inverse],
        [
            ((2 * rows + 8, cells), F32),
            ((2, cells), jnp.int32),
            front_shape,
            (section_layers.shape, jnp.int32),
            half_inverse,
        ],
        [pltpu.VMEM(a.shape, a.dtype) for a in operands[1:]]
        + [pltpu.SemaphoreType.DMA((6,)), pltpu.SemaphoreType.DMA((1,))],
        "first_fronts",
        range(7),
    )
    gathered, owners, slots = within(front)
    after = lax.ppermute(packet, "sweep", [(i + 1, i) for i in range(sections - 1)])
    behind = lax.ppermute(packet, "sweep", [(i, i + 1) for i in range(sections - 1)])

    kept, held = [], [None]
    for step in range(sections):
        final = step == sections - 1
        extra = ([held[step]] if step else []) + ([] if final else [after])
        extra += [] if step else [behind]
        outs = [layers_shape, half_shape if final else front_shape]
        outs += [] if final else [packet_shape]
        outs += [] if step else [half_inverse]
        outs = call(
            functools.partial(
                forward_kernel, step, sections, planes, width, slots, owners
            ),
            [layers, first_inverse, inverse, packet, place, *gathered, *extra],
            outs,
            scratch + ([] if step else [pltpu.SemaphoreType.DMA((1,))]),
            f"forward_section_{step}",
            [] if step else [2],
        )
        if not step:
            inverse = outs[-1]
        kept.append(outs[0])
        if final:
            gathered, owners, slots = within(outs[1])
        else:
            gathered, owners, slots, incoming = between(outs[1], outs[2], step, step + 1)
            held.append(incoming)

    result = incoming = None
    for step in reversed(range(sections)):
        extra = ([] if result is None else [incoming, result]) + ([behind, held[step]] if step else [])
        outs = call(
            functools.partial(
                backward_kernel, step, sections, planes, width, slots, owners
            ),
            [layers, first_inverse, inverse, packet, place, *gathered, kept[step], *extra],
            [layers_shape] + ([front_shape, packet_shape] if step else []),
            scratch,
            f"backward_section_{step}",
        )
        result = outs[0]
        if step:
            gathered, owners, slots, incoming = between(outs[1], outs[2], step, step - 1)
    return result.reshape(rhs_field.shape)


def solution(mesh):
    in_specs = (
        P("sweep", None, None, "plane"),
        P("sweep", None, "plane", None),
        P("sweep", "plane"),
        P("sweep", "plane"),
        P("sweep", "plane"),
        P("sweep", "plane"),
        P(),
    )
    out_specs = P("sweep", None, None, "plane")
    return jax.shard_map(shards, mesh=mesh, in_specs=in_specs, out_specs=out_specs, check_vma=False)
```

```python
import functools

import jax
import jax.numpy as jnp
from jax import lax
from jax.experimental import pallas as pl
from jax.experimental.pallas import tpu as pltpu
from jax.sharding import PartitionSpec as P

LANES = 128
CORES = 2
ISC, FWD, BWD, PICK = 0, 2, 4, 6
SLOPE, TURN, FOLD, CELL, NEEDS = 0, 1, 2, 3, 8
F32, BF16 = jnp.float32, jnp.bfloat16


def split(field):
    return [field[:, at:at + LANES] for at in range(0, field.shape[1], LANES)]


def gather_lanes(chunks, index, beyond=None):
    result = []
    for place, part in enumerate(split(index)):
        part = jnp.broadcast_to(part, chunks[0].shape)
        lane, chunk = part & (LANES - 1), part >> (LANES.bit_length() - 1)
        total = jnp.zeros(chunks[0].shape, F32) if beyond is None else beyond[place]
        for number, source in enumerate(chunks):
            found = jnp.take_along_axis(source, lane, axis=1, mode="promise_in_bounds")
            total = jnp.where(chunk == number, found, total)
        result.append(total)
    return result


def scaled(row, chunks):
    return [part * chunk for part, chunk in zip(split(row), chunks)]


def minus(left, right):
    return [a - b for a, b in zip(left, right)]


def choose(flag, left, right):
    return [jnp.where(flag, a, b) for a, b in zip(left, right)]


def rounded(chunks):
    return [c.astype(BF16).astype(F32) for c in chunks]


def row_of(ref, at):
    return ref[at:at + 1, :]


def picks(ref, at, width):
    return ref[at:at + 1, :width].astype(jnp.int32)


def halves(row):
    chunks = split(row)
    return chunks[:len(chunks) // 2], chunks[len(chunks) // 2:]


def times(left, right):
    return [a * b for a, b in zip(left, right)]


def plus(left, right):
    return [a + b for a, b in zip(left, right)]


def gathered_at(needs, field):
    cells = needs[CELL:CELL + 1, :].astype(jnp.int32)
    half = cells.shape[1] // 2
    return gather_lanes(field, cells[:, :half]), gather_lanes(field, cells[:, half:])


def forward_front(base, needs, incoming):
    (base_a, base_b), (slope_a, slope_b) = halves(base[...]), halves(row_of(needs, SLOPE))
    at_a, at_b = gathered_at(needs, incoming)
    return minus(base_a, times(slope_a, at_a)) + plus(base_b, times(slope_b, at_b))


def backward_front(needs, incoming, second_fwd, both):
    (turn_a, turn_b), (fold, _) = halves(row_of(needs, TURN)), halves(row_of(needs, FOLD))
    at_a, at_b = gathered_at(needs, incoming)
    second_a, _ = gathered_at(needs, second_fwd)
    following = choose(both, minus(second_a, times(fold, at_a)), at_a)
    return times(turn_a, following) + times(turn_b, at_b)


def write_front(ref, chunks, field=()):
    high = [c.astype(BF16) for c in field]
    low = [(c - h.astype(F32)).astype(BF16) for c, h in zip(field, high)]
    for at, chunk in enumerate(chunks + high + low):
        ref[at] = chunk.astype(BF16)


def read_field(packet, count):
    start = packet.shape[0] - 2 * count
    return [
        packet[start + i].astype(F32) + packet[start + count + i].astype(F32)
        for i in range(count)
    ]


def write_field(ref, chunks):
    for at, chunk in enumerate(chunks):
        ref[:, at * LANES:(at + 1) * LANES] = chunk


def owner_of(place, planes):
    if isinstance(place, int):
        return place
    own = lax.axis_index("plane")
    return lax.bitwise_xor(own, jnp.where(lax.rem(own, CORES) == 0, place[0], place[1]))


def stack_fronts(blocks, owners, planes, per_layer, stacked, layer):
    for ref, places in zip(blocks, owners):
        for number, place in enumerate(places):
            owner = owner_of(place, planes)
            for i in range(per_layer):
                at = pl.multiple_of((owner * per_layer + i) * LANES, LANES)
                slot = layer * per_layer + i
                piece = ref[slot] if len(ref.shape) == 3 else ref[number, slot]
                half = piece.shape[0] // 2
                wide = piece.astype(F32)
                turned = jnp.concatenate([-wide[half:], wide[:half]], axis=0)
                stacked[0, :, pl.ds(at, LANES)] = piece
                stacked[1, :, pl.ds(at, LANES)] = turned.astype(BF16)


def product(matrix, columns):
    return lax.dot_general(
        matrix, columns, (((1,), (1,)), ((), ())), preferred_element_type=F32
    )


def store_solved(solved, layer, out):
    rows = out.shape[0]
    if rows % LANES:
        out = jnp.concatenate([out, jnp.zeros((-rows % LANES, out.shape[1]), F32)], axis=0)
    solved[layer] = out.T


def solve(inverse, stacked, solved, layer):
    out = product(inverse[0], stacked[0]) + product(inverse[1], stacked[1])
    store_solved(solved, layer, out)


def places(picked, cells):
    rows = picked.shape[1]
    column = jnp.broadcast_to(picked.astype(F32), (8, rows)).T[:, 0:1].astype(jnp.int32)
    cell = lax.broadcasted_iota(jnp.int32, (rows, cells), 1)
    row = lax.broadcasted_iota(jnp.int32, (rows, cells), 0)
    return jnp.max(jnp.where(column == cell, row, -1), axis=0, keepdims=True)


def first_kernel(
    width, layers_in, rhs_in, isc_in, fwd_in, bwd_in, picked_in, local, ahead, back, place, front,
    layers, rhs, isc, fwd, bwd, picked, sems,
):
    pairs = (
        (rhs_in, rhs), (isc_in, isc), (fwd_in, fwd), (bwd_in, bwd), (picked_in, picked),
        (layers_in, layers),
    )
    copies = [pltpu.make_async_copy(a, b, sems.at[i]) for i, (a, b) in enumerate(pairs)]
    for copy in copies:
        copy.start()
    for copy in copies:
        copy.wait()
    cells = rhs.shape[-1]
    count = rhs.shape[1]
    small = local.at[2 * count:]
    small[ISC:ISC + 2, :] = isc[...]
    small[FWD:FWD + 2, :] = fwd[...]
    small[BWD:BWD + 2, :] = bwd[...]
    small[PICK:PICK + 2, :] = jnp.full((2, cells), -1, F32)
    small[PICK:PICK + 2, :width] = picked[...].astype(F32)
    local[0:count, :] = rhs[0]
    local[count:2 * count, :] = rhs[1]

    at_a, at_b = picked[0:1, :], picked[1:2, :]
    isc_a, isc_b, fwd_a, fwd_b, bwd_a, bwd_b = (
        split(jnp.broadcast_to(row_of(small, at), (8, cells))) for at in range(PICK)
    )
    base_a = gather_lanes(split(rhs[0]), at_a)
    fed = times(fwd_b, isc_a)
    base_b = gather_lanes(
        minus(split(rhs[1]), [f[0:1] * r for f, r in zip(fed, split(rhs[0]))]), at_b
    )
    write_front(front, base_a + base_b)
    zero = [jnp.zeros((8, LANES), F32)] * (width // LANES)
    rows = {
        SLOPE: gather_lanes(fwd_a, at_a) + gather_lanes(times(fed, fwd_a), at_b),
        TURN: gather_lanes(bwd_a, at_a) + gather_lanes(bwd_b, at_b),
        FOLD: gather_lanes(times(isc_b, bwd_b), at_a) + zero,
        CELL: split(at_a.astype(F32)) + split(at_b.astype(F32)),
    }
    back[...] = jnp.zeros(back.shape, F32)
    for at, chunks in rows.items():
        for i, chunk in enumerate(chunks):
            back[at:at + 1, i * LANES:(i + 1) * LANES] = chunk[0:1]
    write_field(ahead.at[0:count], base_a + base_b)
    ahead[count:, :] = back[...]
    for layer in range(2):
        place[layer:layer + 1, :] = places(picked[layer:layer + 1, :], cells)


def load_kernel(inverse, _, loaded, done, sem):
    load = pltpu.make_async_copy(inverse.at[0], loaded, sem.at[0])
    load.start()
    done[...] = jnp.zeros(done.shape, F32)
    load.wait()


def forward_kernel(
    step, sections, planes, width, per_layer, owners, layers, first_inverse, inverse, packet,
    place, *rest
):
    blocks, rest = rest[:len(owners)], rest[len(owners):]
    final = step == sections - 1
    if step:
        incoming, *rest = rest
    if not final:
        after, *rest = rest
    kept, front, *rest = rest
    if not final:
        outgoing_packet, *rest = rest
    if not step:
        second_inverse, stacked, solved, sems = rest
    else:
        second_inverse, (stacked, solved) = inverse, rest
    own = lax.axis_index("sweep")
    cells = packet.shape[-1]
    count = cells // LANES
    rows = kept.shape[1]
    small = packet.at[2 * rows:]
    mine = own == step
    both = layers[step] == 2
    load = None
    if not step:
        load = pltpu.make_async_copy(inverse.at[1], second_inverse, sems.at[0])
        load.start()

    def whole_solve(layer, matrices):
        stack_fronts(blocks, owners, planes, per_layer, stacked, layer)
        solve(matrices, stacked, solved, layer)

    @pl.when(mine)
    def _():
        whole_solve(0, first_inverse)

    if load is not None:
        load.wait()

    @pl.when(mine & both)
    def _():
        whole_solve(1, second_inverse)

    @pl.when(mine)
    def _():
        rhs_a, rhs_b = split(packet[0:rows, :]), split(packet[rows:2 * rows, :])
        first_res = rhs_a
        if step:
            first_res = minus(rhs_a, scaled(row_of(small, FWD), read_field(incoming, count)))
        first = gather_lanes(
            split(solved[0]), place[0:1, :], scaled(row_of(small, ISC), first_res)
        )
        second_res = minus(rhs_b, scaled(row_of(small, FWD + 1), first))
        second = gather_lanes(
            split(solved[1]), place[1:2, :], scaled(row_of(small, ISC + 1), second_res)
        )
        if final:
            z = scaled(row_of(small, BWD), choose(both, second, [jnp.zeros_like(c) for c in first]))
            write_front(front, gather_lanes(rounded(z), picks(small, PICK, width)))
        else:
            outgoing = choose(both, second, first)
            chunks = forward_front(after.at[0:rows], after.at[rows:], outgoing)
            write_front(front, chunks)
            write_front(outgoing_packet, chunks, outgoing)
        write_field(kept.at[0], first)
        write_field(kept.at[1], second)


def backward_kernel(
    step, sections, planes, width, per_layer, owners, layers, first_inverse, second_inverse,
    packet, place, *rest
):
    blocks, rest = rest[:len(owners)], rest[len(owners):]
    kept, *rest = rest
    last = step == sections - 1
    if not last:
        incoming, before, *rest = rest
    if step:
        behind, *rest = rest
        held, *rest = rest
    result, *rest = rest
    if step:
        front, outgoing_packet, *rest = rest
    stacked, solved = rest
    own = lax.axis_index("sweep")
    count = kept.shape[-1] // LANES
    small = packet.at[2 * kept.shape[1]:]
    mine = own == step
    both = layers[step] == 2

    def whole_solve(layer):
        stack_fronts(blocks, owners, planes, per_layer, stacked, layer)
        solve((first_inverse, second_inverse)[layer], stacked, solved, layer)

    if not last:
        @pl.when(own != step)
        def _():
            result[...] = before[...]

        @pl.when(mine & both)
        def _():
            whole_solve(1)

    @pl.when(mine & both if last else mine)
    def _():
        whole_solve(0)

    @pl.when(mine)
    def _():
        first_fwd, second_fwd = split(kept[0]), split(kept[1])
        zero = [jnp.zeros_like(c) for c in first_fwd]
        if last:
            second, arriving = second_fwd, zero
        else:
            arriving = read_field(incoming, count)
            z = scaled(row_of(small, BWD + 1), arriving)
            local = scaled(row_of(small, ISC + 1), z)
            second = minus(second_fwd, gather_lanes(split(solved[1]), place[1:2, :], local))
        following = choose(both, second, arriving)
        z = scaled(row_of(small, BWD), following)
        local = scaled(row_of(small, ISC), z)
        change = gather_lanes(split(solved[0]), place[0:1, :], local)
        if last:
            change = choose(both, change, zero)
        first = minus(first_fwd, change)
        if step:
            chunks = backward_front(
                behind, first, read_field(held, count), layers[step - 1] == 2
            )
            write_front(front, chunks)
            write_front(outgoing_packet, chunks, first)
        write_field(result.at[0], first)
        write_field(result.at[1], choose(both, second, zero))


def whole(space=pltpu.VMEM):
    return pl.BlockSpec(memory_space=space)


def call(kernel, operands, outs, scratch, name, in_place=()):
    outs = [jax.ShapeDtypeStruct(*o) if isinstance(o, tuple) else o for o in outs]
    specs = [whole(pltpu.SMEM if o.ndim == 1 else pltpu.VMEM) for o in operands]
    for at in in_place:
        specs[at] = whole(pltpu.HBM)
    return pl.pallas_call(
        kernel,
        in_specs=specs,
        out_specs=[whole(pltpu.SMEM if len(o.shape) == 1 else pltpu.VMEM) for o in outs],
        out_shape=outs,
        scratch_shapes=scratch,
        compiler_params=pltpu.CompilerParams(vmem_limit_bytes=8 * 2**20),
        name=name,
    )(*operands)


def in_hbm(array):
    return pltpu.with_memory_space_constraint(array, pltpu.HBM)


def shards(
    rhs_field,
    front_inverse,
    interior_scale,
    forward_coupling,
    backward_coupling,
    front_cells,
    section_layers,
):
    sections, planes = lax.axis_size("sweep"), lax.axis_size("plane")
    layer_slots, parts, columns, cells = rhs_field.shape
    rows = parts * columns
    owned, order = front_inverse.shape[2:]
    width = -(-owned // LANES) * LANES
    per_layer = width // LANES
    chips = planes // CORES
    direct = planes in (2, 4, 8) and owned == width

    rhs = rhs_field.reshape(layer_slots, rows, cells)
    picked = jnp.pad(front_cells, ((0, 0), (0, width - owned)), constant_values=-1)
    layers = section_layers

    half_shape = ((per_layer, rows, LANES), BF16)
    front_shape = ((2 * per_layer, rows, LANES), BF16)
    packet_shape = ((2 * per_layer + 2 * (cells // LANES), rows, LANES), BF16)
    layers_shape = ((layer_slots, rows, cells), F32)
    scratch = [
        pltpu.VMEM((2, rows, order), BF16),
        pltpu.VMEM((2, rows, width), F32),
    ]

    def send(block, pair, *flips):
        pairs = [pair] if pair else [(i, i) for i in range(sections)]
        route = [
            (i * planes + own, j * planes + (own ^ flips[own % CORES % len(flips)]))
            for i, j in pairs for own in range(planes)
        ]
        return lax.ppermute(block, ("sweep", "plane"), route)

    def everywhere(front):
        slots = front.shape[0] // per_layer
        gathered = lax.all_gather(front, "plane")
        if owned != width:
            gathered = gathered.reshape(planes, slots, per_layer, rows, LANES)
            gathered = gathered.transpose(1, 3, 0, 2, 4).reshape(slots, rows, planes, width)
            gathered = gathered[..., :owned].reshape(slots, rows, order // LANES, LANES)
            gathered = gathered.transpose(0, 2, 1, 3)
            gathered = gathered.reshape(slots * order // LANES, rows, LANES)
            return [gathered], [[0]], order // LANES
        return [gathered], [list(range(planes))], per_layer

    def spread(front, straight, pair, beside=None):
        blocks, owners, tokens = [straight], [[(0, 0)]], []
        for step in [1] if chips == 2 else range(3, chips):
            blocks.append(send(front, pair, CORES * step))
            owners.append([(CORES * step, CORES * step)])
        if chips == 4:
            both = jnp.stack([front, send(front, None, 1)])
            tokens = beside(both) if beside else []
            blocks.append(send(both, pair, CORES, 2 * CORES))
            owners += [[(CORES + core, 2 * CORES + core) for core in range(CORES)]]
        short = [b[:2 * per_layer] if b.ndim == 3 else b for b in blocks]
        mine = jnp.concatenate([b[None] if b.ndim == 3 else b for b in short])
        for token in tokens:
            mine = mine + jnp.minimum(jnp.abs(token), 0).astype(BF16)
        blocks.append(send(mine, None, 1))
        owners.append([(one ^ 1, zero ^ 1) for places in owners for zero, one in places])
        return blocks, owners, per_layer

    def within(front, beside=None):
        return spread(front, front, None, beside) if direct else everywhere(front)

    def between(front, packet, start, stop):
        if not direct:
            packet = lax.ppermute(packet, "sweep", [(start, stop)])
            return *everywhere(packet[:2 * per_layer]), packet
        packet = send(packet, (start, stop), 0)
        return *spread(front, packet, (start, stop)), packet

    inverse = in_hbm(front_inverse)
    half_inverse = pltpu.VMEM(front_inverse.shape[1:], BF16)
    coefficients = (interior_scale, forward_coupling, backward_coupling)
    operands = [section_layers, rhs, *coefficients, picked]
    local, ahead, back, place, front, layers = call(
        functools.partial(first_kernel, width),
        [in_hbm(a) for a in operands],
        [
            ((2 * rows + 8, cells), F32),
            ((rows + NEEDS, 2 * width), F32),
            ((NEEDS, 2 * width), F32),
            ((2, cells), jnp.int32),
            front_shape,
            (section_layers.shape, jnp.int32),
        ],
        [pltpu.VMEM(a.shape, a.dtype) for a in operands[1:]] + [pltpu.SemaphoreType.DMA((6,))],
        "first_fronts",
        range(6),
    )
    after = lax.ppermute(ahead, "sweep", [(i + 1, i) for i in range(sections - 1)])
    behind = lax.ppermute(back, "sweep", [(i, i + 1) for i in range(sections - 1)])

    def load(token):
        return call(
            load_kernel,
            [inverse, token],
            [half_inverse, ((8, LANES), F32)],
            [pltpu.SemaphoreType.DMA((1,))],
            "load_first",
            [0],
        )

    if chips == 4 and direct:
        loaded = []

        def beside(both):
            loaded.extend(load(both))
            token = loaded[1][0, 0]
            return [after[0, 0], token, jnp.min(jnp.abs(behind - token))]

        gathered, owners, slots = within(front, beside)
        first_inverse = loaded[0]
    else:
        gathered, owners, slots = within(front)
        first_inverse = load(front)[0]

    kept, held = [], [None]
    for step in range(sections):
        final = step == sections - 1
        extra = ([held[step]] if step else []) + ([] if final else [after])
        outs = [layers_shape, half_shape if final else front_shape]
        outs += [] if final else [packet_shape]
        outs += [] if step else [half_inverse]
        outs = call(
            functools.partial(
                forward_kernel, step, sections, planes, width, slots, owners
            ),
            [layers, first_inverse, inverse, local, place, *gathered, *extra],
            outs,
            scratch + ([] if step else [pltpu.SemaphoreType.DMA((1,))]),
            f"forward_section_{step}",
            [] if step else [2],
        )
        if not step:
            inverse = outs[-1]
        kept.append(outs[0])
        if final:
            gathered, owners, slots = within(outs[1])
        else:
            gathered, owners, slots, incoming = between(outs[1], outs[2], step, step + 1)
            held.append(incoming)

    result = incoming = None
    for step in reversed(range(sections)):
        extra = ([] if result is None else [incoming, result]) + ([behind, held[step]] if step else [])
        outs = call(
            functools.partial(
                backward_kernel, step, sections, planes, width, slots, owners
            ),
            [layers, first_inverse, inverse, local, place, *gathered, kept[step], *extra],
            [layers_shape] + ([front_shape, packet_shape] if step else []),
            scratch,
            f"backward_section_{step}",
        )
        result = outs[0]
        if step:
            gathered, owners, slots, incoming = between(outs[1], outs[2], step, step - 1)
    return result.reshape(rhs_field.shape)


def solution(mesh):
    in_specs = (
        P("sweep", None, None, "plane"),
        P("sweep", None, "plane", None),
        P("sweep", "plane"),
        P("sweep", "plane"),
        P("sweep", "plane"),
        P("sweep", "plane"),
        P(),
    )
    out_specs = P("sweep", None, None, "plane")
    return jax.shard_map(shards, mesh=mesh, in_specs=in_specs, out_specs=out_specs, check_vma=False)
```

```python
import functools

import jax
import jax.numpy as jnp
from jax import lax
from jax.experimental import pallas as pl
from jax.experimental.pallas import tpu as pltpu
from jax.sharding import PartitionSpec as P

LANES = 128
CORES = 2
ISC, FWD, BWD, PICK = 0, 2, 4, 6
SLOPE, TURN, FOLD, CELL, NEEDS = 0, 1, 2, 3, 8
F32, BF16 = jnp.float32, jnp.bfloat16


def split(field):
    return [field[:, at:at + LANES] for at in range(0, field.shape[1], LANES)]


def gather_lanes(chunks, index, beyond=None):
    result = []
    for place, part in enumerate(split(index)):
        part = jnp.broadcast_to(part, chunks[0].shape)
        lane, chunk = part & (LANES - 1), part >> (LANES.bit_length() - 1)
        total = jnp.zeros(chunks[0].shape, F32) if beyond is None else beyond[place]
        for number, source in enumerate(chunks):
            found = jnp.take_along_axis(source, lane, axis=1, mode="promise_in_bounds")
            total = jnp.where(chunk == number, found, total)
        result.append(total)
    return result


def scaled(row, chunks):
    return [part * chunk for part, chunk in zip(split(row), chunks)]


def minus(left, right):
    return [a - b for a, b in zip(left, right)]


def choose(flag, left, right):
    return [jnp.where(flag, a, b) for a, b in zip(left, right)]


def rounded(chunks):
    return [c.astype(BF16).astype(F32) for c in chunks]


def row_of(ref, at):
    return ref[at:at + 1, :]


def picks(ref, at, width):
    return ref[at:at + 1, :width].astype(jnp.int32)


def halves(row):
    chunks = split(row)
    return chunks[:len(chunks) // 2], chunks[len(chunks) // 2:]


def times(left, right):
    return [a * b for a, b in zip(left, right)]


def plus(left, right):
    return [a + b for a, b in zip(left, right)]


def gathered_at(needs, field):
    cells = needs[CELL:CELL + 1, :].astype(jnp.int32)
    half = cells.shape[1] // 2
    return gather_lanes(field, cells[:, :half]), gather_lanes(field, cells[:, half:])


def forward_front(base, needs, incoming):
    (base_a, base_b), (slope_a, slope_b) = halves(base[...]), halves(row_of(needs, SLOPE))
    at_a, at_b = gathered_at(needs, incoming)
    return minus(base_a, times(slope_a, at_a)) + plus(base_b, times(slope_b, at_b))


def backward_front(needs, incoming, second_fwd, both):
    (turn_a, turn_b), (fold, _) = halves(row_of(needs, TURN)), halves(row_of(needs, FOLD))
    at_a, at_b = gathered_at(needs, incoming)
    second_a, _ = gathered_at(needs, second_fwd)
    following = choose(both, minus(second_a, times(fold, at_a)), at_a)
    return times(turn_a, following) + times(turn_b, at_b)


def write_front(ref, chunks, field=()):
    high = [c.astype(BF16) for c in field]
    low = [(c - h.astype(F32)).astype(BF16) for c, h in zip(field, high)]
    for at, chunk in enumerate(chunks + high + low):
        ref[at] = chunk.astype(BF16)


def read_field(packet, count):
    start = packet.shape[0] - 2 * count
    return [
        packet[start + i].astype(F32) + packet[start + count + i].astype(F32)
        for i in range(count)
    ]


def write_field(ref, chunks):
    for at, chunk in enumerate(chunks):
        ref[:, at * LANES:(at + 1) * LANES] = chunk


def owner_of(place, planes):
    if isinstance(place, int):
        return place
    own = lax.axis_index("plane")
    return lax.bitwise_xor(own, jnp.where(lax.rem(own, CORES) == 0, place[0], place[1]))


def stack_fronts(blocks, owners, planes, per_layer, stacked, layer):
    for ref, places in zip(blocks, owners):
        for number, place in enumerate(places):
            owner = owner_of(place, planes)
            for i in range(per_layer):
                at = pl.multiple_of((owner * per_layer + i) * LANES, LANES)
                slot = layer * per_layer + i
                piece = ref[slot] if len(ref.shape) == 3 else ref[number, slot]
                half = piece.shape[0] // 2
                wide = piece.astype(F32)
                turned = jnp.concatenate([-wide[half:], wide[:half]], axis=0)
                stacked[0, :, pl.ds(at, LANES)] = piece
                stacked[1, :, pl.ds(at, LANES)] = turned.astype(BF16)


def product(matrix, columns):
    return lax.dot_general(
        matrix, columns, (((1,), (1,)), ((), ())), preferred_element_type=F32
    )


def store_solved(solved, layer, out):
    rows = out.shape[0]
    if rows % LANES:
        out = jnp.concatenate([out, jnp.zeros((-rows % LANES, out.shape[1]), F32)], axis=0)
    solved[layer] = out.T


def solve(inverse, stacked, solved, layer):
    out = product(inverse[0], stacked[0]) + product(inverse[1], stacked[1])
    store_solved(solved, layer, out)


def places(picked, cells):
    rows = picked.shape[1]
    column = jnp.broadcast_to(picked.astype(F32), (8, rows)).T[:, 0:1].astype(jnp.int32)
    cell = lax.broadcasted_iota(jnp.int32, (rows, cells), 1)
    row = lax.broadcasted_iota(jnp.int32, (rows, cells), 0)
    return jnp.max(jnp.where(column == cell, row, -1), axis=0, keepdims=True)


def first_kernel(
    width, layers_in, rhs_in, isc_in, fwd_in, bwd_in, picked_in, local, ahead, place, front,
    layers, rhs, isc, fwd, bwd, picked, sems,
):
    pairs = (
        (rhs_in, rhs), (isc_in, isc), (fwd_in, fwd), (bwd_in, bwd), (picked_in, picked),
        (layers_in, layers),
    )
    copies = [pltpu.make_async_copy(a, b, sems.at[i]) for i, (a, b) in enumerate(pairs)]
    for copy in copies:
        copy.start()
    for copy in copies:
        copy.wait()
    cells = rhs.shape[-1]
    count = rhs.shape[1]
    small = local.at[2 * count:]
    small[ISC:ISC + 2, :] = isc[...]
    small[FWD:FWD + 2, :] = fwd[...]
    small[BWD:BWD + 2, :] = bwd[...]
    small[PICK:PICK + 2, :] = jnp.full((2, cells), -1, F32)
    small[PICK:PICK + 2, :width] = picked[...].astype(F32)
    local[0:count, :] = rhs[0]
    local[count:2 * count, :] = rhs[1]

    at_a, at_b = picked[0:1, :], picked[1:2, :]
    isc_a, isc_b, fwd_a, fwd_b, bwd_a, bwd_b = (
        split(jnp.broadcast_to(row_of(small, at), (8, cells))) for at in range(PICK)
    )
    base_a = gather_lanes(split(rhs[0]), at_a)
    fed = times(fwd_b, isc_a)
    base_b = gather_lanes(
        minus(split(rhs[1]), [f[0:1] * r for f, r in zip(fed, split(rhs[0]))]), at_b
    )
    write_front(front, base_a + base_b)
    zero = [jnp.zeros((8, LANES), F32)] * (width // LANES)
    rows = {
        SLOPE: gather_lanes(fwd_a, at_a) + gather_lanes(times(fed, fwd_a), at_b),
        TURN: gather_lanes(bwd_a, at_a) + gather_lanes(bwd_b, at_b),
        FOLD: gather_lanes(times(isc_b, bwd_b), at_a) + zero,
        CELL: split(at_a.astype(F32)) + split(at_b.astype(F32)),
    }
    ahead[count:, :] = jnp.zeros((NEEDS, ahead.shape[1]), F32)
    for at, chunks in rows.items():
        for i, chunk in enumerate(chunks):
            ahead[count + at:count + at + 1, i * LANES:(i + 1) * LANES] = chunk[0:1]
    write_field(ahead.at[0:count], base_a + base_b)
    for layer in range(2):
        place[layer:layer + 1, :] = places(picked[layer:layer + 1, :], cells)


def load_kernel(inverse, loaded, done, sem):
    load = pltpu.make_async_copy(inverse.at[0], loaded, sem.at[0])
    load.start()
    done[...] = jnp.zeros(done.shape, F32)
    load.wait()


def join_kernel(*refs):
    *blocks, _, _, joined = refs
    at = 0
    for block in blocks:
        for piece in [block] if len(block.shape) == 3 else [block.at[i] for i in range(block.shape[0])]:
            joined[at] = piece[...]
            at += 1


def forward_kernel(
    step, sections, planes, width, per_layer, owners, layers, first_inverse, inverse, packet,
    place, *rest
):
    blocks, rest = rest[:len(owners)], rest[len(owners):]
    final = step == sections - 1
    if step:
        incoming, *rest = rest
    if not final:
        after, *rest = rest
    kept, front, *rest = rest
    if not final:
        outgoing_packet, *rest = rest
    if step == 0:
        stacked, solved, sems, second_inverse = rest
    elif step == 1:
        second_inverse, stacked, solved, sems = rest
    else:
        second_inverse, (stacked, solved) = inverse, rest
    own = lax.axis_index("sweep")
    cells = packet.shape[-1]
    count = cells // LANES
    rows = kept.shape[1]
    small = packet.at[2 * rows:]
    mine = own == step
    both = layers[step] == 2
    loads = [mine, step == 1][step] if step < 2 else False
    load = pltpu.make_async_copy(inverse.at[1], second_inverse, sems.at[0]) if step < 2 else None

    if step < 2:
        pl.when(loads)(load.start)

    def whole_solve(layer, matrices):
        stack_fronts(blocks, owners, planes, per_layer, stacked, layer)
        solve(matrices, stacked, solved, layer)

    @pl.when(mine)
    def _():
        whole_solve(0, first_inverse)

    if step < 2:
        pl.when(loads)(load.wait)

    @pl.when(mine & both)
    def _():
        whole_solve(1, second_inverse)

    @pl.when(mine)
    def _():
        rhs_a, rhs_b = split(packet[0:rows, :]), split(packet[rows:2 * rows, :])
        first_res = rhs_a
        if step:
            first_res = minus(rhs_a, scaled(row_of(small, FWD), read_field(incoming, count)))
        first = gather_lanes(
            split(solved[0]), place[0:1, :], scaled(row_of(small, ISC), first_res)
        )
        second_res = minus(rhs_b, scaled(row_of(small, FWD + 1), first))
        second = gather_lanes(
            split(solved[1]), place[1:2, :], scaled(row_of(small, ISC + 1), second_res)
        )
        if final:
            z = scaled(row_of(small, BWD), choose(both, second, [jnp.zeros_like(c) for c in first]))
            write_front(front, gather_lanes(rounded(z), picks(small, PICK, width)))
        else:
            outgoing = choose(both, second, first)
            chunks = forward_front(after.at[0:rows], after.at[rows:], outgoing)
            write_front(front, chunks)
            write_front(outgoing_packet, chunks, outgoing)
        write_field(kept.at[0], first)
        write_field(kept.at[1], second)


def backward_kernel(
    step, sections, planes, width, per_layer, owners, layers, first_inverse, second_inverse,
    packet, place, *rest
):
    blocks, rest = rest[:len(owners)], rest[len(owners):]
    kept, *rest = rest
    last = step == sections - 1
    if not last:
        incoming, before, *rest = rest
    if step:
        behind, *rest = rest
        held, *rest = rest
    result, *rest = rest
    if step:
        front, outgoing_packet, *rest = rest
    stacked, solved = rest
    own = lax.axis_index("sweep")
    count = kept.shape[-1] // LANES
    small = packet.at[2 * kept.shape[1]:]
    mine = own == step
    both = layers[step] == 2

    def whole_solve(layer):
        stack_fronts(blocks, owners, planes, per_layer, stacked, layer)
        solve((first_inverse, second_inverse)[layer], stacked, solved, layer)

    if not last:
        @pl.when(own != step)
        def _():
            result[...] = before[...]

        @pl.when(mine & both)
        def _():
            whole_solve(1)

    @pl.when(mine & both if last else mine)
    def _():
        whole_solve(0)

    @pl.when(mine)
    def _():
        first_fwd, second_fwd = split(kept[0]), split(kept[1])
        zero = [jnp.zeros_like(c) for c in first_fwd]
        if last:
            second, arriving = second_fwd, zero
        else:
            arriving = read_field(incoming, count)
            z = scaled(row_of(small, BWD + 1), arriving)
            local = scaled(row_of(small, ISC + 1), z)
            second = minus(second_fwd, gather_lanes(split(solved[1]), place[1:2, :], local))
        following = choose(both, second, arriving)
        z = scaled(row_of(small, BWD), following)
        local = scaled(row_of(small, ISC), z)
        change = gather_lanes(split(solved[0]), place[0:1, :], local)
        if last:
            change = choose(both, change, zero)
        first = minus(first_fwd, change)
        if step:
            chunks = backward_front(
                behind.at[kept.shape[1]:], first, read_field(held, count), layers[step - 1] == 2
            )
            write_front(front, chunks)
            write_front(outgoing_packet, chunks, first)
        write_field(result.at[0], first)
        write_field(result.at[1], choose(both, second, zero))


def whole(space=pltpu.VMEM):
    return pl.BlockSpec(memory_space=space)


def call(kernel, operands, outs, scratch, name, in_place=(), more_vmem=0):
    outs = [jax.ShapeDtypeStruct(*o) if isinstance(o, tuple) else o for o in outs]
    specs = [whole(pltpu.SMEM if o.ndim == 1 else pltpu.VMEM) for o in operands]
    for at in in_place:
        specs[at] = whole(pltpu.HBM)
    return pl.pallas_call(
        kernel,
        in_specs=specs,
        out_specs=[whole(pltpu.SMEM if len(o.shape) == 1 else pltpu.VMEM) for o in outs],
        out_shape=outs,
        scratch_shapes=scratch,
        compiler_params=pltpu.CompilerParams(vmem_limit_bytes=8 * 2**20 + more_vmem),
        name=name,
    )(*operands)


def in_hbm(array):
    return pltpu.with_memory_space_constraint(array, pltpu.HBM)


def shards(
    rhs_field,
    front_inverse,
    interior_scale,
    forward_coupling,
    backward_coupling,
    front_cells,
    section_layers,
):
    sections, planes = lax.axis_size("sweep"), lax.axis_size("plane")
    layer_slots, parts, columns, cells = rhs_field.shape
    rows = parts * columns
    owned, order = front_inverse.shape[2:]
    width = -(-owned // LANES) * LANES
    per_layer = width // LANES
    chips = planes // CORES
    direct = planes in (2, 4, 8) and owned == width

    rhs = rhs_field.reshape(layer_slots, rows, cells)
    picked = jnp.pad(front_cells, ((0, 0), (0, width - owned)), constant_values=-1)
    layers = section_layers

    half_shape = ((per_layer, rows, LANES), BF16)
    front_shape = ((2 * per_layer, rows, LANES), BF16)
    packet_shape = ((2 * per_layer + 2 * (cells // LANES), rows, LANES), BF16)
    layers_shape = ((layer_slots, rows, cells), F32)
    scratch = [
        pltpu.VMEM((2, rows, order), BF16),
        pltpu.VMEM((2, rows, width), F32),
    ]

    def send(block, shift, *flips):
        route = [
            (i * planes + own, (i + shift) % sections * planes + (own ^ flips[own % len(flips)]))
            for i in range(sections) for own in range(planes)
        ]
        return lax.ppermute(block, ("sweep", "plane"), route)

    def everywhere(front):
        slots = front.shape[0] // per_layer
        gathered = lax.all_gather(front, "plane")
        if owned != width:
            gathered = gathered.reshape(planes, slots, per_layer, rows, LANES)
            gathered = gathered.transpose(1, 3, 0, 2, 4).reshape(slots, rows, planes, width)
            gathered = gathered[..., :owned].reshape(slots, rows, order // LANES, LANES)
            gathered = gathered.transpose(0, 2, 1, 3)
            gathered = gathered.reshape(slots * order // LANES, rows, LANES)
            return [gathered], [[0]], order // LANES
        return [gathered], [list(range(planes))], per_layer

    def spread(front, straight, shift, join=None):
        blocks, owners = [straight], [[(0, 0)]]
        for step in [1] if chips == 2 else range(3, chips):
            blocks.append(send(front, shift, CORES * step))
            owners.append([(CORES * step, CORES * step)])
        if chips == 4:
            both = jnp.stack([front, send(front, 0, 1)])
            blocks.append(send(both, shift, CORES, 2 * CORES))
            owners += [[(CORES + core, 2 * CORES + core) for core in range(CORES)]]
        if join:
            mine = join(blocks)
        else:
            short = [b[:2 * per_layer] if b.ndim == 3 else b for b in blocks]
            mine = jnp.concatenate([b[None] if b.ndim == 3 else b for b in short])
        blocks.append(send(mine, 0, 1))
        owners.append([(one ^ 1, zero ^ 1) for places in owners for zero, one in places])
        return blocks, owners, per_layer

    def within(front, join=None):
        return spread(front, front, 0, join) if direct else everywhere(front)

    def between(front, packet, start, stop):
        if not direct:
            packet = lax.ppermute(packet, "sweep", [(start, stop)])
            return *everywhere(packet[:2 * per_layer]), packet
        packet = send(packet, stop - start, 0)
        return *spread(front, packet, stop - start), packet

    inverse = in_hbm(front_inverse)
    half_inverse = pltpu.VMEM(front_inverse.shape[1:], BF16)
    coefficients = (interior_scale, forward_coupling, backward_coupling)
    operands = [section_layers, rhs, *coefficients, picked]
    local, ahead, place, front, layers = call(
        functools.partial(first_kernel, width),
        [in_hbm(a) for a in operands],
        [
            ((2 * rows + 8, cells), F32),
            ((rows + NEEDS, 2 * width), F32),
            ((2, cells), jnp.int32),
            front_shape,
            (section_layers.shape, jnp.int32),
        ],
        [pltpu.VMEM(a.shape, a.dtype) for a in operands[1:]] + [pltpu.SemaphoreType.DMA((6,))],
        "first_fronts",
        range(6),
    )
    after = lax.ppermute(ahead, "sweep", [(i + 1, i) for i in range(sections - 1)])
    first_inverse, token = call(
        load_kernel,
        [inverse],
        [half_inverse, ((8, LANES), F32)],
        [pltpu.SemaphoreType.DMA((1,))],
        "load_first",
        [0],
    )

    def join(blocks):
        shape = (sum(b.shape[0] if b.ndim == 4 else 1 for b in blocks), *front_shape[0])
        return call(join_kernel, [*blocks, after, token], [(shape, BF16)], [], "join")[0]

    gathered, owners, slots = within(front, join)

    kept, held = [], [None]
    for step in range(sections):
        final = step == sections - 1
        extra = ([held[step]] if step else []) + ([] if final else [after])
        outs = [layers_shape, half_shape if final else front_shape]
        outs += [] if final else [packet_shape]
        outs += [half_inverse] if step == 1 else []
        room = [pltpu.SemaphoreType.DMA((1,))] if step < 2 else []
        outs = call(
            functools.partial(
                forward_kernel, step, sections, planes, width, slots, owners
            ),
            [layers, first_inverse, inverse, local, place, *gathered, *extra],
            outs,
            scratch + room + ([] if step else [half_inverse]),
            f"forward_section_{step}",
            [2] if step < 2 else [],
            0 if step else front_inverse.size,
        )
        if step == 1:
            inverse = outs[-1]
        kept.append(outs[0])
        if final:
            behind = lax.ppermute(ahead, "sweep", [(i, i + 1) for i in range(sections - 1)])
            gathered, owners, slots = within(outs[1])
        else:
            gathered, owners, slots, incoming = between(outs[1], outs[2], step, step + 1)
            held.append(incoming)

    result = incoming = None
    for step in reversed(range(sections)):
        extra = ([] if result is None else [incoming, result]) + ([behind, held[step]] if step else [])
        outs = call(
            functools.partial(
                backward_kernel, step, sections, planes, width, slots, owners
            ),
            [layers, first_inverse, inverse, local, place, *gathered, kept[step], *extra],
            [layers_shape] + ([front_shape, packet_shape] if step else []),
            scratch,
            f"backward_section_{step}",
        )
        result = outs[0]
        if step:
            gathered, owners, slots, incoming = between(outs[1], outs[2], step, step - 1)
    return result.reshape(rhs_field.shape)


def solution(mesh):
    in_specs = (
        P("sweep", None, None, "plane"),
        P("sweep", None, "plane", None),
        P("sweep", "plane"),
        P("sweep", "plane"),
        P("sweep", "plane"),
        P("sweep", "plane"),
        P(),
    )
    out_specs = P("sweep", None, None, "plane")
    return jax.shard_map(shards, mesh=mesh, in_specs=in_specs, out_specs=out_specs, check_vma=False)
```

```python
import functools

import jax
import jax.numpy as jnp
from jax import lax
from jax.experimental import pallas as pl
from jax.experimental.pallas import tpu as pltpu
from jax.sharding import PartitionSpec as P

LANES = 128
CORES = 2
ISC, FWD, BWD, PICK = 0, 2, 4, 6
SLOPE, TURN, FOLD, CELL, NEEDS = 0, 1, 2, 3, 8
F32, BF16 = jnp.float32, jnp.bfloat16


def split(field):
    return [field[:, at:at + LANES] for at in range(0, field.shape[1], LANES)]


def gather_lanes(chunks, index, beyond=None):
    result = []
    for place, part in enumerate(split(index)):
        part = jnp.broadcast_to(part, chunks[0].shape)
        lane, chunk = part & (LANES - 1), part >> (LANES.bit_length() - 1)
        total = jnp.zeros(chunks[0].shape, F32) if beyond is None else beyond[place]
        for number, source in enumerate(chunks):
            found = jnp.take_along_axis(source, lane, axis=1, mode="promise_in_bounds")
            total = jnp.where(chunk == number, found, total)
        result.append(total)
    return result


def scaled(row, chunks):
    return [part * chunk for part, chunk in zip(split(row), chunks)]


def minus(left, right):
    return [a - b for a, b in zip(left, right)]


def choose(flag, left, right):
    return [jnp.where(flag, a, b) for a, b in zip(left, right)]


def rounded(chunks):
    return [c.astype(BF16).astype(F32) for c in chunks]


def row_of(ref, at):
    return ref[at:at + 1, :]


def picks(ref, at, width):
    return ref[at:at + 1, :width].astype(jnp.int32)


def halves(row):
    chunks = split(row)
    return chunks[:len(chunks) // 2], chunks[len(chunks) // 2:]


def times(left, right):
    return [a * b for a, b in zip(left, right)]


def plus(left, right):
    return [a + b for a, b in zip(left, right)]


def gathered_at(needs, field):
    cells = needs[CELL:CELL + 1, :].astype(jnp.int32)
    half = cells.shape[1] // 2
    return gather_lanes(field, cells[:, :half]), gather_lanes(field, cells[:, half:])


def forward_front(base, needs, incoming):
    (base_a, base_b), (slope_a, slope_b) = halves(base[...]), halves(row_of(needs, SLOPE))
    at_a, at_b = gathered_at(needs, incoming)
    return minus(base_a, times(slope_a, at_a)) + plus(base_b, times(slope_b, at_b))


def backward_front(needs, incoming, second_fwd, both):
    (turn_a, turn_b), (fold, _) = halves(row_of(needs, TURN)), halves(row_of(needs, FOLD))
    at_a, at_b = gathered_at(needs, incoming)
    second_a, _ = gathered_at(needs, second_fwd)
    following = choose(both, minus(second_a, times(fold, at_a)), at_a)
    return times(turn_a, following) + times(turn_b, at_b)


def write_front(ref, chunks, field=()):
    high = [c.astype(BF16) for c in field]
    low = [(c - h.astype(F32)).astype(BF16) for c, h in zip(field, high)]
    for at, chunk in enumerate(chunks + high + low):
        ref[at] = chunk.astype(BF16)


def read_field(packet, count):
    start = packet.shape[0] - 2 * count
    return [
        packet[start + i].astype(F32) + packet[start + count + i].astype(F32)
        for i in range(count)
    ]


def write_field(ref, chunks):
    for at, chunk in enumerate(chunks):
        ref[:, at * LANES:(at + 1) * LANES] = chunk


def owner_of(place, planes):
    if isinstance(place, int):
        return place
    own = lax.axis_index("plane")
    return lax.bitwise_xor(own, jnp.where(lax.rem(own, CORES) == 0, place[0], place[1]))


def stack_fronts(blocks, owners, planes, per_layer, stacked, layer):
    for ref, places in zip(blocks, owners):
        for number, place in enumerate(places):
            owner = owner_of(place, planes)
            for i in range(per_layer):
                at = pl.multiple_of((owner * per_layer + i) * LANES, LANES)
                slot = layer * per_layer + i
                piece = ref[slot] if len(ref.shape) == 3 else ref[number, slot]
                half = piece.shape[0] // 2
                wide = piece.astype(F32)
                turned = jnp.concatenate([-wide[half:], wide[:half]], axis=0)
                stacked[0, :, pl.ds(at, LANES)] = piece
                stacked[1, :, pl.ds(at, LANES)] = turned.astype(BF16)


def product(matrix, columns):
    return lax.dot_general(
        matrix, columns, (((1,), (1,)), ((), ())), preferred_element_type=F32
    )


def store_solved(solved, layer, out):
    rows = out.shape[0]
    if rows % LANES:
        out = jnp.concatenate([out, jnp.zeros((-rows % LANES, out.shape[1]), F32)], axis=0)
    solved[layer] = out.T


def solve(inverse, stacked, solved, layer):
    out = product(inverse[0], stacked[0]) + product(inverse[1], stacked[1])
    store_solved(solved, layer, out)


def places(picked, cells):
    rows = picked.shape[1]
    column = jnp.broadcast_to(picked.astype(F32), (8, rows)).T[:, 0:1].astype(jnp.int32)
    cell = lax.broadcasted_iota(jnp.int32, (rows, cells), 1)
    row = lax.broadcasted_iota(jnp.int32, (rows, cells), 0)
    return jnp.max(jnp.where(column == cell, row, -1), axis=0, keepdims=True)


def first_kernel(
    width, layers_in, rhs_in, isc_in, fwd_in, bwd_in, picked_in, local, ahead, place, front,
    layers, rhs, isc, fwd, bwd, picked, sems,
):
    pairs = (
        (rhs_in, rhs), (isc_in, isc), (fwd_in, fwd), (bwd_in, bwd), (picked_in, picked),
        (layers_in, layers),
    )
    copies = [pltpu.make_async_copy(a, b, sems.at[i]) for i, (a, b) in enumerate(pairs)]
    for copy in copies:
        copy.start()
    for copy in copies:
        copy.wait()
    cells = rhs.shape[-1]
    count = rhs.shape[1]
    small = local.at[2 * count:]
    small[ISC:ISC + 2, :] = isc[...]
    small[FWD:FWD + 2, :] = fwd[...]
    small[BWD:BWD + 2, :] = bwd[...]
    small[PICK:PICK + 2, :] = jnp.full((2, cells), -1, F32)
    small[PICK:PICK + 2, :width] = picked[...].astype(F32)
    local[0:count, :] = rhs[0]
    local[count:2 * count, :] = rhs[1]

    at_a, at_b = picked[0:1, :], picked[1:2, :]
    isc_a, isc_b, fwd_a, fwd_b, bwd_a, bwd_b = (
        split(jnp.broadcast_to(row_of(small, at), (8, cells))) for at in range(PICK)
    )
    base_a = gather_lanes(split(rhs[0]), at_a)
    fed = times(fwd_b, isc_a)
    base_b = gather_lanes(
        minus(split(rhs[1]), [f[0:1] * r for f, r in zip(fed, split(rhs[0]))]), at_b
    )
    write_front(front, base_a + base_b)
    zero = [jnp.zeros((8, LANES), F32)] * (width // LANES)
    rows = {
        SLOPE: gather_lanes(fwd_a, at_a) + gather_lanes(times(fed, fwd_a), at_b),
        TURN: gather_lanes(bwd_a, at_a) + gather_lanes(bwd_b, at_b),
        FOLD: gather_lanes(times(isc_b, bwd_b), at_a) + zero,
        CELL: split(at_a.astype(F32)) + split(at_b.astype(F32)),
    }
    ahead[count:, :] = jnp.zeros((NEEDS, ahead.shape[1]), F32)
    for at, chunks in rows.items():
        for i, chunk in enumerate(chunks):
            ahead[count + at:count + at + 1, i * LANES:(i + 1) * LANES] = chunk[0:1]
    write_field(ahead.at[0:count], base_a + base_b)
    for layer in range(2):
        place[layer:layer + 1, :] = places(picked[layer:layer + 1, :], cells)


def load_kernel(inverse, first, second, done, sems):
    loads = [
        pltpu.make_async_copy(inverse.at[layer], half, sems.at[layer])
        for layer, half in enumerate((first, second))
    ]
    later = lax.axis_index("sweep") == 0
    loads[0].start()
    pl.when(~later)(loads[1].start)
    done[...] = jnp.zeros(done.shape, F32)
    loads[0].wait()
    pl.when(~later)(loads[1].wait)


def join_kernel(*refs):
    *blocks, _, _, joined = refs
    at = 0
    for block in blocks:
        for piece in [block] if len(block.shape) == 3 else [block.at[i] for i in range(block.shape[0])]:
            joined[at] = piece[...]
            at += 1


def forward_kernel(
    step, sections, planes, width, per_layer, owners, layers, first_inverse, second_inverse,
    packet, place, *rest
):
    if not step:
        inverse, *rest = rest
    blocks, rest = rest[:len(owners)], rest[len(owners):]
    final = step == sections - 1
    if step:
        incoming, *rest = rest
    if not final:
        after, *rest = rest
    kept, front, *rest = rest
    if not final:
        outgoing_packet, *rest = rest
    if step:
        stacked, solved = rest
    else:
        second_inverse, stacked, solved, sems = rest
    own = lax.axis_index("sweep")
    cells = packet.shape[-1]
    count = cells // LANES
    rows = kept.shape[1]
    small = packet.at[2 * rows:]
    mine = own == step
    both = layers[step] == 2
    if not step:
        load = pltpu.make_async_copy(inverse.at[1], second_inverse, sems.at[0])
        pl.when(mine)(load.start)

    def whole_solve(layer, matrices):
        stack_fronts(blocks, owners, planes, per_layer, stacked, layer)
        solve(matrices, stacked, solved, layer)

    @pl.when(mine)
    def _():
        whole_solve(0, first_inverse)

    if not step:
        pl.when(mine)(load.wait)

    @pl.when(mine & both)
    def _():
        whole_solve(1, second_inverse)

    @pl.when(mine)
    def _():
        rhs_a, rhs_b = split(packet[0:rows, :]), split(packet[rows:2 * rows, :])
        first_res = rhs_a
        if step:
            first_res = minus(rhs_a, scaled(row_of(small, FWD), read_field(incoming, count)))
        first = gather_lanes(
            split(solved[0]), place[0:1, :], scaled(row_of(small, ISC), first_res)
        )
        second_res = minus(rhs_b, scaled(row_of(small, FWD + 1), first))
        second = gather_lanes(
            split(solved[1]), place[1:2, :], scaled(row_of(small, ISC + 1), second_res)
        )
        if final:
            z = scaled(row_of(small, BWD), choose(both, second, [jnp.zeros_like(c) for c in first]))
            write_front(front, gather_lanes(rounded(z), picks(small, PICK, width)))
        else:
            outgoing = choose(both, second, first)
            chunks = forward_front(after.at[0:rows], after.at[rows:], outgoing)
            write_front(front, chunks)
            write_front(outgoing_packet, chunks, outgoing)
        write_field(kept.at[0], first)
        write_field(kept.at[1], second)


def backward_kernel(
    step, sections, planes, width, per_layer, owners, layers, first_inverse, second_inverse,
    packet, place, *rest
):
    blocks, rest = rest[:len(owners)], rest[len(owners):]
    kept, *rest = rest
    last = step == sections - 1
    if not last:
        incoming, before, *rest = rest
    if step:
        behind, *rest = rest
        held, *rest = rest
    result, *rest = rest
    if step:
        front, outgoing_packet, *rest = rest
    stacked, solved = rest
    own = lax.axis_index("sweep")
    count = kept.shape[-1] // LANES
    small = packet.at[2 * kept.shape[1]:]
    mine = own == step
    both = layers[step] == 2

    def whole_solve(layer):
        stack_fronts(blocks, owners, planes, per_layer, stacked, layer)
        solve((first_inverse, second_inverse)[layer], stacked, solved, layer)

    if not last:
        @pl.when(own != step)
        def _():
            result[...] = before[...]

        @pl.when(mine & both)
        def _():
            whole_solve(1)

    @pl.when(mine & both if last else mine)
    def _():
        whole_solve(0)

    @pl.when(mine)
    def _():
        first_fwd, second_fwd = split(kept[0]), split(kept[1])
        zero = [jnp.zeros_like(c) for c in first_fwd]
        if last:
            second, arriving = second_fwd, zero
        else:
            arriving = read_field(incoming, count)
            z = scaled(row_of(small, BWD + 1), arriving)
            local = scaled(row_of(small, ISC + 1), z)
            second = minus(second_fwd, gather_lanes(split(solved[1]), place[1:2, :], local))
        following = choose(both, second, arriving)
        z = scaled(row_of(small, BWD), following)
        local = scaled(row_of(small, ISC), z)
        change = gather_lanes(split(solved[0]), place[0:1, :], local)
        if last:
            change = choose(both, change, zero)
        first = minus(first_fwd, change)
        if step:
            chunks = backward_front(
                behind.at[kept.shape[1]:], first, read_field(held, count), layers[step - 1] == 2
            )
            write_front(front, chunks)
            write_front(outgoing_packet, chunks, first)
        write_field(result.at[0], first)
        write_field(result.at[1], choose(both, second, zero))


def whole(space=pltpu.VMEM):
    return pl.BlockSpec(memory_space=space)


def call(kernel, operands, outs, scratch, name, in_place=(), aliases={}):
    outs = [jax.ShapeDtypeStruct(*o) if isinstance(o, tuple) else o for o in outs]
    specs = [whole(pltpu.SMEM if o.ndim == 1 else pltpu.VMEM) for o in operands]
    for at in in_place:
        specs[at] = whole(pltpu.HBM)
    return pl.pallas_call(
        kernel,
        in_specs=specs,
        out_specs=[whole(pltpu.SMEM if len(o.shape) == 1 else pltpu.VMEM) for o in outs],
        out_shape=outs,
        scratch_shapes=scratch,
        input_output_aliases=aliases,
        compiler_params=pltpu.CompilerParams(vmem_limit_bytes=8 * 2**20),
        name=name,
    )(*operands)


def in_hbm(array):
    return pltpu.with_memory_space_constraint(array, pltpu.HBM)


def shards(
    rhs_field,
    front_inverse,
    interior_scale,
    forward_coupling,
    backward_coupling,
    front_cells,
    section_layers,
):
    sections, planes = lax.axis_size("sweep"), lax.axis_size("plane")
    layer_slots, parts, columns, cells = rhs_field.shape
    rows = parts * columns
    owned, order = front_inverse.shape[2:]
    width = -(-owned // LANES) * LANES
    per_layer = width // LANES
    chips = planes // CORES
    direct = planes in (2, 4, 8) and owned == width

    rhs = rhs_field.reshape(layer_slots, rows, cells)
    picked = jnp.pad(front_cells, ((0, 0), (0, width - owned)), constant_values=-1)
    layers = section_layers

    half_shape = ((per_layer, rows, LANES), BF16)
    front_shape = ((2 * per_layer, rows, LANES), BF16)
    packet_shape = ((2 * per_layer + 2 * (cells // LANES), rows, LANES), BF16)
    layers_shape = ((layer_slots, rows, cells), F32)
    scratch = [
        pltpu.VMEM((2, rows, order), BF16),
        pltpu.VMEM((2, rows, width), F32),
    ]

    def send(block, shift, *flips):
        route = [
            (i * planes + own, (i + shift) % sections * planes + (own ^ flips[own % len(flips)]))
            for i in range(sections) for own in range(planes)
        ]
        return lax.ppermute(block, ("sweep", "plane"), route)

    def everywhere(front):
        slots = front.shape[0] // per_layer
        gathered = lax.all_gather(front, "plane")
        if owned != width:
            gathered = gathered.reshape(planes, slots, per_layer, rows, LANES)
            gathered = gathered.transpose(1, 3, 0, 2, 4).reshape(slots, rows, planes, width)
            gathered = gathered[..., :owned].reshape(slots, rows, order // LANES, LANES)
            gathered = gathered.transpose(0, 2, 1, 3)
            gathered = gathered.reshape(slots * order // LANES, rows, LANES)
            return [gathered], [[0]], order // LANES
        return [gathered], [list(range(planes))], per_layer

    def spread(front, straight, shift, join=None):
        blocks, owners = [straight], [[(0, 0)]]
        for step in [1] if chips == 2 else range(3, chips):
            blocks.append(send(front, shift, CORES * step))
            owners.append([(CORES * step, CORES * step)])
        if chips == 4:
            both = jnp.stack([front, send(front, 0, 1)])
            blocks.append(send(both, shift, CORES, 2 * CORES))
            owners += [[(CORES + core, 2 * CORES + core) for core in range(CORES)]]
        if join:
            mine = join(blocks)
        else:
            short = [b[:2 * per_layer] if b.ndim == 3 else b for b in blocks]
            mine = jnp.concatenate([b[None] if b.ndim == 3 else b for b in short])
        blocks.append(send(mine, 0, 1))
        owners.append([(one ^ 1, zero ^ 1) for places in owners for zero, one in places])
        return blocks, owners, per_layer

    def within(front, join=None):
        return spread(front, front, 0, join) if direct else everywhere(front)

    def between(front, packet, start, stop):
        packet = lax.ppermute(packet, "sweep", [(start, stop)])
        if not direct:
            return *everywhere(packet[:2 * per_layer]), packet
        return *spread(front, packet, stop - start), packet

    inverse = in_hbm(front_inverse)
    half_inverse = pltpu.VMEM(front_inverse.shape[1:], BF16)
    coefficients = (interior_scale, forward_coupling, backward_coupling)
    operands = [section_layers, rhs, *coefficients, picked]
    local, ahead, place, front, layers = call(
        functools.partial(first_kernel, width),
        [in_hbm(a) for a in operands],
        [
            ((2 * rows + 8, cells), F32),
            ((rows + NEEDS, 2 * width), F32),
            ((2, cells), jnp.int32),
            front_shape,
            (section_layers.shape, jnp.int32),
        ],
        [pltpu.VMEM(a.shape, a.dtype) for a in operands[1:]] + [pltpu.SemaphoreType.DMA((6,))],
        "first_fronts",
        range(6),
    )
    after = lax.ppermute(ahead, "sweep", [(i + 1, i) for i in range(sections - 1)])
    first_inverse, second_inverse, token = call(
        load_kernel,
        [inverse],
        [half_inverse, half_inverse, ((8, LANES), F32)],
        [pltpu.SemaphoreType.DMA((2,))],
        "load_first",
        [0],
    )

    def join(blocks):
        shape = (sum(b.shape[0] if b.ndim == 4 else 1 for b in blocks), *front_shape[0])
        return call(join_kernel, [*blocks, after, token], [(shape, BF16)], [], "join")[0]

    gathered, owners, slots = within(front, join)

    kept, held = [], [None]
    for step in range(sections):
        final = step == sections - 1
        extra = ([held[step]] if step else []) + ([] if final else [after])
        outs = [layers_shape, half_shape if final else front_shape]
        outs += [] if final else [packet_shape]
        outs += [] if step else [half_inverse]
        outs = call(
            functools.partial(
                forward_kernel, step, sections, planes, width, slots, owners
            ),
            [layers, first_inverse, second_inverse, local, place]
            + ([] if step else [inverse]) + [*gathered, *extra],
            outs,
            scratch + ([] if step else [pltpu.SemaphoreType.DMA((1,))]),
            f"forward_section_{step}",
            [] if step else [5],
            {} if step else {2: len(outs) - 1},
        )
        if not step:
            second_inverse = outs[-1]
        kept.append(outs[0])
        if final:
            behind = lax.ppermute(ahead, "sweep", [(i, i + 1) for i in range(sections - 1)])
            gathered, owners, slots = within(outs[1])
        else:
            gathered, owners, slots, incoming = between(outs[1], outs[2], step, step + 1)
            held.append(incoming)

    result = incoming = None
    for step in reversed(range(sections)):
        extra = ([] if result is None else [incoming, result]) + ([behind, held[step]] if step else [])
        outs = call(
            functools.partial(
                backward_kernel, step, sections, planes, width, slots, owners
            ),
            [layers, first_inverse, second_inverse, local, place, *gathered, kept[step], *extra],
            [layers_shape] + ([front_shape, packet_shape] if step else []),
            scratch,
            f"backward_section_{step}",
        )
        result = outs[0]
        if step:
            gathered, owners, slots, incoming = between(outs[1], outs[2], step, step - 1)
    return result.reshape(rhs_field.shape)


def solution(mesh):
    in_specs = (
        P("sweep", None, None, "plane"),
        P("sweep", None, "plane", None),
        P("sweep", "plane"),
        P("sweep", "plane"),
        P("sweep", "plane"),
        P("sweep", "plane"),
        P(),
    )
    out_specs = P("sweep", None, None, "plane")
    return jax.shard_map(shards, mesh=mesh, in_specs=in_specs, out_specs=out_specs, check_vma=False)
```

```python
import functools

import jax
import jax.numpy as jnp
from jax import lax
from jax.experimental import pallas as pl
from jax.experimental.pallas import tpu as pltpu
from jax.sharding import PartitionSpec as P

LANES = 128
CORES = 2
ISC, FWD, BWD, PICK = 0, 2, 4, 6
SLOPE, TURN, FOLD, CELL, NEEDS = 0, 1, 2, 3, 8
F32, BF16 = jnp.float32, jnp.bfloat16


def split(field):
    return [field[:, at:at + LANES] for at in range(0, field.shape[1], LANES)]


def gather_lanes(chunks, index, beyond=None):
    result = []
    for place, part in enumerate(split(index)):
        part = jnp.broadcast_to(part, chunks[0].shape)
        lane, chunk = part & (LANES - 1), part >> (LANES.bit_length() - 1)
        total = jnp.zeros(chunks[0].shape, F32) if beyond is None else beyond[place]
        for number, source in enumerate(chunks):
            found = jnp.take_along_axis(source, lane, axis=1, mode="promise_in_bounds")
            total = jnp.where(chunk == number, found, total)
        result.append(total)
    return result


def scaled(row, chunks):
    return [part * chunk for part, chunk in zip(split(row), chunks)]


def minus(left, right):
    return [a - b for a, b in zip(left, right)]


def choose(flag, left, right):
    return [jnp.where(flag, a, b) for a, b in zip(left, right)]


def rounded(chunks):
    return [c.astype(BF16).astype(F32) for c in chunks]


def row_of(ref, at):
    return ref[at:at + 1, :]


def picks(ref, at, width):
    return ref[at:at + 1, :width].astype(jnp.int32)


def halves(row):
    chunks = split(row)
    return chunks[:len(chunks) // 2], chunks[len(chunks) // 2:]


def times(left, right):
    return [a * b for a, b in zip(left, right)]


def plus(left, right):
    return [a + b for a, b in zip(left, right)]


def gathered_at(needs, field):
    cells = needs[CELL:CELL + 1, :].astype(jnp.int32)
    half = cells.shape[1] // 2
    return gather_lanes(field, cells[:, :half]), gather_lanes(field, cells[:, half:])


def forward_front(base, needs, incoming):
    (base_a, base_b), (slope_a, slope_b) = halves(base[...]), halves(row_of(needs, SLOPE))
    at_a, at_b = gathered_at(needs, incoming)
    return minus(base_a, times(slope_a, at_a)) + plus(base_b, times(slope_b, at_b))


def backward_front(needs, incoming, second_fwd, both):
    (turn_a, turn_b), (fold, _) = halves(row_of(needs, TURN)), halves(row_of(needs, FOLD))
    at_a, at_b = gathered_at(needs, incoming)
    second_a, _ = gathered_at(needs, second_fwd)
    following = choose(both, minus(second_a, times(fold, at_a)), at_a)
    return times(turn_a, following) + times(turn_b, at_b)


def write_front(ref, chunks, field=()):
    high = [c.astype(BF16) for c in field]
    low = [(c - h.astype(F32)).astype(BF16) for c, h in zip(field, high)]
    for at, chunk in enumerate(chunks + high + low):
        ref[at] = chunk.astype(BF16)


def read_field(packet, count):
    start = packet.shape[0] - 2 * count
    return [
        packet[start + i].astype(F32) + packet[start + count + i].astype(F32)
        for i in range(count)
    ]


def write_field(ref, chunks):
    for at, chunk in enumerate(chunks):
        ref[:, at * LANES:(at + 1) * LANES] = chunk


def owner_of(place, planes):
    if isinstance(place, int):
        return place
    own = lax.axis_index("plane")
    return lax.bitwise_xor(own, jnp.where(lax.rem(own, CORES) == 0, place[0], place[1]))


def stack_fronts(blocks, owners, planes, per_layer, stacked, layer):
    for ref, places in zip(blocks, owners):
        for number, place in enumerate(places):
            owner = owner_of(place, planes)
            for i in range(per_layer):
                at = pl.multiple_of((owner * per_layer + i) * LANES, LANES)
                slot = layer * per_layer + i
                piece = ref[slot] if len(ref.shape) == 3 else ref[number, slot]
                half = piece.shape[0] // 2
                wide = piece.astype(F32)
                turned = jnp.concatenate([-wide[half:], wide[:half]], axis=0)
                stacked[0, :, pl.ds(at, LANES)] = piece
                stacked[1, :, pl.ds(at, LANES)] = turned.astype(BF16)


def product(matrix, columns):
    return lax.dot_general(
        matrix, columns, (((1,), (1,)), ((), ())), preferred_element_type=F32
    )


def store_solved(solved, layer, out):
    rows = out.shape[0]
    if rows % LANES:
        out = jnp.concatenate([out, jnp.zeros((-rows % LANES, out.shape[1]), F32)], axis=0)
    solved[layer] = out.T


def solve(inverse, stacked, solved, layer):
    out = product(inverse[0], stacked[0]) + product(inverse[1], stacked[1])
    store_solved(solved, layer, out)


def places(picked, cells):
    rows = picked.shape[1]
    column = jnp.broadcast_to(picked.astype(F32), (8, rows)).T[:, 0:1].astype(jnp.int32)
    cell = lax.broadcasted_iota(jnp.int32, (rows, cells), 1)
    row = lax.broadcasted_iota(jnp.int32, (rows, cells), 0)
    return jnp.max(jnp.where(column == cell, row, -1), axis=0, keepdims=True)


def first_kernel(
    width, layers_in, rhs_in, isc_in, fwd_in, bwd_in, picked_in, local, ahead, place, front,
    layers, rhs, isc, fwd, bwd, picked, sems,
):
    pairs = (
        (rhs_in, rhs), (isc_in, isc), (fwd_in, fwd), (bwd_in, bwd), (picked_in, picked),
        (layers_in, layers),
    )
    copies = [pltpu.make_async_copy(a, b, sems.at[i]) for i, (a, b) in enumerate(pairs)]
    for copy in copies:
        copy.start()
    for copy in copies:
        copy.wait()
    cells = rhs.shape[-1]
    count = rhs.shape[1]
    small = local.at[2 * count:]
    small[ISC:ISC + 2, :] = isc[...]
    small[FWD:FWD + 2, :] = fwd[...]
    small[BWD:BWD + 2, :] = bwd[...]
    small[PICK:PICK + 2, :] = jnp.full((2, cells), -1, F32)
    small[PICK:PICK + 2, :width] = picked[...].astype(F32)
    local[0:count, :] = rhs[0]
    local[count:2 * count, :] = rhs[1]

    at_a, at_b = picked[0:1, :], picked[1:2, :]
    isc_a, isc_b, fwd_a, fwd_b, bwd_a, bwd_b = (
        split(jnp.broadcast_to(row_of(small, at), (8, cells))) for at in range(PICK)
    )
    base_a = gather_lanes(split(rhs[0]), at_a)
    fed = times(fwd_b, isc_a)
    base_b = gather_lanes(
        minus(split(rhs[1]), [f[0:1] * r for f, r in zip(fed, split(rhs[0]))]), at_b
    )
    write_front(front, base_a + base_b)
    zero = [jnp.zeros((8, LANES), F32)] * (width // LANES)
    rows = {
        SLOPE: gather_lanes(fwd_a, at_a) + gather_lanes(times(fed, fwd_a), at_b),
        TURN: gather_lanes(bwd_a, at_a) + gather_lanes(bwd_b, at_b),
        FOLD: gather_lanes(times(isc_b, bwd_b), at_a) + zero,
        CELL: split(at_a.astype(F32)) + split(at_b.astype(F32)),
    }
    ahead[count:, :] = jnp.zeros((NEEDS, ahead.shape[1]), F32)
    for at, chunks in rows.items():
        for i, chunk in enumerate(chunks):
            ahead[count + at:count + at + 1, i * LANES:(i + 1) * LANES] = chunk[0:1]
    write_field(ahead.at[0:count], base_a + base_b)
    for layer in range(2):
        place[layer:layer + 1, :] = places(picked[layer:layer + 1, :], cells)


def load_kernel(inverse, first, second, done, sems):
    loads = [
        pltpu.make_async_copy(inverse.at[layer], half, sems.at[layer])
        for layer, half in enumerate((first, second))
    ]
    later = lax.axis_index("sweep") == 0
    loads[0].start()
    pl.when(~later)(loads[1].start)
    done[...] = jnp.zeros(done.shape, F32)
    loads[0].wait()
    pl.when(~later)(loads[1].wait)


def join_kernel(*refs):
    *blocks, _, _, joined = refs
    at = 0
    for block in blocks:
        for piece in [block] if len(block.shape) == 3 else [block.at[i] for i in range(block.shape[0])]:
            joined[at] = piece[...]
            at += 1


def forward_kernel(
    step, sections, planes, width, per_layer, owners, layers, first_inverse, second_inverse,
    packet, place, *rest
):
    if not step:
        inverse, *rest = rest
    blocks, rest = rest[:len(owners)], rest[len(owners):]
    final = step == sections - 1
    if step:
        incoming, *rest = rest
    if not final:
        after, *rest = rest
    kept, front, *rest = rest
    if not final:
        outgoing_packet, *rest = rest
    if step:
        stacked, solved = rest
    else:
        second_inverse, stacked, solved, sems = rest
    own = lax.axis_index("sweep")
    cells = packet.shape[-1]
    count = cells // LANES
    rows = kept.shape[1]
    small = packet.at[2 * rows:]
    mine = own == step
    both = layers[step] == 2
    if not step:
        load = pltpu.make_async_copy(inverse.at[1], second_inverse, sems.at[0])
        pl.when(mine)(load.start)

    def whole_solve(layer, matrices):
        stack_fronts(blocks, owners, planes, per_layer, stacked, layer)
        solve(matrices, stacked, solved, layer)

    @pl.when(mine)
    def _():
        whole_solve(0, first_inverse)

    if not step:
        pl.when(mine)(load.wait)

    @pl.when(mine & both)
    def _():
        whole_solve(1, second_inverse)

    @pl.when(mine)
    def _():
        rhs_a, rhs_b = split(packet[0:rows, :]), split(packet[rows:2 * rows, :])
        first_res = rhs_a
        if step:
            first_res = minus(rhs_a, scaled(row_of(small, FWD), read_field(incoming, count)))
        first = gather_lanes(
            split(solved[0]), place[0:1, :], scaled(row_of(small, ISC), first_res)
        )
        second_res = minus(rhs_b, scaled(row_of(small, FWD + 1), first))
        second = gather_lanes(
            split(solved[1]), place[1:2, :], scaled(row_of(small, ISC + 1), second_res)
        )
        if final:
            z = scaled(row_of(small, BWD), choose(both, second, [jnp.zeros_like(c) for c in first]))
            write_front(front, gather_lanes(rounded(z), picks(small, PICK, width)))
        else:
            outgoing = choose(both, second, first)
            chunks = forward_front(after.at[0:rows], after.at[rows:], outgoing)
            write_front(front, chunks)
            write_front(outgoing_packet, chunks, outgoing)
        write_field(kept.at[0], first)
        write_field(kept.at[1], second)


def backward_kernel(
    step, sections, planes, width, per_layer, owners, layers, first_inverse, second_inverse,
    packet, place, *rest
):
    blocks, rest = rest[:len(owners)], rest[len(owners):]
    kept, *rest = rest
    last = step == sections - 1
    if not last:
        incoming, before, *rest = rest
    if step:
        behind, *rest = rest
        held, *rest = rest
    result, *rest = rest
    if step:
        front, outgoing_packet, *rest = rest
    stacked, solved = rest
    own = lax.axis_index("sweep")
    count = kept.shape[-1] // LANES
    small = packet.at[2 * kept.shape[1]:]
    mine = own == step
    both = layers[step] == 2

    def whole_solve(layer):
        stack_fronts(blocks, owners, planes, per_layer, stacked, layer)
        solve((first_inverse, second_inverse)[layer], stacked, solved, layer)

    if not last:
        @pl.when(own != step)
        def _():
            result[...] = before[...]

        @pl.when(mine & both)
        def _():
            whole_solve(1)

    @pl.when(mine & both if last else mine)
    def _():
        whole_solve(0)

    @pl.when(mine)
    def _():
        first_fwd, second_fwd = split(kept[0]), split(kept[1])
        zero = [jnp.zeros_like(c) for c in first_fwd]
        if last:
            second, arriving = second_fwd, zero
        else:
            arriving = read_field(incoming, count)
            z = scaled(row_of(small, BWD + 1), arriving)
            local = scaled(row_of(small, ISC + 1), z)
            second = minus(second_fwd, gather_lanes(split(solved[1]), place[1:2, :], local))
        following = choose(both, second, arriving)
        z = scaled(row_of(small, BWD), following)
        local = scaled(row_of(small, ISC), z)
        change = gather_lanes(split(solved[0]), place[0:1, :], local)
        if last:
            change = choose(both, change, zero)
        first = minus(first_fwd, change)
        if step:
            chunks = backward_front(
                behind.at[kept.shape[1]:], first, read_field(held, count), layers[step - 1] == 2
            )
            write_front(front, chunks)
            write_front(outgoing_packet, chunks, first)
        write_field(result.at[0], first)
        write_field(result.at[1], choose(both, second, zero))


def whole(space=pltpu.VMEM):
    return pl.BlockSpec(memory_space=space)


def call(kernel, operands, outs, scratch, name, in_place=(), aliases={}):
    outs = [jax.ShapeDtypeStruct(*o) if isinstance(o, tuple) else o for o in outs]
    specs = [whole(pltpu.SMEM if o.ndim == 1 else pltpu.VMEM) for o in operands]
    for at in in_place:
        specs[at] = whole(pltpu.HBM)
    return pl.pallas_call(
        kernel,
        in_specs=specs,
        out_specs=[whole(pltpu.SMEM if len(o.shape) == 1 else pltpu.VMEM) for o in outs],
        out_shape=outs,
        scratch_shapes=scratch,
        input_output_aliases=aliases,
        compiler_params=pltpu.CompilerParams(vmem_limit_bytes=8 * 2**20),
        name=name,
    )(*operands)


def in_hbm(array):
    return pltpu.with_memory_space_constraint(array, pltpu.HBM)


def shards(
    rhs_field,
    front_inverse,
    interior_scale,
    forward_coupling,
    backward_coupling,
    front_cells,
    section_layers,
):
    sections, planes = lax.axis_size("sweep"), lax.axis_size("plane")
    layer_slots, parts, columns, cells = rhs_field.shape
    rows = parts * columns
    owned, order = front_inverse.shape[2:]
    width = -(-owned // LANES) * LANES
    per_layer = width // LANES
    chips = planes // CORES
    direct = planes in (2, 4, 8) and owned == width

    rhs = rhs_field.reshape(layer_slots, rows, cells)
    picked = jnp.pad(front_cells, ((0, 0), (0, width - owned)), constant_values=-1)
    layers = section_layers

    half_shape = ((per_layer, rows, LANES), BF16)
    front_shape = ((2 * per_layer, rows, LANES), BF16)
    packet_shape = ((2 * per_layer + 2 * (cells // LANES), rows, LANES), BF16)
    layers_shape = ((layer_slots, rows, cells), F32)
    scratch = [
        pltpu.VMEM((2, rows, order), BF16),
        pltpu.VMEM((2, rows, width), F32),
    ]

    def send(block, links, *flips):
        route = [
            (i * planes + own, j * planes + (own ^ flips[own % len(flips)]))
            for i, j in links for own in range(planes)
        ]
        return lax.ppermute(block, ("sweep", "plane"), route)

    inside = [(i, i) for i in range(sections)]

    def swapped_pairs(start, stop):
        order = [start, stop] + [i for i in range(sections) if i not in (start, stop)]
        links = [(i, i) for i in order[len(order) // 2 * 2:]]
        for i, j in zip(order[::2], order[1::2]):
            links += [(i, j), (j, i)]
        return links

    def everywhere(front):
        slots = front.shape[0] // per_layer
        gathered = lax.all_gather(front, "plane")
        if owned != width:
            gathered = gathered.reshape(planes, slots, per_layer, rows, LANES)
            gathered = gathered.transpose(1, 3, 0, 2, 4).reshape(slots, rows, planes, width)
            gathered = gathered[..., :owned].reshape(slots, rows, order // LANES, LANES)
            gathered = gathered.transpose(0, 2, 1, 3)
            gathered = gathered.reshape(slots * order // LANES, rows, LANES)
            return [gathered], [[0]], order // LANES
        return [gathered], [list(range(planes))], per_layer

    def spread(front, straight, some, every, join=None):
        blocks, owners = [straight], [[(0, 0)]]
        for step in [1] if chips == 2 else range(3, chips):
            blocks.append(send(front, some, CORES * step))
            owners.append([(CORES * step, CORES * step)])
        if chips == 4:
            both = jnp.stack([front, send(front, inside, 1)])
            blocks.append(send(both, every, CORES, 2 * CORES))
            owners += [[(CORES + core, 2 * CORES + core) for core in range(CORES)]]
        if join:
            mine = join(blocks)
        else:
            short = [b[:2 * per_layer] if b.ndim == 3 else b for b in blocks]
            mine = jnp.concatenate([b[None] if b.ndim == 3 else b for b in short])
        blocks.append(send(mine, inside, 1))
        owners.append([(one ^ 1, zero ^ 1) for places in owners for zero, one in places])
        return blocks, owners, per_layer

    def within(front, join=None):
        return spread(front, front, inside, inside, join) if direct else everywhere(front)

    def between(front, packet, start, stop):
        packet = lax.ppermute(packet, "sweep", [(start, stop)])
        if not direct:
            return *everywhere(packet[:2 * per_layer]), packet
        return *spread(front, packet, [(start, stop)], swapped_pairs(start, stop)), packet

    inverse = in_hbm(front_inverse)
    half_inverse = pltpu.VMEM(front_inverse.shape[1:], BF16)
    coefficients = (interior_scale, forward_coupling, backward_coupling)
    operands = [section_layers, rhs, *coefficients, picked]
    local, ahead, place, front, layers = call(
        functools.partial(first_kernel, width),
        [in_hbm(a) for a in operands],
        [
            ((2 * rows + 8, cells), F32),
            ((rows + NEEDS, 2 * width), F32),
            ((2, cells), jnp.int32),
            front_shape,
            (section_layers.shape, jnp.int32),
        ],
        [pltpu.VMEM(a.shape, a.dtype) for a in operands[1:]] + [pltpu.SemaphoreType.DMA((6,))],
        "first_fronts",
        range(6),
    )
    after = lax.ppermute(ahead, "sweep", [(i + 1, i) for i in range(sections - 1)])
    first_inverse, second_inverse, token = call(
        load_kernel,
        [inverse],
        [half_inverse, half_inverse, ((8, LANES), F32)],
        [pltpu.SemaphoreType.DMA((2,))],
        "load_first",
        [0],
    )

    def join(blocks):
        shape = (sum(b.shape[0] if b.ndim == 4 else 1 for b in blocks), *front_shape[0])
        return call(join_kernel, [*blocks, after, token], [(shape, BF16)], [], "join")[0]

    gathered, owners, slots = within(front, join)

    kept, held = [], [None]
    for step in range(sections):
        final = step == sections - 1
        extra = ([held[step]] if step else []) + ([] if final else [after])
        outs = [layers_shape, half_shape if final else front_shape]
        outs += [] if final else [packet_shape]
        outs += [] if step else [half_inverse]
        outs = call(
            functools.partial(
                forward_kernel, step, sections, planes, width, slots, owners
            ),
            [layers, first_inverse, second_inverse, local, place]
            + ([] if step else [inverse]) + [*gathered, *extra],
            outs,
            scratch + ([] if step else [pltpu.SemaphoreType.DMA((1,))]),
            f"forward_section_{step}",
            [] if step else [5],
            {} if step else {2: len(outs) - 1},
        )
        if not step:
            second_inverse = outs[-1]
        kept.append(outs[0])
        if final:
            behind = lax.ppermute(ahead, "sweep", [(i, i + 1) for i in range(sections - 1)])
            gathered, owners, slots = within(outs[1])
        else:
            gathered, owners, slots, incoming = between(outs[1], outs[2], step, step + 1)
            held.append(incoming)

    result = incoming = None
    for step in reversed(range(sections)):
        extra = ([] if result is None else [incoming, result]) + ([behind, held[step]] if step else [])
        outs = call(
            functools.partial(
                backward_kernel, step, sections, planes, width, slots, owners
            ),
            [layers, first_inverse, second_inverse, local, place, *gathered, kept[step], *extra],
            [layers_shape] + ([front_shape, packet_shape] if step else []),
            scratch,
            f"backward_section_{step}",
        )
        result = outs[0]
        if step:
            gathered, owners, slots, incoming = between(outs[1], outs[2], step, step - 1)
    return result.reshape(rhs_field.shape)


def solution(mesh):
    in_specs = (
        P("sweep", None, None, "plane"),
        P("sweep", None, "plane", None),
        P("sweep", "plane"),
        P("sweep", "plane"),
        P("sweep", "plane"),
        P("sweep", "plane"),
        P(),
    )
    out_specs = P("sweep", None, None, "plane")
    return jax.shard_map(shards, mesh=mesh, in_specs=in_specs, out_specs=out_specs, check_vma=False)
```

```python
import functools

import jax
import jax.numpy as jnp
from jax import lax
from jax.experimental import pallas as pl
from jax.experimental.pallas import tpu as pltpu
from jax.sharding import PartitionSpec as P

LANES = 128
CORES = 2
ISC, FWD, BWD, PICK = 0, 2, 4, 6
SLOPE, TURN, FOLD, CELL, NEEDS = 0, 1, 2, 3, 8
F32, BF16 = jnp.float32, jnp.bfloat16


def split(field):
    return [field[:, at:at + LANES] for at in range(0, field.shape[1], LANES)]


def gather_lanes(chunks, index, beyond=None):
    result = []
    for place, part in enumerate(split(index)):
        part = jnp.broadcast_to(part, chunks[0].shape)
        lane, chunk = part & (LANES - 1), part >> (LANES.bit_length() - 1)
        total = jnp.zeros(chunks[0].shape, F32) if beyond is None else beyond[place]
        for number, source in enumerate(chunks):
            found = jnp.take_along_axis(source, lane, axis=1, mode="promise_in_bounds")
            total = jnp.where(chunk == number, found, total)
        result.append(total)
    return result


def scaled(row, chunks):
    return [part * chunk for part, chunk in zip(split(row), chunks)]


def minus(left, right):
    return [a - b for a, b in zip(left, right)]


def choose(flag, left, right):
    return [jnp.where(flag, a, b) for a, b in zip(left, right)]


def rounded(chunks):
    return [c.astype(BF16).astype(F32) for c in chunks]


def row_of(ref, at):
    return ref[at:at + 1, :]


def picks(ref, at, width):
    return ref[at:at + 1, :width].astype(jnp.int32)


def halves(row):
    chunks = split(row)
    return chunks[:len(chunks) // 2], chunks[len(chunks) // 2:]


def times(left, right):
    return [a * b for a, b in zip(left, right)]


def plus(left, right):
    return [a + b for a, b in zip(left, right)]


def gathered_at(needs, field):
    cells = needs[CELL:CELL + 1, :].astype(jnp.int32)
    half = cells.shape[1] // 2
    return gather_lanes(field, cells[:, :half]), gather_lanes(field, cells[:, half:])


def forward_front(base, needs, incoming):
    (base_a, base_b), (slope_a, slope_b) = halves(base[...]), halves(row_of(needs, SLOPE))
    at_a, at_b = gathered_at(needs, incoming)
    return minus(base_a, times(slope_a, at_a)) + plus(base_b, times(slope_b, at_b))


def backward_front(needs, incoming, second_fwd, both):
    (turn_a, turn_b), (fold, _) = halves(row_of(needs, TURN)), halves(row_of(needs, FOLD))
    at_a, at_b = gathered_at(needs, incoming)
    second_a, _ = gathered_at(needs, second_fwd)
    following = choose(both, minus(second_a, times(fold, at_a)), at_a)
    return times(turn_a, following) + times(turn_b, at_b)


def write_front(ref, chunks, field=()):
    for at, chunk in enumerate([*chunks, *field]):
        ref[at] = chunk.astype(BF16)


def read_field(packet, count):
    start = packet.shape[0] - count
    return [packet[start + i].astype(F32) for i in range(count)]


def write_field(ref, chunks):
    for at, chunk in enumerate(chunks):
        ref[:, at * LANES:(at + 1) * LANES] = chunk


def owner_of(place, planes):
    if isinstance(place, int):
        return place
    own = lax.axis_index("plane")
    return lax.bitwise_xor(own, jnp.where(lax.rem(own, CORES) == 0, place[0], place[1]))


def stack_fronts(blocks, owners, planes, per_layer, stacked, layer):
    for ref, places in zip(blocks, owners):
        for number, place in enumerate(places):
            owner = owner_of(place, planes)
            for i in range(per_layer):
                at = pl.multiple_of((owner * per_layer + i) * LANES, LANES)
                slot = layer * per_layer + i
                piece = ref[slot] if len(ref.shape) == 3 else ref[number, slot]
                half = piece.shape[0] // 2
                wide = piece.astype(F32)
                turned = jnp.concatenate([-wide[half:], wide[:half]], axis=0)
                stacked[0, :, pl.ds(at, LANES)] = piece
                stacked[1, :, pl.ds(at, LANES)] = turned.astype(BF16)


def product(matrix, columns):
    return lax.dot_general(
        matrix, columns, (((1,), (1,)), ((), ())), preferred_element_type=F32
    )


def store_solved(solved, layer, out):
    rows = out.shape[0]
    if rows % LANES:
        out = jnp.concatenate([out, jnp.zeros((-rows % LANES, out.shape[1]), F32)], axis=0)
    solved[layer] = out.T


def solve(inverse, stacked, solved, layer):
    out = product(inverse[0], stacked[0]) + product(inverse[1], stacked[1])
    store_solved(solved, layer, out)


def places(picked, cells):
    rows = picked.shape[1]
    column = jnp.broadcast_to(picked.astype(F32), (8, rows)).T[:, 0:1].astype(jnp.int32)
    cell = lax.broadcasted_iota(jnp.int32, (rows, cells), 1)
    row = lax.broadcasted_iota(jnp.int32, (rows, cells), 0)
    return jnp.max(jnp.where(column == cell, row, -1), axis=0, keepdims=True)


def first_kernel(
    width, layers_in, rhs_in, isc_in, fwd_in, bwd_in, picked_in, local, ahead, longer, place, front,
    layers, rhs, isc, fwd, bwd, picked, sems,
):
    pairs = (
        (rhs_in, rhs), (isc_in, isc), (fwd_in, fwd), (bwd_in, bwd), (picked_in, picked),
        (layers_in, layers),
    )
    copies = [pltpu.make_async_copy(a, b, sems.at[i]) for i, (a, b) in enumerate(pairs)]
    for copy in copies:
        copy.start()
    for copy in copies:
        copy.wait()
    cells = rhs.shape[-1]
    count = rhs.shape[1]
    small = local.at[2 * count:]
    small[ISC:ISC + 2, :] = isc[...]
    small[FWD:FWD + 2, :] = fwd[...]
    small[BWD:BWD + 2, :] = bwd[...]
    small[PICK:PICK + 2, :] = jnp.full((2, cells), -1, F32)
    small[PICK:PICK + 2, :width] = picked[...].astype(F32)
    local[0:count, :] = rhs[0]
    local[count:2 * count, :] = rhs[1]

    at_a, at_b = picked[0:1, :], picked[1:2, :]
    isc_a, isc_b, fwd_a, fwd_b, bwd_a, bwd_b = (
        split(jnp.broadcast_to(row_of(small, at), (8, cells))) for at in range(PICK)
    )
    base_a = gather_lanes(split(rhs[0]), at_a)
    fed = times(fwd_b, isc_a)
    base_b = gather_lanes(
        minus(split(rhs[1]), [f[0:1] * r for f, r in zip(fed, split(rhs[0]))]), at_b
    )
    write_front(front, base_a + base_b)
    zero = [jnp.zeros((8, LANES), F32)] * (width // LANES)
    rows = {
        SLOPE: gather_lanes(fwd_a, at_a) + gather_lanes(times(fed, fwd_a), at_b),
        TURN: gather_lanes(bwd_a, at_a) + gather_lanes(bwd_b, at_b),
        FOLD: gather_lanes(times(isc_b, bwd_b), at_a) + zero,
        CELL: split(at_a.astype(F32)) + split(at_b.astype(F32)),
    }
    ahead[count:, :] = jnp.zeros((NEEDS, ahead.shape[1]), F32)
    for at, chunks in rows.items():
        for i, chunk in enumerate(chunks):
            ahead[count + at:count + at + 1, i * LANES:(i + 1) * LANES] = chunk[0:1]
    write_field(ahead.at[0:count], base_a + base_b)
    longer[0:ahead.shape[0], :] = ahead[...]
    longer[ahead.shape[0]:, :] = jnp.zeros((longer.shape[0] - ahead.shape[0], longer.shape[1]), F32)
    for layer in range(2):
        place[layer:layer + 1, :] = places(picked[layer:layer + 1, :], cells)


def load_kernel(inverse, first, second, done, sems):
    loads = [
        pltpu.make_async_copy(inverse.at[layer], half, sems.at[layer])
        for layer, half in enumerate((first, second))
    ]
    later = lax.axis_index("sweep") == 0
    loads[0].start()
    pl.when(~later)(loads[1].start)
    done[...] = jnp.zeros(done.shape, F32)
    loads[0].wait()
    pl.when(~later)(loads[1].wait)


def join_kernel(*refs):
    *blocks, _, _, joined = refs
    at = 0
    for block in blocks:
        for piece in [block] if len(block.shape) == 3 else [block.at[i] for i in range(block.shape[0])]:
            joined[at] = piece[...]
            at += 1


def forward_kernel(
    step, sections, planes, width, per_layer, owners, layers, first_inverse, second_inverse,
    packet, place, *rest
):
    if not step:
        inverse, *rest = rest
    blocks, rest = rest[:len(owners)], rest[len(owners):]
    final = step == sections - 1
    if step:
        incoming, *rest = rest
    if not final:
        after, *rest = rest
    kept, front, *rest = rest
    if not final:
        outgoing_packet, *rest = rest
    if step:
        stacked, solved = rest
    else:
        second_inverse, stacked, solved, sems = rest
    own = lax.axis_index("sweep")
    cells = packet.shape[-1]
    count = cells // LANES
    rows = kept.shape[1]
    small = packet.at[2 * rows:]
    mine = own == step
    both = layers[step] == 2
    if not step:
        load = pltpu.make_async_copy(inverse.at[1], second_inverse, sems.at[0])
        pl.when(mine)(load.start)

    def whole_solve(layer, matrices):
        stack_fronts(blocks, owners, planes, per_layer, stacked, layer)
        solve(matrices, stacked, solved, layer)

    @pl.when(mine)
    def _():
        whole_solve(0, first_inverse)

    if not step:
        pl.when(mine)(load.wait)

    @pl.when(mine & both)
    def _():
        whole_solve(1, second_inverse)

    @pl.when(mine)
    def _():
        rhs_a, rhs_b = split(packet[0:rows, :]), split(packet[rows:2 * rows, :])
        first_res = rhs_a
        if step:
            first_res = minus(rhs_a, scaled(row_of(small, FWD), read_field(incoming, count)))
        first = gather_lanes(
            split(solved[0]), place[0:1, :], scaled(row_of(small, ISC), first_res)
        )
        second_res = minus(rhs_b, scaled(row_of(small, FWD + 1), first))
        second = gather_lanes(
            split(solved[1]), place[1:2, :], scaled(row_of(small, ISC + 1), second_res)
        )
        if final:
            z = scaled(row_of(small, BWD), choose(both, second, [jnp.zeros_like(c) for c in first]))
            write_front(front, gather_lanes(rounded(z), picks(small, PICK, width)))
        else:
            outgoing = choose(both, second, first)
            chunks = forward_front(after.at[0:rows], after.at[rows:rows + NEEDS], outgoing)
            write_front(front, chunks)
            write_front(outgoing_packet, chunks, outgoing)
        write_field(kept.at[0], first)
        write_field(kept.at[1], second)


def backward_kernel(
    step, sections, planes, width, per_layer, owners, layers, first_inverse, second_inverse,
    packet, place, *rest
):
    blocks, rest = rest[:len(owners)], rest[len(owners):]
    kept, *rest = rest
    last = step == sections - 1
    if not last:
        incoming, before, *rest = rest
    if step:
        behind, *rest = rest
        held, *rest = rest
    result, *rest = rest
    if step:
        front, outgoing_packet, *rest = rest
    stacked, solved = rest
    own = lax.axis_index("sweep")
    count = kept.shape[-1] // LANES
    small = packet.at[2 * kept.shape[1]:]
    mine = own == step
    both = layers[step] == 2

    def whole_solve(layer):
        stack_fronts(blocks, owners, planes, per_layer, stacked, layer)
        solve((first_inverse, second_inverse)[layer], stacked, solved, layer)

    if not last:
        @pl.when(own != step)
        def _():
            result[...] = before[...]

        @pl.when(mine & both)
        def _():
            whole_solve(1)

    @pl.when(mine & both if last else mine)
    def _():
        whole_solve(0)

    @pl.when(mine)
    def _():
        first_fwd, second_fwd = split(kept[0]), split(kept[1])
        zero = [jnp.zeros_like(c) for c in first_fwd]
        if last:
            second, arriving = second_fwd, zero
        else:
            arriving = read_field(incoming, count)
            z = scaled(row_of(small, BWD + 1), arriving)
            local = scaled(row_of(small, ISC + 1), z)
            second = minus(second_fwd, gather_lanes(split(solved[1]), place[1:2, :], local))
        following = choose(both, second, arriving)
        z = scaled(row_of(small, BWD), following)
        local = scaled(row_of(small, ISC), z)
        change = gather_lanes(split(solved[0]), place[0:1, :], local)
        if last:
            change = choose(both, change, zero)
        first = minus(first_fwd, change)
        if step:
            chunks = backward_front(
                behind.at[kept.shape[1]:kept.shape[1] + NEEDS], first, read_field(held, count), layers[step - 1] == 2
            )
            write_front(front, chunks)
            write_front(outgoing_packet, chunks, first)
        write_field(result.at[0], first)
        write_field(result.at[1], choose(both, second, zero))


def whole(space=pltpu.VMEM):
    return pl.BlockSpec(memory_space=space)


def call(kernel, operands, outs, scratch, name, in_place=(), aliases={}):
    outs = [jax.ShapeDtypeStruct(*o) if isinstance(o, tuple) else o for o in outs]
    specs = [whole(pltpu.SMEM if o.ndim == 1 else pltpu.VMEM) for o in operands]
    for at in in_place:
        specs[at] = whole(pltpu.HBM)
    return pl.pallas_call(
        kernel,
        in_specs=specs,
        out_specs=[whole(pltpu.SMEM if len(o.shape) == 1 else pltpu.VMEM) for o in outs],
        out_shape=outs,
        scratch_shapes=scratch,
        input_output_aliases=aliases,
        compiler_params=pltpu.CompilerParams(vmem_limit_bytes=8 * 2**20),
        name=name,
    )(*operands)


def in_hbm(array):
    return pltpu.with_memory_space_constraint(array, pltpu.HBM)


def shards(
    rhs_field,
    front_inverse,
    interior_scale,
    forward_coupling,
    backward_coupling,
    front_cells,
    section_layers,
):
    sections, planes = lax.axis_size("sweep"), lax.axis_size("plane")
    layer_slots, parts, columns, cells = rhs_field.shape
    rows = parts * columns
    owned, order = front_inverse.shape[2:]
    width = -(-owned // LANES) * LANES
    per_layer = width // LANES
    chips = planes // CORES
    direct = planes in (2, 4, 8) and owned == width

    rhs = rhs_field.reshape(layer_slots, rows, cells)
    picked = jnp.pad(front_cells, ((0, 0), (0, width - owned)), constant_values=-1)
    layers = section_layers

    half_shape = ((per_layer, rows, LANES), BF16)
    front_shape = ((2 * per_layer, rows, LANES), BF16)
    packet_shape = ((2 * per_layer + cells // LANES, rows, LANES), BF16)
    layers_shape = ((layer_slots, rows, cells), F32)
    scratch = [
        pltpu.VMEM((2, rows, order), BF16),
        pltpu.VMEM((2, rows, width), F32),
    ]

    def send(block, links, *flips):
        route = []
        for i, j in links:
            for own in range(planes):
                flip = flips[own % len(flips)] or (i == j and planes % CORES == 0)
                route.append((i * planes + own, j * planes + (own ^ int(flip))))
        return lax.ppermute(block, ("sweep", "plane"), route)

    inside = [(i, i) for i in range(sections)]

    def cycle(*members):
        links = list(zip(members, members[1:] + members[:1]))
        return links + [(i, i) for i in range(sections) if i not in members]

    def everywhere(front):
        slots = front.shape[0] // per_layer
        gathered = lax.all_gather(front, "plane")
        if owned != width:
            gathered = gathered.reshape(planes, slots, per_layer, rows, LANES)
            gathered = gathered.transpose(1, 3, 0, 2, 4).reshape(slots, rows, planes, width)
            gathered = gathered[..., :owned].reshape(slots, rows, order // LANES, LANES)
            gathered = gathered.transpose(0, 2, 1, 3)
            gathered = gathered.reshape(slots * order // LANES, rows, LANES)
            return [gathered], [[0]], order // LANES
        return [gathered], [list(range(planes))], per_layer

    def spread(front, straight, some, every, join=None):
        blocks, owners = [straight], [[(0, 0)]]
        for step in [1] if chips == 2 else range(3, chips):
            blocks.append(send(front, some, CORES * step))
            owners.append([(CORES * step, CORES * step)])
        if chips == 4:
            both = jnp.stack([front, send(front, inside, 1)])
            blocks.append(send(both, every, CORES, 2 * CORES))
            owners += [[(CORES + core, 2 * CORES + core) for core in range(CORES)]]
        if join:
            mine = join(blocks)
        else:
            short = [b[:2 * per_layer] if b.ndim == 3 else b for b in blocks]
            mine = jnp.concatenate([b[None] if b.ndim == 3 else b for b in short])
        blocks.append(send(mine, inside, 1))
        owners.append([(one ^ 1, zero ^ 1) for places in owners for zero, one in places])
        return blocks, owners, per_layer

    def within(front, join=None):
        return spread(front, front, inside, inside, join) if direct else everywhere(front)

    def between(front, packet, start, stop):
        packet = lax.ppermute(packet, "sweep", [(start, stop)])
        if not direct:
            return *everywhere(packet[:2 * per_layer]), packet
        third = [i for i in (2 * start - stop, 2 * stop - start) if 0 <= i < sections]
        some, every = cycle(start, stop, *third[:1]), cycle(start, stop)
        return *spread(front, packet, some, every), packet

    inverse = in_hbm(front_inverse)
    half_inverse = pltpu.VMEM(front_inverse.shape[1:], BF16)
    coefficients = (interior_scale, forward_coupling, backward_coupling)
    operands = [section_layers, rhs, *coefficients, picked]
    local, ahead, longer, place, front, layers = call(
        functools.partial(first_kernel, width),
        [in_hbm(a) for a in operands],
        [
            ((2 * rows + 8, cells), F32),
            ((rows + NEEDS, 2 * width), F32),
            ((2 * rows + NEEDS, 2 * width), F32),
            ((2, cells), jnp.int32),
            front_shape,
            (section_layers.shape, jnp.int32),
        ],
        [pltpu.VMEM(a.shape, a.dtype) for a in operands[1:]] + [pltpu.SemaphoreType.DMA((6,))],
        "first_fronts",
        range(6),
    )
    def neighbours(first):
        pairs = [(i, i + 1) for i in range(first, sections - 1, 2)]
        alone = [i for i in range(sections) if not any(i in pair for pair in pairs)]
        return pairs + [(j, i) for i, j in pairs] + [(i, i) for i in alone]

    near = [send(ahead, neighbours(0), 0, 0), None]
    first_inverse, second_inverse, token = call(
        load_kernel,
        [inverse],
        [half_inverse, half_inverse, ((8, LANES), F32)],
        [pltpu.SemaphoreType.DMA((2,))],
        "load_first",
        [0],
    )

    def join(blocks):
        shape = (sum(b.shape[0] if b.ndim == 4 else 1 for b in blocks), *front_shape[0])
        return call(join_kernel, [*blocks, near[0], token], [(shape, BF16)], [], "join")[0]

    gathered, owners, slots = within(front, join)

    near[1] = send(longer, neighbours(1), 0)
    kept, held = [], [None]
    for step in range(sections):
        final = step == sections - 1
        extra = ([held[step]] if step else []) + ([] if final else [near[step % 2]])
        outs = [layers_shape, half_shape if final else front_shape]
        outs += [] if final else [packet_shape]
        outs += [] if step else [half_inverse]
        outs = call(
            functools.partial(
                forward_kernel, step, sections, planes, width, slots, owners
            ),
            [layers, first_inverse, second_inverse, local, place]
            + ([] if step else [inverse]) + [*gathered, *extra],
            outs,
            scratch + ([] if step else [pltpu.SemaphoreType.DMA((1,))]),
            f"forward_section_{step}",
            [] if step else [5],
            {} if step else {2: len(outs) - 1},
        )
        if not step:
            second_inverse = outs[-1]
        kept.append(outs[0])
        if final:
            gathered, owners, slots = within(outs[1])
        else:
            gathered, owners, slots, incoming = between(outs[1], outs[2], step, step + 1)
            held.append(incoming)

    result = incoming = None
    for step in reversed(range(sections)):
        extra = ([] if result is None else [incoming, result]) + ([near[(step - 1) % 2], held[step]] if step else [])
        outs = call(
            functools.partial(
                backward_kernel, step, sections, planes, width, slots, owners
            ),
            [layers, first_inverse, second_inverse, local, place, *gathered, kept[step], *extra],
            [layers_shape] + ([front_shape, packet_shape] if step else []),
            scratch,
            f"backward_section_{step}",
        )
        result = outs[0]
        if step:
            gathered, owners, slots, incoming = between(outs[1], outs[2], step, step - 1)
    return result.reshape(rhs_field.shape)


def solution(mesh):
    in_specs = (
        P("sweep", None, None, "plane"),
        P("sweep", None, "plane", None),
        P("sweep", "plane"),
        P("sweep", "plane"),
        P("sweep", "plane"),
        P("sweep", "plane"),
        P(),
    )
    out_specs = P("sweep", None, None, "plane")
    return jax.shard_map(shards, mesh=mesh, in_specs=in_specs, out_specs=out_specs, check_vma=False)
```

```python
import functools

import jax
import jax.numpy as jnp
from jax import lax
from jax.experimental import pallas as pl
from jax.experimental.pallas import tpu as pltpu
from jax.sharding import PartitionSpec as P

LANES = 128
CORES = 2
ISC, FWD, BWD, PICK = 0, 2, 4, 6
SLOPE, TURN, FOLD, CELL, NEEDS = 0, 1, 2, 3, 8
F32, BF16 = jnp.float32, jnp.bfloat16


def split(field):
    return [field[:, at:at + LANES] for at in range(0, field.shape[1], LANES)]


def gather_lanes(chunks, index, beyond=None):
    result = []
    for place, part in enumerate(split(index)):
        part = jnp.broadcast_to(part, chunks[0].shape)
        lane, chunk = part & (LANES - 1), part >> (LANES.bit_length() - 1)
        total = jnp.zeros(chunks[0].shape, F32) if beyond is None else beyond[place]
        for number, source in enumerate(chunks):
            found = jnp.take_along_axis(source, lane, axis=1, mode="promise_in_bounds")
            total = jnp.where(chunk == number, found, total)
        result.append(total)
    return result


def scaled(row, chunks):
    return [part * chunk for part, chunk in zip(split(row), chunks)]


def minus(left, right):
    return [a - b for a, b in zip(left, right)]


def choose(flag, left, right):
    return [jnp.where(flag, a, b) for a, b in zip(left, right)]


def rounded(chunks):
    return [c.astype(BF16).astype(F32) for c in chunks]


def row_of(ref, at):
    return ref[at:at + 1, :]


def picks(ref, at, width):
    return ref[at:at + 1, :width].astype(jnp.int32)


def halves(row):
    chunks = split(row)
    return chunks[:len(chunks) // 2], chunks[len(chunks) // 2:]


def times(left, right):
    return [a * b for a, b in zip(left, right)]


def plus(left, right):
    return [a + b for a, b in zip(left, right)]


def gathered_at(needs, field):
    cells = needs[CELL:CELL + 1, :].astype(jnp.int32)
    half = cells.shape[1] // 2
    return gather_lanes(field, cells[:, :half]), gather_lanes(field, cells[:, half:])


def forward_front(base, needs, incoming):
    (base_a, base_b), (slope_a, slope_b) = halves(base[...]), halves(row_of(needs, SLOPE))
    at_a, at_b = gathered_at(needs, incoming)
    return minus(base_a, times(slope_a, at_a)) + plus(base_b, times(slope_b, at_b))


def backward_front(needs, incoming, second_fwd, both):
    (turn_a, turn_b), (fold, _) = halves(row_of(needs, TURN)), halves(row_of(needs, FOLD))
    at_a, at_b = gathered_at(needs, incoming)
    second_a, _ = gathered_at(needs, second_fwd)
    following = choose(both, minus(second_a, times(fold, at_a)), at_a)
    return times(turn_a, following) + times(turn_b, at_b)


def write_front(ref, chunks, field=()):
    for at, chunk in enumerate([*chunks, *field]):
        ref[at] = chunk.astype(BF16)


def read_field(packet, count):
    start = packet.shape[0] - count
    return [packet[start + i].astype(F32) for i in range(count)]


def write_field(ref, chunks):
    for at, chunk in enumerate(chunks):
        ref[:, at * LANES:(at + 1) * LANES] = chunk


def owner_of(place, planes):
    if isinstance(place, int):
        return place
    own = lax.axis_index("plane")
    return lax.bitwise_xor(own, jnp.where(lax.rem(own, CORES) == 0, place[0], place[1]))


def stack_fronts(blocks, owners, planes, per_layer, stacked, layer):
    for ref, places in zip(blocks, owners):
        for number, place in enumerate(places):
            owner = owner_of(place, planes)
            for i in range(per_layer):
                at = pl.multiple_of((owner * per_layer + i) * LANES, LANES)
                slot = layer * per_layer + i
                piece = ref[slot] if len(ref.shape) == 3 else ref[number, slot]
                half = piece.shape[0] // 2
                wide = piece.astype(F32)
                turned = jnp.concatenate([-wide[half:], wide[:half]], axis=0)
                stacked[0, :, pl.ds(at, LANES)] = piece
                stacked[1, :, pl.ds(at, LANES)] = turned.astype(BF16)


def product(matrix, columns):
    return lax.dot_general(
        matrix, columns, (((1,), (1,)), ((), ())), preferred_element_type=F32
    )


def store_solved(solved, layer, out):
    rows = out.shape[0]
    if rows % LANES:
        out = jnp.concatenate([out, jnp.zeros((-rows % LANES, out.shape[1]), F32)], axis=0)
    solved[layer] = out.T


def solve(inverse, stacked, solved, layer):
    out = product(inverse[0], stacked[0]) + product(inverse[1], stacked[1])
    store_solved(solved, layer, out)


def places(picked, cells):
    rows = picked.shape[1]
    column = jnp.broadcast_to(picked.astype(F32), (8, rows)).T[:, 0:1].astype(jnp.int32)
    cell = lax.broadcasted_iota(jnp.int32, (rows, cells), 1)
    row = lax.broadcasted_iota(jnp.int32, (rows, cells), 0)
    return jnp.max(jnp.where(column == cell, row, -1), axis=0, keepdims=True)


def first_kernel(
    width, layers_in, rhs_in, isc_in, fwd_in, bwd_in, picked_in, local, ahead, longer, place, front,
    layers, rhs, isc, fwd, bwd, picked, counts, sems,
):
    pairs = (
        (rhs_in, rhs), (isc_in, isc), (fwd_in, fwd), (bwd_in, bwd), (picked_in, picked),
        (layers_in, counts),
    )
    copies = [pltpu.make_async_copy(a, b, sems.at[i]) for i, (a, b) in enumerate(pairs)]
    for copy in copies:
        copy.start()
    for copy in copies:
        copy.wait()
    cells = rhs.shape[-1]
    count = rhs.shape[1]
    layers[...] = jnp.zeros(layers.shape, jnp.int32)
    for section in range(counts.shape[0]):
        layers[section:section + 1, :] = jnp.full((1, LANES), counts[section], jnp.int32)
    small = local.at[2 * count:]
    small[ISC:ISC + 2, :] = isc[...]
    small[FWD:FWD + 2, :] = fwd[...]
    small[BWD:BWD + 2, :] = bwd[...]
    small[PICK:PICK + 2, :] = jnp.full((2, cells), -1, F32)
    small[PICK:PICK + 2, :width] = picked[...].astype(F32)
    local[0:count, :] = rhs[0]
    local[count:2 * count, :] = rhs[1]

    at_a, at_b = picked[0:1, :], picked[1:2, :]
    isc_a, isc_b, fwd_a, fwd_b, bwd_a, bwd_b = (
        split(jnp.broadcast_to(row_of(small, at), (8, cells))) for at in range(PICK)
    )
    base_a = gather_lanes(split(rhs[0]), at_a)
    fed = times(fwd_b, isc_a)
    base_b = gather_lanes(
        minus(split(rhs[1]), [f[0:1] * r for f, r in zip(fed, split(rhs[0]))]), at_b
    )
    write_front(front, base_a + base_b)
    zero = [jnp.zeros((8, LANES), F32)] * (width // LANES)
    rows = {
        SLOPE: gather_lanes(fwd_a, at_a) + gather_lanes(times(fed, fwd_a), at_b),
        TURN: gather_lanes(bwd_a, at_a) + gather_lanes(bwd_b, at_b),
        FOLD: gather_lanes(times(isc_b, bwd_b), at_a) + zero,
        CELL: split(at_a.astype(F32)) + split(at_b.astype(F32)),
    }
    ahead[count:, :] = jnp.zeros((NEEDS, ahead.shape[1]), F32)
    for at, chunks in rows.items():
        for i, chunk in enumerate(chunks):
            ahead[count + at:count + at + 1, i * LANES:(i + 1) * LANES] = chunk[0:1]
    write_field(ahead.at[0:count], base_a + base_b)
    longer[0:ahead.shape[0], :] = ahead[...]
    longer[ahead.shape[0]:, :] = jnp.zeros((longer.shape[0] - ahead.shape[0], longer.shape[1]), F32)
    for layer in range(2):
        place[layer:layer + 1, :] = places(picked[layer:layer + 1, :], cells)


def load_kernel(inverse, first, second, done, sem):
    load = pltpu.make_async_copy(inverse.at[0], first, sem.at[0])
    load.start()
    done[...] = jnp.zeros(done.shape, F32)
    second[:, 0:16, 0:LANES] = jnp.zeros((2, 16, LANES), BF16)
    load.wait()


def join_kernel(*refs):
    *blocks, _, _, joined = refs
    at = 0
    for block in blocks:
        for piece in [block] if len(block.shape) == 3 else [block.at[i] for i in range(block.shape[0])]:
            joined[at] = piece[...]
            at += 1


def two_layers(layers, section):
    return jnp.max(layers[section:section + 1, :]) == 2


def forward_kernel(
    step, sections, planes, width, per_layer, owners, layers, first_inverse, _, inverse, packet,
    place, *rest
):
    blocks, rest = rest[:len(owners)], rest[len(owners):]
    final = step == sections - 1
    if step:
        incoming, *rest = rest
    if not final:
        after, *rest = rest
    kept, front, *rest = rest
    if not final:
        outgoing_packet, *rest = rest
    second_inverse, stacked, solved, sems = rest
    own = lax.axis_index("sweep")
    cells = packet.shape[-1]
    count = cells // LANES
    rows = kept.shape[1]
    small = packet.at[2 * rows:]
    mine = own == step
    both = two_layers(layers, step)

    cuts = 2
    depth = inverse.shape[-1] // cuts
    spans = [(slice(None), slice(None), pl.ds(cut * depth, depth)) for cut in range(cuts)]
    loads = [
        pltpu.make_async_copy(inverse.at[(1, *span)], second_inverse.at[span], sems.at[cut])
        for cut, span in enumerate(spans)
    ]

    @pl.when(mine & both)
    def _():
        for load in loads:
            load.start()

    @pl.when(mine)
    def _():
        stack_fronts(blocks, owners, planes, per_layer, stacked, 0)
        solve(first_inverse, stacked, solved, 0)

    @pl.when(mine & both)
    def _():
        stack_fronts(blocks, owners, planes, per_layer, stacked, 1)
        out = 0
        for load, (_, _, columns) in zip(loads, spans):
            load.wait()
            out = out + product(second_inverse[0, :, columns], stacked[0, :, columns])
            out = out + product(second_inverse[1, :, columns], stacked[1, :, columns])
        store_solved(solved, 1, out)

    @pl.when(mine)
    def _():
        rhs_a, rhs_b = split(packet[0:rows, :]), split(packet[rows:2 * rows, :])
        first_res = rhs_a
        if step:
            first_res = minus(rhs_a, scaled(row_of(small, FWD), read_field(incoming, count)))
        first = gather_lanes(
            split(solved[0]), place[0:1, :], scaled(row_of(small, ISC), first_res)
        )
        second_res = minus(rhs_b, scaled(row_of(small, FWD + 1), first))
        second = gather_lanes(
            split(solved[1]), place[1:2, :], scaled(row_of(small, ISC + 1), second_res)
        )
        if final:
            z = scaled(row_of(small, BWD), choose(both, second, [jnp.zeros_like(c) for c in first]))
            write_front(front, gather_lanes(rounded(z), picks(small, PICK, width)))
        else:
            outgoing = choose(both, second, first)
            chunks = forward_front(after.at[0:rows], after.at[rows:rows + NEEDS], outgoing)
            write_front(front, chunks)
            write_front(outgoing_packet, chunks, outgoing)
        write_field(kept.at[0], first)
        write_field(kept.at[1], second)


def backward_kernel(
    step, sections, planes, width, per_layer, owners, layers, first_inverse, second_inverse,
    packet, place, *rest
):
    blocks, rest = rest[:len(owners)], rest[len(owners):]
    kept, *rest = rest
    last = step == sections - 1
    if not last:
        incoming, before, *rest = rest
    if step:
        behind, *rest = rest
        held, *rest = rest
    result, *rest = rest
    if step:
        front, outgoing_packet, *rest = rest
    stacked, solved = rest
    own = lax.axis_index("sweep")
    count = kept.shape[-1] // LANES
    small = packet.at[2 * kept.shape[1]:]
    mine = own == step
    both = two_layers(layers, step)

    def whole_solve(layer):
        stack_fronts(blocks, owners, planes, per_layer, stacked, layer)
        solve((first_inverse, second_inverse)[layer], stacked, solved, layer)

    if not last:
        @pl.when(own != step)
        def _():
            result[...] = before[...]

        @pl.when(mine & both)
        def _():
            whole_solve(1)

    @pl.when(mine & both if last else mine)
    def _():
        whole_solve(0)

    @pl.when(mine)
    def _():
        first_fwd, second_fwd = split(kept[0]), split(kept[1])
        zero = [jnp.zeros_like(c) for c in first_fwd]
        if last:
            second, arriving = second_fwd, zero
        else:
            arriving = read_field(incoming, count)
            z = scaled(row_of(small, BWD + 1), arriving)
            local = scaled(row_of(small, ISC + 1), z)
            second = minus(second_fwd, gather_lanes(split(solved[1]), place[1:2, :], local))
        following = choose(both, second, arriving)
        z = scaled(row_of(small, BWD), following)
        local = scaled(row_of(small, ISC), z)
        change = gather_lanes(split(solved[0]), place[0:1, :], local)
        if last:
            change = choose(both, change, zero)
        first = minus(first_fwd, change)
        if step:
            chunks = backward_front(
                behind.at[kept.shape[1]:kept.shape[1] + NEEDS], first, read_field(held, count), two_layers(layers, step - 1)
            )
            write_front(front, chunks)
            write_front(outgoing_packet, chunks, first)
        write_field(result.at[0], first)
        write_field(result.at[1], choose(both, second, zero))


def whole(space=pltpu.VMEM):
    return pl.BlockSpec(memory_space=space)


def call(kernel, operands, outs, scratch, name, in_place=(), aliases={}):
    outs = [jax.ShapeDtypeStruct(*o) if isinstance(o, tuple) else o for o in outs]
    specs = [whole(pltpu.SMEM if o.ndim == 1 else pltpu.VMEM) for o in operands]
    for at in in_place:
        specs[at] = whole(pltpu.HBM)
    return pl.pallas_call(
        kernel,
        in_specs=specs,
        out_specs=[whole(pltpu.SMEM if len(o.shape) == 1 else pltpu.VMEM) for o in outs],
        out_shape=outs,
        scratch_shapes=scratch,
        input_output_aliases=aliases,
        compiler_params=pltpu.CompilerParams(vmem_limit_bytes=8 * 2**20),
        name=name,
    )(*operands)


def in_hbm(array):
    return pltpu.with_memory_space_constraint(array, pltpu.HBM)


def shards(
    rhs_field,
    front_inverse,
    interior_scale,
    forward_coupling,
    backward_coupling,
    front_cells,
    section_layers,
):
    sections, planes = lax.axis_size("sweep"), lax.axis_size("plane")
    layer_slots, parts, columns, cells = rhs_field.shape
    rows = parts * columns
    owned, order = front_inverse.shape[2:]
    width = -(-owned // LANES) * LANES
    per_layer = width // LANES
    chips = planes // CORES
    direct = planes in (2, 4, 8) and owned == width

    rhs = rhs_field.reshape(layer_slots, rows, cells)
    picked = jnp.pad(front_cells, ((0, 0), (0, width - owned)), constant_values=-1)
    layers = section_layers

    half_shape = ((per_layer, rows, LANES), BF16)
    front_shape = ((2 * per_layer, rows, LANES), BF16)
    packet_shape = ((2 * per_layer + cells // LANES, rows, LANES), BF16)
    layers_shape = ((layer_slots, rows, cells), F32)
    scratch = [
        pltpu.VMEM((2, rows, order), BF16),
        pltpu.VMEM((2, rows, width), F32),
    ]

    def send(block, links, *flips):
        route = []
        for i, j in links:
            for own in range(planes):
                flip = flips[own % len(flips)] or (i == j and planes % CORES == 0)
                route.append((i * planes + own, j * planes + (own ^ int(flip))))
        return lax.ppermute(block, ("sweep", "plane"), route)

    inside = [(i, i) for i in range(sections)]

    def cycle(*members):
        links = list(zip(members, members[1:] + members[:1]))
        return links + [(i, i) for i in range(sections) if i not in members]

    def everywhere(front):
        slots = front.shape[0] // per_layer
        gathered = lax.all_gather(front, "plane")
        if owned != width:
            gathered = gathered.reshape(planes, slots, per_layer, rows, LANES)
            gathered = gathered.transpose(1, 3, 0, 2, 4).reshape(slots, rows, planes, width)
            gathered = gathered[..., :owned].reshape(slots, rows, order // LANES, LANES)
            gathered = gathered.transpose(0, 2, 1, 3)
            gathered = gathered.reshape(slots * order // LANES, rows, LANES)
            return [gathered], [[0]], order // LANES
        return [gathered], [list(range(planes))], per_layer

    def spread(front, straight, some, every, join=None):
        blocks, owners = [straight], [[(0, 0)]]
        for step in [1] if chips == 2 else range(3, chips):
            blocks.append(send(front, some, CORES * step))
            owners.append([(CORES * step, CORES * step)])
        if chips == 4:
            both = jnp.stack([front, send(front, inside, 1)])
            blocks.append(send(both, every, CORES, 2 * CORES))
            owners += [[(CORES + core, 2 * CORES + core) for core in range(CORES)]]
        if join:
            mine = join(blocks)
        else:
            short = [b[:2 * per_layer] if b.ndim == 3 else b for b in blocks]
            mine = jnp.concatenate([b[None] if b.ndim == 3 else b for b in short])
        blocks.append(send(mine, inside, 1))
        owners.append([(one ^ 1, zero ^ 1) for places in owners for zero, one in places])
        return blocks, owners, per_layer

    def within(front, join=None):
        return spread(front, front, inside, inside, join) if direct else everywhere(front)

    def between(front, packet, start, stop):
        packet = lax.ppermute(packet, "sweep", [(start, stop)])
        if not direct:
            return *everywhere(packet[:2 * per_layer]), packet
        third = [i for i in (2 * stop - start, 2 * start - stop) if 0 <= i < sections]
        some, every = cycle(start, stop, *third[:1]), cycle(start, stop)
        return *spread(front, packet, some, every), packet

    inverse = in_hbm(front_inverse)
    half_inverse = pltpu.VMEM(front_inverse.shape[1:], BF16)
    coefficients = (interior_scale, forward_coupling, backward_coupling)
    operands = [section_layers, rhs, *coefficients, picked]
    local, ahead, longer, place, front, layers = call(
        functools.partial(first_kernel, width),
        [in_hbm(a) for a in operands],
        [
            ((2 * rows + 8, cells), F32),
            ((rows + NEEDS, 2 * width), F32),
            ((2 * rows + NEEDS, 2 * width), F32),
            ((2, cells), jnp.int32),
            front_shape,
            ((-(-sections // 8) * 8, LANES), jnp.int32),
        ],
        [pltpu.VMEM(a.shape, a.dtype) for a in operands[1:]]
        + [pltpu.SMEM(section_layers.shape, jnp.int32), pltpu.SemaphoreType.DMA((6,))],
        "first_fronts",
        range(6),
    )
    def neighbours(first):
        pairs = [(i, i + 1) for i in range(first, sections - 1, 2)]
        alone = [i for i in range(sections) if not any(i in pair for pair in pairs)]
        return pairs + [(j, i) for i, j in pairs] + [(i, i) for i in alone]

    near = [send(ahead, neighbours(0), 0, 0), None]
    first_inverse, second_inverse, token = call(
        load_kernel,
        [inverse],
        [half_inverse, half_inverse, ((8, LANES), F32)],
        [pltpu.SemaphoreType.DMA((1,))],
        "load_first",
        [0],
    )

    def join(blocks):
        shape = (sum(b.shape[0] if b.ndim == 4 else 1 for b in blocks), *front_shape[0])
        return call(join_kernel, [*blocks, near[0], token], [(shape, BF16)], [], "join")[0]

    gathered, owners, slots = within(front, join)

    near[1] = send(longer, neighbours(1), 0)
    kept, held = [], [None]
    for step in range(sections):
        final = step == sections - 1
        extra = ([held[step]] if step else []) + ([] if final else [near[step % 2]])
        outs = [layers_shape, half_shape if final else front_shape]
        outs += [] if final else [packet_shape]
        outs += [half_inverse]
        outs = call(
            functools.partial(
                forward_kernel, step, sections, planes, width, slots, owners
            ),
            [layers, first_inverse, second_inverse, inverse, local, place, *gathered, *extra],
            outs,
            scratch + [pltpu.SemaphoreType.DMA((2,))],
            f"forward_section_{step}",
            [3],
            {2: len(outs) - 1},
        )
        second_inverse = outs[-1]
        kept.append(outs[0])
        if final:
            gathered, owners, slots = within(outs[1])
        else:
            gathered, owners, slots, incoming = between(outs[1], outs[2], step, step + 1)
            held.append(incoming)

    result = incoming = None
    for step in reversed(range(sections)):
        extra = ([] if result is None else [incoming, result]) + ([near[(step - 1) % 2], held[step]] if step else [])
        outs = call(
            functools.partial(
                backward_kernel, step, sections, planes, width, slots, owners
            ),
            [layers, first_inverse, second_inverse, local, place, *gathered, kept[step], *extra],
            [layers_shape] + ([front_shape, packet_shape] if step else []),
            scratch,
            f"backward_section_{step}",
        )
        result = outs[0]
        if step:
            gathered, owners, slots, incoming = between(outs[1], outs[2], step, step - 1)
    return result.reshape(rhs_field.shape)


def solution(mesh):
    in_specs = (
        P("sweep", None, None, "plane"),
        P("sweep", None, "plane", None),
        P("sweep", "plane"),
        P("sweep", "plane"),
        P("sweep", "plane"),
        P("sweep", "plane"),
        P(),
    )
    out_specs = P("sweep", None, None, "plane")
    return jax.shard_map(shards, mesh=mesh, in_specs=in_specs, out_specs=out_specs, check_vma=False)
```

```python
import functools

import jax
import jax.numpy as jnp
from jax import lax
from jax.experimental import pallas as pl
from jax.experimental.pallas import tpu as pltpu
from jax.sharding import PartitionSpec as P

LANES = 128
CORES = 2
ISC, FWD, BWD, PICK = 0, 2, 4, 6
SLOPE, TURN, FOLD, CELL, NEEDS = 0, 1, 2, 3, 8
F32, BF16 = jnp.float32, jnp.bfloat16


def split(field):
    return [field[:, at:at + LANES] for at in range(0, field.shape[1], LANES)]


def gather_lanes(chunks, index, beyond=None):
    result = []
    for place, part in enumerate(split(index)):
        part = jnp.broadcast_to(part, chunks[0].shape)
        lane, chunk = part & (LANES - 1), part >> (LANES.bit_length() - 1)
        total = jnp.zeros(chunks[0].shape, F32) if beyond is None else beyond[place]
        for number, source in enumerate(chunks):
            found = jnp.take_along_axis(source, lane, axis=1, mode="promise_in_bounds")
            total = jnp.where(chunk == number, found, total)
        result.append(total)
    return result


def scaled(row, chunks):
    return [part * chunk for part, chunk in zip(split(row), chunks)]


def minus(left, right):
    return [a - b for a, b in zip(left, right)]


def choose(flag, left, right):
    return [jnp.where(flag, a, b) for a, b in zip(left, right)]


def rounded(chunks):
    return [c.astype(BF16).astype(F32) for c in chunks]


def row_of(ref, at):
    return ref[at:at + 1, :]


def picks(ref, at, width):
    return ref[at:at + 1, :width].astype(jnp.int32)


def halves(row):
    chunks = split(row)
    return chunks[:len(chunks) // 2], chunks[len(chunks) // 2:]


def times(left, right):
    return [a * b for a, b in zip(left, right)]


def plus(left, right):
    return [a + b for a, b in zip(left, right)]


def gathered_at(needs, field):
    cells = needs[CELL:CELL + 1, :].astype(jnp.int32)
    half = cells.shape[1] // 2
    return gather_lanes(field, cells[:, :half]), gather_lanes(field, cells[:, half:])


def forward_front(base, needs, incoming):
    (base_a, base_b), (slope_a, slope_b) = halves(base[...]), halves(row_of(needs, SLOPE))
    at_a, at_b = gathered_at(needs, incoming)
    return minus(base_a, times(slope_a, at_a)) + plus(base_b, times(slope_b, at_b))


def backward_front(needs, incoming, second_fwd, both):
    (turn_a, turn_b), (fold, _) = halves(row_of(needs, TURN)), halves(row_of(needs, FOLD))
    at_a, at_b = gathered_at(needs, incoming)
    second_a, _ = gathered_at(needs, second_fwd)
    following = choose(both, minus(second_a, times(fold, at_a)), at_a)
    return times(turn_a, following) + times(turn_b, at_b)


def write_front(ref, chunks, field=()):
    for at, chunk in enumerate([*chunks, *field]):
        ref[at] = chunk.astype(BF16)


def read_field(packet, count):
    start = packet.shape[0] - count
    return [packet[start + i].astype(F32) for i in range(count)]


def write_field(ref, chunks):
    for at, chunk in enumerate(chunks):
        ref[:, at * LANES:(at + 1) * LANES] = chunk


def owner_of(place, planes):
    if isinstance(place, int):
        return place
    own = lax.axis_index("plane")
    return lax.bitwise_xor(own, jnp.where(lax.rem(own, CORES) == 0, place[0], place[1]))


def stack_fronts(blocks, owners, planes, per_layer, stacked, layer):
    for ref, places in zip(blocks, owners):
        for number, place in enumerate(places):
            owner = owner_of(place, planes)
            for i in range(per_layer):
                at = pl.multiple_of((owner * per_layer + i) * LANES, LANES)
                slot = layer * per_layer + i
                piece = ref[slot] if len(ref.shape) == 3 else ref[number, slot]
                half = piece.shape[0] // 2
                wide = piece.astype(F32)
                turned = jnp.concatenate([-wide[half:], wide[:half]], axis=0)
                stacked[0, :, pl.ds(at, LANES)] = piece
                stacked[1, :, pl.ds(at, LANES)] = turned.astype(BF16)


def product(matrix, columns):
    return lax.dot_general(
        matrix, columns, (((1,), (1,)), ((), ())), preferred_element_type=F32
    )


def store_solved(solved, layer, out):
    rows = out.shape[0]
    if rows % LANES:
        out = jnp.concatenate([out, jnp.zeros((-rows % LANES, out.shape[1]), F32)], axis=0)
    solved[layer] = out.T


def solve(inverse, stacked, solved, layer):
    out = product(inverse[0], stacked[0]) + product(inverse[1], stacked[1])
    store_solved(solved, layer, out)


def places(picked, cells):
    rows = picked.shape[1]
    column = jnp.broadcast_to(picked.astype(F32), (8, rows)).T[:, 0:1].astype(jnp.int32)
    cell = lax.broadcasted_iota(jnp.int32, (rows, cells), 1)
    row = lax.broadcasted_iota(jnp.int32, (rows, cells), 0)
    return jnp.max(jnp.where(column == cell, row, -1), axis=0, keepdims=True)


def first_kernel(
    width, layers_in, rhs_in, isc_in, fwd_in, bwd_in, picked_in, local, ahead, longer, place, front,
    layers, rhs, isc, fwd, bwd, picked, counts, sems,
):
    pairs = (
        (rhs_in, rhs), (isc_in, isc), (fwd_in, fwd), (bwd_in, bwd), (picked_in, picked),
        (layers_in, counts),
    )
    copies = [pltpu.make_async_copy(a, b, sems.at[i]) for i, (a, b) in enumerate(pairs)]
    for copy in copies:
        copy.start()
    for copy in copies:
        copy.wait()
    cells = rhs.shape[-1]
    count = rhs.shape[1]
    layers[...] = jnp.zeros(layers.shape, jnp.int32)
    for section in range(counts.shape[0]):
        layers[section:section + 1, :] = jnp.full((1, LANES), counts[section], jnp.int32)
    small = local.at[2 * count:]
    small[ISC:ISC + 2, :] = isc[...]
    small[FWD:FWD + 2, :] = fwd[...]
    small[BWD:BWD + 2, :] = bwd[...]
    small[PICK:PICK + 2, :] = jnp.full((2, cells), -1, F32)
    small[PICK:PICK + 2, :width] = picked[...].astype(F32)
    local[0:count, :] = rhs[0]
    local[count:2 * count, :] = rhs[1]

    at_a, at_b = picked[0:1, :], picked[1:2, :]
    isc_a, isc_b, fwd_a, fwd_b, bwd_a, bwd_b = (
        split(jnp.broadcast_to(row_of(small, at), (8, cells))) for at in range(PICK)
    )
    base_a = gather_lanes(split(rhs[0]), at_a)
    fed = times(fwd_b, isc_a)
    base_b = gather_lanes(
        minus(split(rhs[1]), [f[0:1] * r for f, r in zip(fed, split(rhs[0]))]), at_b
    )
    write_front(front, base_a + base_b)
    zero = [jnp.zeros((8, LANES), F32)] * (width // LANES)
    rows = {
        SLOPE: gather_lanes(fwd_a, at_a) + gather_lanes(times(fed, fwd_a), at_b),
        TURN: gather_lanes(bwd_a, at_a) + gather_lanes(bwd_b, at_b),
        FOLD: gather_lanes(times(isc_b, bwd_b), at_a) + zero,
        CELL: split(at_a.astype(F32)) + split(at_b.astype(F32)),
    }
    ahead[count:, :] = jnp.zeros((NEEDS, ahead.shape[1]), F32)
    for at, chunks in rows.items():
        for i, chunk in enumerate(chunks):
            ahead[count + at:count + at + 1, i * LANES:(i + 1) * LANES] = chunk[0:1]
    write_field(ahead.at[0:count], base_a + base_b)
    longer[0:ahead.shape[0], :] = ahead[...]
    longer[ahead.shape[0]:, :] = jnp.zeros((longer.shape[0] - ahead.shape[0], longer.shape[1]), F32)
    for layer in range(2):
        place[layer:layer + 1, :] = places(picked[layer:layer + 1, :], cells)


def load_kernel(inverse, first, second, done, sem):
    load = pltpu.make_async_copy(inverse.at[0], first, sem.at[0])
    load.start()
    done[...] = jnp.zeros(done.shape, F32)
    second[:, 0:16, 0:LANES] = jnp.zeros((2, 16, LANES), BF16)
    load.wait()


def join_kernel(*refs):
    *blocks, _, _, joined = refs
    at = 0
    for block in blocks:
        for piece in [block] if len(block.shape) == 3 else [block.at[i] for i in range(block.shape[0])]:
            joined[at] = piece[...]
            at += 1


def two_layers(layers, section):
    return jnp.max(layers[section:section + 1, :]) == 2


def forward_kernel(
    step, sections, planes, width, per_layer, owners, layers, first_inverse, _, inverse, packet,
    place, *rest
):
    blocks, rest = rest[:len(owners)], rest[len(owners):]
    final = step == sections - 1
    if step:
        incoming, *rest = rest
    if not final:
        after, *rest = rest
    kept, front, *rest = rest
    if not final:
        outgoing_packet, *rest = rest
    second_inverse, stacked, solved, sems = rest
    own = lax.axis_index("sweep")
    cells = packet.shape[-1]
    count = cells // LANES
    rows = kept.shape[1]
    small = packet.at[2 * rows:]
    mine = own == step
    both = two_layers(layers, step)

    loads = [
        pltpu.make_async_copy(inverse.at[1, part], second_inverse.at[part], sems.at[part])
        for part in range(2)
    ]
    early = own >= 3

    def when(condition, *actions):
        @pl.when(condition)
        def _():
            for action in actions:
                action()

    starts, waits = [load.start for load in loads], [load.wait for load in loads]
    if step == 1:
        when(early, *starts, *waits)
    when(mine & both & ~early, *starts)

    @pl.when(mine)
    def _():
        stack_fronts(blocks, owners, planes, per_layer, stacked, 0)
        solve(first_inverse, stacked, solved, 0)

    @pl.when(mine & both)
    def _():
        stack_fronts(blocks, owners, planes, per_layer, stacked, 1)
        when(~early, waits[0])
        out = product(second_inverse[0], stacked[0])
        when(~early, waits[1])
        store_solved(solved, 1, out + product(second_inverse[1], stacked[1]))

    @pl.when(mine)
    def _():
        rhs_a, rhs_b = split(packet[0:rows, :]), split(packet[rows:2 * rows, :])
        first_res = rhs_a
        if step:
            first_res = minus(rhs_a, scaled(row_of(small, FWD), read_field(incoming, count)))
        first = gather_lanes(
            split(solved[0]), place[0:1, :], scaled(row_of(small, ISC), first_res)
        )
        second_res = minus(rhs_b, scaled(row_of(small, FWD + 1), first))
        second = gather_lanes(
            split(solved[1]), place[1:2, :], scaled(row_of(small, ISC + 1), second_res)
        )
        if final:
            z = scaled(row_of(small, BWD), choose(both, second, [jnp.zeros_like(c) for c in first]))
            write_front(front, gather_lanes(rounded(z), picks(small, PICK, width)))
        else:
            outgoing = choose(both, second, first)
            chunks = forward_front(after.at[0:rows], after.at[rows:rows + NEEDS], outgoing)
            write_front(front, chunks)
            write_front(outgoing_packet, chunks, outgoing)
        write_field(kept.at[0], first)
        write_field(kept.at[1], second)


def backward_kernel(
    step, sections, planes, width, per_layer, owners, layers, first_inverse, second_inverse,
    packet, place, *rest
):
    blocks, rest = rest[:len(owners)], rest[len(owners):]
    kept, *rest = rest
    last = step == sections - 1
    if not last:
        incoming, before, *rest = rest
    if step:
        behind, *rest = rest
        held, *rest = rest
    result, *rest = rest
    if step:
        front, outgoing_packet, *rest = rest
    stacked, solved = rest
    own = lax.axis_index("sweep")
    count = kept.shape[-1] // LANES
    small = packet.at[2 * kept.shape[1]:]
    mine = own == step
    both = two_layers(layers, step)

    def whole_solve(layer):
        stack_fronts(blocks, owners, planes, per_layer, stacked, layer)
        solve((first_inverse, second_inverse)[layer], stacked, solved, layer)

    if not last:
        @pl.when(own != step)
        def _():
            result[...] = before[...]

        @pl.when(mine & both)
        def _():
            whole_solve(1)

    @pl.when(mine & both if last else mine)
    def _():
        whole_solve(0)

    @pl.when(mine)
    def _():
        first_fwd, second_fwd = split(kept[0]), split(kept[1])
        zero = [jnp.zeros_like(c) for c in first_fwd]
        if last:
            second, arriving = second_fwd, zero
        else:
            arriving = read_field(incoming, count)
            z = scaled(row_of(small, BWD + 1), arriving)
            local = scaled(row_of(small, ISC + 1), z)
            second = minus(second_fwd, gather_lanes(split(solved[1]), place[1:2, :], local))
        following = choose(both, second, arriving)
        z = scaled(row_of(small, BWD), following)
        local = scaled(row_of(small, ISC), z)
        change = gather_lanes(split(solved[0]), place[0:1, :], local)
        if last:
            change = choose(both, change, zero)
        first = minus(first_fwd, change)
        if step:
            chunks = backward_front(
                behind.at[kept.shape[1]:kept.shape[1] + NEEDS], first, read_field(held, count), two_layers(layers, step - 1)
            )
            write_front(front, chunks)
            write_front(outgoing_packet, chunks, first)
        write_field(result.at[0], first)
        write_field(result.at[1], choose(both, second, zero))


def whole(space=pltpu.VMEM):
    return pl.BlockSpec(memory_space=space)


def call(kernel, operands, outs, scratch, name, in_place=(), aliases={}):
    outs = [jax.ShapeDtypeStruct(*o) if isinstance(o, tuple) else o for o in outs]
    specs = [whole(pltpu.SMEM if o.ndim == 1 else pltpu.VMEM) for o in operands]
    for at in in_place:
        specs[at] = whole(pltpu.HBM)
    return pl.pallas_call(
        kernel,
        in_specs=specs,
        out_specs=[whole(pltpu.SMEM if len(o.shape) == 1 else pltpu.VMEM) for o in outs],
        out_shape=outs,
        scratch_shapes=scratch,
        input_output_aliases=aliases,
        compiler_params=pltpu.CompilerParams(vmem_limit_bytes=8 * 2**20),
        name=name,
    )(*operands)


def in_hbm(array):
    return pltpu.with_memory_space_constraint(array, pltpu.HBM)


def shards(
    rhs_field,
    front_inverse,
    interior_scale,
    forward_coupling,
    backward_coupling,
    front_cells,
    section_layers,
):
    sections, planes = lax.axis_size("sweep"), lax.axis_size("plane")
    layer_slots, parts, columns, cells = rhs_field.shape
    rows = parts * columns
    owned, order = front_inverse.shape[2:]
    width = -(-owned // LANES) * LANES
    per_layer = width // LANES
    chips = planes // CORES
    direct = planes in (2, 4, 8) and owned == width

    rhs = rhs_field.reshape(layer_slots, rows, cells)
    picked = jnp.pad(front_cells, ((0, 0), (0, width - owned)), constant_values=-1)
    layers = section_layers

    half_shape = ((per_layer, rows, LANES), BF16)
    front_shape = ((2 * per_layer, rows, LANES), BF16)
    packet_shape = ((2 * per_layer + cells // LANES, rows, LANES), BF16)
    layers_shape = ((layer_slots, rows, cells), F32)
    scratch = [
        pltpu.VMEM((2, rows, order), BF16),
        pltpu.VMEM((2, rows, width), F32),
    ]

    def send(block, links, *flips):
        route = []
        for i, j in links:
            for own in range(planes):
                flip = flips[own % len(flips)] or (i == j and planes % CORES == 0)
                route.append((i * planes + own, j * planes + (own ^ int(flip))))
        return lax.ppermute(block, ("sweep", "plane"), route)

    inside = [(i, i) for i in range(sections)]

    def cycle(*members):
        links = list(zip(members, members[1:] + members[:1]))
        return links + [(i, i) for i in range(sections) if i not in members]

    def everywhere(front):
        slots = front.shape[0] // per_layer
        gathered = lax.all_gather(front, "plane")
        if owned != width:
            gathered = gathered.reshape(planes, slots, per_layer, rows, LANES)
            gathered = gathered.transpose(1, 3, 0, 2, 4).reshape(slots, rows, planes, width)
            gathered = gathered[..., :owned].reshape(slots, rows, order // LANES, LANES)
            gathered = gathered.transpose(0, 2, 1, 3)
            gathered = gathered.reshape(slots * order // LANES, rows, LANES)
            return [gathered], [[0]], order // LANES
        return [gathered], [list(range(planes))], per_layer

    def spread(front, straight, some, every, join=None):
        blocks, owners = [straight], [[(0, 0)]]
        for step in [1] if chips == 2 else range(3, chips):
            blocks.append(send(front, some, CORES * step))
            owners.append([(CORES * step, CORES * step)])
        if chips == 4:
            both = jnp.stack([front, send(front, inside, 1)])
            blocks.append(send(both, every, CORES, 2 * CORES))
            owners += [[(CORES + core, 2 * CORES + core) for core in range(CORES)]]
        if join:
            mine = join(blocks)
        else:
            short = [b[:2 * per_layer] if b.ndim == 3 else b for b in blocks]
            mine = jnp.concatenate([b[None] if b.ndim == 3 else b for b in short])
        blocks.append(send(mine, inside, 1))
        owners.append([(one ^ 1, zero ^ 1) for places in owners for zero, one in places])
        return blocks, owners, per_layer

    def within(front, join=None):
        return spread(front, front, inside, inside, join) if direct else everywhere(front)

    def between(front, packet, start, stop):
        packet = lax.ppermute(packet, "sweep", [(start, stop)])
        if not direct:
            return *everywhere(packet[:2 * per_layer]), packet
        ahead_of = 2 * stop - start, 3 * start - 2 * stop, 2 * start - stop
        third = [i for i in ahead_of if 0 <= i < sections]
        some, every = cycle(start, stop, *third[:1]), cycle(start, stop)
        return *spread(front, packet, some, every), packet

    inverse = in_hbm(front_inverse)
    half_inverse = pltpu.VMEM(front_inverse.shape[1:], BF16)
    coefficients = (interior_scale, forward_coupling, backward_coupling)
    operands = [section_layers, rhs, *coefficients, picked]
    local, ahead, longer, place, front, layers = call(
        functools.partial(first_kernel, width),
        [in_hbm(a) for a in operands],
        [
            ((2 * rows + 8, cells), F32),
            ((rows + NEEDS, 2 * width), F32),
            ((2 * rows + NEEDS, 2 * width), F32),
            ((2, cells), jnp.int32),
            front_shape,
            ((-(-sections // 8) * 8, LANES), jnp.int32),
        ],
        [pltpu.VMEM(a.shape, a.dtype) for a in operands[1:]]
        + [pltpu.SMEM(section_layers.shape, jnp.int32), pltpu.SemaphoreType.DMA((6,))],
        "first_fronts",
        range(6),
    )
    def neighbours(first):
        pairs = [(i, i + 1) for i in range(first, sections - 1, 2)]
        alone = [i for i in range(sections) if not any(i in pair for pair in pairs)]
        return pairs + [(j, i) for i, j in pairs] + [(i, i) for i in alone]

    near = [send(ahead, neighbours(0), 0, 0), None]
    first_inverse, second_inverse, token = call(
        load_kernel,
        [inverse],
        [half_inverse, half_inverse, ((8, LANES), F32)],
        [pltpu.SemaphoreType.DMA((1,))],
        "load_first",
        [0],
    )

    def join(blocks):
        shape = (sum(b.shape[0] if b.ndim == 4 else 1 for b in blocks), *front_shape[0])
        return call(join_kernel, [*blocks, near[0], token], [(shape, BF16)], [], "join")[0]

    gathered, owners, slots = within(front, join)

    near[1] = send(longer, neighbours(1), 0)
    kept, held = [], [None]
    for step in range(sections):
        final = step == sections - 1
        extra = ([held[step]] if step else []) + ([] if final else [near[step % 2]])
        outs = [layers_shape, half_shape if final else front_shape]
        outs += [] if final else [packet_shape]
        outs += [half_inverse]
        outs = call(
            functools.partial(
                forward_kernel, step, sections, planes, width, slots, owners
            ),
            [layers, first_inverse, second_inverse, inverse, local, place, *gathered, *extra],
            outs,
            scratch + [pltpu.SemaphoreType.DMA((2,))],
            f"forward_section_{step}",
            [3],
            {2: len(outs) - 1},
        )
        second_inverse = outs[-1]
        kept.append(outs[0])
        if final:
            gathered, owners, slots = within(outs[1])
        else:
            gathered, owners, slots, incoming = between(outs[1], outs[2], step, step + 1)
            held.append(incoming)

    result = incoming = None
    for step in reversed(range(sections)):
        extra = ([] if result is None else [incoming, result]) + ([near[(step - 1) % 2], held[step]] if step else [])
        outs = call(
            functools.partial(
                backward_kernel, step, sections, planes, width, slots, owners
            ),
            [layers, first_inverse, second_inverse, local, place, *gathered, kept[step], *extra],
            [layers_shape] + ([front_shape, packet_shape] if step else []),
            scratch,
            f"backward_section_{step}",
        )
        result = outs[0]
        if step:
            gathered, owners, slots, incoming = between(outs[1], outs[2], step, step - 1)
    return result.reshape(rhs_field.shape)


def solution(mesh):
    in_specs = (
        P("sweep", None, None, "plane"),
        P("sweep", None, "plane", None),
        P("sweep", "plane"),
        P("sweep", "plane"),
        P("sweep", "plane"),
        P("sweep", "plane"),
        P(),
    )
    out_specs = P("sweep", None, None, "plane")
    return jax.shard_map(shards, mesh=mesh, in_specs=in_specs, out_specs=out_specs, check_vma=False)
```

```python
import functools

import jax
import jax.numpy as jnp
from jax import lax
from jax.experimental import pallas as pl
from jax.experimental.pallas import tpu as pltpu
from jax.sharding import PartitionSpec as P

LANES = 128
CORES = 2
ISC, FWD, BWD, PICK = 0, 2, 4, 6
SLOPE, TURN, FOLD, CELL, NEEDS = 0, 1, 2, 3, 8
F32, BF16 = jnp.float32, jnp.bfloat16


def split(field):
    return [field[:, at:at + LANES] for at in range(0, field.shape[1], LANES)]


def gather_lanes(chunks, index, beyond=None):
    result = []
    for place, part in enumerate(split(index)):
        part = jnp.broadcast_to(part, chunks[0].shape)
        lane, chunk = part & (LANES - 1), part >> (LANES.bit_length() - 1)
        total = jnp.zeros(chunks[0].shape, F32) if beyond is None else beyond[place]
        for number, source in enumerate(chunks):
            found = jnp.take_along_axis(source, lane, axis=1, mode="promise_in_bounds")
            total = jnp.where(chunk == number, found, total)
        result.append(total)
    return result


def scaled(row, chunks):
    return [part * chunk for part, chunk in zip(split(row), chunks)]


def minus(left, right):
    return [a - b for a, b in zip(left, right)]


def choose(flag, left, right):
    return [jnp.where(flag, a, b) for a, b in zip(left, right)]


def rounded(chunks):
    return [c.astype(BF16).astype(F32) for c in chunks]


def row_of(ref, at):
    return ref[at:at + 1, :]


def picks(ref, at, width):
    return ref[at:at + 1, :width].astype(jnp.int32)


def halves(row):
    chunks = split(row)
    return chunks[:len(chunks) // 2], chunks[len(chunks) // 2:]


def times(left, right):
    return [a * b for a, b in zip(left, right)]


def plus(left, right):
    return [a + b for a, b in zip(left, right)]


def gathered_at(needs, field):
    cells = needs[CELL:CELL + 1, :].astype(jnp.int32)
    half = cells.shape[1] // 2
    return gather_lanes(field, cells[:, :half]), gather_lanes(field, cells[:, half:])


def forward_front(base, needs, incoming):
    (base_a, base_b), (slope_a, slope_b) = halves(base[...]), halves(row_of(needs, SLOPE))
    at_a, at_b = gathered_at(needs, incoming)
    return minus(base_a, times(slope_a, at_a)) + plus(base_b, times(slope_b, at_b))


def backward_front(needs, incoming, second_fwd, both):
    (turn_a, turn_b), (fold, _) = halves(row_of(needs, TURN)), halves(row_of(needs, FOLD))
    at_a, at_b = gathered_at(needs, incoming)
    second_a, _ = gathered_at(needs, second_fwd)
    following = choose(both, minus(second_a, times(fold, at_a)), at_a)
    return times(turn_a, following) + times(turn_b, at_b)


def write_front(ref, chunks, field=()):
    for at, chunk in enumerate([*chunks, *field]):
        ref[at] = chunk.astype(BF16)


def read_field(packet, count):
    start = packet.shape[0] - count
    return [packet[start + i].astype(F32) for i in range(count)]


def write_field(ref, chunks):
    for at, chunk in enumerate(chunks):
        ref[:, at * LANES:(at + 1) * LANES] = chunk


def owner_of(place, planes):
    if isinstance(place, int):
        return place
    own = lax.axis_index("plane")
    return lax.bitwise_xor(own, jnp.where(lax.rem(own, CORES) == 0, place[0], place[1]))


def stack_fronts(blocks, owners, planes, per_layer, stacked, layer):
    for ref, places in zip(blocks, owners):
        for number, place in enumerate(places):
            owner = owner_of(place, planes)
            for i in range(per_layer):
                at = pl.multiple_of((owner * per_layer + i) * LANES, LANES)
                slot = layer * per_layer + i
                piece = ref[slot] if len(ref.shape) == 3 else ref[number, slot]
                half = piece.shape[0] // 2
                wide = piece.astype(F32)
                turned = jnp.concatenate([-wide[half:], wide[:half]], axis=0)
                stacked[0, :, pl.ds(at, LANES)] = piece
                stacked[1, :, pl.ds(at, LANES)] = turned.astype(BF16)


def product(matrix, columns):
    return lax.dot_general(
        matrix, columns, (((1,), (1,)), ((), ())), preferred_element_type=F32
    )


def store_solved(solved, layer, out):
    rows = out.shape[0]
    if rows % LANES:
        out = jnp.concatenate([out, jnp.zeros((-rows % LANES, out.shape[1]), F32)], axis=0)
    solved[layer] = out.T


def solve(inverse, stacked, solved, layer):
    out = product(inverse[0], stacked[0]) + product(inverse[1], stacked[1])
    store_solved(solved, layer, out)


def places(picked, cells):
    rows = picked.shape[1]
    column = jnp.broadcast_to(picked.astype(F32), (8, rows)).T[:, 0:1].astype(jnp.int32)
    cell = lax.broadcasted_iota(jnp.int32, (rows, cells), 1)
    row = lax.broadcasted_iota(jnp.int32, (rows, cells), 0)
    return jnp.max(jnp.where(column == cell, row, -1), axis=0, keepdims=True)


def first_kernel(
    width, layers_in, rhs_in, isc_in, fwd_in, bwd_in, picked_in, local, ahead, longer, place, front,
    layers, rhs, isc, fwd, bwd, picked, counts, sems,
):
    pairs = (
        (rhs_in, rhs), (isc_in, isc), (fwd_in, fwd), (bwd_in, bwd), (picked_in, picked),
        (layers_in, counts),
    )
    copies = [pltpu.make_async_copy(a, b, sems.at[i]) for i, (a, b) in enumerate(pairs)]
    for copy in copies:
        copy.start()
    for copy in copies:
        copy.wait()
    cells = rhs.shape[-1]
    count = rhs.shape[1]
    layers[...] = jnp.zeros(layers.shape, jnp.int32)
    for section in range(counts.shape[0]):
        layers[section:section + 1, :] = jnp.full((1, LANES), counts[section], jnp.int32)
    small = local.at[2 * count:]
    small[ISC:ISC + 2, :] = isc[...]
    small[FWD:FWD + 2, :] = fwd[...]
    small[BWD:BWD + 2, :] = bwd[...]
    small[PICK:PICK + 2, :] = jnp.full((2, cells), -1, F32)
    small[PICK:PICK + 2, :width] = picked[...].astype(F32)
    local[0:count, :] = rhs[0]
    local[count:2 * count, :] = rhs[1]

    at_a, at_b = picked[0:1, :], picked[1:2, :]
    isc_a, isc_b, fwd_a, fwd_b, bwd_a, bwd_b = (
        split(jnp.broadcast_to(row_of(small, at), (8, cells))) for at in range(PICK)
    )
    base_a = gather_lanes(split(rhs[0]), at_a)
    fed = times(fwd_b, isc_a)
    base_b = gather_lanes(
        minus(split(rhs[1]), [f[0:1] * r for f, r in zip(fed, split(rhs[0]))]), at_b
    )
    write_front(front, base_a + base_b)
    zero = [jnp.zeros((8, LANES), F32)] * (width // LANES)
    rows = {
        SLOPE: gather_lanes(fwd_a, at_a) + gather_lanes(times(fed, fwd_a), at_b),
        TURN: gather_lanes(bwd_a, at_a) + gather_lanes(bwd_b, at_b),
        FOLD: gather_lanes(times(isc_b, bwd_b), at_a) + zero,
        CELL: split(at_a.astype(F32)) + split(at_b.astype(F32)),
    }
    ahead[count:, :] = jnp.zeros((NEEDS, ahead.shape[1]), F32)
    for at, chunks in rows.items():
        for i, chunk in enumerate(chunks):
            ahead[count + at:count + at + 1, i * LANES:(i + 1) * LANES] = chunk[0:1]
    write_field(ahead.at[0:count], base_a + base_b)
    longer[0:ahead.shape[0], :] = ahead[...]
    longer[ahead.shape[0]:, :] = jnp.zeros((longer.shape[0] - ahead.shape[0], longer.shape[1]), F32)
    for layer in range(2):
        place[layer:layer + 1, :] = places(picked[layer:layer + 1, :], cells)


def load_kernel(inverse, first, second, done, sem):
    load = pltpu.make_async_copy(inverse.at[0], first, sem.at[0])
    load.start()
    done[...] = jnp.zeros(done.shape, F32)
    second[:, 0:16, 0:LANES] = jnp.zeros((2, 16, LANES), BF16)
    load.wait()


def join_kernel(*refs):
    *blocks, _, _, joined = refs
    at = 0
    for block in blocks:
        for piece in [block] if len(block.shape) == 3 else [block.at[i] for i in range(block.shape[0])]:
            joined[at] = piece[...]
            at += 1


def two_layers(layers, section):
    return jnp.max(layers[section:section + 1, :]) == 2


def forward_kernel(
    step, sections, planes, width, per_layer, owners, layers, first_inverse, _, inverse, packet,
    place, *rest
):
    blocks, rest = rest[:len(owners)], rest[len(owners):]
    final = step == sections - 1
    if step:
        incoming, *rest = rest
    if not final:
        after, *rest = rest
    kept, front, *rest = rest
    if not final:
        outgoing_packet, *rest = rest
    second_inverse, stacked, solved, sems = rest
    own = lax.axis_index("sweep")
    cells = packet.shape[-1]
    count = cells // LANES
    rows = kept.shape[1]
    small = packet.at[2 * rows:]
    mine = own == step
    both = two_layers(layers, step)

    loads = [
        pltpu.make_async_copy(inverse.at[1, part], second_inverse.at[part], sems.at[part])
        for part in range(2)
    ]
    early = own >= 3

    def when(condition, *actions):
        @pl.when(condition)
        def _():
            for action in actions:
                action()

    starts, waits = [load.start for load in loads], [load.wait for load in loads]
    if step == 1:
        when(early, *starts, *waits)
    when(mine & both & ~early, *starts)

    @pl.when(mine)
    def _():
        stack_fronts(blocks, owners, planes, per_layer, stacked, 0)
        solve(first_inverse, stacked, solved, 0)

    @pl.when(mine & both)
    def _():
        stack_fronts(blocks, owners, planes, per_layer, stacked, 1)
        when(~early, waits[0])
        out = product(second_inverse[0], stacked[0])
        when(~early, waits[1])
        store_solved(solved, 1, out + product(second_inverse[1], stacked[1]))

    @pl.when(mine)
    def _():
        rhs_a, rhs_b = split(packet[0:rows, :]), split(packet[rows:2 * rows, :])
        first_res = rhs_a
        if step:
            first_res = minus(rhs_a, scaled(row_of(small, FWD), read_field(incoming, count)))
        first = gather_lanes(
            split(solved[0]), place[0:1, :], scaled(row_of(small, ISC), first_res)
        )
        second_res = minus(rhs_b, scaled(row_of(small, FWD + 1), first))
        second = gather_lanes(
            split(solved[1]), place[1:2, :], scaled(row_of(small, ISC + 1), second_res)
        )
        if final:
            z = scaled(row_of(small, BWD), choose(both, second, [jnp.zeros_like(c) for c in first]))
            write_front(front, gather_lanes(rounded(z), picks(small, PICK, width)))
        else:
            outgoing = choose(both, second, first)
            chunks = forward_front(after.at[0:rows], after.at[rows:rows + NEEDS], outgoing)
            write_front(front, chunks)
            write_front(outgoing_packet, chunks, outgoing)
        write_field(kept.at[0], first)
        write_field(kept.at[1], second)


def backward_kernel(
    step, sections, planes, width, per_layer, owners, layers, first_inverse, second_inverse,
    packet, place, *rest
):
    blocks, rest = rest[:len(owners)], rest[len(owners):]
    kept, *rest = rest
    last = step == sections - 1
    if not last:
        incoming, before, *rest = rest
    if step:
        behind, *rest = rest
        held, *rest = rest
    result, *rest = rest
    if step:
        front, outgoing_packet, *rest = rest
    stacked, solved = rest
    own = lax.axis_index("sweep")
    count = kept.shape[-1] // LANES
    small = packet.at[2 * kept.shape[1]:]
    mine = own == step
    both = two_layers(layers, step)

    def whole_solve(layer):
        stack_fronts(blocks, owners, planes, per_layer, stacked, layer)
        solve((first_inverse, second_inverse)[layer], stacked, solved, layer)

    if not last:
        @pl.when(own != step)
        def _():
            result[...] = before[...]

        @pl.when(mine & both)
        def _():
            whole_solve(1)

    @pl.when(mine & both if last else mine)
    def _():
        whole_solve(0)

    @pl.when(mine)
    def _():
        first_fwd, second_fwd = split(kept[0]), split(kept[1])
        zero = [jnp.zeros_like(c) for c in first_fwd]
        if last:
            second, arriving = second_fwd, zero
        else:
            arriving = read_field(incoming, count)
            z = scaled(row_of(small, BWD + 1), arriving)
            local = scaled(row_of(small, ISC + 1), z)
            second = minus(second_fwd, gather_lanes(split(solved[1]), place[1:2, :], local))
        following = choose(both, second, arriving)
        z = scaled(row_of(small, BWD), following)
        local = scaled(row_of(small, ISC), z)
        change = gather_lanes(split(solved[0]), place[0:1, :], local)
        if last:
            change = choose(both, change, zero)
        first = minus(first_fwd, change)
        if step:
            chunks = backward_front(
                behind.at[kept.shape[1]:kept.shape[1] + NEEDS], first, read_field(held, count), two_layers(layers, step - 1)
            )
            write_front(front, chunks)
            write_front(outgoing_packet, chunks, first)
        write_field(result.at[0], first)
        write_field(result.at[1], choose(both, second, zero))


def whole(space=pltpu.VMEM):
    return pl.BlockSpec(memory_space=space)


def call(kernel, operands, outs, scratch, name, in_place=(), aliases={}):
    outs = [jax.ShapeDtypeStruct(*o) if isinstance(o, tuple) else o for o in outs]
    specs = [whole(pltpu.SMEM if o.ndim == 1 else pltpu.VMEM) for o in operands]
    for at in in_place:
        specs[at] = whole(pltpu.HBM)
    return pl.pallas_call(
        kernel,
        in_specs=specs,
        out_specs=[whole(pltpu.SMEM if len(o.shape) == 1 else pltpu.VMEM) for o in outs],
        out_shape=outs,
        scratch_shapes=scratch,
        input_output_aliases=aliases,
        compiler_params=pltpu.CompilerParams(vmem_limit_bytes=8 * 2**20),
        name=name,
    )(*operands)


def in_hbm(array):
    return pltpu.with_memory_space_constraint(array, pltpu.HBM)


def shards(
    rhs_field,
    front_inverse,
    interior_scale,
    forward_coupling,
    backward_coupling,
    front_cells,
    section_layers,
):
    sections, planes = lax.axis_size("sweep"), lax.axis_size("plane")
    layer_slots, parts, columns, cells = rhs_field.shape
    rows = parts * columns
    owned, order = front_inverse.shape[2:]
    width = -(-owned // LANES) * LANES
    per_layer = width // LANES
    chips = planes // CORES
    direct = planes in (2, 4, 8) and owned == width

    rhs = rhs_field.reshape(layer_slots, rows, cells)
    picked = jnp.pad(front_cells, ((0, 0), (0, width - owned)), constant_values=-1)
    layers = section_layers

    half_shape = ((per_layer, rows, LANES), BF16)
    front_shape = ((2 * per_layer, rows, LANES), BF16)
    packet_shape = ((2 * per_layer + cells // LANES, rows, LANES), BF16)
    layers_shape = ((layer_slots, rows, cells), F32)
    scratch = [
        pltpu.VMEM((2, rows, order), BF16),
        pltpu.VMEM((2, rows, width), F32),
    ]

    def send(block, links, *flips):
        route = []
        for i, j in links:
            for own in range(planes):
                flip = flips[own % len(flips)] or (i == j and planes % CORES == 0)
                route.append((i * planes + own, j * planes + (own ^ int(flip))))
        return lax.ppermute(block, ("sweep", "plane"), route)

    inside = [(i, i) for i in range(sections)]

    def cycle(*members):
        links = list(zip(members, members[1:] + members[:1]))
        return links + [(i, i) for i in range(sections) if i not in members]

    def everywhere(front):
        slots = front.shape[0] // per_layer
        gathered = lax.all_gather(front, "plane")
        if owned != width:
            gathered = gathered.reshape(planes, slots, per_layer, rows, LANES)
            gathered = gathered.transpose(1, 3, 0, 2, 4).reshape(slots, rows, planes, width)
            gathered = gathered[..., :owned].reshape(slots, rows, order // LANES, LANES)
            gathered = gathered.transpose(0, 2, 1, 3)
            gathered = gathered.reshape(slots * order // LANES, rows, LANES)
            return [gathered], [[0]], order // LANES
        return [gathered], [list(range(planes))], per_layer

    def spread(front, straight, some, every, join=None):
        blocks, owners = [straight], [[(0, 0)]]
        for step in [1] if chips == 2 else range(3, chips):
            blocks.append(send(front, some, CORES * step))
            owners.append([(CORES * step, CORES * step)])
        if chips == 4:
            both = jnp.stack([front, send(front, inside, 1)])
            blocks.append(send(both, every, CORES, 2 * CORES))
            owners += [[(CORES + core, 2 * CORES + core) for core in range(CORES)]]
        if join:
            mine = join(blocks)
        else:
            short = [b[:2 * per_layer] if b.ndim == 3 else b for b in blocks]
            mine = jnp.concatenate([b[None] if b.ndim == 3 else b for b in short])
        blocks.append(send(mine, inside, 1))
        owners.append([(one ^ 1, zero ^ 1) for places in owners for zero, one in places])
        return blocks, owners, per_layer

    def within(front, join=None):
        return spread(front, front, inside, inside, join) if direct else everywhere(front)

    def between(front, packet, start, stop):
        if not direct:
            packet = lax.ppermute(packet, "sweep", [(start, stop)])
            return *everywhere(packet[:2 * per_layer]), packet
        ahead_of = 2 * stop - start, 3 * start - 2 * stop, 2 * start - stop
        third = [i for i in ahead_of if 0 <= i < sections]
        some, every = cycle(start, stop, *third[:1]), cycle(start, stop)
        fourth = [i for i in range(sections) if i not in (start, stop, *third[:1])]
        packet = send(packet, cycle(start, stop, *fourth[:1]), 0)
        return *spread(front, packet, some, every), packet

    inverse = in_hbm(front_inverse)
    half_inverse = pltpu.VMEM(front_inverse.shape[1:], BF16)
    coefficients = (interior_scale, forward_coupling, backward_coupling)
    operands = [section_layers, rhs, *coefficients, picked]
    local, ahead, longer, place, front, layers = call(
        functools.partial(first_kernel, width),
        [in_hbm(a) for a in operands],
        [
            ((2 * rows + 8, cells), F32),
            ((rows + NEEDS, 2 * width), F32),
            ((2 * rows + NEEDS, 2 * width), F32),
            ((2, cells), jnp.int32),
            front_shape,
            ((-(-sections // 8) * 8, LANES), jnp.int32),
        ],
        [pltpu.VMEM(a.shape, a.dtype) for a in operands[1:]]
        + [pltpu.SMEM(section_layers.shape, jnp.int32), pltpu.SemaphoreType.DMA((6,))],
        "first_fronts",
        range(6),
    )
    def neighbours(first):
        pairs = [(i, i + 1) for i in range(first, sections - 1, 2)]
        alone = [i for i in range(sections) if not any(i in pair for pair in pairs)]
        return pairs + [(j, i) for i, j in pairs] + [(i, i) for i in alone]

    near = [send(ahead, neighbours(0), 0, 0), None]
    first_inverse, second_inverse, token = call(
        load_kernel,
        [inverse],
        [half_inverse, half_inverse, ((8, LANES), F32)],
        [pltpu.SemaphoreType.DMA((1,))],
        "load_first",
        [0],
    )

    def join(blocks):
        shape = (sum(b.shape[0] if b.ndim == 4 else 1 for b in blocks), *front_shape[0])
        return call(join_kernel, [*blocks, near[0], token], [(shape, BF16)], [], "join")[0]

    gathered, owners, slots = within(front, join)

    near[1] = send(longer, neighbours(1), 0)
    kept, held = [], [None]
    for step in range(sections):
        final = step == sections - 1
        extra = ([held[step]] if step else []) + ([] if final else [near[step % 2]])
        outs = [layers_shape, half_shape if final else front_shape]
        outs += [] if final else [packet_shape]
        outs += [half_inverse]
        outs = call(
            functools.partial(
                forward_kernel, step, sections, planes, width, slots, owners
            ),
            [layers, first_inverse, second_inverse, inverse, local, place, *gathered, *extra],
            outs,
            scratch + [pltpu.SemaphoreType.DMA((2,))],
            f"forward_section_{step}",
            [3],
            {2: len(outs) - 1},
        )
        second_inverse = outs[-1]
        kept.append(outs[0])
        if final:
            gathered, owners, slots = within(outs[1])
        else:
            gathered, owners, slots, incoming = between(outs[1], outs[2], step, step + 1)
            held.append(incoming)

    result = incoming = None
    for step in reversed(range(sections)):
        extra = ([] if result is None else [incoming, result]) + ([near[(step - 1) % 2], held[step]] if step else [])
        outs = call(
            functools.partial(
                backward_kernel, step, sections, planes, width, slots, owners
            ),
            [layers, first_inverse, second_inverse, local, place, *gathered, kept[step], *extra],
            [layers_shape] + ([front_shape, packet_shape] if step else []),
            scratch,
            f"backward_section_{step}",
        )
        result = outs[0]
        if step:
            gathered, owners, slots, incoming = between(outs[1], outs[2], step, step - 1)
    return result.reshape(rhs_field.shape)


def solution(mesh):
    in_specs = (
        P("sweep", None, None, "plane"),
        P("sweep", None, "plane", None),
        P("sweep", "plane"),
        P("sweep", "plane"),
        P("sweep", "plane"),
        P("sweep", "plane"),
        P(),
    )
    out_specs = P("sweep", None, None, "plane")
    return jax.shard_map(shards, mesh=mesh, in_specs=in_specs, out_specs=out_specs, check_vma=False)
```

```python
import functools

import jax
import jax.numpy as jnp
from jax import lax
from jax.experimental import pallas as pl
from jax.experimental.pallas import tpu as pltpu
from jax.sharding import PartitionSpec as P

LANES = 128
CORES = 2
ISC, FWD, BWD, PICK = 0, 2, 4, 6
SLOPE, TURN, FOLD, CELL, NEEDS = 0, 1, 2, 3, 8
F32, BF16 = jnp.float32, jnp.bfloat16


def split(field):
    return [field[:, at:at + LANES] for at in range(0, field.shape[1], LANES)]


def gather_lanes(chunks, index, beyond=None):
    result = []
    for place, part in enumerate(split(index)):
        part = jnp.broadcast_to(part, chunks[0].shape)
        lane, chunk = part & (LANES - 1), part >> (LANES.bit_length() - 1)
        total = jnp.zeros(chunks[0].shape, F32) if beyond is None else beyond[place]
        for number, source in enumerate(chunks):
            found = jnp.take_along_axis(source, lane, axis=1, mode="promise_in_bounds")
            total = jnp.where(chunk == number, found, total)
        result.append(total)
    return result


def scaled(row, chunks):
    return [part * chunk for part, chunk in zip(split(row), chunks)]


def minus(left, right):
    return [a - b for a, b in zip(left, right)]


def choose(flag, left, right):
    return [jnp.where(flag, a, b) for a, b in zip(left, right)]


def rounded(chunks):
    return [c.astype(BF16).astype(F32) for c in chunks]


def row_of(ref, at):
    return ref[at:at + 1, :]


def picks(ref, at, width):
    return ref[at:at + 1, :width].astype(jnp.int32)


def halves(row):
    chunks = split(row)
    return chunks[:len(chunks) // 2], chunks[len(chunks) // 2:]


def times(left, right):
    return [a * b for a, b in zip(left, right)]


def plus(left, right):
    return [a + b for a, b in zip(left, right)]


def gathered_at(needs, field):
    cells = needs[CELL:CELL + 1, :].astype(jnp.int32)
    half = cells.shape[1] // 2
    return gather_lanes(field, cells[:, :half]), gather_lanes(field, cells[:, half:])


def forward_front(base, needs, incoming):
    (base_a, base_b), (slope_a, slope_b) = halves(base[...]), halves(row_of(needs, SLOPE))
    at_a, at_b = gathered_at(needs, incoming)
    return minus(base_a, times(slope_a, at_a)) + plus(base_b, times(slope_b, at_b))


def backward_front(needs, incoming, second_fwd, both):
    (turn_a, turn_b), (fold, _) = halves(row_of(needs, TURN)), halves(row_of(needs, FOLD))
    at_a, at_b = gathered_at(needs, incoming)
    second_a, _ = gathered_at(needs, second_fwd)
    following = choose(both, minus(second_a, times(fold, at_a)), at_a)
    return times(turn_a, following) + times(turn_b, at_b)


def write_front(ref, chunks, field=()):
    for at, chunk in enumerate([*chunks, *field]):
        ref[at] = chunk.astype(BF16)


def read_field(packet, count):
    start = packet.shape[0] - count
    return [packet[start + i].astype(F32) for i in range(count)]


def write_field(ref, chunks):
    for at, chunk in enumerate(chunks):
        ref[:, at * LANES:(at + 1) * LANES] = chunk


def owner_of(place, planes):
    if isinstance(place, int):
        return place
    own = lax.axis_index("plane")
    return lax.bitwise_xor(own, jnp.where(lax.rem(own, CORES) == 0, place[0], place[1]))


def stack_fronts(blocks, owners, planes, per_layer, stacked, layer):
    for ref, places in zip(blocks, owners):
        for number, place in enumerate(places):
            owner = owner_of(place, planes)
            for i in range(per_layer):
                at = pl.multiple_of((owner * per_layer + i) * LANES, LANES)
                slot = layer * per_layer + i
                piece = ref[slot] if len(ref.shape) == 3 else ref[number, slot]
                half = piece.shape[0] // 2
                wide = piece.astype(F32)
                turned = jnp.concatenate([-wide[half:], wide[:half]], axis=0)
                stacked[0, :, pl.ds(at, LANES)] = piece
                stacked[1, :, pl.ds(at, LANES)] = turned.astype(BF16)


def product(matrix, columns):
    return lax.dot_general(
        matrix, columns, (((1,), (1,)), ((), ())), preferred_element_type=F32
    )


def store_solved(solved, layer, out):
    rows = out.shape[0]
    if rows % LANES:
        out = jnp.concatenate([out, jnp.zeros((-rows % LANES, out.shape[1]), F32)], axis=0)
    solved[layer] = out.T


def solve(inverse, stacked, solved, layer):
    out = product(inverse[0], stacked[0]) + product(inverse[1], stacked[1])
    store_solved(solved, layer, out)


def places(picked, cells):
    rows = picked.shape[1]
    column = jnp.broadcast_to(picked.astype(F32), (8, rows)).T[:, 0:1].astype(jnp.int32)
    cell = lax.broadcasted_iota(jnp.int32, (rows, cells), 1)
    row = lax.broadcasted_iota(jnp.int32, (rows, cells), 0)
    return jnp.max(jnp.where(column == cell, row, -1), axis=0, keepdims=True)


def first_kernel(
    width, layers_in, rhs_in, isc_in, fwd_in, bwd_in, picked_in, local, ahead, longer, place, front,
    layers, rhs, isc, fwd, bwd, picked, counts, sems,
):
    pairs = (
        (rhs_in, rhs), (isc_in, isc), (fwd_in, fwd), (bwd_in, bwd), (picked_in, picked),
        (layers_in, counts),
    )
    copies = [pltpu.make_async_copy(a, b, sems.at[i]) for i, (a, b) in enumerate(pairs)]
    for copy in copies:
        copy.start()
    for copy in copies:
        copy.wait()
    cells = rhs.shape[-1]
    count = rhs.shape[1]
    layers[...] = jnp.zeros(layers.shape, jnp.int32)
    for section in range(counts.shape[0]):
        layers[section:section + 1, :] = jnp.full((1, LANES), counts[section], jnp.int32)
    small = local.at[2 * count:]
    small[ISC:ISC + 2, :] = isc[...]
    small[FWD:FWD + 2, :] = fwd[...]
    small[BWD:BWD + 2, :] = bwd[...]
    small[PICK:PICK + 2, :] = jnp.full((2, cells), -1, F32)
    small[PICK:PICK + 2, :width] = picked[...].astype(F32)
    local[0:count, :] = rhs[0]
    local[count:2 * count, :] = rhs[1]

    at_a, at_b = picked[0:1, :], picked[1:2, :]
    isc_a, isc_b, fwd_a, fwd_b, bwd_a, bwd_b = (
        split(jnp.broadcast_to(row_of(small, at), (8, cells))) for at in range(PICK)
    )
    base_a = gather_lanes(split(rhs[0]), at_a)
    fed = times(fwd_b, isc_a)
    base_b = gather_lanes(
        minus(split(rhs[1]), [f[0:1] * r for f, r in zip(fed, split(rhs[0]))]), at_b
    )
    write_front(front, base_a + base_b)
    zero = [jnp.zeros((8, LANES), F32)] * (width // LANES)
    rows = {
        SLOPE: gather_lanes(fwd_a, at_a) + gather_lanes(times(fed, fwd_a), at_b),
        TURN: gather_lanes(bwd_a, at_a) + gather_lanes(bwd_b, at_b),
        FOLD: gather_lanes(times(isc_b, bwd_b), at_a) + zero,
        CELL: split(at_a.astype(F32)) + split(at_b.astype(F32)),
    }
    ahead[count:, :] = jnp.zeros((NEEDS, ahead.shape[1]), F32)
    for at, chunks in rows.items():
        for i, chunk in enumerate(chunks):
            ahead[count + at:count + at + 1, i * LANES:(i + 1) * LANES] = chunk[0:1]
    write_field(ahead.at[0:count], base_a + base_b)
    longer[0:ahead.shape[0], :] = ahead[...]
    longer[ahead.shape[0]:, :] = jnp.zeros((longer.shape[0] - ahead.shape[0], longer.shape[1]), F32)
    for layer in range(2):
        place[layer:layer + 1, :] = places(picked[layer:layer + 1, :], cells)


def load_kernel(inverse, first, second, done, sem):
    load = pltpu.make_async_copy(inverse.at[0], first, sem.at[0])
    load.start()
    done[...] = jnp.zeros(done.shape, F32)
    second[:, 0:16, 0:LANES] = jnp.zeros((2, 16, LANES), BF16)
    load.wait()


def join_kernel(*refs):
    *blocks, _, _, joined = refs
    at = 0
    for block in blocks:
        for piece in [block] if len(block.shape) == 3 else [block.at[i] for i in range(block.shape[0])]:
            joined[at] = piece[...]
            at += 1


def two_layers(layers, section):
    return jnp.max(layers[section:section + 1, :]) == 2


def forward_kernel(
    step, sections, planes, width, per_layer, owners, layers, first_inverse, _, inverse, packet,
    place, *rest
):
    blocks, rest = rest[:len(owners)], rest[len(owners):]
    final = step == sections - 1
    if step:
        incoming, *rest = rest
    if not final:
        after, *rest = rest
    kept, front, *rest = rest
    if not final:
        outgoing_packet, *rest = rest
    second_inverse, stacked, solved, sems = rest
    own = lax.axis_index("sweep")
    cells = packet.shape[-1]
    count = cells // LANES
    rows = kept.shape[1]
    small = packet.at[2 * rows:]
    mine = own == step
    both = two_layers(layers, step)

    loads = [
        pltpu.make_async_copy(inverse.at[1, part], second_inverse.at[part], sems.at[part])
        for part in range(2)
    ]
    early = own >= 3

    def when(condition, *actions):
        @pl.when(condition)
        def _():
            for action in actions:
                action()

    starts, waits = [load.start for load in loads], [load.wait for load in loads]
    if step == 1:
        when(early, *starts, *waits)
    when(mine & both & ~early, *starts)

    @pl.when(mine)
    def _():
        stack_fronts(blocks, owners, planes, per_layer, stacked, 0)
        solve(first_inverse, stacked, solved, 0)

    @pl.when(mine & both)
    def _():
        stack_fronts(blocks, owners, planes, per_layer, stacked, 1)
        when(~early, waits[0])
        out = product(second_inverse[0], stacked[0])
        when(~early, waits[1])
        store_solved(solved, 1, out + product(second_inverse[1], stacked[1]))

    @pl.when(mine)
    def _():
        rhs_a, rhs_b = split(packet[0:rows, :]), split(packet[rows:2 * rows, :])
        first_res = rhs_a
        if step:
            first_res = minus(rhs_a, scaled(row_of(small, FWD), read_field(incoming, count)))
        first = gather_lanes(
            split(solved[0]), place[0:1, :], scaled(row_of(small, ISC), first_res)
        )
        second_res = minus(rhs_b, scaled(row_of(small, FWD + 1), first))
        second = gather_lanes(
            split(solved[1]), place[1:2, :], scaled(row_of(small, ISC + 1), second_res)
        )
        if final:
            z = scaled(row_of(small, BWD), choose(both, second, [jnp.zeros_like(c) for c in first]))
            write_front(front, gather_lanes(rounded(z), picks(small, PICK, width)))
        else:
            outgoing = choose(both, second, first)
            chunks = forward_front(after.at[0:rows], after.at[rows:rows + NEEDS], outgoing)
            write_front(front, chunks)
            write_front(outgoing_packet, chunks, outgoing)
        write_field(kept.at[0], first)
        write_field(kept.at[1], second)


def backward_kernel(
    step, sections, planes, width, per_layer, owners, layers, first_inverse, second_inverse,
    packet, place, *rest
):
    blocks, rest = rest[:len(owners)], rest[len(owners):]
    kept, *rest = rest
    last = step == sections - 1
    if not last:
        incoming, before, *rest = rest
    if step:
        behind, *rest = rest
        held, *rest = rest
    result, *rest = rest
    if step:
        front, outgoing_packet, *rest = rest
    stacked, solved = rest
    own = lax.axis_index("sweep")
    count = kept.shape[-1] // LANES
    small = packet.at[2 * kept.shape[1]:]
    mine = own == step
    both = two_layers(layers, step)

    def whole_solve(layer):
        stack_fronts(blocks, owners, planes, per_layer, stacked, layer)
        solve((first_inverse, second_inverse)[layer], stacked, solved, layer)

    if not last:
        @pl.when(own != step)
        def _():
            result[...] = before[...]

        @pl.when(mine & both)
        def _():
            whole_solve(1)

    @pl.when(mine & both if last else mine)
    def _():
        whole_solve(0)

    @pl.when(mine)
    def _():
        first_fwd, second_fwd = split(kept[0]), split(kept[1])
        zero = [jnp.zeros_like(c) for c in first_fwd]
        if last:
            second, arriving = second_fwd, zero
        else:
            arriving = read_field(incoming, count)
            z = scaled(row_of(small, BWD + 1), arriving)
            local = scaled(row_of(small, ISC + 1), z)
            second = minus(second_fwd, gather_lanes(split(solved[1]), place[1:2, :], local))
        following = choose(both, second, arriving)
        z = scaled(row_of(small, BWD), following)
        local = scaled(row_of(small, ISC), z)
        change = gather_lanes(split(solved[0]), place[0:1, :], local)
        if last:
            change = choose(both, change, zero)
        first = minus(first_fwd, change)
        if step:
            chunks = backward_front(
                behind.at[kept.shape[1]:kept.shape[1] + NEEDS], first, read_field(held, count), two_layers(layers, step - 1)
            )
            write_front(front, chunks)
            write_front(outgoing_packet, chunks, first)
        write_field(result.at[0], first)
        write_field(result.at[1], choose(both, second, zero))


def whole(space=pltpu.VMEM):
    return pl.BlockSpec(memory_space=space)


def call(kernel, operands, outs, scratch, name, in_place=(), aliases={}):
    outs = [jax.ShapeDtypeStruct(*o) if isinstance(o, tuple) else o for o in outs]
    specs = [whole(pltpu.SMEM if o.ndim == 1 else pltpu.VMEM) for o in operands]
    for at in in_place:
        specs[at] = whole(pltpu.HBM)
    return pl.pallas_call(
        kernel,
        in_specs=specs,
        out_specs=[whole(pltpu.SMEM if len(o.shape) == 1 else pltpu.VMEM) for o in outs],
        out_shape=outs,
        scratch_shapes=scratch,
        input_output_aliases=aliases,
        compiler_params=pltpu.CompilerParams(vmem_limit_bytes=8 * 2**20),
        name=name,
    )(*operands)


def in_hbm(array):
    return pltpu.with_memory_space_constraint(array, pltpu.HBM)


def shards(
    rhs_field,
    front_inverse,
    interior_scale,
    forward_coupling,
    backward_coupling,
    front_cells,
    section_layers,
):
    sections, planes = lax.axis_size("sweep"), lax.axis_size("plane")
    layer_slots, parts, columns, cells = rhs_field.shape
    rows = parts * columns
    owned, order = front_inverse.shape[2:]
    width = -(-owned // LANES) * LANES
    per_layer = width // LANES
    chips = planes // CORES
    direct = planes in (2, 4, 8) and owned == width

    rhs = rhs_field.reshape(layer_slots, rows, cells)
    picked = jnp.pad(front_cells, ((0, 0), (0, width - owned)), constant_values=-1)
    layers = section_layers

    half_shape = ((per_layer, rows, LANES), BF16)
    front_shape = ((2 * per_layer, rows, LANES), BF16)
    packet_shape = ((2 * per_layer + cells // LANES, rows, LANES), BF16)
    layers_shape = ((layer_slots, rows, cells), F32)
    scratch = [
        pltpu.VMEM((2, rows, order), BF16),
        pltpu.VMEM((2, rows, width), F32),
    ]

    def send(block, links, *flips):
        route = []
        for i, j in links:
            for own in range(planes):
                flip = flips[own % len(flips)] or (i == j and planes % CORES == 0)
                route.append((i * planes + own, j * planes + (own ^ int(flip))))
        return lax.ppermute(block, ("sweep", "plane"), route)

    inside = [(i, i) for i in range(sections)]

    def cycle(*members):
        links = list(zip(members, members[1:] + members[:1]))
        return links + [(i, i) for i in range(sections) if i not in members]

    def everywhere(front):
        slots = front.shape[0] // per_layer
        gathered = lax.all_gather(front, "plane")
        if owned != width:
            gathered = gathered.reshape(planes, slots, per_layer, rows, LANES)
            gathered = gathered.transpose(1, 3, 0, 2, 4).reshape(slots, rows, planes, width)
            gathered = gathered[..., :owned].reshape(slots, rows, order // LANES, LANES)
            gathered = gathered.transpose(0, 2, 1, 3)
            gathered = gathered.reshape(slots * order // LANES, rows, LANES)
            return [gathered], [[0]], order // LANES
        return [gathered], [list(range(planes))], per_layer

    def spread(front, straight, some, every, join=None):
        blocks, owners = [straight], [[(0, 0)]]
        for step in [1] if chips == 2 else range(3, chips):
            blocks.append(send(front, some, CORES * step))
            owners.append([(CORES * step, CORES * step)])
        if chips == 4:
            both = jnp.stack([front, send(front, inside, 1)])
            blocks.append(send(both, every, CORES, 2 * CORES))
            owners += [[(CORES + core, 2 * CORES + core) for core in range(CORES)]]
        if join:
            mine = join(blocks)
        else:
            short = [b[:2 * per_layer] if b.ndim == 3 else b for b in blocks]
            mine = jnp.concatenate([b[None] if b.ndim == 3 else b for b in short])
        blocks.append(send(mine, inside, 1))
        owners.append([(one ^ 1, zero ^ 1) for places in owners for zero, one in places])
        return blocks, owners, per_layer

    def within(front, join=None):
        return spread(front, front, inside, inside, join) if direct else everywhere(front)

    def between(front, packet, start, stop):
        if not direct:
            packet = lax.ppermute(packet, "sweep", [(start, stop)])
            return *everywhere(packet[:2 * per_layer]), packet
        ahead_of = 2 * stop - start, 3 * start - 2 * stop, 2 * start - stop
        third = [i for i in ahead_of if 0 <= i < sections]
        some, every = cycle(start, stop, *third[:1]), cycle(start, stop)
        fourth = [i for i in range(sections) if i not in (start, stop, *third[:1])]
        packet = send(packet, cycle(start, stop, *fourth[:1]), 0)
        return *spread(front, packet, some, every), packet

    inverse = in_hbm(front_inverse)
    half_inverse = pltpu.VMEM(front_inverse.shape[1:], BF16)
    coefficients = (interior_scale, forward_coupling, backward_coupling)
    operands = [section_layers, rhs, *coefficients, picked]
    local, ahead, longer, place, front, layers = call(
        functools.partial(first_kernel, width),
        [in_hbm(a) for a in operands],
        [
            ((2 * rows + 8, cells), F32),
            ((rows + NEEDS, 2 * width), F32),
            ((2 * rows + NEEDS, 2 * width), F32),
            ((2, cells), jnp.int32),
            front_shape,
            ((-(-sections // 8) * 8, LANES), jnp.int32),
        ],
        [pltpu.VMEM(a.shape, a.dtype) for a in operands[1:]]
        + [pltpu.SMEM(section_layers.shape, jnp.int32), pltpu.SemaphoreType.DMA((6,))],
        "first_fronts",
        range(6),
    )
    def neighbours(first):
        pairs = [(i, i + 1) for i in range(first, sections - 1, 2)]
        alone = [i for i in range(sections) if not any(i in pair for pair in pairs)]
        return pairs + [(j, i) for i, j in pairs] + [(i, i) for i in alone]

    near = [send(ahead, neighbours(0), 0, 0), None]
    first_inverse, second_inverse, token = call(
        load_kernel,
        [inverse],
        [half_inverse, half_inverse, ((8, LANES), F32)],
        [pltpu.SemaphoreType.DMA((1,))],
        "load_first",
        [0],
    )

    def join(blocks):
        shape = (sum(b.shape[0] if b.ndim == 4 else 1 for b in blocks), *front_shape[0])
        return call(join_kernel, [*blocks, near[0], token], [(shape, BF16)], [], "join")[0]

    gathered, owners, slots = within(front, join)

    def only_if(condition, exchange, front):
        known = []

        def needed(front):
            gathered, *fixed = exchange(front)
            known.append(fixed)
            return gathered

        shapes = jax.eval_shape(needed, front)
        gathered = lax.cond(
            condition, needed, lambda _: [jnp.zeros(o.shape, o.dtype) for o in shapes], front
        )
        return gathered, *known[-1]

    near[1] = send(longer, neighbours(1), 0)
    kept, held = [], [None]
    for step in range(sections):
        final = step == sections - 1
        extra = ([held[step]] if step else []) + ([] if final else [near[step % 2]])
        outs = [layers_shape, half_shape if final else front_shape]
        outs += [] if final else [packet_shape]
        outs += [half_inverse]
        outs = call(
            functools.partial(
                forward_kernel, step, sections, planes, width, slots, owners
            ),
            [layers, first_inverse, second_inverse, inverse, local, place, *gathered, *extra],
            outs,
            scratch + [pltpu.SemaphoreType.DMA((2,))],
            f"forward_section_{step}",
            [3],
            {2: len(outs) - 1},
        )
        second_inverse = outs[-1]
        kept.append(outs[0])
        if final:
            gathered, owners, slots = only_if(section_layers[step] == 2, within, outs[1])
        else:
            gathered, owners, slots, incoming = between(outs[1], outs[2], step, step + 1)
            held.append(incoming)

    result = incoming = None
    for step in reversed(range(sections)):
        extra = ([] if result is None else [incoming, result]) + ([near[(step - 1) % 2], held[step]] if step else [])
        outs = call(
            functools.partial(
                backward_kernel, step, sections, planes, width, slots, owners
            ),
            [layers, first_inverse, second_inverse, local, place, *gathered, kept[step], *extra],
            [layers_shape] + ([front_shape, packet_shape] if step else []),
            scratch,
            f"backward_section_{step}",
        )
        result = outs[0]
        if step:
            gathered, owners, slots, incoming = between(outs[1], outs[2], step, step - 1)
    return result.reshape(rhs_field.shape)


def solution(mesh):
    in_specs = (
        P("sweep", None, None, "plane"),
        P("sweep", None, "plane", None),
        P("sweep", "plane"),
        P("sweep", "plane"),
        P("sweep", "plane"),
        P("sweep", "plane"),
        P(),
    )
    out_specs = P("sweep", None, None, "plane")
    return jax.shard_map(shards, mesh=mesh, in_specs=in_specs, out_specs=out_specs, check_vma=False)
```

```python
import functools

import jax
import jax.numpy as jnp
from jax import lax
from jax.experimental import pallas as pl
from jax.experimental.pallas import tpu as pltpu
from jax.sharding import PartitionSpec as P

LANES = 128
CORES = 2
ISC, FWD, BWD, PICK = 0, 2, 4, 6
SLOPE, TURN, FOLD, CELL, NEEDS = 0, 1, 2, 3, 8
F32, BF16 = jnp.float32, jnp.bfloat16


def split(field):
    return [field[:, at:at + LANES] for at in range(0, field.shape[1], LANES)]


def gather_lanes(chunks, index, beyond=None):
    result = []
    for place, part in enumerate(split(index)):
        part = jnp.broadcast_to(part, chunks[0].shape)
        lane, chunk = part & (LANES - 1), part >> (LANES.bit_length() - 1)
        total = jnp.zeros(chunks[0].shape, F32) if beyond is None else beyond[place]
        for number, source in enumerate(chunks):
            found = jnp.take_along_axis(source, lane, axis=1, mode="promise_in_bounds")
            total = jnp.where(chunk == number, found, total)
        result.append(total)
    return result


def scaled(row, chunks):
    return [part * chunk for part, chunk in zip(split(row), chunks)]


def minus(left, right):
    return [a - b for a, b in zip(left, right)]


def choose(flag, left, right):
    return [jnp.where(flag, a, b) for a, b in zip(left, right)]


def rounded(chunks):
    return [c.astype(BF16).astype(F32) for c in chunks]


def row_of(ref, at):
    return ref[at:at + 1, :]


def picks(ref, at, width):
    return ref[at:at + 1, :width].astype(jnp.int32)


def halves(row):
    chunks = split(row)
    return chunks[:len(chunks) // 2], chunks[len(chunks) // 2:]


def times(left, right):
    return [a * b for a, b in zip(left, right)]


def plus(left, right):
    return [a + b for a, b in zip(left, right)]


def gathered_at(needs, field):
    cells = needs[CELL:CELL + 1, :].astype(jnp.int32)
    half = cells.shape[1] // 2
    return gather_lanes(field, cells[:, :half]), gather_lanes(field, cells[:, half:])


def forward_front(base, needs, incoming):
    (base_a, base_b), (slope_a, slope_b) = halves(base[...]), halves(row_of(needs, SLOPE))
    at_a, at_b = gathered_at(needs, incoming)
    return minus(base_a, times(slope_a, at_a)) + plus(base_b, times(slope_b, at_b))


def backward_front(needs, incoming, second_fwd, both):
    (turn_a, turn_b), (fold, _) = halves(row_of(needs, TURN)), halves(row_of(needs, FOLD))
    at_a, at_b = gathered_at(needs, incoming)
    second_a, _ = gathered_at(needs, second_fwd)
    following = choose(both, minus(second_a, times(fold, at_a)), at_a)
    return times(turn_a, following) + times(turn_b, at_b)


def write_front(ref, chunks, field=()):
    for at, chunk in enumerate([*chunks, *field]):
        ref[at] = chunk.astype(BF16)


def read_field(packet, count):
    start = packet.shape[0] - count
    return [packet[start + i].astype(F32) for i in range(count)]


def write_field(ref, chunks):
    for at, chunk in enumerate(chunks):
        ref[:, at * LANES:(at + 1) * LANES] = chunk


def owner_of(place, planes):
    if isinstance(place, int):
        return place
    own = lax.axis_index("plane")
    return lax.bitwise_xor(own, jnp.where(lax.rem(own, CORES) == 0, place[0], place[1]))


def stack_fronts(blocks, owners, planes, per_layer, stacked, layer):
    for ref, places in zip(blocks, owners):
        for number, place in enumerate(places):
            owner = owner_of(place, planes)
            for i in range(per_layer):
                at = pl.multiple_of((owner * per_layer + i) * LANES, LANES)
                slot = layer * per_layer + i
                piece = ref[slot] if len(ref.shape) == 3 else ref[number, slot]
                half = piece.shape[0] // 2
                wide = piece.astype(F32)
                turned = jnp.concatenate([-wide[half:], wide[:half]], axis=0)
                stacked[0, :, pl.ds(at, LANES)] = piece
                stacked[1, :, pl.ds(at, LANES)] = turned.astype(BF16)


def product(matrix, columns):
    return lax.dot_general(
        columns, matrix, (((1,), (1,)), ((), ())), preferred_element_type=F32
    )


def store_solved(solved, layer, out):
    rows = out.shape[1]
    if rows % LANES:
        out = jnp.concatenate([out, jnp.zeros((out.shape[0], -rows % LANES), F32)], axis=1)
    solved[layer] = out


def solve(inverse, stacked, solved, layer):
    out = product(inverse[0], stacked[0]) + product(inverse[1], stacked[1])
    store_solved(solved, layer, out)


def places(picked, cells):
    rows = picked.shape[1]
    column = jnp.broadcast_to(picked.astype(F32), (8, rows)).T[:, 0:1].astype(jnp.int32)
    cell = lax.broadcasted_iota(jnp.int32, (rows, cells), 1)
    row = lax.broadcasted_iota(jnp.int32, (rows, cells), 0)
    return jnp.max(jnp.where(column == cell, row, -1), axis=0, keepdims=True)


def first_kernel(
    width, layers_in, rhs_in, isc_in, fwd_in, bwd_in, picked_in, local, ahead, longer, place, front,
    layers, rhs, isc, fwd, bwd, picked, counts, sems,
):
    pairs = (
        (rhs_in, rhs), (isc_in, isc), (fwd_in, fwd), (bwd_in, bwd), (picked_in, picked),
        (layers_in, counts),
    )
    copies = [pltpu.make_async_copy(a, b, sems.at[i]) for i, (a, b) in enumerate(pairs)]
    for copy in copies:
        copy.start()
    for copy in copies:
        copy.wait()
    cells = rhs.shape[-1]
    count = rhs.shape[1]
    layers[...] = jnp.zeros(layers.shape, jnp.int32)
    for section in range(counts.shape[0]):
        layers[section:section + 1, :] = jnp.full((1, LANES), counts[section], jnp.int32)
    small = local.at[2 * count:]
    small[ISC:ISC + 2, :] = isc[...]
    small[FWD:FWD + 2, :] = fwd[...]
    small[BWD:BWD + 2, :] = bwd[...]
    small[PICK:PICK + 2, :] = jnp.full((2, cells), -1, F32)
    small[PICK:PICK + 2, :width] = picked[...].astype(F32)
    local[0:count, :] = rhs[0]
    local[count:2 * count, :] = rhs[1]

    at_a, at_b = picked[0:1, :], picked[1:2, :]
    isc_a, isc_b, fwd_a, fwd_b, bwd_a, bwd_b = (
        split(jnp.broadcast_to(row_of(small, at), (8, cells))) for at in range(PICK)
    )
    base_a = gather_lanes(split(rhs[0]), at_a)
    fed = times(fwd_b, isc_a)
    base_b = gather_lanes(
        minus(split(rhs[1]), [f[0:1] * r for f, r in zip(fed, split(rhs[0]))]), at_b
    )
    write_front(front, base_a + base_b)
    zero = [jnp.zeros((8, LANES), F32)] * (width // LANES)
    rows = {
        SLOPE: gather_lanes(fwd_a, at_a) + gather_lanes(times(fed, fwd_a), at_b),
        TURN: gather_lanes(bwd_a, at_a) + gather_lanes(bwd_b, at_b),
        FOLD: gather_lanes(times(isc_b, bwd_b), at_a) + zero,
        CELL: split(at_a.astype(F32)) + split(at_b.astype(F32)),
    }
    ahead[count:, :] = jnp.zeros((NEEDS, ahead.shape[1]), F32)
    for at, chunks in rows.items():
        for i, chunk in enumerate(chunks):
            ahead[count + at:count + at + 1, i * LANES:(i + 1) * LANES] = chunk[0:1]
    write_field(ahead.at[0:count], base_a + base_b)
    longer[0:ahead.shape[0], :] = ahead[...]
    longer[ahead.shape[0]:, :] = jnp.zeros((longer.shape[0] - ahead.shape[0], longer.shape[1]), F32)
    for layer in range(2):
        place[layer:layer + 1, :] = places(picked[layer:layer + 1, :], cells)


def load_kernel(inverse, first, second, done, sem):
    load = pltpu.make_async_copy(inverse.at[0], first, sem.at[0])
    load.start()
    done[...] = jnp.zeros(done.shape, F32)
    second[:, 0:16, 0:LANES] = jnp.zeros((2, 16, LANES), BF16)
    load.wait()


def join_kernel(*refs):
    *blocks, _, _, joined = refs
    at = 0
    for block in blocks:
        for piece in [block] if len(block.shape) == 3 else [block.at[i] for i in range(block.shape[0])]:
            joined[at] = piece[...]
            at += 1


def two_layers(layers, section):
    return jnp.max(layers[section:section + 1, :]) == 2


def forward_kernel(
    step, sections, planes, width, per_layer, owners, layers, first_inverse, _, inverse, packet,
    place, *rest
):
    blocks, rest = rest[:len(owners)], rest[len(owners):]
    final = step == sections - 1
    if step:
        incoming, *rest = rest
    if not final:
        after, *rest = rest
    kept, front, *rest = rest
    if not final:
        outgoing_packet, *rest = rest
    second_inverse, stacked, solved, sems = rest
    own = lax.axis_index("sweep")
    cells = packet.shape[-1]
    count = cells // LANES
    rows = kept.shape[1]
    small = packet.at[2 * rows:]
    mine = own == step
    both = two_layers(layers, step)

    loads = [
        pltpu.make_async_copy(inverse.at[1, part], second_inverse.at[part], sems.at[part])
        for part in range(2)
    ]
    early = own >= 3

    def when(condition, *actions):
        @pl.when(condition)
        def _():
            for action in actions:
                action()

    starts, waits = [load.start for load in loads], [load.wait for load in loads]
    if step == 1:
        when(early, *starts, *waits)
    when(mine & both & ~early, *starts)

    @pl.when(mine)
    def _():
        stack_fronts(blocks, owners, planes, per_layer, stacked, 0)
        solve(first_inverse, stacked, solved, 0)

    @pl.when(mine & both)
    def _():
        stack_fronts(blocks, owners, planes, per_layer, stacked, 1)
        when(~early, waits[0])
        out = product(second_inverse[0], stacked[0])
        when(~early, waits[1])
        store_solved(solved, 1, out + product(second_inverse[1], stacked[1]))

    @pl.when(mine)
    def _():
        rhs_a, rhs_b = split(packet[0:rows, :]), split(packet[rows:2 * rows, :])
        first_res = rhs_a
        if step:
            first_res = minus(rhs_a, scaled(row_of(small, FWD), read_field(incoming, count)))
        first = gather_lanes(
            split(solved[0]), place[0:1, :], scaled(row_of(small, ISC), first_res)
        )
        second_res = minus(rhs_b, scaled(row_of(small, FWD + 1), first))
        second = gather_lanes(
            split(solved[1]), place[1:2, :], scaled(row_of(small, ISC + 1), second_res)
        )
        if final:
            z = scaled(row_of(small, BWD), choose(both, second, [jnp.zeros_like(c) for c in first]))
            write_front(front, gather_lanes(rounded(z), picks(small, PICK, width)))
        else:
            outgoing = choose(both, second, first)
            chunks = forward_front(after.at[0:rows], after.at[rows:rows + NEEDS], outgoing)
            write_front(front, chunks)
            write_front(outgoing_packet, chunks, outgoing)
        write_field(kept.at[0], first)
        write_field(kept.at[1], second)


def backward_kernel(
    step, sections, planes, width, per_layer, owners, layers, first_inverse, second_inverse,
    packet, place, *rest
):
    blocks, rest = rest[:len(owners)], rest[len(owners):]
    kept, *rest = rest
    last = step == sections - 1
    if not last:
        incoming, before, *rest = rest
    if step:
        behind, *rest = rest
        held, *rest = rest
    result, *rest = rest
    if step:
        front, outgoing_packet, *rest = rest
    stacked, solved = rest
    own = lax.axis_index("sweep")
    count = kept.shape[-1] // LANES
    small = packet.at[2 * kept.shape[1]:]
    mine = own == step
    both = two_layers(layers, step)

    def whole_solve(layer):
        stack_fronts(blocks, owners, planes, per_layer, stacked, layer)
        solve((first_inverse, second_inverse)[layer], stacked, solved, layer)

    if not last:
        @pl.when(own != step)
        def _():
            result[...] = before[...]

        @pl.when(mine & both)
        def _():
            whole_solve(1)

    @pl.when(mine & both if last else mine)
    def _():
        whole_solve(0)

    @pl.when(mine)
    def _():
        first_fwd, second_fwd = split(kept[0]), split(kept[1])
        zero = [jnp.zeros_like(c) for c in first_fwd]
        if last:
            second, arriving = second_fwd, zero
        else:
            arriving = read_field(incoming, count)
            z = scaled(row_of(small, BWD + 1), arriving)
            local = scaled(row_of(small, ISC + 1), z)
            second = minus(second_fwd, gather_lanes(split(solved[1]), place[1:2, :], local))
        following = choose(both, second, arriving)
        z = scaled(row_of(small, BWD), following)
        local = scaled(row_of(small, ISC), z)
        change = gather_lanes(split(solved[0]), place[0:1, :], local)
        if last:
            change = choose(both, change, zero)
        first = minus(first_fwd, change)
        if step:
            chunks = backward_front(
                behind.at[kept.shape[1]:kept.shape[1] + NEEDS], first, read_field(held, count), two_layers(layers, step - 1)
            )
            write_front(front, chunks)
            write_front(outgoing_packet, chunks, first)
        write_field(result.at[0], first)
        write_field(result.at[1], choose(both, second, zero))


def whole(space=pltpu.VMEM):
    return pl.BlockSpec(memory_space=space)


def call(kernel, operands, outs, scratch, name, in_place=(), aliases={}):
    outs = [jax.ShapeDtypeStruct(*o) if isinstance(o, tuple) else o for o in outs]
    specs = [whole(pltpu.SMEM if o.ndim == 1 else pltpu.VMEM) for o in operands]
    for at in in_place:
        specs[at] = whole(pltpu.HBM)
    return pl.pallas_call(
        kernel,
        in_specs=specs,
        out_specs=[whole(pltpu.SMEM if len(o.shape) == 1 else pltpu.VMEM) for o in outs],
        out_shape=outs,
        scratch_shapes=scratch,
        input_output_aliases=aliases,
        compiler_params=pltpu.CompilerParams(vmem_limit_bytes=8 * 2**20),
        name=name,
    )(*operands)


def in_hbm(array):
    return pltpu.with_memory_space_constraint(array, pltpu.HBM)


def shards(
    rhs_field,
    front_inverse,
    interior_scale,
    forward_coupling,
    backward_coupling,
    front_cells,
    section_layers,
):
    sections, planes = lax.axis_size("sweep"), lax.axis_size("plane")
    layer_slots, parts, columns, cells = rhs_field.shape
    rows = parts * columns
    owned, order = front_inverse.shape[2:]
    width = -(-owned // LANES) * LANES
    per_layer = width // LANES
    chips = planes // CORES
    direct = planes in (2, 4, 8) and owned == width

    rhs = rhs_field.reshape(layer_slots, rows, cells)
    picked = jnp.pad(front_cells, ((0, 0), (0, width - owned)), constant_values=-1)
    layers = section_layers

    half_shape = ((per_layer, rows, LANES), BF16)
    front_shape = ((2 * per_layer, rows, LANES), BF16)
    packet_shape = ((2 * per_layer + cells // LANES, rows, LANES), BF16)
    layers_shape = ((layer_slots, rows, cells), F32)
    scratch = [
        pltpu.VMEM((2, rows, order), BF16),
        pltpu.VMEM((2, rows, width), F32),
    ]

    def send(block, links, *flips):
        route = []
        for i, j in links:
            for own in range(planes):
                flip = flips[own % len(flips)] or (i == j and planes % CORES == 0)
                route.append((i * planes + own, j * planes + (own ^ int(flip))))
        return lax.ppermute(block, ("sweep", "plane"), route)

    inside = [(i, i) for i in range(sections)]

    def cycle(*members):
        links = list(zip(members, members[1:] + members[:1]))
        return links + [(i, i) for i in range(sections) if i not in members]

    def everywhere(front):
        slots = front.shape[0] // per_layer
        gathered = lax.all_gather(front, "plane")
        if owned != width:
            gathered = gathered.reshape(planes, slots, per_layer, rows, LANES)
            gathered = gathered.transpose(1, 3, 0, 2, 4).reshape(slots, rows, planes, width)
            gathered = gathered[..., :owned].reshape(slots, rows, order // LANES, LANES)
            gathered = gathered.transpose(0, 2, 1, 3)
            gathered = gathered.reshape(slots * order // LANES, rows, LANES)
            return [gathered], [[0]], order // LANES
        return [gathered], [list(range(planes))], per_layer

    def spread(front, straight, some, every, join=None):
        blocks, owners = [straight], [[(0, 0)]]
        for step in [1] if chips == 2 else range(3, chips):
            blocks.append(send(front, some, CORES * step))
            owners.append([(CORES * step, CORES * step)])
        if chips == 4:
            both = jnp.stack([front, send(front, inside, 1)])
            blocks.append(send(both, every, CORES, 2 * CORES))
            owners += [[(CORES + core, 2 * CORES + core) for core in range(CORES)]]
        if join:
            mine = join(blocks)
        else:
            short = [b[:2 * per_layer] if b.ndim == 3 else b for b in blocks]
            mine = jnp.concatenate([b[None] if b.ndim == 3 else b for b in short])
        blocks.append(send(mine, inside, 1))
        owners.append([(one ^ 1, zero ^ 1) for places in owners for zero, one in places])
        return blocks, owners, per_layer

    def within(front, join=None):
        return spread(front, front, inside, inside, join) if direct else everywhere(front)

    def between(front, packet, start, stop):
        if not direct:
            packet = lax.ppermute(packet, "sweep", [(start, stop)])
            return *everywhere(packet[:2 * per_layer]), packet
        ahead_of = 2 * stop - start, 3 * start - 2 * stop, 2 * start - stop
        third = [i for i in ahead_of if 0 <= i < sections]
        some, every = cycle(start, stop, *third[:1]), cycle(start, stop)
        fourth = [i for i in range(sections) if i not in (start, stop, *third[:1])]
        packet = send(packet, cycle(start, stop, *fourth[:1]), 0)
        return *spread(front, packet, some, every), packet

    inverse = in_hbm(front_inverse)
    half_inverse = pltpu.VMEM(front_inverse.shape[1:], BF16)
    coefficients = (interior_scale, forward_coupling, backward_coupling)
    operands = [section_layers, rhs, *coefficients, picked]
    local, ahead, longer, place, front, layers = call(
        functools.partial(first_kernel, width),
        [in_hbm(a) for a in operands],
        [
            ((2 * rows + 8, cells), F32),
            ((rows + NEEDS, 2 * width), F32),
            ((2 * rows + NEEDS, 2 * width), F32),
            ((2, cells), jnp.int32),
            front_shape,
            ((-(-sections // 8) * 8, LANES), jnp.int32),
        ],
        [pltpu.VMEM(a.shape, a.dtype) for a in operands[1:]]
        + [pltpu.SMEM(section_layers.shape, jnp.int32), pltpu.SemaphoreType.DMA((6,))],
        "first_fronts",
        range(6),
    )
    def neighbours(first):
        pairs = [(i, i + 1) for i in range(first, sections - 1, 2)]
        alone = [i for i in range(sections) if not any(i in pair for pair in pairs)]
        return pairs + [(j, i) for i, j in pairs] + [(i, i) for i in alone]

    near = [send(ahead, neighbours(0), 0, 0), None]
    first_inverse, second_inverse, token = call(
        load_kernel,
        [inverse],
        [half_inverse, half_inverse, ((8, LANES), F32)],
        [pltpu.SemaphoreType.DMA((1,))],
        "load_first",
        [0],
    )

    def join(blocks):
        shape = (sum(b.shape[0] if b.ndim == 4 else 1 for b in blocks), *front_shape[0])
        return call(join_kernel, [*blocks, near[0], token], [(shape, BF16)], [], "join")[0]

    gathered, owners, slots = within(front, join)

    near[1] = send(longer, neighbours(1), 0)
    kept, held = [], [None]
    for step in range(sections):
        final = step == sections - 1
        extra = ([held[step]] if step else []) + ([] if final else [near[step % 2]])
        outs = [layers_shape, half_shape if final else front_shape]
        outs += [] if final else [packet_shape]
        outs += [half_inverse]
        outs = call(
            functools.partial(
                forward_kernel, step, sections, planes, width, slots, owners
            ),
            [layers, first_inverse, second_inverse, inverse, local, place, *gathered, *extra],
            outs,
            scratch + [pltpu.SemaphoreType.DMA((2,))],
            f"forward_section_{step}",
            [3],
            {2: len(outs) - 1},
        )
        second_inverse = outs[-1]
        kept.append(outs[0])
        if final:
            gathered, owners, slots = within(outs[1])
        else:
            gathered, owners, slots, incoming = between(outs[1], outs[2], step, step + 1)
            held.append(incoming)

    result = incoming = None
    for step in reversed(range(sections)):
        extra = ([] if result is None else [incoming, result]) + ([near[(step - 1) % 2], held[step]] if step else [])
        outs = call(
            functools.partial(
                backward_kernel, step, sections, planes, width, slots, owners
            ),
            [layers, first_inverse, second_inverse, local, place, *gathered, kept[step], *extra],
            [layers_shape] + ([front_shape, packet_shape] if step else []),
            scratch,
            f"backward_section_{step}",
        )
        result = outs[0]
        if step:
            gathered, owners, slots, incoming = between(outs[1], outs[2], step, step - 1)
    return result.reshape(rhs_field.shape)


def solution(mesh):
    in_specs = (
        P("sweep", None, None, "plane"),
        P("sweep", None, "plane", None),
        P("sweep", "plane"),
        P("sweep", "plane"),
        P("sweep", "plane"),
        P("sweep", "plane"),
        P(),
    )
    out_specs = P("sweep", None, None, "plane")
    return jax.shard_map(shards, mesh=mesh, in_specs=in_specs, out_specs=out_specs, check_vma=False)
```

```python
import functools

import jax
import jax.numpy as jnp
from jax import lax
from jax.experimental import pallas as pl
from jax.experimental.pallas import tpu as pltpu
from jax.sharding import PartitionSpec as P

LANES = 128
CORES = 2
ISC, FWD, BWD, PICK = 0, 2, 4, 6
SLOPE, TURN, FOLD, CELL, NEEDS = 0, 1, 2, 3, 8
F32, BF16 = jnp.float32, jnp.bfloat16


def split(field):
    return [field[:, at:at + LANES] for at in range(0, field.shape[1], LANES)]


def gather_lanes(chunks, index, beyond=None):
    result = []
    for place, part in enumerate(split(index)):
        part = jnp.broadcast_to(part, chunks[0].shape)
        lane, chunk = part & (LANES - 1), part >> (LANES.bit_length() - 1)
        total = jnp.zeros(chunks[0].shape, F32) if beyond is None else beyond[place]
        for number, source in enumerate(chunks):
            found = jnp.take_along_axis(source, lane, axis=1, mode="promise_in_bounds")
            total = jnp.where(chunk == number, found, total)
        result.append(total)
    return result


def scaled(row, chunks):
    return [part * chunk for part, chunk in zip(split(row), chunks)]


def minus(left, right):
    return [a - b for a, b in zip(left, right)]


def choose(flag, left, right):
    return [jnp.where(flag, a, b) for a, b in zip(left, right)]


def rounded(chunks):
    return [c.astype(BF16).astype(F32) for c in chunks]


def row_of(ref, at):
    return ref[at:at + 1, :]


def picks(ref, at, width):
    return ref[at:at + 1, :width].astype(jnp.int32)


def halves(row):
    chunks = split(row)
    return chunks[:len(chunks) // 2], chunks[len(chunks) // 2:]


def times(left, right):
    return [a * b for a, b in zip(left, right)]


def plus(left, right):
    return [a + b for a, b in zip(left, right)]


def gathered_at(needs, field):
    cells = needs[CELL:CELL + 1, :].astype(jnp.int32)
    half = cells.shape[1] // 2
    return gather_lanes(field, cells[:, :half]), gather_lanes(field, cells[:, half:])


def forward_front(base, needs, incoming):
    (base_a, base_b), (slope_a, slope_b) = halves(base[...]), halves(row_of(needs, SLOPE))
    at_a, at_b = gathered_at(needs, incoming)
    return minus(base_a, times(slope_a, at_a)) + plus(base_b, times(slope_b, at_b))


def backward_front(needs, incoming, second_fwd, both):
    (turn_a, turn_b), (fold, _) = halves(row_of(needs, TURN)), halves(row_of(needs, FOLD))
    at_a, at_b = gathered_at(needs, incoming)
    second_a, _ = gathered_at(needs, second_fwd)
    following = choose(both, minus(second_a, times(fold, at_a)), at_a)
    return times(turn_a, following) + times(turn_b, at_b)


def write_front(ref, chunks, field=()):
    for at, chunk in enumerate([*chunks, *field]):
        ref[at] = chunk.astype(BF16)


def read_field(packet, count):
    start = packet.shape[0] - count
    return [packet[start + i].astype(F32) for i in range(count)]


def write_field(ref, chunks):
    for at, chunk in enumerate(chunks):
        ref[:, at * LANES:(at + 1) * LANES] = chunk


def owner_of(place, planes):
    if isinstance(place, int):
        return place
    own = lax.axis_index("plane")
    return lax.bitwise_xor(own, jnp.where(lax.rem(own, CORES) == 0, place[0], place[1]))


def stack_fronts(blocks, owners, planes, per_layer, stacked, layer):
    for ref, places in zip(blocks, owners):
        for number, place in enumerate(places):
            owner = owner_of(place, planes)
            for i in range(per_layer):
                at = pl.multiple_of((owner * per_layer + i) * LANES, LANES)
                slot = layer * per_layer + i
                piece = ref[slot] if len(ref.shape) == 3 else ref[number, slot]
                half = piece.shape[0] // 2
                wide = piece.astype(F32)
                turned = jnp.concatenate([-wide[half:], wide[:half]], axis=0)
                stacked[0, :, pl.ds(at, LANES)] = piece
                stacked[1, :, pl.ds(at, LANES)] = turned.astype(BF16)


def product(matrix, columns):
    return lax.dot_general(
        columns, matrix, (((1,), (1,)), ((), ())), preferred_element_type=F32
    )


def store_solved(solved, layer, out):
    rows = out.shape[1]
    if rows % LANES:
        out = jnp.concatenate([out, jnp.zeros((out.shape[0], -rows % LANES), F32)], axis=1)
    solved[layer] = out


def solve(inverse, stacked, solved, layer):
    out = product(inverse[0], stacked[0]) + product(inverse[1], stacked[1])
    store_solved(solved, layer, out)


def places(picked, cells):
    rows = picked.shape[1]
    column = jnp.broadcast_to(picked.astype(F32), (8, rows)).T[:, 0:1].astype(jnp.int32)
    cell = lax.broadcasted_iota(jnp.int32, (rows, cells), 1)
    row = lax.broadcasted_iota(jnp.int32, (rows, cells), 0)
    return jnp.max(jnp.where(column == cell, row, -1), axis=0, keepdims=True)


def first_kernel(
    width, layers_in, rhs_in, isc_in, fwd_in, bwd_in, picked_in, local, ahead, longer, place, front,
    layers, rhs, isc, fwd, bwd, picked, counts, sems,
):
    pairs = (
        (rhs_in, rhs), (isc_in, isc), (fwd_in, fwd), (bwd_in, bwd), (picked_in, picked),
        (layers_in, counts),
    )
    copies = [pltpu.make_async_copy(a, b, sems.at[i]) for i, (a, b) in enumerate(pairs)]
    for copy in copies:
        copy.start()
    for copy in copies:
        copy.wait()
    cells = rhs.shape[-1]
    count = rhs.shape[1]
    layers[...] = jnp.zeros(layers.shape, jnp.int32)
    for section in range(counts.shape[0]):
        layers[section:section + 1, :] = jnp.full((1, LANES), counts[section], jnp.int32)
    small = local.at[2 * count:]
    small[ISC:ISC + 2, :] = isc[...]
    small[FWD:FWD + 2, :] = fwd[...]
    small[BWD:BWD + 2, :] = bwd[...]
    small[PICK:PICK + 2, :] = jnp.full((2, cells), -1, F32)
    small[PICK:PICK + 2, :width] = picked[...].astype(F32)
    local[0:count, :] = rhs[0]
    local[count:2 * count, :] = rhs[1]

    at_a, at_b = picked[0:1, :], picked[1:2, :]
    isc_a, isc_b, fwd_a, fwd_b, bwd_a, bwd_b = (
        split(jnp.broadcast_to(row_of(small, at), (8, cells))) for at in range(PICK)
    )
    base_a = gather_lanes(split(rhs[0]), at_a)
    fed = times(fwd_b, isc_a)
    base_b = gather_lanes(
        minus(split(rhs[1]), [f[0:1] * r for f, r in zip(fed, split(rhs[0]))]), at_b
    )
    write_front(front, base_a + base_b)
    zero = [jnp.zeros((8, LANES), F32)] * (width // LANES)
    rows = {
        SLOPE: gather_lanes(fwd_a, at_a) + gather_lanes(times(fed, fwd_a), at_b),
        TURN: gather_lanes(bwd_a, at_a) + gather_lanes(bwd_b, at_b),
        FOLD: gather_lanes(times(isc_b, bwd_b), at_a) + zero,
        CELL: split(at_a.astype(F32)) + split(at_b.astype(F32)),
    }
    ahead[count:, :] = jnp.zeros((NEEDS, ahead.shape[1]), F32)
    for at, chunks in rows.items():
        for i, chunk in enumerate(chunks):
            ahead[count + at:count + at + 1, i * LANES:(i + 1) * LANES] = chunk[0:1]
    write_field(ahead.at[0:count], base_a + base_b)
    longer[0:ahead.shape[0], :] = ahead[...]
    longer[ahead.shape[0]:, :] = jnp.zeros((longer.shape[0] - ahead.shape[0], longer.shape[1]), F32)
    for layer in range(2):
        place[layer:layer + 1, :] = places(picked[layer:layer + 1, :], cells)


def load_kernel(inverse, first, second, done, sem):
    load = pltpu.make_async_copy(inverse.at[0], first, sem.at[0])
    load.start()
    done[...] = jnp.zeros(done.shape, F32)
    second[:, 0:16, 0:LANES] = jnp.zeros((2, 16, LANES), BF16)
    load.wait()


def join_kernel(*refs):
    *blocks, _, _, joined = refs
    at = 0
    for block in blocks:
        for piece in [block] if len(block.shape) == 3 else [block.at[i] for i in range(block.shape[0])]:
            joined[at] = piece[...]
            at += 1


def two_layers(layers, section):
    return jnp.max(layers[section:section + 1, :]) == 2


def forward_kernel(
    step, sections, planes, width, per_layer, owners, layers, first_inverse, _, inverse, packet,
    place, *rest
):
    blocks, rest = rest[:len(owners)], rest[len(owners):]
    final = step == sections - 1
    if step:
        incoming, *rest = rest
    if not final:
        after, *rest = rest
    kept, front, *rest = rest
    if not final:
        outgoing_packet, *rest = rest
    second_inverse, stacked, solved, sems = rest
    own = lax.axis_index("sweep")
    cells = packet.shape[-1]
    count = cells // LANES
    rows = kept.shape[1]
    small = packet.at[2 * rows:]
    mine = own == step
    both = two_layers(layers, step)

    loads = [
        pltpu.make_async_copy(inverse.at[1, part], second_inverse.at[part], sems.at[part])
        for part in range(2)
    ]
    early = own >= 3

    def when(condition, *actions):
        @pl.when(condition)
        def _():
            for action in actions:
                action()

    starts, waits = [load.start for load in loads], [load.wait for load in loads]
    if step == 1:
        when(early, *starts, *waits)
    when(mine & both & ~early, *starts)

    @pl.when(mine)
    def _():
        stack_fronts(blocks, owners, planes, per_layer, stacked, 0)
        solve(first_inverse, stacked, solved, 0)

    @pl.when(mine & both)
    def _():
        stack_fronts(blocks, owners, planes, per_layer, stacked, 1)
        when(~early, waits[0])
        out = product(second_inverse[0], stacked[0])
        when(~early, waits[1])
        store_solved(solved, 1, out + product(second_inverse[1], stacked[1]))

    @pl.when(mine)
    def _():
        rhs_a, rhs_b = split(packet[0:rows, :]), split(packet[rows:2 * rows, :])
        first_res = rhs_a
        if step:
            first_res = minus(rhs_a, scaled(row_of(small, FWD), read_field(incoming, count)))
        first = gather_lanes(
            split(solved[0]), place[0:1, :], scaled(row_of(small, ISC), first_res)
        )
        second_res = minus(rhs_b, scaled(row_of(small, FWD + 1), first))
        second = gather_lanes(
            split(solved[1]), place[1:2, :], scaled(row_of(small, ISC + 1), second_res)
        )
        if final:
            z = scaled(row_of(small, BWD), choose(both, second, [jnp.zeros_like(c) for c in first]))
            chunks = gather_lanes(rounded(z), picks(small, PICK, width))
            write_front(front, chunks, [jnp.zeros_like(c) for c in chunks])
        else:
            outgoing = choose(both, second, first)
            chunks = forward_front(after.at[0:rows], after.at[rows:rows + NEEDS], outgoing)
            write_front(front, chunks)
            write_front(outgoing_packet, chunks, outgoing)
        write_field(kept.at[0], first)
        write_field(kept.at[1], second)


def backward_kernel(
    step, sections, planes, width, per_layer, owners, layers, first_inverse, second_inverse,
    packet, place, *rest
):
    blocks, rest = rest[:len(owners)], rest[len(owners):]
    kept, *rest = rest
    last = step == sections - 1
    if not last:
        incoming, before, *rest = rest
    if step:
        behind, *rest = rest
        held, *rest = rest
    result, *rest = rest
    if step:
        front, outgoing_packet, *rest = rest
    stacked, solved = rest
    own = lax.axis_index("sweep")
    count = kept.shape[-1] // LANES
    small = packet.at[2 * kept.shape[1]:]
    mine = own == step
    both = two_layers(layers, step)

    def whole_solve(layer):
        stack_fronts(blocks, owners, planes, per_layer, stacked, layer)
        solve((first_inverse, second_inverse)[layer], stacked, solved, layer)

    if not last:
        @pl.when(own != step)
        def _():
            result[...] = before[...]

        @pl.when(mine & both)
        def _():
            whole_solve(1)

    @pl.when(mine & both if last else mine)
    def _():
        whole_solve(0)

    @pl.when(mine)
    def _():
        first_fwd, second_fwd = split(kept[0]), split(kept[1])
        zero = [jnp.zeros_like(c) for c in first_fwd]
        if last:
            second, arriving = second_fwd, zero
        else:
            arriving = read_field(incoming, count)
            z = scaled(row_of(small, BWD + 1), arriving)
            local = scaled(row_of(small, ISC + 1), z)
            second = minus(second_fwd, gather_lanes(split(solved[1]), place[1:2, :], local))
        following = choose(both, second, arriving)
        z = scaled(row_of(small, BWD), following)
        local = scaled(row_of(small, ISC), z)
        change = gather_lanes(split(solved[0]), place[0:1, :], local)
        if last:
            change = choose(both, change, zero)
        first = minus(first_fwd, change)
        if step:
            chunks = backward_front(
                behind.at[kept.shape[1]:kept.shape[1] + NEEDS], first, read_field(held, count), two_layers(layers, step - 1)
            )
            write_front(front, chunks)
            write_front(outgoing_packet, chunks, first)
        write_field(result.at[0], first)
        write_field(result.at[1], choose(both, second, zero))


def whole(space=pltpu.VMEM):
    return pl.BlockSpec(memory_space=space)


def call(kernel, operands, outs, scratch, name, in_place=(), aliases={}):
    outs = [jax.ShapeDtypeStruct(*o) if isinstance(o, tuple) else o for o in outs]
    specs = [whole(pltpu.SMEM if o.ndim == 1 else pltpu.VMEM) for o in operands]
    for at in in_place:
        specs[at] = whole(pltpu.HBM)
    return pl.pallas_call(
        kernel,
        in_specs=specs,
        out_specs=[whole(pltpu.SMEM if len(o.shape) == 1 else pltpu.VMEM) for o in outs],
        out_shape=outs,
        scratch_shapes=scratch,
        input_output_aliases=aliases,
        compiler_params=pltpu.CompilerParams(vmem_limit_bytes=8 * 2**20),
        name=name,
    )(*operands)


def in_hbm(array):
    return pltpu.with_memory_space_constraint(array, pltpu.HBM)


def shards(
    rhs_field,
    front_inverse,
    interior_scale,
    forward_coupling,
    backward_coupling,
    front_cells,
    section_layers,
):
    sections, planes = lax.axis_size("sweep"), lax.axis_size("plane")
    layer_slots, parts, columns, cells = rhs_field.shape
    rows = parts * columns
    owned, order = front_inverse.shape[2:]
    width = -(-owned // LANES) * LANES
    per_layer = width // LANES
    chips = planes // CORES
    direct = planes in (2, 4, 8) and owned == width

    rhs = rhs_field.reshape(layer_slots, rows, cells)
    picked = jnp.pad(front_cells, ((0, 0), (0, width - owned)), constant_values=-1)
    layers = section_layers

    front_shape = ((2 * per_layer, rows, LANES), BF16)
    packet_shape = ((2 * per_layer + cells // LANES, rows, LANES), BF16)
    layers_shape = ((layer_slots, rows, cells), F32)
    scratch = [
        pltpu.VMEM((2, rows, order), BF16),
        pltpu.VMEM((2, rows, width), F32),
    ]

    def send(block, links, *flips):
        route = []
        for i, j in links:
            for own in range(planes):
                flip = flips[own % len(flips)] or (i == j and planes % CORES == 0)
                route.append((i * planes + own, j * planes + (own ^ int(flip))))
        return lax.ppermute(block, ("sweep", "plane"), route)

    inside = [(i, i) for i in range(sections)]

    def cycle(*members):
        links = list(zip(members, members[1:] + members[:1]))
        return links + [(i, i) for i in range(sections) if i not in members]

    def everywhere(front):
        slots = front.shape[0] // per_layer
        gathered = lax.all_gather(front, "plane")
        if owned != width:
            gathered = gathered.reshape(planes, slots, per_layer, rows, LANES)
            gathered = gathered.transpose(1, 3, 0, 2, 4).reshape(slots, rows, planes, width)
            gathered = gathered[..., :owned].reshape(slots, rows, order // LANES, LANES)
            gathered = gathered.transpose(0, 2, 1, 3)
            gathered = gathered.reshape(slots * order // LANES, rows, LANES)
            return [gathered], [[0]], order // LANES
        return [gathered], [list(range(planes))], per_layer

    def spread(front, straight, some, every, join=None, diagonal=None):
        blocks, owners = [straight], [[(0, 0)]]
        for step in [1] if chips == 2 else range(3, chips):
            blocks.append(send(front if diagonal is None else diagonal, some, CORES * step))
            owners.append([(CORES * step, CORES * step)])
        if chips == 4:
            both = jnp.stack([front, send(front, inside, 1)])
            blocks.append(send(both, every, CORES, 2 * CORES))
            owners += [[(CORES + core, 2 * CORES + core) for core in range(CORES)]]
        if join:
            mine = join(blocks)
        else:
            short = [b[:front.shape[0]] if b.ndim == 3 else b for b in blocks]
            mine = jnp.concatenate([b[None] if b.ndim == 3 else b for b in short])
        blocks.append(send(mine, inside, 1))
        owners.append([(one ^ 1, zero ^ 1) for places in owners for zero, one in places])
        return blocks, owners, per_layer

    def within(front, join=None, used=None):
        if not direct:
            return everywhere(front[:used])
        return spread(front[:used], front, inside, inside, join, front)

    def between(front, packet, start, stop):
        if not direct:
            packet = lax.ppermute(packet, "sweep", [(start, stop)])
            return *everywhere(packet[:2 * per_layer]), packet
        ahead_of = 2 * stop - start, 3 * start - 2 * stop, 2 * start - stop
        third = [i for i in ahead_of if 0 <= i < sections]
        some, every = cycle(start, stop, *third[:1]), cycle(start, stop)
        fourth = [i for i in range(sections) if i not in (start, stop, *third[:1])]
        packet = send(packet, cycle(start, stop, *fourth[:1]), 0)
        return *spread(front, packet, some, every), packet

    inverse = in_hbm(front_inverse)
    half_inverse = pltpu.VMEM(front_inverse.shape[1:], BF16)
    coefficients = (interior_scale, forward_coupling, backward_coupling)
    operands = [section_layers, rhs, *coefficients, picked]
    local, ahead, longer, place, front, layers = call(
        functools.partial(first_kernel, width),
        [in_hbm(a) for a in operands],
        [
            ((2 * rows + 8, cells), F32),
            ((rows + NEEDS, 2 * width), F32),
            ((2 * rows + NEEDS, 2 * width), F32),
            ((2, cells), jnp.int32),
            front_shape,
            ((-(-sections // 8) * 8, LANES), jnp.int32),
        ],
        [pltpu.VMEM(a.shape, a.dtype) for a in operands[1:]]
        + [pltpu.SMEM(section_layers.shape, jnp.int32), pltpu.SemaphoreType.DMA((6,))],
        "first_fronts",
        range(6),
    )
    def neighbours(first):
        pairs = [(i, i + 1) for i in range(first, sections - 1, 2)]
        alone = [i for i in range(sections) if not any(i in pair for pair in pairs)]
        return pairs + [(j, i) for i, j in pairs] + [(i, i) for i in alone]

    near = [send(ahead, neighbours(0), 0, 0), None]
    first_inverse, second_inverse, token = call(
        load_kernel,
        [inverse],
        [half_inverse, half_inverse, ((8, LANES), F32)],
        [pltpu.SemaphoreType.DMA((1,))],
        "load_first",
        [0],
    )

    def join(blocks):
        shape = (sum(b.shape[0] if b.ndim == 4 else 1 for b in blocks), *front_shape[0])
        return call(join_kernel, [*blocks, near[0], token], [(shape, BF16)], [], "join")[0]

    gathered, owners, slots = within(front, join)

    near[1] = send(longer, neighbours(1), 0)
    kept, held = [], [None]
    for step in range(sections):
        final = step == sections - 1
        extra = ([held[step]] if step else []) + ([] if final else [near[step % 2]])
        outs = [layers_shape, front_shape]
        outs += [] if final else [packet_shape]
        outs += [half_inverse]
        outs = call(
            functools.partial(
                forward_kernel, step, sections, planes, width, slots, owners
            ),
            [layers, first_inverse, second_inverse, inverse, local, place, *gathered, *extra],
            outs,
            scratch + [pltpu.SemaphoreType.DMA((2,))],
            f"forward_section_{step}",
            [3],
            {2: len(outs) - 1},
        )
        second_inverse = outs[-1]
        kept.append(outs[0])
        if final:
            gathered, owners, slots = within(outs[1], used=per_layer)
        else:
            gathered, owners, slots, incoming = between(outs[1], outs[2], step, step + 1)
            held.append(incoming)

    result = incoming = None
    for step in reversed(range(sections)):
        extra = ([] if result is None else [incoming, result]) + ([near[(step - 1) % 2], held[step]] if step else [])
        outs = call(
            functools.partial(
                backward_kernel, step, sections, planes, width, slots, owners
            ),
            [layers, first_inverse, second_inverse, local, place, *gathered, kept[step], *extra],
            [layers_shape] + ([front_shape, packet_shape] if step else []),
            scratch,
            f"backward_section_{step}",
        )
        result = outs[0]
        if step:
            gathered, owners, slots, incoming = between(outs[1], outs[2], step, step - 1)
    return result.reshape(rhs_field.shape)


def solution(mesh):
    in_specs = (
        P("sweep", None, None, "plane"),
        P("sweep", None, "plane", None),
        P("sweep", "plane"),
        P("sweep", "plane"),
        P("sweep", "plane"),
        P("sweep", "plane"),
        P(),
    )
    out_specs = P("sweep", None, None, "plane")
    return jax.shard_map(shards, mesh=mesh, in_specs=in_specs, out_specs=out_specs, check_vma=False)
```

```python
import functools

import jax
import jax.numpy as jnp
from jax import lax
from jax.experimental import pallas as pl
from jax.experimental.pallas import tpu as pltpu
from jax.sharding import PartitionSpec as P

LANES = 128
CORES = 2
ISC, FWD, BWD, PICK = 0, 2, 4, 6
SLOPE, TURN, FOLD, CELL, NEEDS = 0, 1, 2, 3, 8
F32, BF16 = jnp.float32, jnp.bfloat16


def split(field):
    return [field[:, at:at + LANES] for at in range(0, field.shape[1], LANES)]


def gather_lanes(chunks, index, beyond=None):
    result = []
    for place, part in enumerate(split(index)):
        part = jnp.broadcast_to(part, chunks[0].shape)
        lane, chunk = part & (LANES - 1), part >> (LANES.bit_length() - 1)
        total = jnp.zeros(chunks[0].shape, F32) if beyond is None else beyond[place]
        for number, source in enumerate(chunks):
            found = jnp.take_along_axis(source, lane, axis=1, mode="promise_in_bounds")
            total = jnp.where(chunk == number, found, total)
        result.append(total)
    return result


def scaled(row, chunks):
    return [part * chunk for part, chunk in zip(split(row), chunks)]


def minus(left, right):
    return [a - b for a, b in zip(left, right)]


def choose(flag, left, right):
    return [jnp.where(flag, a, b) for a, b in zip(left, right)]


def rounded(chunks):
    return [c.astype(BF16).astype(F32) for c in chunks]


def row_of(ref, at):
    return ref[at:at + 1, :]


def picks(ref, at, width):
    return ref[at:at + 1, :width].astype(jnp.int32)


def halves(row):
    chunks = split(row)
    return chunks[:len(chunks) // 2], chunks[len(chunks) // 2:]


def times(left, right):
    return [a * b for a, b in zip(left, right)]


def plus(left, right):
    return [a + b for a, b in zip(left, right)]


def gathered_at(needs, field):
    cells = needs[CELL:CELL + 1, :].astype(jnp.int32)
    half = cells.shape[1] // 2
    return gather_lanes(field, cells[:, :half]), gather_lanes(field, cells[:, half:])


def forward_front(base, needs, incoming):
    (base_a, base_b), (slope_a, slope_b) = halves(base[...]), halves(row_of(needs, SLOPE))
    at_a, at_b = gathered_at(needs, incoming)
    return minus(base_a, times(slope_a, at_a)) + plus(base_b, times(slope_b, at_b))


def backward_front(needs, incoming, second_fwd, both):
    (turn_a, turn_b), (fold, _) = halves(row_of(needs, TURN)), halves(row_of(needs, FOLD))
    at_a, at_b = gathered_at(needs, incoming)
    second_a, _ = gathered_at(needs, second_fwd)
    following = choose(both, minus(second_a, times(fold, at_a)), at_a)
    return times(turn_a, following) + times(turn_b, at_b)


def write_front(ref, chunks, field=()):
    for at, chunk in enumerate([*chunks, *field]):
        ref[at] = chunk.astype(BF16)


def read_field(packet, count):
    start = packet.shape[0] - count
    return [packet[start + i].astype(F32) for i in range(count)]


def write_field(ref, chunks):
    for at, chunk in enumerate(chunks):
        ref[:, at * LANES:(at + 1) * LANES] = chunk


def owner_of(place, planes):
    if isinstance(place, int):
        return place
    own = lax.axis_index("plane")
    return lax.bitwise_xor(own, jnp.where(lax.rem(own, CORES) == 0, place[0], place[1]))


def stack_fronts(blocks, owners, planes, per_layer, stacked, layer):
    for ref, places in zip(blocks, owners):
        for number, place in enumerate(places):
            owner = owner_of(place, planes)
            for i in range(per_layer):
                at = pl.multiple_of((owner * per_layer + i) * LANES, LANES)
                slot = layer * per_layer + i
                piece = ref[slot] if len(ref.shape) == 3 else ref[number, slot]
                half = piece.shape[0] // 2
                wide = piece.astype(F32)
                turned = jnp.concatenate([-wide[half:], wide[:half]], axis=0)
                stacked[0, :, pl.ds(at, LANES)] = piece
                stacked[1, :, pl.ds(at, LANES)] = turned.astype(BF16)


def product(matrix, columns):
    return lax.dot_general(
        columns, matrix, (((1,), (1,)), ((), ())), preferred_element_type=F32
    )


def store_solved(solved, layer, out):
    rows = out.shape[1]
    if rows % LANES:
        out = jnp.concatenate([out, jnp.zeros((out.shape[0], -rows % LANES), F32)], axis=1)
    solved[layer] = out


def solve(inverse, stacked, solved, layer):
    out = product(inverse[0], stacked[0]) + product(inverse[1], stacked[1])
    store_solved(solved, layer, out)


def places(picked, cells):
    rows = picked.shape[1]
    column = jnp.broadcast_to(picked.astype(F32), (8, rows)).T[:, 0:1].astype(jnp.int32)
    cell = lax.broadcasted_iota(jnp.int32, (rows, cells), 1)
    row = lax.broadcasted_iota(jnp.int32, (rows, cells), 0)
    return jnp.max(jnp.where(column == cell, row, -1), axis=0, keepdims=True)


def first_kernel(
    width, layers_in, rhs_in, isc_in, fwd_in, bwd_in, picked_in, local, ahead, longer, place, front,
    layers, rhs, isc, fwd, bwd, picked, counts, sems,
):
    pairs = (
        (rhs_in, rhs), (isc_in, isc), (fwd_in, fwd), (bwd_in, bwd), (picked_in, picked),
        (layers_in, counts),
    )
    copies = [pltpu.make_async_copy(a, b, sems.at[i]) for i, (a, b) in enumerate(pairs)]
    for copy in copies:
        copy.start()
    for copy in copies:
        copy.wait()
    cells = rhs.shape[-1]
    count = rhs.shape[1]
    layers[...] = jnp.zeros(layers.shape, jnp.int32)
    for section in range(counts.shape[0]):
        layers[section:section + 1, :] = jnp.full((1, LANES), counts[section], jnp.int32)
    small = local.at[2 * count:]
    small[ISC:ISC + 2, :] = isc[...]
    small[FWD:FWD + 2, :] = fwd[...]
    small[BWD:BWD + 2, :] = bwd[...]
    small[PICK:PICK + 2, :] = jnp.full((2, cells), -1, F32)
    small[PICK:PICK + 2, :width] = picked[...].astype(F32)
    local[0:count, :] = rhs[0]
    local[count:2 * count, :] = rhs[1]

    at_a, at_b = picked[0:1, :], picked[1:2, :]
    isc_a, isc_b, fwd_a, fwd_b, bwd_a, bwd_b = (
        split(jnp.broadcast_to(row_of(small, at), (8, cells))) for at in range(PICK)
    )
    base_a = gather_lanes(split(rhs[0]), at_a)
    fed = times(fwd_b, isc_a)
    base_b = gather_lanes(
        minus(split(rhs[1]), [f[0:1] * r for f, r in zip(fed, split(rhs[0]))]), at_b
    )
    write_front(front, base_a + base_b)
    zero = [jnp.zeros((8, LANES), F32)] * (width // LANES)
    rows = {
        SLOPE: gather_lanes(fwd_a, at_a) + gather_lanes(times(fed, fwd_a), at_b),
        TURN: gather_lanes(bwd_a, at_a) + gather_lanes(bwd_b, at_b),
        FOLD: gather_lanes(times(isc_b, bwd_b), at_a) + zero,
        CELL: split(at_a.astype(F32)) + split(at_b.astype(F32)),
    }
    ahead[count:, :] = jnp.zeros((NEEDS, ahead.shape[1]), F32)
    for at, chunks in rows.items():
        for i, chunk in enumerate(chunks):
            ahead[count + at:count + at + 1, i * LANES:(i + 1) * LANES] = chunk[0:1]
    write_field(ahead.at[0:count], base_a + base_b)
    longer[0:ahead.shape[0], :] = ahead[...]
    longer[ahead.shape[0]:, :] = jnp.zeros((longer.shape[0] - ahead.shape[0], longer.shape[1]), F32)
    for layer in range(2):
        place[layer:layer + 1, :] = places(picked[layer:layer + 1, :], cells)


def load_kernel(inverse, first, second, done, sem):
    load = pltpu.make_async_copy(inverse.at[0], first, sem.at[0])
    load.start()
    done[...] = jnp.zeros(done.shape, F32)
    second[:, 0:16, 0:LANES] = jnp.zeros((2, 16, LANES), BF16)
    load.wait()


def join_kernel(*refs):
    *blocks, _, _, joined = refs
    at = 0
    for block in blocks:
        for piece in [block] if len(block.shape) == 3 else [block.at[i] for i in range(block.shape[0])]:
            joined[at] = piece[...]
            at += 1


def two_layers(layers, section):
    return jnp.max(layers[section:section + 1, :]) == 2


def forward_kernel(
    step, sections, planes, width, per_layer, owners, layers, first_inverse, _, inverse, packet,
    place, *rest
):
    blocks, rest = rest[:len(owners)], rest[len(owners):]
    final = step == sections - 1
    if step:
        incoming, *rest = rest
    if not final:
        after, *rest = rest
    kept, front, *rest = rest
    if not final:
        outgoing_packet, *rest = rest
    second_inverse, stacked, solved, sems = rest
    own = lax.axis_index("sweep")
    cells = packet.shape[-1]
    count = cells // LANES
    rows = kept.shape[1]
    small = packet.at[2 * rows:]
    mine = own == step
    both = two_layers(layers, step)

    loads = [
        pltpu.make_async_copy(inverse.at[1, part], second_inverse.at[part], sems.at[part])
        for part in range(2)
    ]
    early = own >= 3

    def when(condition, *actions):
        @pl.when(condition)
        def _():
            for action in actions:
                action()

    starts, waits = [load.start for load in loads], [load.wait for load in loads]
    if step == 1:
        when(early, *starts, *waits)
    when(mine & both & ~early, *starts)

    @pl.when(mine)
    def _():
        stack_fronts(blocks, owners, planes, per_layer, stacked, 0)
        solve(first_inverse, stacked, solved, 0)

    @pl.when(mine & both)
    def _():
        stack_fronts(blocks, owners, planes, per_layer, stacked, 1)
        when(~early, waits[0])
        out = product(second_inverse[0], stacked[0])
        when(~early, waits[1])
        store_solved(solved, 1, out + product(second_inverse[1], stacked[1]))

    @pl.when(mine)
    def _():
        rhs_a, rhs_b = split(packet[0:rows, :]), split(packet[rows:2 * rows, :])
        first_res = rhs_a
        if step:
            first_res = minus(rhs_a, scaled(row_of(small, FWD), read_field(incoming, count)))
        first = gather_lanes(
            split(solved[0]), place[0:1, :], scaled(row_of(small, ISC), first_res)
        )
        second_res = minus(rhs_b, scaled(row_of(small, FWD + 1), first))
        second = gather_lanes(
            split(solved[1]), place[1:2, :], scaled(row_of(small, ISC + 1), second_res)
        )
        if final:
            z = scaled(row_of(small, BWD), choose(both, second, [jnp.zeros_like(c) for c in first]))
            chunks = gather_lanes(rounded(z), picks(small, PICK, width))
            write_front(front, chunks, [jnp.zeros_like(c) for c in chunks])
        else:
            outgoing = choose(both, second, first)
            chunks = forward_front(after.at[0:rows], after.at[rows:rows + NEEDS], outgoing)
            write_front(front, chunks)
            write_front(outgoing_packet, chunks, outgoing)
        write_field(kept.at[0], first)
        write_field(kept.at[1], second)


def backward_kernel(
    step, sections, planes, width, per_layer, owners, layers, first_inverse, second_inverse,
    packet, place, *rest
):
    blocks, rest = rest[:len(owners)], rest[len(owners):]
    kept, *rest = rest
    last = step == sections - 1
    if not last:
        incoming, before, *rest = rest
    if step:
        behind, *rest = rest
        held, *rest = rest
    result, *rest = rest
    if step:
        front, outgoing_packet, *rest = rest
    stacked, solved = rest
    own = lax.axis_index("sweep")
    count = kept.shape[-1] // LANES
    small = packet.at[2 * kept.shape[1]:]
    mine = own == step
    both = two_layers(layers, step)

    def whole_solve(layer):
        stack_fronts(blocks, owners, planes, per_layer, stacked, layer)
        solve((first_inverse, second_inverse)[layer], stacked, solved, layer)

    if not last:
        @pl.when(own != step)
        def _():
            result[...] = before[...]

        @pl.when(mine & both)
        def _():
            whole_solve(1)

    @pl.when(mine & both if last else mine)
    def _():
        whole_solve(0)

    @pl.when(mine)
    def _():
        first_fwd, second_fwd = split(kept[0]), split(kept[1])
        zero = [jnp.zeros_like(c) for c in first_fwd]
        if last:
            second, arriving = second_fwd, zero
        else:
            arriving = read_field(incoming, count)
            z = scaled(row_of(small, BWD + 1), arriving)
            local = scaled(row_of(small, ISC + 1), z)
            second = minus(second_fwd, gather_lanes(split(solved[1]), place[1:2, :], local))
        following = choose(both, second, arriving)
        z = scaled(row_of(small, BWD), following)
        local = scaled(row_of(small, ISC), z)
        change = gather_lanes(split(solved[0]), place[0:1, :], local)
        if last:
            change = choose(both, change, zero)
        first = minus(first_fwd, change)
        if step:
            chunks = backward_front(
                behind.at[kept.shape[1]:kept.shape[1] + NEEDS], first, read_field(held, count), two_layers(layers, step - 1)
            )
            write_front(front, chunks)
            write_front(outgoing_packet, chunks, first)
        write_field(result.at[0], first)
        write_field(result.at[1], choose(both, second, zero))


def whole(space=pltpu.VMEM):
    return pl.BlockSpec(memory_space=space)


def call(kernel, operands, outs, scratch, name, in_place=(), aliases={}):
    outs = [jax.ShapeDtypeStruct(*o) if isinstance(o, tuple) else o for o in outs]
    specs = [whole(pltpu.SMEM if o.ndim == 1 else pltpu.VMEM) for o in operands]
    for at in in_place:
        specs[at] = whole(pltpu.HBM)
    return pl.pallas_call(
        kernel,
        in_specs=specs,
        out_specs=[whole(pltpu.SMEM if len(o.shape) == 1 else pltpu.VMEM) for o in outs],
        out_shape=outs,
        scratch_shapes=scratch,
        input_output_aliases=aliases,
        compiler_params=pltpu.CompilerParams(vmem_limit_bytes=8 * 2**20),
        name=name,
    )(*operands)


def in_hbm(array):
    return pltpu.with_memory_space_constraint(array, pltpu.HBM)


def shards(
    rhs_field,
    front_inverse,
    interior_scale,
    forward_coupling,
    backward_coupling,
    front_cells,
    section_layers,
):
    sections, planes = lax.axis_size("sweep"), lax.axis_size("plane")
    layer_slots, parts, columns, cells = rhs_field.shape
    rows = parts * columns
    owned, order = front_inverse.shape[2:]
    width = -(-owned // LANES) * LANES
    per_layer = width // LANES
    chips = planes // CORES
    direct = planes in (2, 4, 8) and owned == width

    rhs = rhs_field.reshape(layer_slots, rows, cells)
    picked = jnp.pad(front_cells, ((0, 0), (0, width - owned)), constant_values=-1)
    layers = section_layers

    front_shape = ((2 * per_layer, rows, LANES), BF16)
    packet_shape = ((2 * per_layer + cells // LANES, rows, LANES), BF16)
    layers_shape = ((layer_slots, rows, cells), F32)
    scratch = [
        pltpu.VMEM((2, rows, order), BF16),
        pltpu.VMEM((2, rows, width), F32),
    ]

    def send(block, links, *flips):
        route = []
        for i, j in links:
            for own in range(planes):
                flip = flips[own % len(flips)] or (i == j and planes % CORES == 0)
                route.append((i * planes + own, j * planes + (own ^ int(flip))))
        return lax.ppermute(block, ("sweep", "plane"), route)

    inside = [(i, i) for i in range(sections)]

    def cycle(*members):
        links = list(zip(members, members[1:] + members[:1]))
        return links + [(i, i) for i in range(sections) if i not in members]

    def everywhere(front):
        slots = front.shape[0] // per_layer
        gathered = lax.all_gather(front, "plane")
        if owned != width:
            gathered = gathered.reshape(planes, slots, per_layer, rows, LANES)
            gathered = gathered.transpose(1, 3, 0, 2, 4).reshape(slots, rows, planes, width)
            gathered = gathered[..., :owned].reshape(slots, rows, order // LANES, LANES)
            gathered = gathered.transpose(0, 2, 1, 3)
            gathered = gathered.reshape(slots * order // LANES, rows, LANES)
            return [gathered], [[0]], order // LANES
        return [gathered], [list(range(planes))], per_layer

    def spread(front, straight, some, every, join=None, diagonal=None):
        blocks, owners = [straight], [[(0, 0)]]
        for step in [1] if chips == 2 else range(3, chips):
            blocks.append(send(front if diagonal is None else diagonal, some, CORES * step))
            owners.append([(CORES * step, CORES * step)])
        if chips == 4:
            both = jnp.stack([front, send(front, inside, 1)])
            blocks.append(send(both, every, CORES, 2 * CORES))
            owners += [[(CORES + core, 2 * CORES + core) for core in range(CORES)]]
        if join:
            mine = join(blocks)
        else:
            short = [b[:front.shape[0]] if b.ndim == 3 else b for b in blocks]
            mine = jnp.concatenate([b[None] if b.ndim == 3 else b for b in short])
        blocks.append(send(mine, inside, 1))
        owners.append([(one ^ 1, zero ^ 1) for places in owners for zero, one in places])
        return blocks, owners, per_layer

    def within(front, join=None, used=None):
        if not direct:
            return everywhere(front[:used])
        return spread(front[:used], front, inside, inside, join, front)

    def between(front, packet, start, stop):
        if not direct:
            packet = lax.ppermute(packet, "sweep", [(start, stop)])
            return *everywhere(packet[:2 * per_layer]), packet
        ahead_of = 2 * stop - start, 3 * start - 2 * stop, 2 * start - stop
        third = [i for i in ahead_of if 0 <= i < sections]
        some, every = cycle(start, stop, *third[:1]), cycle(start, stop)
        packet = send(packet, every, 0)
        return *spread(front, packet, some, every), packet

    inverse = in_hbm(front_inverse)
    half_inverse = pltpu.VMEM(front_inverse.shape[1:], BF16)
    coefficients = (interior_scale, forward_coupling, backward_coupling)
    operands = [section_layers, rhs, *coefficients, picked]
    local, ahead, longer, place, front, layers = call(
        functools.partial(first_kernel, width),
        [in_hbm(a) for a in operands],
        [
            ((2 * rows + 8, cells), F32),
            ((rows + NEEDS, 2 * width), F32),
            ((2 * rows + NEEDS, 2 * width), F32),
            ((2, cells), jnp.int32),
            front_shape,
            ((-(-sections // 8) * 8, LANES), jnp.int32),
        ],
        [pltpu.VMEM(a.shape, a.dtype) for a in operands[1:]]
        + [pltpu.SMEM(section_layers.shape, jnp.int32), pltpu.SemaphoreType.DMA((6,))],
        "first_fronts",
        range(6),
    )
    def neighbours(first):
        pairs = [(i, i + 1) for i in range(first, sections - 1, 2)]
        alone = [i for i in range(sections) if not any(i in pair for pair in pairs)]
        return pairs + [(j, i) for i, j in pairs] + [(i, i) for i in alone]

    near = [send(ahead, neighbours(0), 0, 0), None]
    first_inverse, second_inverse, token = call(
        load_kernel,
        [inverse],
        [half_inverse, half_inverse, ((8, LANES), F32)],
        [pltpu.SemaphoreType.DMA((1,))],
        "load_first",
        [0],
    )

    def join(blocks):
        shape = (sum(b.shape[0] if b.ndim == 4 else 1 for b in blocks), *front_shape[0])
        return call(join_kernel, [*blocks, near[0], token], [(shape, BF16)], [], "join")[0]

    gathered, owners, slots = within(front, join)

    near[1] = send(longer, neighbours(1), 0)
    kept, held = [], [None]
    for step in range(sections):
        final = step == sections - 1
        extra = ([held[step]] if step else []) + ([] if final else [near[step % 2]])
        outs = [layers_shape, front_shape]
        outs += [] if final else [packet_shape]
        outs += [half_inverse]
        outs = call(
            functools.partial(
                forward_kernel, step, sections, planes, width, slots, owners
            ),
            [layers, first_inverse, second_inverse, inverse, local, place, *gathered, *extra],
            outs,
            scratch + [pltpu.SemaphoreType.DMA((2,))],
            f"forward_section_{step}",
            [3],
            {2: len(outs) - 1},
        )
        second_inverse = outs[-1]
        kept.append(outs[0])
        if final:
            gathered, owners, slots = within(outs[1], used=per_layer)
        else:
            gathered, owners, slots, incoming = between(outs[1], outs[2], step, step + 1)
            held.append(incoming)

    result = incoming = None
    for step in reversed(range(sections)):
        extra = ([] if result is None else [incoming, result]) + ([near[(step - 1) % 2], held[step]] if step else [])
        outs = call(
            functools.partial(
                backward_kernel, step, sections, planes, width, slots, owners
            ),
            [layers, first_inverse, second_inverse, local, place, *gathered, kept[step], *extra],
            [layers_shape] + ([front_shape, packet_shape] if step else []),
            scratch,
            f"backward_section_{step}",
        )
        result = outs[0]
        if step:
            gathered, owners, slots, incoming = between(outs[1], outs[2], step, step - 1)
    return result.reshape(rhs_field.shape)


def solution(mesh):
    in_specs = (
        P("sweep", None, None, "plane"),
        P("sweep", None, "plane", None),
        P("sweep", "plane"),
        P("sweep", "plane"),
        P("sweep", "plane"),
        P("sweep", "plane"),
        P(),
    )
    out_specs = P("sweep", None, None, "plane")
    return jax.shard_map(shards, mesh=mesh, in_specs=in_specs, out_specs=out_specs, check_vma=False)
```

```python
import functools

import jax
import jax.numpy as jnp
from jax import lax
from jax.experimental import pallas as pl
from jax.experimental.pallas import tpu as pltpu
from jax.sharding import PartitionSpec as P

LANES = 128
CORES = 2
ISC, FWD, BWD, PICK = 0, 2, 4, 6
SLOPE, TURN, FOLD, CELL, NEEDS = 0, 1, 2, 3, 8
F32, BF16 = jnp.float32, jnp.bfloat16


def split(field):
    return [field[:, at:at + LANES] for at in range(0, field.shape[1], LANES)]


def gather_lanes(chunks, index, beyond=None):
    result = []
    for place, part in enumerate(split(index)):
        part = jnp.broadcast_to(part, chunks[0].shape)
        lane, chunk = part & (LANES - 1), part >> (LANES.bit_length() - 1)
        total = jnp.zeros(chunks[0].shape, F32) if beyond is None else beyond[place]
        for number, source in enumerate(chunks):
            found = jnp.take_along_axis(source, lane, axis=1, mode="promise_in_bounds")
            total = jnp.where(chunk == number, found, total)
        result.append(total)
    return result


def scaled(row, chunks):
    return [part * chunk for part, chunk in zip(split(row), chunks)]


def minus(left, right):
    return [a - b for a, b in zip(left, right)]


def choose(flag, left, right):
    return [jnp.where(flag, a, b) for a, b in zip(left, right)]


def rounded(chunks):
    return [c.astype(BF16).astype(F32) for c in chunks]


def row_of(ref, at):
    return ref[at:at + 1, :]


def picks(ref, at, width):
    return ref[at:at + 1, :width].astype(jnp.int32)


def halves(row):
    chunks = split(row)
    return chunks[:len(chunks) // 2], chunks[len(chunks) // 2:]


def times(left, right):
    return [a * b for a, b in zip(left, right)]


def plus(left, right):
    return [a + b for a, b in zip(left, right)]


def gathered_at(needs, field):
    cells = needs[CELL:CELL + 1, :].astype(jnp.int32)
    half = cells.shape[1] // 2
    return gather_lanes(field, cells[:, :half]), gather_lanes(field, cells[:, half:])


def forward_front(base, needs, incoming):
    (base_a, base_b), (slope_a, slope_b) = halves(base[...]), halves(row_of(needs, SLOPE))
    at_a, at_b = gathered_at(needs, incoming)
    return minus(base_a, times(slope_a, at_a)) + plus(base_b, times(slope_b, at_b))


def backward_front(needs, incoming, second_fwd, both):
    (turn_a, turn_b), (fold, _) = halves(row_of(needs, TURN)), halves(row_of(needs, FOLD))
    at_a, at_b = gathered_at(needs, incoming)
    second_a, _ = gathered_at(needs, second_fwd)
    following = choose(both, minus(second_a, times(fold, at_a)), at_a)
    return times(turn_a, following) + times(turn_b, at_b)


def write_front(ref, chunks, field=()):
    for at, chunk in enumerate([*chunks, *field]):
        ref[at] = chunk.astype(BF16)


def read_field(packet, count):
    start = packet.shape[0] - count
    return [packet[start + i].astype(F32) for i in range(count)]


def write_field(ref, chunks):
    for at, chunk in enumerate(chunks):
        ref[:, at * LANES:(at + 1) * LANES] = chunk


def owner_of(place, planes):
    if isinstance(place, int):
        return place
    own = lax.axis_index("plane")
    return lax.bitwise_xor(own, jnp.where(lax.rem(own, CORES) == 0, place[0], place[1]))


def stack_fronts(blocks, owners, planes, per_layer, stacked, layer):
    for ref, places in zip(blocks, owners):
        for number, place in enumerate(places):
            owner = owner_of(place, planes)
            for i in range(per_layer):
                at = pl.multiple_of((owner * per_layer + i) * LANES, LANES)
                slot = layer * per_layer + i
                piece = ref[slot] if len(ref.shape) == 3 else ref[number, slot]
                half = piece.shape[0] // 2
                wide = piece.astype(F32)
                turned = jnp.concatenate([-wide[half:], wide[:half]], axis=0)
                stacked[0, :, pl.ds(at, LANES)] = piece
                stacked[1, :, pl.ds(at, LANES)] = turned.astype(BF16)


def product(matrix, columns):
    return lax.dot_general(
        columns, matrix, (((1,), (1,)), ((), ())), preferred_element_type=F32
    )


def store_solved(solved, layer, out):
    rows = out.shape[1]
    if rows % LANES:
        out = jnp.concatenate([out, jnp.zeros((out.shape[0], -rows % LANES), F32)], axis=1)
    solved[layer] = out


def solve(inverse, stacked, solved, layer):
    out = product(inverse[0], stacked[0]) + product(inverse[1], stacked[1])
    store_solved(solved, layer, out)


def places(picked, cells):
    rows = picked.shape[1]
    column = jnp.broadcast_to(picked.astype(F32), (8, rows)).T[:, 0:1].astype(jnp.int32)
    cell = lax.broadcasted_iota(jnp.int32, (rows, cells), 1)
    row = lax.broadcasted_iota(jnp.int32, (rows, cells), 0)
    return jnp.max(jnp.where(column == cell, row, -1), axis=0, keepdims=True)


def first_kernel(
    width, layers_in, rhs_in, isc_in, fwd_in, bwd_in, picked_in, local, ahead, longer, front,
    layers, rhs, isc, fwd, bwd, picked, counts, sems,
):
    pairs = (
        (rhs_in, rhs), (isc_in, isc), (fwd_in, fwd), (bwd_in, bwd), (picked_in, picked),
        (layers_in, counts),
    )
    copies = [pltpu.make_async_copy(a, b, sems.at[i]) for i, (a, b) in enumerate(pairs)]
    for copy in copies:
        copy.start()
    for copy in copies:
        copy.wait()
    cells = rhs.shape[-1]
    count = rhs.shape[1]
    layers[...] = jnp.zeros(layers.shape, jnp.int32)
    for section in range(counts.shape[0]):
        layers[section:section + 1, :] = jnp.full((1, LANES), counts[section], jnp.int32)
    small = local.at[2 * count:]
    small[ISC:ISC + 2, :] = isc[...]
    small[FWD:FWD + 2, :] = fwd[...]
    small[BWD:BWD + 2, :] = bwd[...]
    small[PICK:PICK + 2, :] = jnp.full((2, cells), -1, F32)
    small[PICK:PICK + 2, :width] = picked[...].astype(F32)
    local[0:count, :] = rhs[0]
    local[count:2 * count, :] = rhs[1]

    at_a, at_b = picked[0:1, :], picked[1:2, :]
    isc_a, isc_b, fwd_a, fwd_b, bwd_a, bwd_b = (
        split(jnp.broadcast_to(row_of(small, at), (8, cells))) for at in range(PICK)
    )
    base_a = gather_lanes(split(rhs[0]), at_a)
    fed = times(fwd_b, isc_a)
    base_b = gather_lanes(
        minus(split(rhs[1]), [f[0:1] * r for f, r in zip(fed, split(rhs[0]))]), at_b
    )
    write_front(front, base_a + base_b)
    zero = [jnp.zeros((8, LANES), F32)] * (width // LANES)
    rows = {
        SLOPE: gather_lanes(fwd_a, at_a) + gather_lanes(times(fed, fwd_a), at_b),
        TURN: gather_lanes(bwd_a, at_a) + gather_lanes(bwd_b, at_b),
        FOLD: gather_lanes(times(isc_b, bwd_b), at_a) + zero,
        CELL: split(at_a.astype(F32)) + split(at_b.astype(F32)),
    }
    ahead[count:, :] = jnp.zeros((NEEDS, ahead.shape[1]), F32)
    for at, chunks in rows.items():
        for i, chunk in enumerate(chunks):
            ahead[count + at:count + at + 1, i * LANES:(i + 1) * LANES] = chunk[0:1]
    write_field(ahead.at[0:count], base_a + base_b)
    longer[0:ahead.shape[0], :] = ahead[...]
    longer[ahead.shape[0]:, :] = jnp.zeros((longer.shape[0] - ahead.shape[0], longer.shape[1]), F32)


def load_kernel(width, inverse, local, first, second, place, done, sem):
    load = pltpu.make_async_copy(inverse.at[0], first, sem.at[0])
    load.start()
    done[...] = jnp.zeros(done.shape, F32)
    second[:, 0:16, 0:LANES] = jnp.zeros((2, 16, LANES), BF16)
    small = local.at[local.shape[0] - 8:]
    for layer in range(2):
        place[layer:layer + 1, :] = places(picks(small, PICK + layer, width), local.shape[1])
    load.wait()


def join_kernel(*refs):
    *blocks, _, _, joined = refs
    at = 0
    for block in blocks:
        for piece in [block] if len(block.shape) == 3 else [block.at[i] for i in range(block.shape[0])]:
            joined[at] = piece[...]
            at += 1


def two_layers(layers, section):
    return jnp.max(layers[section:section + 1, :]) == 2


def forward_kernel(
    step, sections, planes, width, per_layer, owners, layers, first_inverse, _, inverse, packet,
    place, *rest
):
    blocks, rest = rest[:len(owners)], rest[len(owners):]
    final = step == sections - 1
    if step:
        incoming, *rest = rest
    if not final:
        after, *rest = rest
    kept, front, *rest = rest
    if not final:
        outgoing_packet, *rest = rest
    second_inverse, stacked, solved, sems = rest
    own = lax.axis_index("sweep")
    cells = packet.shape[-1]
    count = cells // LANES
    rows = kept.shape[1]
    small = packet.at[2 * rows:]
    mine = own == step
    both = two_layers(layers, step)

    loads = [
        pltpu.make_async_copy(inverse.at[1, part], second_inverse.at[part], sems.at[part])
        for part in range(2)
    ]
    early = own >= 3

    def when(condition, *actions):
        @pl.when(condition)
        def _():
            for action in actions:
                action()

    starts, waits = [load.start for load in loads], [load.wait for load in loads]
    if step == 1:
        when(early, *starts, *waits)
    when(mine & both & ~early, *starts)

    @pl.when(mine)
    def _():
        stack_fronts(blocks, owners, planes, per_layer, stacked, 0)
        solve(first_inverse, stacked, solved, 0)

    @pl.when(mine & both)
    def _():
        stack_fronts(blocks, owners, planes, per_layer, stacked, 1)
        when(~early, waits[0])
        out = product(second_inverse[0], stacked[0])
        when(~early, waits[1])
        store_solved(solved, 1, out + product(second_inverse[1], stacked[1]))

    @pl.when(mine)
    def _():
        rhs_a, rhs_b = split(packet[0:rows, :]), split(packet[rows:2 * rows, :])
        first_res = rhs_a
        if step:
            first_res = minus(rhs_a, scaled(row_of(small, FWD), read_field(incoming, count)))
        first = gather_lanes(
            split(solved[0]), place[0:1, :], scaled(row_of(small, ISC), first_res)
        )
        second_res = minus(rhs_b, scaled(row_of(small, FWD + 1), first))
        second = gather_lanes(
            split(solved[1]), place[1:2, :], scaled(row_of(small, ISC + 1), second_res)
        )
        if final:
            z = scaled(row_of(small, BWD), choose(both, second, [jnp.zeros_like(c) for c in first]))
            chunks = gather_lanes(rounded(z), picks(small, PICK, width))
            write_front(front, chunks, [jnp.zeros_like(c) for c in chunks])
        else:
            outgoing = choose(both, second, first)
            chunks = forward_front(after.at[0:rows], after.at[rows:rows + NEEDS], outgoing)
            write_front(front, chunks)
            write_front(outgoing_packet, chunks, outgoing)
        write_field(kept.at[0], first)
        write_field(kept.at[1], second)


def backward_kernel(
    step, sections, planes, width, per_layer, owners, layers, first_inverse, second_inverse,
    packet, place, *rest
):
    blocks, rest = rest[:len(owners)], rest[len(owners):]
    kept, *rest = rest
    last = step == sections - 1
    if not last:
        incoming, before, *rest = rest
    if step:
        behind, *rest = rest
        held, *rest = rest
    result, *rest = rest
    if step:
        front, outgoing_packet, *rest = rest
    stacked, solved = rest
    own = lax.axis_index("sweep")
    count = kept.shape[-1] // LANES
    small = packet.at[2 * kept.shape[1]:]
    mine = own == step
    both = two_layers(layers, step)

    def whole_solve(layer):
        stack_fronts(blocks, owners, planes, per_layer, stacked, layer)
        solve((first_inverse, second_inverse)[layer], stacked, solved, layer)

    if not last:
        @pl.when(own != step)
        def _():
            result[...] = before[...]

        @pl.when(mine & both)
        def _():
            whole_solve(1)

    @pl.when(mine & both if last else mine)
    def _():
        whole_solve(0)

    @pl.when(mine)
    def _():
        first_fwd, second_fwd = split(kept[0]), split(kept[1])
        zero = [jnp.zeros_like(c) for c in first_fwd]
        if last:
            second, arriving = second_fwd, zero
        else:
            arriving = read_field(incoming, count)
            z = scaled(row_of(small, BWD + 1), arriving)
            local = scaled(row_of(small, ISC + 1), z)
            second = minus(second_fwd, gather_lanes(split(solved[1]), place[1:2, :], local))
        following = choose(both, second, arriving)
        z = scaled(row_of(small, BWD), following)
        local = scaled(row_of(small, ISC), z)
        change = gather_lanes(split(solved[0]), place[0:1, :], local)
        if last:
            change = choose(both, change, zero)
        first = minus(first_fwd, change)
        if step:
            chunks = backward_front(
                behind.at[kept.shape[1]:kept.shape[1] + NEEDS], first, read_field(held, count), two_layers(layers, step - 1)
            )
            write_front(front, chunks)
            write_front(outgoing_packet, chunks, first)
        write_field(result.at[0], first)
        write_field(result.at[1], choose(both, second, zero))


def whole(space=pltpu.VMEM):
    return pl.BlockSpec(memory_space=space)


def call(kernel, operands, outs, scratch, name, in_place=(), aliases={}):
    outs = [jax.ShapeDtypeStruct(*o) if isinstance(o, tuple) else o for o in outs]
    specs = [whole(pltpu.SMEM if o.ndim == 1 else pltpu.VMEM) for o in operands]
    for at in in_place:
        specs[at] = whole(pltpu.HBM)
    return pl.pallas_call(
        kernel,
        in_specs=specs,
        out_specs=[whole(pltpu.SMEM if len(o.shape) == 1 else pltpu.VMEM) for o in outs],
        out_shape=outs,
        scratch_shapes=scratch,
        input_output_aliases=aliases,
        compiler_params=pltpu.CompilerParams(vmem_limit_bytes=8 * 2**20),
        name=name,
    )(*operands)


def in_hbm(array):
    return pltpu.with_memory_space_constraint(array, pltpu.HBM)


def shards(
    rhs_field,
    front_inverse,
    interior_scale,
    forward_coupling,
    backward_coupling,
    front_cells,
    section_layers,
):
    sections, planes = lax.axis_size("sweep"), lax.axis_size("plane")
    layer_slots, parts, columns, cells = rhs_field.shape
    rows = parts * columns
    owned, order = front_inverse.shape[2:]
    width = -(-owned // LANES) * LANES
    per_layer = width // LANES
    chips = planes // CORES
    direct = planes in (2, 4, 8) and owned == width

    rhs = rhs_field.reshape(layer_slots, rows, cells)
    picked = jnp.pad(front_cells, ((0, 0), (0, width - owned)), constant_values=-1)
    layers = section_layers

    front_shape = ((2 * per_layer, rows, LANES), BF16)
    packet_shape = ((2 * per_layer + cells // LANES, rows, LANES), BF16)
    layers_shape = ((layer_slots, rows, cells), F32)
    scratch = [
        pltpu.VMEM((2, rows, order), BF16),
        pltpu.VMEM((2, rows, width), F32),
    ]

    def send(block, links, *flips):
        route = []
        for i, j in links:
            for own in range(planes):
                flip = flips[own % len(flips)] or (i == j and planes % CORES == 0)
                route.append((i * planes + own, j * planes + (own ^ int(flip))))
        return lax.ppermute(block, ("sweep", "plane"), route)

    inside = [(i, i) for i in range(sections)]

    def cycle(*members):
        links = list(zip(members, members[1:] + members[:1]))
        return links + [(i, i) for i in range(sections) if i not in members]

    def everywhere(front):
        slots = front.shape[0] // per_layer
        gathered = lax.all_gather(front, "plane")
        if owned != width:
            gathered = gathered.reshape(planes, slots, per_layer, rows, LANES)
            gathered = gathered.transpose(1, 3, 0, 2, 4).reshape(slots, rows, planes, width)
            gathered = gathered[..., :owned].reshape(slots, rows, order // LANES, LANES)
            gathered = gathered.transpose(0, 2, 1, 3)
            gathered = gathered.reshape(slots * order // LANES, rows, LANES)
            return [gathered], [[0]], order // LANES
        return [gathered], [list(range(planes))], per_layer

    def spread(front, straight, some, every, join=None, diagonal=None):
        blocks, owners = [straight], [[(0, 0)]]
        for step in [1] if chips == 2 else range(3, chips):
            blocks.append(send(front if diagonal is None else diagonal, some, CORES * step))
            owners.append([(CORES * step, CORES * step)])
        if chips == 4:
            both = jnp.stack([front, send(front, inside, 1)])
            blocks.append(send(both, every, CORES, 2 * CORES))
            owners += [[(CORES + core, 2 * CORES + core) for core in range(CORES)]]
        if join:
            mine = join(blocks)
        else:
            short = [b[:front.shape[0]] if b.ndim == 3 else b for b in blocks]
            mine = jnp.concatenate([b[None] if b.ndim == 3 else b for b in short])
        blocks.append(send(mine, inside, 1))
        owners.append([(one ^ 1, zero ^ 1) for places in owners for zero, one in places])
        return blocks, owners, per_layer

    def within(front, join=None, used=None):
        if not direct:
            return everywhere(front[:used])
        return spread(front[:used], front, inside, inside, join, front)

    def between(front, packet, start, stop):
        if not direct:
            packet = lax.ppermute(packet, "sweep", [(start, stop)])
            return *everywhere(packet[:2 * per_layer]), packet
        ahead_of = 2 * stop - start, 3 * start - 2 * stop, 2 * start - stop
        third = [i for i in ahead_of if 0 <= i < sections]
        some, every = cycle(start, stop, *third[:1]), cycle(start, stop)
        packet = send(packet, every, 0)
        return *spread(front, packet, some, every), packet

    inverse = in_hbm(front_inverse)
    half_inverse = pltpu.VMEM(front_inverse.shape[1:], BF16)
    coefficients = (interior_scale, forward_coupling, backward_coupling)
    operands = [section_layers, rhs, *coefficients, picked]
    local, ahead, longer, front, layers = call(
        functools.partial(first_kernel, width),
        [in_hbm(a) for a in operands],
        [
            ((2 * rows + 8, cells), F32),
            ((rows + NEEDS, 2 * width), F32),
            ((2 * rows + NEEDS, 2 * width), F32),
            front_shape,
            ((-(-sections // 8) * 8, LANES), jnp.int32),
        ],
        [pltpu.VMEM(a.shape, a.dtype) for a in operands[1:]]
        + [pltpu.SMEM(section_layers.shape, jnp.int32), pltpu.SemaphoreType.DMA((6,))],
        "first_fronts",
        range(6),
    )
    def neighbours(first):
        pairs = [(i, i + 1) for i in range(first, sections - 1, 2)]
        alone = [i for i in range(sections) if not any(i in pair for pair in pairs)]
        return pairs + [(j, i) for i, j in pairs] + [(i, i) for i in alone]

    near = [send(ahead, neighbours(0), 0, 0), None]
    first_inverse, second_inverse, place, token = call(
        functools.partial(load_kernel, width),
        [inverse, local],
        [half_inverse, half_inverse, ((2, cells), jnp.int32), ((8, LANES), F32)],
        [pltpu.SemaphoreType.DMA((1,))],
        "load_first",
        [0],
    )

    def join(blocks):
        shape = (sum(b.shape[0] if b.ndim == 4 else 1 for b in blocks), *front_shape[0])
        return call(join_kernel, [*blocks, near[0], token], [(shape, BF16)], [], "join")[0]

    gathered, owners, slots = within(front, join)

    near[1] = send(longer, neighbours(1), 0)
    kept, held = [], [None]
    for step in range(sections):
        final = step == sections - 1
        extra = ([held[step]] if step else []) + ([] if final else [near[step % 2]])
        outs = [layers_shape, front_shape]
        outs += [] if final else [packet_shape]
        outs += [half_inverse]
        outs = call(
            functools.partial(
                forward_kernel, step, sections, planes, width, slots, owners
            ),
            [layers, first_inverse, second_inverse, inverse, local, place, *gathered, *extra],
            outs,
            scratch + [pltpu.SemaphoreType.DMA((2,))],
            f"forward_section_{step}",
            [3],
            {2: len(outs) - 1},
        )
        second_inverse = outs[-1]
        kept.append(outs[0])
        if final:
            gathered, owners, slots = within(outs[1], used=per_layer)
        else:
            gathered, owners, slots, incoming = between(outs[1], outs[2], step, step + 1)
            held.append(incoming)

    result = incoming = None
    for step in reversed(range(sections)):
        extra = ([] if result is None else [incoming, result]) + ([near[(step - 1) % 2], held[step]] if step else [])
        outs = call(
            functools.partial(
                backward_kernel, step, sections, planes, width, slots, owners
            ),
            [layers, first_inverse, second_inverse, local, place, *gathered, kept[step], *extra],
            [layers_shape] + ([front_shape, packet_shape] if step else []),
            scratch,
            f"backward_section_{step}",
        )
        result = outs[0]
        if step:
            gathered, owners, slots, incoming = between(outs[1], outs[2], step, step - 1)
    return result.reshape(rhs_field.shape)


def solution(mesh):
    in_specs = (
        P("sweep", None, None, "plane"),
        P("sweep", None, "plane", None),
        P("sweep", "plane"),
        P("sweep", "plane"),
        P("sweep", "plane"),
        P("sweep", "plane"),
        P(),
    )
    out_specs = P("sweep", None, None, "plane")
    return jax.shard_map(shards, mesh=mesh, in_specs=in_specs, out_specs=out_specs, check_vma=False)
```

```python
import functools

import jax
import jax.numpy as jnp
from jax import lax
from jax.experimental import pallas as pl
from jax.experimental.pallas import tpu as pltpu
from jax.sharding import PartitionSpec as P

LANES = 128
CORES = 2
ISC, FWD, BWD, PICK = 0, 2, 4, 6
SLOPE, TURN, FOLD, CELL, NEEDS = 0, 1, 2, 3, 8
F32, BF16 = jnp.float32, jnp.bfloat16


def split(field):
    return [field[:, at:at + LANES] for at in range(0, field.shape[1], LANES)]


def gather_lanes(chunks, index, beyond=None):
    result = []
    for place, part in enumerate(split(index)):
        part = jnp.broadcast_to(part, chunks[0].shape)
        lane, chunk = part & (LANES - 1), part >> (LANES.bit_length() - 1)
        total = jnp.zeros(chunks[0].shape, F32) if beyond is None else beyond[place]
        for number, source in enumerate(chunks):
            found = jnp.take_along_axis(source, lane, axis=1, mode="promise_in_bounds")
            total = jnp.where(chunk == number, found, total)
        result.append(total)
    return result


def scaled(row, chunks):
    return [part * chunk for part, chunk in zip(split(row), chunks)]


def minus(left, right):
    return [a - b for a, b in zip(left, right)]


def choose(flag, left, right):
    return [jnp.where(flag, a, b) for a, b in zip(left, right)]


def rounded(chunks):
    return [c.astype(BF16).astype(F32) for c in chunks]


def row_of(ref, at):
    return ref[at:at + 1, :]


def picks(ref, at, width):
    return ref[at:at + 1, :width].astype(jnp.int32)


def halves(row):
    chunks = split(row)
    return chunks[:len(chunks) // 2], chunks[len(chunks) // 2:]


def times(left, right):
    return [a * b for a, b in zip(left, right)]


def plus(left, right):
    return [a + b for a, b in zip(left, right)]


def gathered_at(needs, field):
    cells = needs[CELL:CELL + 1, :].astype(jnp.int32)
    half = cells.shape[1] // 2
    return gather_lanes(field, cells[:, :half]), gather_lanes(field, cells[:, half:])


def forward_front(base, needs, incoming):
    (base_a, base_b), (slope_a, slope_b) = halves(base[...]), halves(row_of(needs, SLOPE))
    at_a, at_b = gathered_at(needs, incoming)
    return minus(base_a, times(slope_a, at_a)) + plus(base_b, times(slope_b, at_b))


def backward_front(needs, incoming, second_fwd, both):
    (turn_a, turn_b), (fold, _) = halves(row_of(needs, TURN)), halves(row_of(needs, FOLD))
    at_a, at_b = gathered_at(needs, incoming)
    second_a, _ = gathered_at(needs, second_fwd)
    following = choose(both, minus(second_a, times(fold, at_a)), at_a)
    return times(turn_a, following) + times(turn_b, at_b)


def write_front(ref, chunks, field=()):
    for at, chunk in enumerate([*chunks, *field]):
        ref[at] = chunk.astype(BF16)


def read_field(packet, count):
    start = packet.shape[0] - count
    return [packet[start + i].astype(F32) for i in range(count)]


def write_field(ref, chunks):
    for at, chunk in enumerate(chunks):
        ref[:, at * LANES:(at + 1) * LANES] = chunk


def owner_of(place, planes):
    if isinstance(place, int):
        return place
    own = lax.axis_index("plane")
    return lax.bitwise_xor(own, jnp.where(lax.rem(own, CORES) == 0, place[0], place[1]))


def stack_fronts(blocks, owners, planes, per_layer, stacked, layer):
    for ref, places in zip(blocks, owners):
        for number, place in enumerate(places):
            owner = owner_of(place, planes)
            for i in range(per_layer):
                at = pl.multiple_of((owner * per_layer + i) * LANES, LANES)
                slot = layer * per_layer + i
                piece = ref[slot] if len(ref.shape) == 3 else ref[number, slot]
                half = piece.shape[0] // 2
                wide = piece.astype(F32)
                turned = jnp.concatenate([-wide[half:], wide[:half]], axis=0)
                stacked[0, :, pl.ds(at, LANES)] = piece
                stacked[1, :, pl.ds(at, LANES)] = turned.astype(BF16)


def product(matrix, columns):
    return lax.dot_general(
        columns, matrix, (((1,), (1,)), ((), ())), preferred_element_type=F32
    )


def store_solved(solved, layer, out):
    rows = out.shape[1]
    if rows % LANES:
        out = jnp.concatenate([out, jnp.zeros((out.shape[0], -rows % LANES), F32)], axis=1)
    solved[layer] = out


def solve(inverse, stacked, solved, layer):
    out = product(inverse[0], stacked[0]) + product(inverse[1], stacked[1])
    store_solved(solved, layer, out)


def places(picked, cells):
    rows = picked.shape[1]
    column = jnp.broadcast_to(picked.astype(F32), (8, rows)).T[:, 0:1].astype(jnp.int32)
    cell = lax.broadcasted_iota(jnp.int32, (rows, cells), 1)
    row = lax.broadcasted_iota(jnp.int32, (rows, cells), 0)
    return jnp.max(jnp.where(column == cell, row, -1), axis=0, keepdims=True)


def first_kernel(
    width, layers_in, rhs_in, isc_in, fwd_in, bwd_in, picked_in, local, ahead, longer, front,
    layers, rhs, isc, fwd, bwd, picked, counts, sems,
):
    pairs = (
        (rhs_in, rhs), (isc_in, isc), (fwd_in, fwd), (bwd_in, bwd), (picked_in, picked),
        (layers_in, counts),
    )
    copies = [pltpu.make_async_copy(a, b, sems.at[i]) for i, (a, b) in enumerate(pairs)]
    for copy in copies:
        copy.start()
    for copy in copies:
        copy.wait()
    cells = rhs.shape[-1]
    count = rhs.shape[1]
    layers[...] = jnp.zeros(layers.shape, jnp.int32)
    for section in range(counts.shape[0]):
        layers[section:section + 1, :] = jnp.full((1, LANES), counts[section], jnp.int32)
    small = local.at[2 * count:]
    small[ISC:ISC + 2, :] = isc[...]
    small[FWD:FWD + 2, :] = fwd[...]
    small[BWD:BWD + 2, :] = bwd[...]
    small[PICK:PICK + 2, :] = jnp.full((2, cells), -1, F32)
    small[PICK:PICK + 2, :width] = picked[...].astype(F32)
    local[0:count, :] = rhs[0]
    local[count:2 * count, :] = rhs[1]

    at_a, at_b = picked[0:1, :], picked[1:2, :]
    isc_a, isc_b, fwd_a, fwd_b, bwd_a, bwd_b = (
        split(jnp.broadcast_to(row_of(small, at), (8, cells))) for at in range(PICK)
    )
    base_a = gather_lanes(split(rhs[0]), at_a)
    fed = times(fwd_b, isc_a)
    base_b = gather_lanes(
        minus(split(rhs[1]), [f[0:1] * r for f, r in zip(fed, split(rhs[0]))]), at_b
    )
    write_front(front, base_a + base_b)
    zero = [jnp.zeros((8, LANES), F32)] * (width // LANES)
    rows = {
        SLOPE: gather_lanes(fwd_a, at_a) + gather_lanes(times(fed, fwd_a), at_b),
        TURN: gather_lanes(bwd_a, at_a) + gather_lanes(bwd_b, at_b),
        FOLD: gather_lanes(times(isc_b, bwd_b), at_a) + zero,
        CELL: split(at_a.astype(F32)) + split(at_b.astype(F32)),
    }
    ahead[count:, :] = jnp.zeros((NEEDS, ahead.shape[1]), F32)
    for at, chunks in rows.items():
        for i, chunk in enumerate(chunks):
            ahead[count + at:count + at + 1, i * LANES:(i + 1) * LANES] = chunk[0:1]
    write_field(ahead.at[0:count], base_a + base_b)
    longer[0:ahead.shape[0], :] = ahead[...]
    longer[ahead.shape[0]:, :] = jnp.zeros((longer.shape[0] - ahead.shape[0], longer.shape[1]), F32)


def load_kernel(width, inverse, local, first, second, place, done, sem):
    load = pltpu.make_async_copy(inverse.at[0], first, sem.at[0])
    load.start()
    done[...] = jnp.zeros(done.shape, F32)
    second[:, 0:16, 0:LANES] = jnp.zeros((2, 16, LANES), BF16)
    small = local.at[local.shape[0] - 8:]
    for layer in range(2):
        place[layer:layer + 1, :] = places(picks(small, PICK + layer, width), local.shape[1])
    load.wait()


def join_kernel(*refs):
    *blocks, _, _, joined = refs
    at = 0
    for block in blocks:
        for piece in [block] if len(block.shape) == 3 else [block.at[i] for i in range(block.shape[0])]:
            joined[at] = piece[...]
            at += 1


def two_layers(layers, section):
    return jnp.max(layers[section:section + 1, :]) == 2


def forward_kernel(
    step, sections, planes, width, per_layer, owners, layers, first_inverse, _, inverse, packet,
    place, *rest
):
    blocks, rest = rest[:len(owners)], rest[len(owners):]
    final = step == sections - 1
    if step:
        incoming, *rest = rest
    if not final:
        after, *rest = rest
    kept, front, *rest = rest
    if not final:
        outgoing_packet, *rest = rest
    second_inverse, stacked, solved, sems = rest
    own = lax.axis_index("sweep")
    cells = packet.shape[-1]
    count = cells // LANES
    rows = kept.shape[1]
    small = packet.at[2 * rows:]
    mine = own == step
    both = two_layers(layers, step)

    loads = [
        pltpu.make_async_copy(inverse.at[1, part], second_inverse.at[part], sems.at[part])
        for part in range(2)
    ]
    early = jnp.bool_(step >= 3)
    if step in (1, 2):
        early = two_layers(layers, step - 1)

    def when(condition, *actions):
        @pl.when(condition)
        def _():
            for action in actions:
                action()

    starts, waits = [load.start for load in loads], [load.wait for load in loads]
    if step == 1:
        when(own >= 3, *starts, *waits)
    if step < 2 and not final:
        ahead = (own == step + 1) & two_layers(layers, step + 1)
        when(ahead & both, *starts, *waits)
    when(mine & both & ~early, *starts)

    @pl.when(mine)
    def _():
        stack_fronts(blocks, owners, planes, per_layer, stacked, 0)
        solve(first_inverse, stacked, solved, 0)

    @pl.when(mine & both)
    def _():
        stack_fronts(blocks, owners, planes, per_layer, stacked, 1)
        when(~early, waits[0])
        out = product(second_inverse[0], stacked[0])
        when(~early, waits[1])
        store_solved(solved, 1, out + product(second_inverse[1], stacked[1]))

    @pl.when(mine)
    def _():
        rhs_a, rhs_b = split(packet[0:rows, :]), split(packet[rows:2 * rows, :])
        first_res = rhs_a
        if step:
            first_res = minus(rhs_a, scaled(row_of(small, FWD), read_field(incoming, count)))
        first = gather_lanes(
            split(solved[0]), place[0:1, :], scaled(row_of(small, ISC), first_res)
        )
        second_res = minus(rhs_b, scaled(row_of(small, FWD + 1), first))
        second = gather_lanes(
            split(solved[1]), place[1:2, :], scaled(row_of(small, ISC + 1), second_res)
        )
        if final:
            z = scaled(row_of(small, BWD), choose(both, second, [jnp.zeros_like(c) for c in first]))
            chunks = gather_lanes(rounded(z), picks(small, PICK, width))
            write_front(front, chunks, [jnp.zeros_like(c) for c in chunks])
        else:
            outgoing = choose(both, second, first)
            chunks = forward_front(after.at[0:rows], after.at[rows:rows + NEEDS], outgoing)
            write_front(front, chunks)
            write_front(outgoing_packet, chunks, outgoing)
        write_field(kept.at[0], first)
        write_field(kept.at[1], second)


def backward_kernel(
    step, sections, planes, width, per_layer, owners, layers, first_inverse, second_inverse,
    packet, place, *rest
):
    blocks, rest = rest[:len(owners)], rest[len(owners):]
    kept, *rest = rest
    last = step == sections - 1
    if not last:
        incoming, before, *rest = rest
    if step:
        behind, *rest = rest
        held, *rest = rest
    result, *rest = rest
    if step:
        front, outgoing_packet, *rest = rest
    stacked, solved = rest
    own = lax.axis_index("sweep")
    count = kept.shape[-1] // LANES
    small = packet.at[2 * kept.shape[1]:]
    mine = own == step
    both = two_layers(layers, step)

    def whole_solve(layer):
        stack_fronts(blocks, owners, planes, per_layer, stacked, layer)
        solve((first_inverse, second_inverse)[layer], stacked, solved, layer)

    if not last:
        @pl.when(own != step)
        def _():
            result[...] = before[...]

        @pl.when(mine & both)
        def _():
            whole_solve(1)

    @pl.when(mine & both if last else mine)
    def _():
        whole_solve(0)

    @pl.when(mine)
    def _():
        first_fwd, second_fwd = split(kept[0]), split(kept[1])
        zero = [jnp.zeros_like(c) for c in first_fwd]
        if last:
            second, arriving = second_fwd, zero
        else:
            arriving = read_field(incoming, count)
            z = scaled(row_of(small, BWD + 1), arriving)
            local = scaled(row_of(small, ISC + 1), z)
            second = minus(second_fwd, gather_lanes(split(solved[1]), place[1:2, :], local))
        following = choose(both, second, arriving)
        z = scaled(row_of(small, BWD), following)
        local = scaled(row_of(small, ISC), z)
        change = gather_lanes(split(solved[0]), place[0:1, :], local)
        if last:
            change = choose(both, change, zero)
        first = minus(first_fwd, change)
        if step:
            chunks = backward_front(
                behind.at[kept.shape[1]:kept.shape[1] + NEEDS], first, read_field(held, count), two_layers(layers, step - 1)
            )
            write_front(front, chunks)
            write_front(outgoing_packet, chunks, first)
        write_field(result.at[0], first)
        write_field(result.at[1], choose(both, second, zero))


def whole(space=pltpu.VMEM):
    return pl.BlockSpec(memory_space=space)


def call(kernel, operands, outs, scratch, name, in_place=(), aliases={}):
    outs = [jax.ShapeDtypeStruct(*o) if isinstance(o, tuple) else o for o in outs]
    specs = [whole(pltpu.SMEM if o.ndim == 1 else pltpu.VMEM) for o in operands]
    for at in in_place:
        specs[at] = whole(pltpu.HBM)
    return pl.pallas_call(
        kernel,
        in_specs=specs,
        out_specs=[whole(pltpu.SMEM if len(o.shape) == 1 else pltpu.VMEM) for o in outs],
        out_shape=outs,
        scratch_shapes=scratch,
        input_output_aliases=aliases,
        compiler_params=pltpu.CompilerParams(vmem_limit_bytes=8 * 2**20),
        name=name,
    )(*operands)


def in_hbm(array):
    return pltpu.with_memory_space_constraint(array, pltpu.HBM)


def shards(
    rhs_field,
    front_inverse,
    interior_scale,
    forward_coupling,
    backward_coupling,
    front_cells,
    section_layers,
):
    sections, planes = lax.axis_size("sweep"), lax.axis_size("plane")
    layer_slots, parts, columns, cells = rhs_field.shape
    rows = parts * columns
    owned, order = front_inverse.shape[2:]
    width = -(-owned // LANES) * LANES
    per_layer = width // LANES
    chips = planes // CORES
    direct = planes in (2, 4, 8) and owned == width

    rhs = rhs_field.reshape(layer_slots, rows, cells)
    picked = jnp.pad(front_cells, ((0, 0), (0, width - owned)), constant_values=-1)
    layers = section_layers

    front_shape = ((2 * per_layer, rows, LANES), BF16)
    packet_shape = ((2 * per_layer + cells // LANES, rows, LANES), BF16)
    layers_shape = ((layer_slots, rows, cells), F32)
    scratch = [
        pltpu.VMEM((2, rows, order), BF16),
        pltpu.VMEM((2, rows, width), F32),
    ]

    def send(block, links, *flips):
        route = []
        for i, j in links:
            for own in range(planes):
                flip = flips[own % len(flips)] or (i == j and planes % CORES == 0)
                route.append((i * planes + own, j * planes + (own ^ int(flip))))
        return lax.ppermute(block, ("sweep", "plane"), route)

    inside = [(i, i) for i in range(sections)]

    def cycle(*members):
        links = list(zip(members, members[1:] + members[:1]))
        return links + [(i, i) for i in range(sections) if i not in members]

    def everywhere(front):
        slots = front.shape[0] // per_layer
        gathered = lax.all_gather(front, "plane")
        if owned != width:
            gathered = gathered.reshape(planes, slots, per_layer, rows, LANES)
            gathered = gathered.transpose(1, 3, 0, 2, 4).reshape(slots, rows, planes, width)
            gathered = gathered[..., :owned].reshape(slots, rows, order // LANES, LANES)
            gathered = gathered.transpose(0, 2, 1, 3)
            gathered = gathered.reshape(slots * order // LANES, rows, LANES)
            return [gathered], [[0]], order // LANES
        return [gathered], [list(range(planes))], per_layer

    def spread(front, straight, some, every, join=None, diagonal=None):
        blocks, owners = [straight], [[(0, 0)]]
        for step in [1] if chips == 2 else range(3, chips):
            blocks.append(send(front if diagonal is None else diagonal, some, CORES * step))
            owners.append([(CORES * step, CORES * step)])
        if chips == 4:
            both = jnp.stack([front, send(front, inside, 1)])
            blocks.append(send(both, every, CORES, 2 * CORES))
            owners += [[(CORES + core, 2 * CORES + core) for core in range(CORES)]]
        if join:
            mine = join(blocks)
        else:
            short = [b[:front.shape[0]] if b.ndim == 3 else b for b in blocks]
            mine = jnp.concatenate([b[None] if b.ndim == 3 else b for b in short])
        blocks.append(send(mine, inside, 1))
        owners.append([(one ^ 1, zero ^ 1) for places in owners for zero, one in places])
        return blocks, owners, per_layer

    def within(front, join=None, used=None):
        if not direct:
            return everywhere(front[:used])
        return spread(front[:used], front, inside, inside, join, front)

    def between(front, packet, start, stop):
        if not direct:
            packet = lax.ppermute(packet, "sweep", [(start, stop)])
            return *everywhere(packet[:2 * per_layer]), packet
        ahead_of = 2 * stop - start, 3 * start - 2 * stop, 2 * start - stop
        third = [i for i in ahead_of if 0 <= i < sections]
        some, every = cycle(start, stop, *third[:1]), cycle(start, stop)
        packet = send(packet, every, 0)
        return *spread(front, packet, some, every), packet

    inverse = in_hbm(front_inverse)
    half_inverse = pltpu.VMEM(front_inverse.shape[1:], BF16)
    coefficients = (interior_scale, forward_coupling, backward_coupling)
    operands = [section_layers, rhs, *coefficients, picked]
    local, ahead, longer, front, layers = call(
        functools.partial(first_kernel, width),
        [in_hbm(a) for a in operands],
        [
            ((2 * rows + 8, cells), F32),
            ((rows + NEEDS, 2 * width), F32),
            ((2 * rows + NEEDS, 2 * width), F32),
            front_shape,
            ((-(-sections // 8) * 8, LANES), jnp.int32),
        ],
        [pltpu.VMEM(a.shape, a.dtype) for a in operands[1:]]
        + [pltpu.SMEM(section_layers.shape, jnp.int32), pltpu.SemaphoreType.DMA((6,))],
        "first_fronts",
        range(6),
    )
    def neighbours(first):
        pairs = [(i, i + 1) for i in range(first, sections - 1, 2)]
        alone = [i for i in range(sections) if not any(i in pair for pair in pairs)]
        return pairs + [(j, i) for i, j in pairs] + [(i, i) for i in alone]

    near = [send(ahead, neighbours(0), 0, 0), None]
    first_inverse, second_inverse, place, token = call(
        functools.partial(load_kernel, width),
        [inverse, local],
        [half_inverse, half_inverse, ((2, cells), jnp.int32), ((8, LANES), F32)],
        [pltpu.SemaphoreType.DMA((1,))],
        "load_first",
        [0],
    )

    def join(blocks):
        shape = (sum(b.shape[0] if b.ndim == 4 else 1 for b in blocks), *front_shape[0])
        return call(join_kernel, [*blocks, near[0], token], [(shape, BF16)], [], "join")[0]

    gathered, owners, slots = within(front, join)

    near[1] = send(longer, neighbours(1), 0)
    kept, held = [], [None]
    for step in range(sections):
        final = step == sections - 1
        extra = ([held[step]] if step else []) + ([] if final else [near[step % 2]])
        outs = [layers_shape, front_shape]
        outs += [] if final else [packet_shape]
        outs += [half_inverse]
        outs = call(
            functools.partial(
                forward_kernel, step, sections, planes, width, slots, owners
            ),
            [layers, first_inverse, second_inverse, inverse, local, place, *gathered, *extra],
            outs,
            scratch + [pltpu.SemaphoreType.DMA((2,))],
            f"forward_section_{step}",
            [3],
            {2: len(outs) - 1},
        )
        second_inverse = outs[-1]
        kept.append(outs[0])
        if final:
            gathered, owners, slots = within(outs[1], used=per_layer)
        else:
            gathered, owners, slots, incoming = between(outs[1], outs[2], step, step + 1)
            held.append(incoming)

    result = incoming = None
    for step in reversed(range(sections)):
        extra = ([] if result is None else [incoming, result]) + ([near[(step - 1) % 2], held[step]] if step else [])
        outs = call(
            functools.partial(
                backward_kernel, step, sections, planes, width, slots, owners
            ),
            [layers, first_inverse, second_inverse, local, place, *gathered, kept[step], *extra],
            [layers_shape] + ([front_shape, packet_shape] if step else []),
            scratch,
            f"backward_section_{step}",
        )
        result = outs[0]
        if step:
            gathered, owners, slots, incoming = between(outs[1], outs[2], step, step - 1)
    return result.reshape(rhs_field.shape)


def solution(mesh):
    in_specs = (
        P("sweep", None, None, "plane"),
        P("sweep", None, "plane", None),
        P("sweep", "plane"),
        P("sweep", "plane"),
        P("sweep", "plane"),
        P("sweep", "plane"),
        P(),
    )
    out_specs = P("sweep", None, None, "plane")
    return jax.shard_map(shards, mesh=mesh, in_specs=in_specs, out_specs=out_specs, check_vma=False)
```
